128 devices in a mesh: gx: 8 (over x, core), gy: 16 (over y, z).
Axes of the slice: x: 4, y: 4, z: 4, core: 2. Of those that a mesh axis runs over, the one named last changes fastest.
Arguments:
- ocean_state: float32 [4, 16, 768, 2304], P(None, None, 'gy', 'gx'), may hold values from -8 to 8, as said below
- layer_thickness: float32 [16], replicated, may hold values from 0.05 to 0.3
- vertical_mixing: float32 [768, 2304], P('gy', 'gx'), may hold values from 0.1 to 10
- damping: float32 [768, 2304], P('gy', 'gx'), may hold values from 0.02 to 3
- ocean_blocks: int32 [32, 64], replicated, may hold values from 0 to 1, as said below
Outputs:
- tracer_next: float32 [2, 16, 768, 2304], P(None, None, 'gy', 'gx')
- surface_height: float32 [768, 2304], P('gy', 'gx')
The draws below stay inside these ranges and needn't reach their ends.
Inputs may be any that keep to these rules, and one draw needn't show every extreme that they name: `ocean_state`: the first two components are temperature and salinity, the last two the eastward and northward velocity. `ocean_blocks`: each device's patch of 2 x 8 blocks (latitude rows from j * 2, longitude columns from i * 8, for gy index j and gx index i) holds 3 to 16 ocean blocks; in every draw some patch and the patches on both sides of it along latitude are wholly ocean, and a patch next to that run of three along latitude holds exactly 3.
All inputs are finite; a program needn't handle non-finite values.
Results may differ from the reference program's by a relative error of at most 0.0003.
Values sent between devices are 32-bit elements; how exact they have to be, the bound alone decides.
A program may use at most 64 MiB of HBM per device.

```python
import math
import jax
import jax.numpy as jnp
from jax import lax

BLAT = 24
BLON = 36
BPX = 8
BPY = 2
LEV = 16
ITERS = 4
NBX = 64
NBY = 32
NX = 2304
NY = 768


def draw_ocean_state(key, part):
    key = jax.random.fold_in(key, 5)
    shape = (4, LEV, NY, NX)
    lon_scale = 0.6 * (1.0 + 2.0 * jnp.arange(NX, dtype=jnp.float32) / NX)
    values = jnp.clip(jax.random.normal(key, shape, jnp.float32), -4.0, 4.0)
    return values * lon_scale[None, None, None, :]


def draw_ocean_blocks(key, part):
    key = jax.random.fold_in(key, 11)
    count_key, lon_key, lat_key, score_key = jax.random.split(key, 4)
    lat_groups = NBY // BPY
    lon_groups = NBX // BPX
    patch_size = BPX * BPY
    counts = jax.random.randint(count_key, (lat_groups, lon_groups), 3, patch_size + 1)
    full_lon = jax.random.randint(lon_key, (), 0, lon_groups)
    full_lat = jax.random.randint(lat_key, (), 0, lat_groups - 2)
    lat_index = jnp.arange(lat_groups)[:, None]
    lon_index = jnp.arange(lon_groups)[None, :]
    wholly = (lon_index == full_lon) & (lat_index >= full_lat) & (lat_index < full_lat + 3)
    counts = jnp.where(wholly, patch_size, counts)
    sparse_lat = jnp.where(full_lat >= 1, full_lat - 1, full_lat + 3)
    sparse = (lon_index == full_lon) & (lat_index == sparse_lat)
    counts = jnp.where(sparse, 3, counts)
    scores = jax.random.randint(score_key, (lat_groups, lon_groups, patch_size), 0, 2 ** 20) * patch_size
    scores = scores + jnp.arange(patch_size)[None, None, :]
    ordering = jnp.argsort(scores, axis=-1, stable=True)
    ranking = jnp.argsort(ordering, axis=-1, stable=True)
    ocean = (ranking < counts[:, :, None]).astype(jnp.int32)
    ocean = ocean.reshape(lat_groups, lon_groups, BPY, BPX).transpose(0, 2, 1, 3)
    return ocean.reshape(NBY, NBX)


def block_scale(own_key, dims, pieces, low, top_value):
    loudness = 1.0
    for dim, shards_of in pieces:
        heights = jax.random.uniform(jax.random.fold_in(jax.random.fold_in(own_key, 6), dim), (shards_of,), jnp.float32, low / len(pieces), top_value / len(pieces))
        loudness = loudness * jnp.repeat(jnp.exp(heights), dims[dim] // shards_of).reshape((-1,) + (1,) * (len(dims) - 1 - dim))
    return loudness


def setup_inputs(seed: int = 0) -> dict:
    splits = jax.random.split(jax.random.key(seed), 6)
    return {
        "ocean_state": draw_ocean_state(jax.random.fold_in(splits[5], 71), 0),
        "layer_thickness": jnp.clip(jnp.exp(jax.random.uniform(splits[1], (LEV,), jnp.float32, math.log(0.05), math.log(0.3))), 0.05, 0.3),
        "vertical_mixing": jnp.clip(jnp.exp(math.log(10.0) - 4.6051702 * jax.random.uniform(splits[2], (NY, NX), jnp.float32) ** block_scale(splits[2], (NY, NX), ((0, 16), (1, 8)), -0.2, 0.2)), 0.1, 10.0),
        "damping": jnp.clip(jnp.exp(math.log(3.0) - 5.0106353 * jax.random.uniform(splits[3], (NY, NX), jnp.float32) ** block_scale(splits[3], (NY, NX), ((0, 16), (1, 8)), -0.2, 0.2)), 0.02, 3.0),
        "ocean_blocks": draw_ocean_blocks(jax.random.fold_in(splits[5], 71), 0),
    }


advect_rate = 0.2
diffuse_rate = 0.1
salt_weight = 0.5


def middle(field):
    return field[..., 1:-1, 1:-1]


def eastern(field):
    return field[..., 1:-1, 2:]


def western(field):
    return field[..., 1:-1, :-2]


def northern(field):
    return field[..., 2:, 1:-1]


def southern(field):
    return field[..., :-2, 1:-1]


def horizontal(fields, margin):
    tracers = fields[0:2] * margin
    east_speed = fields[2] * margin
    north_speed = fields[3] * margin
    flux_east = 0.25 * (middle(east_speed) + eastern(east_speed)) * (middle(tracers) + eastern(tracers))
    flux_west = 0.25 * (western(east_speed) + middle(east_speed)) * (western(tracers) + middle(tracers))
    flux_north = 0.25 * (middle(north_speed) + northern(north_speed)) * (middle(tracers) + northern(tracers))
    flux_south = 0.25 * (southern(north_speed) + middle(north_speed)) * (southern(tracers) + middle(tracers))
    advection = flux_east - flux_west + flux_north - flux_south
    diffusion = eastern(tracers) + western(tracers) + northern(tracers) + southern(tracers) - 4.0 * middle(tracers)
    return middle(margin) * (middle(tracers) - advect_rate * advection + diffuse_rate * diffusion)


def vertical_mix(advected, thickness, mixing):
    levels = advected.shape[1]
    coupling = [mixing / (thickness[level] + thickness[level + 1]) for level in range(levels - 1)]
    ratios = []
    values = []
    for level in range(levels):
        below = coupling[level - 1] if level > 0 else 0.0
        above = coupling[level] if level < levels - 1 else 0.0
        diagonal = thickness[level] + below + above
        source = thickness[level] * advected[:, level]
        if level == 0:
            denom = diagonal
            value = source / denom
        else:
            denom = diagonal - below * ratios[-1]
            value = (source + below * values[-1]) / denom
        ratios.append(above / denom)
        values.append(value)
    result = [values[-1]]
    for level in range(levels - 2, -1, -1):
        result.insert(0, values[level] + ratios[level] * result[0])
    return jnp.stack(result, axis=1)


def nine_point(frame, diagonal):
    edges = northern(frame) + southern(frame) + eastern(frame) + western(frame)
    corners = frame[..., 2:, 2:] + frame[..., 2:, :-2] + frame[..., :-2, 2:] + frame[..., :-2, :-2]
    return diagonal * middle(frame) - edges - 0.5 * corners


def wrap_pad(field):
    along = jnp.concatenate([field[..., -1:], field, field[..., :1]], axis=-1)
    zeros = jnp.zeros_like(along[..., :1, :])
    return jnp.concatenate([zeros, along, zeros], axis=-2)


def reference(ocean_state, layer_thickness, vertical_mixing, damping, ocean_blocks):
    mask_cells = jnp.repeat(jnp.repeat(ocean_blocks, BLAT, axis=0), BLON, axis=1).astype(jnp.float32)
    margin = wrap_pad(mask_cells)

    def level_step(level):
        fields = lax.dynamic_index_in_dim(ocean_state, level, axis=1, keepdims=False)
        return horizontal(wrap_pad(fields), margin)

    advected = jnp.transpose(lax.map(level_step, jnp.arange(LEV)), (1, 0, 2, 3))
    tracer_next = vertical_mix(advected, layer_thickness, vertical_mixing)
    forcing = jnp.sum(layer_thickness[:, None, None] * (tracer_next[0] - salt_weight * tracer_next[1]), axis=0)
    diagonal = 6.0 + damping

    def apply_op(field):
        return nine_point(wrap_pad(field), diagonal) * mask_cells

    surface = jnp.zeros_like(forcing)
    residual = forcing
    scaled = residual / diagonal
    direction = scaled
    norm_now = jnp.sum(residual * scaled)
    for iteration in range(ITERS):
        image = apply_op(direction)
        step_size = norm_now / jnp.sum(direction * image)
        surface = surface + step_size * direction
        if iteration + 1 < ITERS:
            residual = residual - step_size * image
            scaled = residual / diagonal
            norm_next = jnp.sum(residual * scaled)
            direction = scaled + (norm_next / norm_now) * direction
            norm_now = norm_next
    return tracer_next, surface
```

```python
import functools

import jax
import jax.numpy as jnp
from jax import lax
from jax.experimental import pallas as pl
from jax.experimental.pallas import tpu as pltpu
from jax.sharding import PartitionSpec as P

BLAT = 24
BLON = 36
LEV = 16
ROWS = 48
COLS = 288
WIDE = 384
EXT = 56
TILES = ROWS // 8

f32 = jnp.float32
MESH = pl.DeviceIdType.MESH

NORTH, SOUTH, EAST, WEST = (0, 1), (0, -1), (1, 0), (-1, 0)
DIAGONAL = ((1, 1), (-1, 1), (1, -1), (-1, -1))


def iota(shape, dim):
    return lax.broadcasted_iota(jnp.int32, shape, dim)


def padded(value):
    return jnp.concatenate([value, jnp.zeros((value.shape[0], WIDE - COLS), f32)], axis=1)


def east_of(value):
    return pltpu.roll(value, WIDE - 1, 1)


def west_of(value):
    return pltpu.roll(value, 1, 1)


def inverse(value):
    guess = pl.reciprocal(value, approx=True)
    return guess * (2.0 - value * guess)


def row_pack(low, high):
    return jnp.where(iota(low.shape, 0) < 4, low, high)


def column_pack(first, last):
    lane = iota(first.shape, 1)
    low = pltpu.roll(first, 32, 1)
    high = pltpu.roll(last, 96, 1)
    return jnp.where(
        (lane >= 32) & (lane < 36), low, jnp.where(lane >= 124, high, 0.0)
    )


def kernel(
    nx,
    ny,
    ocean,
    thick,
    mixing,
    damping,
    blocks,
    tracer_out,
    surface_out,
    state,
    h,
    mix,
    damp,
    blk,
    mask,
    level_inv,
    flat,
    send_rows,
    send_heat,
    recv_rows,
    recv_heat,
    send_cols,
    recv_cols,
    send_corner,
    recv_corner,
    flux_lon,
    flux_north,
    flux_prev,
    ratio,
    scale,
    basis,
    halo_rows,
    halo_cols,
    halo_corner,
    recv_halo_rows,
    recv_halo_cols,
    recv_halo_corner,
    message,
    first_sum,
    second_message,
    second_sum,
    load_sem,
    small_sem,
    send_sem,
    recv_sem,
    halo_send_sem,
    halo_recv_sem,
    sum_send_sem,
    sum_recv_sem,
):
    gx = lax.axis_index("gx")
    gy = lax.axis_index("gy")

    def device(step):
        return {"gx": lax.rem(gx + step[0] + nx, nx), "gy": lax.rem(gy + step[1] + ny, ny)}

    partners = []
    for step in (
        [NORTH, SOUTH, EAST, WEST, *DIAGONAL]
        + [(d, 0) for d in range(1, nx)]
        + [(0, d) for d in range(1, ny)]
    ):
        step = (step[0] % nx, step[1] % ny)
        if step != (0, 0) and step not in partners:
            partners.append(step)

    barrier = pltpu.get_barrier_semaphore()
    for step in partners:
        pl.semaphore_signal(barrier, inc=1, device_id=device(step), device_id_type=MESH)

    small = [
        pltpu.make_async_copy(blocks, blk, small_sem.at[0]),
        pltpu.make_async_copy(thick, h, small_sem.at[1]),
        pltpu.make_async_copy(damping, damp, small_sem.at[2]),
        pltpu.make_async_copy(mixing, mix, small_sem.at[3]),
    ]
    loads = []
    for index, (start, size) in enumerate(((0, 8), (40, 8), (8, 16), (24, 16))):
        rows = pl.ds(start, size)
        loads.append(
            pltpu.make_async_copy(
                ocean.at[:, :, rows, :], state.at[:, :, rows, :], load_sem.at[index]
            )
        )
    for copy in small[:3] + loads + small[3:]:
        copy.start()

    block_rows, block_cols = blk.shape
    small[0].wait()
    row = iota((EXT, block_rows), 0)
    row = gy * ROWS + jnp.where(row < ROWS + 4, row, row - EXT)
    edge = iota((EXT, block_rows), 1) * BLAT
    pick_rows = jnp.where((row >= edge) & (row < edge + BLAT), 1.0, 0.0)
    lane = iota((block_cols, WIDE), 1)
    total = block_cols * BLON
    col = gx * COLS + jnp.where(lane < COLS + 4, lane, lane - WIDE)
    col = jnp.where(col < 0, col + total, jnp.where(col >= total, col - total, col))
    edge = iota((block_cols, WIDE), 0) * BLON
    inside = (lane < COLS + 4) | (lane >= WIDE - 4)
    pick_cols = jnp.where(inside & (col >= edge) & (col < edge + BLON), 1.0, 0.0)
    coarse = jnp.dot(pick_rows, blk[...].astype(f32), preferred_element_type=f32)
    mask[...] = jnp.dot(coarse, pick_cols, preferred_element_type=f32)

    small[1].wait()
    level_inv[...] = jnp.zeros(level_inv.shape, f32)
    for k in range(1, LEV):
        level_inv[k : k + 1, :] = 1.0 / jnp.full((1, WIDE), h[k - 1] + h[k], f32)

    small[2].wait()
    damp_low = padded(damp[0:8, :])
    damp_high = padded(damp[ROWS - 8 : ROWS, :])
    damp_rows = row_pack(damp_low, damp_high)
    for side in range(2):
        send_rows[side, 32:40, :] = damp_rows
    damp_all = padded(damp[...])
    send_cols[ROWS:, :] = column_pack(damp_all[:, 0:128], damp_all[:, 256:384])
    send_corner[...] = column_pack(damp_rows[:, 0:128], damp_rows[:, 256:384])

    def remote(source, target, index, step, sends=send_sem, recvs=recv_sem):
        return pltpu.make_async_remote_copy(
            src_ref=source,
            dst_ref=target,
            send_sem=sends.at[index],
            recv_sem=recvs.at[index],
            device_id=device(step),
            device_id_type=MESH,
        )

    loads[0].wait()
    loads[1].wait()
    pl.semaphore_wait(barrier, len(partners))
    first_round = []
    for side, (edge_row, step) in enumerate(((ROWS - 1, NORTH), (0, SOUTH))):
        edge_mask = mask[edge_row : edge_row + 1, :]
        heat = padded(state[0, :, edge_row, :]) * edge_mask
        salt = padded(state[1, :, edge_row, :]) * edge_mask
        send_heat[side] = heat
        send_rows[side, 0:16, :] = heat - 0.5 * salt
        send_rows[side, 16:32, :] = padded(state[3, :, edge_row, :]) * edge_mask
        copy = remote(send_rows.at[side], recv_rows.at[side], side, step)
        copy.start()
        first_round.append(copy)

    lane128 = iota((8, 128), 1)

    def pack_columns(i, _):
        rows = pl.ds(pl.multiple_of(8 * i, 8), 8)
        edge_mask = jnp.where(lane128 == 31, mask[rows, 256:384], mask[rows, 0:128])
        acc_west = jnp.zeros((8, 128), f32)
        acc_east = jnp.zeros((8, 128), f32)
        for field, base in ((0, 0), (1, 16), (2, 64)):
            for k in range(LEV):
                first = state[field, k, rows, 0:128]
                last = jnp.concatenate(
                    [state[field, k, rows, 256:COLS], jnp.zeros((8, WIDE - COLS), f32)], axis=1
                )
                merged = jnp.where(lane128 == 31, last, first)
                turned = pltpu.roll(merged, base + k, 1) if base + k else merged
                acc_west = jnp.where(lane128 == base + k, turned, acc_west)
                acc_east = jnp.where(lane128 == base + k + 31, turned, acc_east)
        west_mask = jnp.broadcast_to(edge_mask[:, 0:1], (8, 128))
        east_mask = jnp.broadcast_to(edge_mask[:, 31:32], (8, 128))
        send_cols[rows, :] = acc_west * west_mask + pltpu.roll(acc_east, 1, 1) * east_mask
        return 0

    pack_columns(0, 0)
    pack_columns(5, 0)
    loads[2].wait()
    lax.fori_loop(1, 3, pack_columns, 0)
    loads[3].wait()
    lax.fori_loop(3, 5, pack_columns, 0)
    for side, step in enumerate((EAST, WEST)):
        copy = remote(send_cols, recv_cols.at[side], 2 + side, step)
        copy.start()
        first_round.append(copy)
    for place, step in enumerate(DIAGONAL):
        copy = remote(send_corner, recv_corner.at[place], 4 + place, step)
        copy.start()
        first_round.append(copy)
    heat_round = []
    for side, step in enumerate((NORTH, SOUTH)):
        copy = remote(send_heat.at[side], recv_heat.at[side], 8 + side, step)
        copy.start()
        heat_round.append(copy)

    sub = iota((8, WIDE), 0)

    def next_row(i):
        return jnp.minimum(8 * i + 8, ROWS - 1)

    def level_sums(i, _):
        rows = pl.ds(pl.multiple_of(8 * i, 8), 8)
        row = pl.ds(next_row(i), 1)
        here = mask[rows, :]
        beyond = mask[row, :]

        def level(k, carry):
            plain, lon, lat = carry
            s = padded(state[0, k, rows, :] - 0.5 * state[1, k, rows, :]) * here
            u = padded(state[2, k, rows, :]) * here
            v = padded(state[3, k, rows, :]) * here
            s_row = padded(state[0, k, row, :] - 0.5 * state[1, k, row, :]) * beyond
            v_row = padded(state[3, k, row, :]) * beyond
            s_north = jnp.where(sub == 7, s_row, pltpu.roll(s, 7, 0))
            v_north = jnp.where(sub == 7, v_row, pltpu.roll(v, 7, 0))
            weight = 0.05 * h[k]
            plain = plain + h[k] * s
            lon = lon + weight * (u + east_of(u)) * (s + east_of(s))
            lat = lat + weight * (v + v_north) * (s + s_north)
            return plain, lon, lat

        zero = jnp.zeros((8, WIDE), f32)
        plain, lon, lat = lax.fori_loop(0, LEV, level, (zero, zero, zero), unroll=4)
        flat[0, rows, :] = plain
        flat[1, rows, :] = lon
        flat[2, rows, :] = lat
        return 0

    lax.fori_loop(0, TILES, level_sums, 0)

    for copy in first_round:
        copy.wait()

    lane_c = iota((ROWS, 128), 1)
    own = send_cols[0:ROWS, :]
    is_east = (lane_c & 32) != 0
    other = jnp.where(
        is_east,
        pltpu.roll(recv_cols[1, 0:ROWS, :], 32, 1),
        pltpu.roll(recv_cols[0, 0:ROWS, :], 96, 1),
    )
    both = own + other
    speed = pltpu.roll(both, 64, 1)
    speed = jnp.where((lane_c & 16) != 0, pltpu.roll(speed, 16, 1), speed)
    slope = jnp.where(is_east, 0.1, -0.1) * (other - own)
    through = 0.05 * speed * both - slope
    flux_lon[...] = through
    weight = jnp.zeros((1, 128), f32)
    lane_w = iota((1, 128), 1)
    for k in range(LEV):
        weight = jnp.where((lane_w & 15) == k, h[k], weight)
    weight = weight * jnp.where((lane_w & 16) != 0, -0.5, 1.0)
    weighed = through * weight
    side_west = jnp.sum(jnp.where(lane_c < 32, weighed, 0.0), axis=1, keepdims=True)
    side_east = jnp.sum(
        jnp.where(is_east & (lane_c < 64), weighed, 0.0), axis=1, keepdims=True
    )

    level_weight = jnp.zeros((LEV, WIDE), f32)
    level_row = iota((LEV, WIDE), 0)
    for k in range(LEV):
        level_weight = jnp.where(level_row == k, h[k], level_weight)
    exists = (
        jnp.where(gy < ny - 1, 1.0, 0.0).astype(f32),
        jnp.where(gy > 0, 1.0, 0.0).astype(f32),
    )

    def side_flux(mine, theirs, speeds, sign):
        return speeds * (mine + theirs) - (0.1 * sign) * (theirs - mine)

    side_lat = []
    speed_lat = []
    for side, sign in ((0, 1.0), (1, -1.0)):
        slot = 1 - side
        s_mine = send_rows[side, 0:16, :]
        s_theirs = recv_rows[slot, 0:16, :] * exists[side]
        speeds = 0.05 * (send_rows[side, 16:32, :] + recv_rows[slot, 16:32, :] * exists[side])
        speed_lat.append(speeds)
        flux = side_flux(s_mine, s_theirs, speeds, sign)
        side_lat.append(jnp.sum(flux * level_weight, axis=0, keepdims=True))

    def assemble(center, rows_in, cols_in, corner_in):
        lane8 = iota((8, 128), 1)
        lane48 = iota((ROWS, 128), 1)
        third = jnp.where(
            lane48 < 32, center[:, 256:384], jnp.where(lane48 < 64, cols_in(1), cols_in(0))
        )
        upper = jnp.concatenate([center[:, 0:256], third], axis=1)
        north_south = jnp.where(sub < 4, rows_in(1), rows_in(0))
        north = jnp.where(lane8 < 64, corner_in(3), corner_in(2))
        south = jnp.where(lane8 < 64, corner_in(1), corner_in(0))
        corner = jnp.where(iota((8, 128), 0) < 4, north, south)
        third = jnp.where(lane8 < 32, north_south[:, 256:384], corner)
        lower = jnp.concatenate([north_south[:, 0:256], third], axis=1)
        return jnp.concatenate([upper, lower], axis=0)

    damp_ext = assemble(
        damp_all,
        lambda slot: recv_rows[slot, 32:40, :],
        lambda slot: recv_cols[slot, ROWS:, :],
        lambda place: recv_corner[place],
    )
    inv = mask[...] * inverse(6.0 + damp_ext)
    scale[...] = 1.5 * inv

    lane_f = iota((ROWS, WIDE), 1)
    row_f = iota((ROWS, WIDE), 0)
    plain = flat[0]
    lon = flat[1] - 0.1 * (east_of(plain) - plain)
    lon = jnp.where(lane_f == COLS - 1, side_east, jnp.where(lane_f == WIDE - 1, side_west, lon))
    lat = flat[2] - 0.1 * (pltpu.roll(plain, ROWS - 1, 0) - plain)
    lat = jnp.where(row_f == ROWS - 1, side_lat[0], lat)
    lat_south = jnp.where(row_f == 0, side_lat[1], pltpu.roll(lat, 1, 0))
    start = plain - (lon - west_of(lon)) - (lat - lat_south)
    start = jnp.where(lane_f < COLS, start, 0.0) * inv[0:ROWS, :]

    packed_rows = row_pack(start[0:8, :], start[ROWS - 8 : ROWS, :])
    halo_rows[...] = packed_rows
    halo_cols[...] = column_pack(start[:, 0:128], start[:, 256:384])
    halo_corner[...] = column_pack(packed_rows[:, 0:128], packed_rows[:, 256:384])
    second_round = []
    for side, step in enumerate((NORTH, SOUTH)):
        second_round.append(
            remote(halo_rows, recv_halo_rows.at[side], side, step, halo_send_sem, halo_recv_sem)
        )
    for side, step in enumerate((EAST, WEST)):
        second_round.append(
            remote(halo_cols, recv_halo_cols.at[side], 2 + side, step, halo_send_sem, halo_recv_sem)
        )
    for place, step in enumerate(DIAGONAL):
        second_round.append(
            remote(
                halo_corner,
                recv_halo_corner.at[place],
                4 + place,
                step,
                halo_send_sem,
                halo_recv_sem,
            )
        )
    for copy in second_round:
        copy.start()

    for copy in heat_round:
        copy.wait()
    for side, sign in ((0, 1.0), (1, -1.0)):
        slot = 1 - side
        target = flux_north if side == 0 else flux_prev
        heat_mine = send_heat[side]
        heat_theirs = recv_heat[slot] * exists[side]
        salt_mine = 2.0 * (heat_mine - send_rows[side, 0:16, :])
        salt_theirs = 2.0 * (heat_theirs - recv_rows[slot, 0:16, :] * exists[side])
        target[0:16, :] = side_flux(heat_mine, heat_theirs, speed_lat[side], sign)
        target[16:32, :] = side_flux(salt_mine, salt_theirs, speed_lat[side], sign)
    small[3].wait()

    edge_lane = (lane128 == 31) | (lane128 == 127)

    def mix_tile(i, _):
        rows = pl.ds(pl.multiple_of(8 * i, 8), 8)
        row = pl.ds(next_row(i), 1)
        here = mask[rows, :]
        beyond = mask[row, :]
        coefficient = padded(mix[rows, :])
        through = flux_lon[rows, :]
        use_north = (sub == 7) & (i == TILES - 1)

        def level(k, carry):
            ratio_low, heat_low, salt_low = carry
            u = padded(state[2, k, rows, :]) * here
            v = padded(state[3, k, rows, :]) * here
            v_row = padded(state[3, k, row, :]) * beyond
            v_north = jnp.where(sub == 7, v_row, pltpu.roll(v, 7, 0))
            u_pair = 0.05 * (u + east_of(u))
            v_pair = 0.05 * (v + v_north)
            lon_far, lon_near = u_pair - 0.1, u_pair + 0.1
            lat_far, lat_near = v_pair - 0.1, v_pair + 0.1
            below = coefficient * level_inv[pl.ds(k, 1), :]
            above = coefficient * level_inv[pl.ds(k + 1, 1), :]
            pivot = inverse(h[k] + above + below * (1.0 - ratio_low))
            ratio_now = above * pivot
            ratio[k] = ratio_now
            found = []
            for tracer, low in ((0, heat_low), (1, salt_low)):
                plane = tracer * LEV + k
                c = padded(state[tracer, k, rows, :]) * here
                c_row = padded(state[tracer, k, row, :]) * beyond
                c_north = jnp.where(sub == 7, c_row, pltpu.roll(c, 7, 0))
                lon = lon_far * east_of(c) + lon_near * c
                turned = pltpu.roll(through, 127 - plane, 1)
                lon = jnp.concatenate(
                    [lon[:, 0:256], jnp.where(edge_lane, turned, lon[:, 256:384])], axis=1
                )
                lat = lat_far * c_north + lat_near * c
                lat = jnp.where(use_north, flux_north[pl.ds(plane, 1), :], lat)
                lat_south = jnp.where(
                    sub == 0, flux_prev[pl.ds(plane, 1), :], pltpu.roll(lat, 1, 0)
                )
                flux_prev[pl.ds(plane, 1), :] = lat[7:8, :]
                advected = here * (c - (lon - west_of(lon)) - (lat - lat_south))
                value = (h[k] * advected + below * low) * pivot
                tracer_out[tracer, k, rows, :] = value[:, 0:COLS]
                found.append(value)
            return ratio_now, found[0], found[1]

        zero = jnp.zeros((8, WIDE), f32)
        _, heat, salt = lax.fori_loop(0, LEV, level, (zero, zero, zero), unroll=4)

        def back(step, carry):
            k = LEV - 2 - step
            heat_up, salt_up = carry
            share = ratio[k][:, 0:COLS]
            heat_up = tracer_out[0, k, rows, :] + share * heat_up
            salt_up = tracer_out[1, k, rows, :] + share * salt_up
            tracer_out[0, k, rows, :] = heat_up
            tracer_out[1, k, rows, :] = salt_up
            return heat_up, salt_up

        lax.fori_loop(0, LEV - 1, back, (heat[:, 0:COLS], salt[:, 0:COLS]), unroll=5)
        return 0

    lax.fori_loop(0, 2, mix_tile, 0)

    for copy in second_round:
        copy.wait()

    q = assemble(
        start,
        lambda slot: recv_halo_rows[slot],
        lambda slot: recv_halo_cols[slot],
        lambda place: recv_halo_corner[place],
    )
    q = q * mask[...]
    weight = jnp.where(lane_f < COLS, 6.0 + damp_all, 0.0)
    basis[0] = q
    previous = None
    message_rows = []
    for index in range(4):
        pair = east_of(q) + west_of(q)
        column = q + 0.5 * pair
        around = pair + pltpu.roll(column, EXT - 1, 0) + pltpu.roll(column, 1, 0)
        image = scale[...] * around - 0.5 * q
        after = image if previous is None else 2.0 * image - previous
        if index < 3:
            basis[index + 1] = after
        weighed = weight * q[0:ROWS, :]
        message_rows.append(weighed * q[0:ROWS, :])
        message_rows.append(weighed * after[0:ROWS, :])
        previous, q = q, after

    def folded(value):
        value = value[:, 0:128] + value[:, 128:256] + value[:, 256:384]
        return jnp.sum(value, axis=0, keepdims=True)

    message[...] = jnp.concatenate([folded(value) for value in message_rows], axis=0)

    def spread(source, target, count, axis, mine, base):
        target[mine] = source[...]
        copies = []
        for d in range(1, count):
            step = (d, 0) if axis == "gx" else (0, d)
            copies.append(
                pltpu.make_async_remote_copy(
                    src_ref=source,
                    dst_ref=target.at[mine],
                    send_sem=sum_send_sem.at[base],
                    recv_sem=sum_recv_sem.at[base],
                    device_id=device(step),
                    device_id_type=MESH,
                )
            )
        for copy in copies:
            copy.start()

    def gathered(target, count, base):
        part = target.at[pl.ds(0, count - 1)]
        done = pltpu.make_async_remote_copy(
            src_ref=part,
            dst_ref=part,
            send_sem=sum_send_sem.at[base],
            recv_sem=sum_recv_sem.at[base],
            device_id=device(EAST),
            device_id_type=MESH,
        )
        done.wait_recv()
        done.wait_send()
        return jnp.sum(target[...], axis=0)

    spread(message, first_sum, nx, "gx", gx, 0)
    lax.fori_loop(2, 4, mix_tile, 0)
    second_message[...] = gathered(first_sum, nx, 0)
    spread(second_message, second_sum, ny, "gy", gy, 1)
    lax.fori_loop(4, 6, mix_tile, 0)
    sums = gathered(second_sum, ny, 1)

    sums = jnp.broadcast_to(jnp.sum(sums, axis=1, keepdims=True), (8, 128))
    dots = [sums[i : i + 1, :] for i in range(8)]
    moment = dots[0:2] + [2.0 * dots[i] - dots[i % 2] for i in range(2, 8)]

    def gram(i, j):
        return 0.5 * (moment[i + j] + moment[abs(i - j)])

    lower = {}
    pivots = []
    right = []
    for i in range(4):
        value = moment[i]
        for j in range(i + 1):
            entry = gram(i, j) - 0.5 * (gram(j, i + 1) + gram(j, abs(i - 1)))
            for k in range(j):
                entry = entry - lower[i, k] * lower[j, k] * pivots[k]
            if j < i:
                lower[i, j] = entry / pivots[j]
                value = value - lower[i, j] * right[j]
            else:
                pivots.append(entry)
        right.append(value)
    solved = [None] * 4
    for i in range(3, -1, -1):
        value = right[i] / pivots[i]
        for j in range(i + 1, 4):
            value = value - lower[j, i] * solved[j]
        solved[i] = value
    surface = None
    for i in range(4):
        factor = 1.5 * solved[i]
        factor = jnp.concatenate([factor, factor, factor], axis=1)
        term = factor * basis[i, 0:ROWS, :]
        surface = term if surface is None else surface + term
    surface_out[...] = surface[:, 0:COLS]


def scratch(nx, ny):
    vmem = lambda *shape: pltpu.VMEM(shape, f32)
    dma = pltpu.SemaphoreType.DMA
    return [
        vmem(4, LEV, ROWS, COLS),
        pltpu.SMEM((LEV,), f32),
        vmem(ROWS, COLS),
        vmem(ROWS, COLS),
        None,
        vmem(EXT, WIDE),
        vmem(24, WIDE),
        vmem(3, ROWS, WIDE),
        vmem(2, 40, WIDE),
        vmem(2, LEV, WIDE),
        vmem(2, 40, WIDE),
        vmem(2, LEV, WIDE),
        vmem(2 * ROWS, 128),
        vmem(2, 2 * ROWS, 128),
        vmem(8, 128),
        vmem(4, 8, 128),
        vmem(ROWS, 128),
        vmem(2 * LEV, WIDE),
        vmem(2 * LEV, WIDE),
        vmem(LEV, 8, WIDE),
        vmem(EXT, WIDE),
        vmem(4, EXT, WIDE),
        vmem(8, WIDE),
        vmem(ROWS, 128),
        vmem(8, 128),
        vmem(2, 8, WIDE),
        vmem(2, ROWS, 128),
        vmem(4, 8, 128),
        vmem(8, 128),
        vmem(nx, 8, 128),
        vmem(8, 128),
        vmem(ny, 8, 128),
        dma((4,)),
        dma((4,)),
        dma((10,)),
        dma((10,)),
        dma((8,)),
        dma((8,)),
        dma((2,)),
        dma((2,)),
    ]


def solution(mesh):
    nx, ny = mesh.shape["gx"], mesh.shape["gy"]

    def body(ocean_state, layer_thickness, vertical_mixing, damping, ocean_blocks):
        shapes = scratch(nx, ny)
        shapes[4] = pltpu.VMEM(ocean_blocks.shape, jnp.int32)
        call = pl.pallas_call(
            functools.partial(kernel, nx, ny),
            out_shape=[
                pltpu.VMEM((2, LEV, ROWS, COLS), f32),
                pltpu.VMEM((ROWS, COLS), f32),
            ],
            in_specs=[pl.BlockSpec(memory_space=pltpu.HBM)] * 5,
            out_specs=[pl.BlockSpec(memory_space=pltpu.VMEM)] * 2,
            scratch_shapes=shapes,
            compiler_params=pltpu.CompilerParams(
                collective_id=0, has_side_effects=True, vmem_limit_bytes=32 * 1024 * 1024
            ),
        )
        operands = [
            pltpu.with_memory_space_constraint(operand, pltpu.HBM)
            for operand in (ocean_state, layer_thickness, vertical_mixing, damping, ocean_blocks)
        ]
        return tuple(call(*operands))

    def wrapped(*args):
        with jax.sharding.use_abstract_mesh(mesh.abstract_mesh):
            return jax.shard_map(
                body,
                mesh=mesh,
                in_specs=(P(None, None, "gy", "gx"), P(), P("gy", "gx"), P("gy", "gx"), P()),
                out_specs=(P(None, None, "gy", "gx"), P("gy", "gx")),
                check_vma=False,
            )(*args)

    return wrapped
```

```python
import functools

import jax
import jax.numpy as jnp
from jax import lax
from jax.experimental import pallas as pl
from jax.experimental.pallas import tpu as pltpu
from jax.sharding import PartitionSpec as P

BLAT = 24
BLON = 36
LEV = 16
ROWS = 48
COLS = 288
WIDE = 384
EXT = 56
TILES = ROWS // 8

f32 = jnp.float32
MESH = pl.DeviceIdType.MESH

NORTH, SOUTH, EAST, WEST = (0, 1), (0, -1), (1, 0), (-1, 0)
DIAGONAL = ((1, 1), (-1, 1), (1, -1), (-1, -1))


def iota(shape, dim):
    return lax.broadcasted_iota(jnp.int32, shape, dim)


def padded(value):
    return jnp.concatenate([value, jnp.zeros((value.shape[0], WIDE - COLS), f32)], axis=1)


def east_of(value):
    return pltpu.roll(value, WIDE - 1, 1)


def west_of(value):
    return pltpu.roll(value, 1, 1)


def inverse(value):
    guess = pl.reciprocal(value, approx=True)
    return guess * (2.0 - value * guess)


def row_pack(low, high):
    return jnp.where(iota(low.shape, 0) < 4, low, high)


def column_pack(first, last):
    lane = iota(first.shape, 1)
    low = pltpu.roll(first, 32, 1)
    high = pltpu.roll(last, 96, 1)
    return jnp.where(
        (lane >= 32) & (lane < 36), low, jnp.where(lane >= 124, high, 0.0)
    )


def kernel(
    nx,
    ny,
    ocean,
    thick,
    mixing,
    damping,
    blocks,
    tracer_out,
    surface_out,
    state,
    h,
    mix,
    damp,
    blk,
    mask,
    level_inv,
    flat,
    send_rows,
    send_heat,
    recv_rows,
    recv_heat,
    send_cols,
    recv_cols,
    send_corner,
    recv_corner,
    flux_lon,
    flux_north,
    flux_prev,
    ratio,
    scale,
    weigh,
    basis,
    halo_rows,
    halo_cols,
    halo_corner,
    recv_halo_rows,
    recv_halo_cols,
    recv_halo_corner,
    message,
    first_sum,
    second_message,
    second_sum,
    load_sem,
    small_sem,
    send_sem,
    recv_sem,
    halo_send_sem,
    halo_recv_sem,
    sum_send_sem,
    sum_recv_sem,
):
    gx = lax.axis_index("gx")
    gy = lax.axis_index("gy")

    def device(step):
        return {"gx": lax.rem(gx + step[0] + nx, nx), "gy": lax.rem(gy + step[1] + ny, ny)}

    def greet(step):
        pl.semaphore_signal(barrier, inc=1, device_id=device(step), device_id_type=MESH)

    barrier = pltpu.get_barrier_semaphore()
    for step in DIAGONAL:
        greet(step)
    pl.loop(1, nx)(lambda d: greet((d, 0)))
    pl.loop(1, ny)(lambda d: greet((0, d)))
    partners = len(DIAGONAL) + nx - 1 + ny - 1

    small = [
        pltpu.make_async_copy(blocks, blk, small_sem.at[0]),
        pltpu.make_async_copy(thick, h, small_sem.at[1]),
        pltpu.make_async_copy(damping, damp, small_sem.at[2]),
        pltpu.make_async_copy(mixing, mix, small_sem.at[3]),
    ]
    loads = []
    for index, (start, size) in enumerate(((0, 8), (40, 8), (8, 16), (24, 16))):
        rows = pl.ds(start, size)
        loads.append(
            pltpu.make_async_copy(
                ocean.at[:, :, rows, :], state.at[:, :, rows, :], load_sem.at[index]
            )
        )
    for copy in small[:3] + loads + small[3:]:
        copy.start()

    block_rows, block_cols = blk.shape
    small[0].wait()
    row = iota((EXT, block_rows), 0)
    row = gy * ROWS + jnp.where(row < ROWS + 4, row, row - EXT)
    edge = iota((EXT, block_rows), 1) * BLAT
    pick_rows = jnp.where((row >= edge) & (row < edge + BLAT), 1.0, 0.0)
    lane = iota((block_cols, WIDE), 1)
    total = block_cols * BLON
    col = gx * COLS + jnp.where(lane < COLS + 4, lane, lane - WIDE)
    col = jnp.where(col < 0, col + total, jnp.where(col >= total, col - total, col))
    edge = iota((block_cols, WIDE), 0) * BLON
    inside = (lane < COLS + 4) | (lane >= WIDE - 4)
    pick_cols = jnp.where(inside & (col >= edge) & (col < edge + BLON), 1.0, 0.0)
    coarse = jnp.dot(pick_rows, blk[...].astype(f32), preferred_element_type=f32)
    mask[...] = jnp.dot(coarse, pick_cols, preferred_element_type=f32)

    small[1].wait()
    level_inv[...] = jnp.zeros(level_inv.shape, f32)

    @pl.loop(1, LEV)
    def _(k):
        level_inv[pl.ds(k, 1), :] = 1.0 / jnp.full((1, WIDE), h[k - 1] + h[k], f32)


    small[2].wait()
    damp_low = padded(damp[0:8, :])
    damp_high = padded(damp[ROWS - 8 : ROWS, :])
    damp_rows = row_pack(damp_low, damp_high)
    for side in range(2):
        send_rows[side, 32:40, :] = damp_rows
    damp_all = padded(damp[...])
    send_cols[ROWS:, :] = column_pack(damp_all[:, 0:128], damp_all[:, 256:384])
    send_corner[...] = column_pack(damp_rows[:, 0:128], damp_rows[:, 256:384])

    def remote(source, target, index, step, sends=send_sem, recvs=recv_sem):
        return pltpu.make_async_remote_copy(
            src_ref=source,
            dst_ref=target,
            send_sem=sends.at[index],
            recv_sem=recvs.at[index],
            device_id=device(step),
            device_id_type=MESH,
        )

    loads[0].wait()
    loads[1].wait()
    pl.semaphore_wait(barrier, partners)
    first_round = []
    for side, (edge_row, step) in enumerate(((ROWS - 1, NORTH), (0, SOUTH))):
        edge_mask = mask[edge_row : edge_row + 1, :]
        heat = padded(state[0, :, edge_row, :]) * edge_mask
        salt = padded(state[1, :, edge_row, :]) * edge_mask
        send_heat[side] = heat
        send_rows[side, 0:16, :] = heat - 0.5 * salt
        send_rows[side, 16:32, :] = padded(state[3, :, edge_row, :]) * edge_mask
        copy = remote(send_rows.at[side], recv_rows.at[side], side, step)
        copy.start()
        first_round.append(copy)

    lane128 = iota((8, 128), 1)

    @pl.loop(0, TILES)
    def _(turn):
        @pl.when(turn == 2)
        def _():
            loads[2].wait()

        @pl.when(turn == 4)
        def _():
            loads[3].wait()

        i = jnp.where(turn == 0, 0, jnp.where(turn == 1, TILES - 1, turn - 1))
        rows = pl.ds(pl.multiple_of(8 * i, 8), 8)
        edge_mask = jnp.where(lane128 == 31, mask[rows, 256:384], mask[rows, 0:128])
        acc_west = jnp.zeros((8, 128), f32)
        acc_east = jnp.zeros((8, 128), f32)
        for field, base in ((0, 0), (1, 16), (2, 64)):
            for k in range(LEV):
                first = state[field, k, rows, 0:128]
                last = jnp.concatenate(
                    [state[field, k, rows, 256:COLS], jnp.zeros((8, WIDE - COLS), f32)], axis=1
                )
                merged = jnp.where(lane128 == 31, last, first)
                turned = pltpu.roll(merged, base + k, 1) if base + k else merged
                acc_west = jnp.where(lane128 == base + k, turned, acc_west)
                acc_east = jnp.where(lane128 == base + k + 31, turned, acc_east)
        west_mask = jnp.broadcast_to(edge_mask[:, 0:1], (8, 128))
        east_mask = jnp.broadcast_to(edge_mask[:, 31:32], (8, 128))
        send_cols[rows, :] = acc_west * west_mask + pltpu.roll(acc_east, 1, 1) * east_mask

    for side, step in enumerate((EAST, WEST)):
        copy = remote(send_cols, recv_cols.at[side], 2 + side, step)
        copy.start()
        first_round.append(copy)
    for place, step in enumerate(DIAGONAL):
        copy = remote(send_corner, recv_corner.at[place], 4 + place, step)
        copy.start()
        first_round.append(copy)
    heat_round = []
    for side, step in enumerate((NORTH, SOUTH)):
        copy = remote(send_heat.at[side], recv_heat.at[side], 8 + side, step)
        copy.start()
        heat_round.append(copy)

    sub = iota((8, WIDE), 0)

    def next_row(i):
        return jnp.minimum(8 * i + 8, ROWS - 1)

    def level_sums(i, _):
        rows = pl.ds(pl.multiple_of(8 * i, 8), 8)
        row = pl.ds(next_row(i), 1)
        here = mask[rows, :]
        beyond = mask[row, :]

        def level(k, carry):
            plain, lon, lat = carry
            s = padded(state[0, k, rows, :] - 0.5 * state[1, k, rows, :]) * here
            u = padded(state[2, k, rows, :]) * here
            v = padded(state[3, k, rows, :]) * here
            s_row = padded(state[0, k, row, :] - 0.5 * state[1, k, row, :]) * beyond
            v_row = padded(state[3, k, row, :]) * beyond
            s_north = jnp.where(sub == 7, s_row, pltpu.roll(s, 7, 0))
            v_north = jnp.where(sub == 7, v_row, pltpu.roll(v, 7, 0))
            weight = 0.05 * h[k]
            plain = plain + h[k] * s
            lon = lon + weight * (u + east_of(u)) * (s + east_of(s))
            lat = lat + weight * (v + v_north) * (s + s_north)
            return plain, lon, lat

        zero = jnp.zeros((8, WIDE), f32)
        plain, lon, lat = lax.fori_loop(0, LEV, level, (zero, zero, zero), unroll=4)
        flat[0, rows, :] = plain
        flat[1, rows, :] = lon
        flat[2, rows, :] = lat
        return 0

    lax.fori_loop(0, TILES, level_sums, 0)

    for copy in first_round:
        copy.wait()

    lane_c = iota((ROWS, 128), 1)
    own = send_cols[0:ROWS, :]
    is_east = (lane_c & 32) != 0
    other = jnp.where(
        is_east,
        pltpu.roll(recv_cols[1, 0:ROWS, :], 32, 1),
        pltpu.roll(recv_cols[0, 0:ROWS, :], 96, 1),
    )
    both = own + other
    speed = pltpu.roll(both, 64, 1)
    speed = jnp.where((lane_c & 16) != 0, pltpu.roll(speed, 16, 1), speed)
    slope = jnp.where(is_east, 0.1, -0.1) * (other - own)
    through = 0.05 * speed * both - slope
    flux_lon[...] = through
    weight = jnp.zeros((1, 128), f32)
    lane_w = iota((1, 128), 1)
    for k in range(LEV):
        weight = jnp.where((lane_w & 15) == k, h[k], weight)
    weight = weight * jnp.where((lane_w & 16) != 0, -0.5, 1.0)
    weighed = through * weight
    side_west = jnp.sum(jnp.where(lane_c < 32, weighed, 0.0), axis=1, keepdims=True)
    side_east = jnp.sum(
        jnp.where(is_east & (lane_c < 64), weighed, 0.0), axis=1, keepdims=True
    )

    level_weight = jnp.zeros((LEV, WIDE), f32)
    level_row = iota((LEV, WIDE), 0)
    for k in range(LEV):
        level_weight = jnp.where(level_row == k, h[k], level_weight)
    exists = (
        jnp.where(gy < ny - 1, 1.0, 0.0).astype(f32),
        jnp.where(gy > 0, 1.0, 0.0).astype(f32),
    )

    def side_flux(mine, theirs, speeds, sign):
        return speeds * (mine + theirs) - (0.1 * sign) * (theirs - mine)

    side_lat = []
    speed_lat = []
    for side, sign in ((0, 1.0), (1, -1.0)):
        slot = 1 - side
        s_mine = send_rows[side, 0:16, :]
        s_theirs = recv_rows[slot, 0:16, :] * exists[side]
        speeds = 0.05 * (send_rows[side, 16:32, :] + recv_rows[slot, 16:32, :] * exists[side])
        speed_lat.append(speeds)
        flux = side_flux(s_mine, s_theirs, speeds, sign)
        side_lat.append(jnp.sum(flux * level_weight, axis=0, keepdims=True))

    def assemble(center, rows_in, cols_in, corner_in):
        lane8 = iota((8, 128), 1)
        lane48 = iota((ROWS, 128), 1)
        third = jnp.where(
            lane48 < 32, center[:, 256:384], jnp.where(lane48 < 64, cols_in(1), cols_in(0))
        )
        upper = jnp.concatenate([center[:, 0:256], third], axis=1)
        north_south = jnp.where(sub < 4, rows_in(1), rows_in(0))
        north = jnp.where(lane8 < 64, corner_in(3), corner_in(2))
        south = jnp.where(lane8 < 64, corner_in(1), corner_in(0))
        corner = jnp.where(iota((8, 128), 0) < 4, north, south)
        third = jnp.where(lane8 < 32, north_south[:, 256:384], corner)
        lower = jnp.concatenate([north_south[:, 0:256], third], axis=1)
        return jnp.concatenate([upper, lower], axis=0)

    damp_ext = assemble(
        damp_all,
        lambda slot: recv_rows[slot, 32:40, :],
        lambda slot: recv_cols[slot, ROWS:, :],
        lambda place: recv_corner[place],
    )
    inv = mask[...] * inverse(6.0 + damp_ext)
    scale[...] = 1.5 * inv
    weigh[...] = jnp.where(iota((ROWS, WIDE), 1) < COLS, 6.0 + damp_all, 0.0)

    lane_f = iota((ROWS, WIDE), 1)
    row_f = iota((ROWS, WIDE), 0)
    plain = flat[0]
    lon = flat[1] - 0.1 * (east_of(plain) - plain)
    lon = jnp.where(lane_f == COLS - 1, side_east, jnp.where(lane_f == WIDE - 1, side_west, lon))
    lat = flat[2] - 0.1 * (pltpu.roll(plain, ROWS - 1, 0) - plain)
    lat = jnp.where(row_f == ROWS - 1, side_lat[0], lat)
    lat_south = jnp.where(row_f == 0, side_lat[1], pltpu.roll(lat, 1, 0))
    start = plain - (lon - west_of(lon)) - (lat - lat_south)
    start = jnp.where(lane_f < COLS, start, 0.0) * inv[0:ROWS, :]
    basis[0] = jnp.zeros((EXT, WIDE), f32)
    basis[1, 0:ROWS, :] = start

    packed_rows = row_pack(start[0:8, :], start[ROWS - 8 : ROWS, :])
    halo_rows[...] = packed_rows
    halo_cols[...] = column_pack(start[:, 0:128], start[:, 256:384])
    halo_corner[...] = column_pack(packed_rows[:, 0:128], packed_rows[:, 256:384])
    second_round = []
    for side, step in enumerate((NORTH, SOUTH)):
        second_round.append(
            remote(halo_rows, recv_halo_rows.at[side], side, step, halo_send_sem, halo_recv_sem)
        )
    for side, step in enumerate((EAST, WEST)):
        second_round.append(
            remote(halo_cols, recv_halo_cols.at[side], 2 + side, step, halo_send_sem, halo_recv_sem)
        )
    for place, step in enumerate(DIAGONAL):
        second_round.append(
            remote(
                halo_corner,
                recv_halo_corner.at[place],
                4 + place,
                step,
                halo_send_sem,
                halo_recv_sem,
            )
        )
    for copy in second_round:
        copy.start()

    for copy in heat_round:
        copy.wait()
    for side, sign in ((0, 1.0), (1, -1.0)):
        slot = 1 - side
        target = flux_north if side == 0 else flux_prev
        heat_mine = send_heat[side]
        heat_theirs = recv_heat[slot] * exists[side]
        salt_mine = 2.0 * (heat_mine - send_rows[side, 0:16, :])
        salt_theirs = 2.0 * (heat_theirs - recv_rows[slot, 0:16, :] * exists[side])
        target[0:16, :] = side_flux(heat_mine, heat_theirs, speed_lat[side], sign)
        target[16:32, :] = side_flux(salt_mine, salt_theirs, speed_lat[side], sign)
    small[3].wait()

    edge_lane = (lane128 == 31) | (lane128 == 127)

    def mix_tile(i, _):
        rows = pl.ds(pl.multiple_of(8 * i, 8), 8)
        row = pl.ds(next_row(i), 1)
        here = mask[rows, :]
        beyond = mask[row, :]
        coefficient = padded(mix[rows, :])
        through = flux_lon[rows, :]
        use_north = (sub == 7) & (i == TILES - 1)

        def level(k, carry):
            ratio_low, heat_low, salt_low = carry
            u = padded(state[2, k, rows, :]) * here
            v = padded(state[3, k, rows, :]) * here
            v_row = padded(state[3, k, row, :]) * beyond
            v_north = jnp.where(sub == 7, v_row, pltpu.roll(v, 7, 0))
            u_pair = 0.05 * (u + east_of(u))
            v_pair = 0.05 * (v + v_north)
            lon_far, lon_near = u_pair - 0.1, u_pair + 0.1
            lat_far, lat_near = v_pair - 0.1, v_pair + 0.1
            below = coefficient * level_inv[pl.ds(k, 1), :]
            above = coefficient * level_inv[pl.ds(k + 1, 1), :]
            pivot = inverse(h[k] + above + below * (1.0 - ratio_low))
            ratio_now = above * pivot
            ratio[k] = ratio_now
            found = []
            for tracer, low in ((0, heat_low), (1, salt_low)):
                plane = tracer * LEV + k
                c = padded(state[tracer, k, rows, :]) * here
                c_row = padded(state[tracer, k, row, :]) * beyond
                c_north = jnp.where(sub == 7, c_row, pltpu.roll(c, 7, 0))
                lon = lon_far * east_of(c) + lon_near * c
                turned = pltpu.roll(through, 127 - plane, 1)
                lon = jnp.concatenate(
                    [lon[:, 0:256], jnp.where(edge_lane, turned, lon[:, 256:384])], axis=1
                )
                lat = lat_far * c_north + lat_near * c
                lat = jnp.where(use_north, flux_north[pl.ds(plane, 1), :], lat)
                lat_south = jnp.where(
                    sub == 0, flux_prev[pl.ds(plane, 1), :], pltpu.roll(lat, 1, 0)
                )
                flux_prev[pl.ds(plane, 1), :] = lat[7:8, :]
                advected = here * (c - (lon - west_of(lon)) - (lat - lat_south))
                value = (h[k] * advected + below * low) * pivot
                tracer_out[tracer, k, rows, :] = value[:, 0:COLS]
                found.append(value)
            return ratio_now, found[0], found[1]

        zero = jnp.zeros((8, WIDE), f32)
        _, heat, salt = lax.fori_loop(0, LEV, level, (zero, zero, zero), unroll=4)

        def back(step, carry):
            k = LEV - 2 - step
            heat_up, salt_up = carry
            share = ratio[k][:, 0:COLS]
            heat_up = tracer_out[0, k, rows, :] + share * heat_up
            salt_up = tracer_out[1, k, rows, :] + share * salt_up
            tracer_out[0, k, rows, :] = heat_up
            tracer_out[1, k, rows, :] = salt_up
            return heat_up, salt_up

        lax.fori_loop(0, LEV - 1, back, (heat[:, 0:COLS], salt[:, 0:COLS]), unroll=5)
        return 0

    def moments():
        for copy in second_round:
            copy.wait()
        basis[1] = mask[...] * assemble(
            basis[1, 0:ROWS, :],
            lambda slot: recv_halo_rows[slot],
            lambda slot: recv_halo_cols[slot],
            lambda place: recv_halo_corner[place],
        )

        @pl.loop(0, 4)
        def _(index):
            q = basis[index + 1]
            pair = east_of(q) + west_of(q)
            column = q + 0.5 * pair
            around = pair + pltpu.roll(column, EXT - 1, 0) + pltpu.roll(column, 1, 0)
            image = scale[...] * around - 0.5 * q
            later = jnp.where(index == 0, 0.0, 1.0)
            after = image + later * (image - basis[index])
            basis[index + 2] = after
            weighed = weigh[...] * q[0:ROWS, :]
            message[pl.ds(2 * index, 1), :] = folded(weighed * q[0:ROWS, :])
            message[pl.ds(2 * index + 1, 1), :] = folded(weighed * after[0:ROWS, :])

    def folded(value):
        value = value[:, 0:128] + value[:, 128:256] + value[:, 256:384]
        return jnp.sum(value, axis=0, keepdims=True)

    def spread(source, target, count, along, mine, base):
        target[mine] = source[...]

        @pl.loop(1, count)
        def _(d):
            pltpu.make_async_remote_copy(
                src_ref=source,
                dst_ref=target.at[mine],
                send_sem=sum_send_sem.at[base],
                recv_sem=sum_recv_sem.at[base],
                device_id=device(along(d)),
                device_id_type=MESH,
            ).start()

    def gathered(target, count, base):
        part = target.at[pl.ds(0, count - 1)]
        done = pltpu.make_async_remote_copy(
            src_ref=part,
            dst_ref=part,
            send_sem=sum_send_sem.at[base],
            recv_sem=sum_recv_sem.at[base],
            device_id=device(EAST),
            device_id_type=MESH,
        )
        done.wait_recv()
        done.wait_send()
        return jnp.sum(target[...], axis=0)

    @pl.loop(0, TILES)
    def _(i):
        mix_tile(i, 0)

        @pl.when(i == 1)
        def _():
            moments()
            spread(message, first_sum, nx, lambda d: (d, 0), gx, 0)

        @pl.when(i == 3)
        def _():
            second_message[...] = gathered(first_sum, nx, 0)
            spread(second_message, second_sum, ny, lambda d: (0, d), gy, 1)

    sums = gathered(second_sum, ny, 1)

    sums = jnp.broadcast_to(jnp.sum(sums, axis=1, keepdims=True), (8, 128))
    dots = [sums[i : i + 1, :] for i in range(8)]
    moment = dots[0:2] + [2.0 * dots[i] - dots[i % 2] for i in range(2, 8)]

    def gram(i, j):
        return 0.5 * (moment[i + j] + moment[abs(i - j)])

    lower = {}
    pivots = []
    right = []
    for i in range(4):
        value = moment[i]
        for j in range(i + 1):
            entry = gram(i, j) - 0.5 * (gram(j, i + 1) + gram(j, abs(i - 1)))
            for k in range(j):
                entry = entry - lower[i, k] * lower[j, k] * pivots[k]
            if j < i:
                lower[i, j] = entry / pivots[j]
                value = value - lower[i, j] * right[j]
            else:
                pivots.append(entry)
        right.append(value)
    solved = [None] * 4
    for i in range(3, -1, -1):
        value = right[i] / pivots[i]
        for j in range(i + 1, 4):
            value = value - lower[j, i] * solved[j]
        solved[i] = value
    surface = None
    for i in range(4):
        factor = 1.5 * solved[i]
        factor = jnp.concatenate([factor, factor, factor], axis=1)
        term = factor * basis[i + 1, 0:ROWS, :]
        surface = term if surface is None else surface + term
    surface_out[...] = surface[:, 0:COLS]


def scratch(nx, ny):
    vmem = lambda *shape: pltpu.VMEM(shape, f32)
    dma = pltpu.SemaphoreType.DMA
    return [
        vmem(4, LEV, ROWS, COLS),
        pltpu.SMEM((LEV,), f32),
        vmem(ROWS, COLS),
        vmem(ROWS, COLS),
        None,
        vmem(EXT, WIDE),
        vmem(24, WIDE),
        vmem(3, ROWS, WIDE),
        vmem(2, 40, WIDE),
        vmem(2, LEV, WIDE),
        vmem(2, 40, WIDE),
        vmem(2, LEV, WIDE),
        vmem(2 * ROWS, 128),
        vmem(2, 2 * ROWS, 128),
        vmem(8, 128),
        vmem(4, 8, 128),
        vmem(ROWS, 128),
        vmem(2 * LEV, WIDE),
        vmem(2 * LEV, WIDE),
        vmem(LEV, 8, WIDE),
        vmem(EXT, WIDE),
        vmem(ROWS, WIDE),
        vmem(6, EXT, WIDE),
        vmem(8, WIDE),
        vmem(ROWS, 128),
        vmem(8, 128),
        vmem(2, 8, WIDE),
        vmem(2, ROWS, 128),
        vmem(4, 8, 128),
        vmem(8, 128),
        vmem(nx, 8, 128),
        vmem(8, 128),
        vmem(ny, 8, 128),
        dma((4,)),
        dma((4,)),
        dma((10,)),
        dma((10,)),
        dma((8,)),
        dma((8,)),
        dma((2,)),
        dma((2,)),
    ]


def solution(mesh):
    nx, ny = mesh.shape["gx"], mesh.shape["gy"]

    def body(ocean_state, layer_thickness, vertical_mixing, damping, ocean_blocks):
        shapes = scratch(nx, ny)
        shapes[4] = pltpu.VMEM(ocean_blocks.shape, jnp.int32)
        call = pl.pallas_call(
            functools.partial(kernel, nx, ny),
            out_shape=[
                pltpu.VMEM((2, LEV, ROWS, COLS), f32),
                pltpu.VMEM((ROWS, COLS), f32),
            ],
            in_specs=[pl.BlockSpec(memory_space=pltpu.HBM)] * 5,
            out_specs=[pl.BlockSpec(memory_space=pltpu.VMEM)] * 2,
            scratch_shapes=shapes,
            compiler_params=pltpu.CompilerParams(
                collective_id=0, has_side_effects=True, vmem_limit_bytes=32 * 1024 * 1024
            ),
        )
        operands = [
            pltpu.with_memory_space_constraint(operand, pltpu.HBM)
            for operand in (ocean_state, layer_thickness, vertical_mixing, damping, ocean_blocks)
        ]
        return tuple(call(*operands))

    def wrapped(*args):
        with jax.sharding.use_abstract_mesh(mesh.abstract_mesh):
            return jax.shard_map(
                body,
                mesh=mesh,
                in_specs=(P(None, None, "gy", "gx"), P(), P("gy", "gx"), P("gy", "gx"), P()),
                out_specs=(P(None, None, "gy", "gx"), P("gy", "gx")),
                check_vma=False,
            )(*args)

    return wrapped
```

```python
import functools

import jax
import jax.numpy as jnp
from jax import lax
from jax.experimental import pallas as pl
from jax.experimental.pallas import tpu as pltpu
from jax.sharding import PartitionSpec as P

BLAT = 24
BLON = 36
LEV = 16
ROWS = 48
COLS = 288
WIDE = 384
EXT = 56
TILES = ROWS // 8

f32 = jnp.float32
MESH = pl.DeviceIdType.MESH

NORTH, SOUTH, EAST, WEST = (0, 1), (0, -1), (1, 0), (-1, 0)
DIAGONAL = ((1, 1), (-1, 1), (1, -1), (-1, -1))


def iota(shape, dim):
    return lax.broadcasted_iota(jnp.int32, shape, dim)


def padded(value):
    return jnp.concatenate([value, jnp.zeros((value.shape[0], WIDE - COLS), f32)], axis=1)


def east_of(value):
    return pltpu.roll(value, WIDE - 1, 1)


def west_of(value):
    return pltpu.roll(value, 1, 1)


def inverse(value):
    guess = pl.reciprocal(value, approx=True)
    return guess * (2.0 - value * guess)


def row_pack(low, high):
    return jnp.where(iota(low.shape, 0) < 4, low, high)


def column_pack(first, last):
    lane = iota(first.shape, 1)
    low = pltpu.roll(first, 32, 1)
    high = pltpu.roll(last, 96, 1)
    return jnp.where(
        (lane >= 32) & (lane < 36), low, jnp.where(lane >= 124, high, 0.0)
    )


def kernel(
    nx,
    ny,
    ocean,
    thick,
    mixing,
    damping,
    blocks,
    tracer_out,
    surface_out,
    state,
    h,
    mix,
    damp,
    blk,
    mask,
    level_inv,
    flat,
    send_rows,
    send_heat,
    recv_rows,
    recv_heat,
    send_cols,
    recv_cols,
    send_corner,
    recv_corner,
    flux_lon,
    flux_north,
    flux_prev,
    ratio,
    scale,
    weigh,
    basis,
    halo_rows,
    halo_cols,
    halo_corner,
    recv_halo_rows,
    recv_halo_cols,
    recv_halo_corner,
    message,
    first_sum,
    second_message,
    second_sum,
    load_sem,
    small_sem,
    send_sem,
    recv_sem,
    halo_send_sem,
    halo_recv_sem,
    sum_send_sem,
    sum_recv_sem,
):
    gx = lax.axis_index("gx")
    gy = lax.axis_index("gy")

    def device(step):
        return {"gx": lax.rem(gx + step[0] + nx, nx), "gy": lax.rem(gy + step[1] + ny, ny)}

    def greet(step):
        pl.semaphore_signal(barrier, inc=1, device_id=device(step), device_id_type=MESH)

    barrier = pltpu.get_barrier_semaphore()
    for step in DIAGONAL:
        greet(step)
    pl.loop(1, nx)(lambda d: greet((d, 0)))
    pl.loop(1, ny)(lambda d: greet((0, d)))
    partners = len(DIAGONAL) + nx - 1 + ny - 1

    small = [
        pltpu.make_async_copy(blocks, blk, small_sem.at[0]),
        pltpu.make_async_copy(thick, h, small_sem.at[1]),
        pltpu.make_async_copy(damping, damp, small_sem.at[2]),
        pltpu.make_async_copy(mixing, mix, small_sem.at[3]),
    ]
    loads = []
    for index, (start, size) in enumerate(((0, 8), (40, 8), (8, 16), (24, 16))):
        rows = pl.ds(start, size)
        loads.append(
            pltpu.make_async_copy(
                ocean.at[:, :, rows, :], state.at[:, :, rows, :], load_sem.at[index]
            )
        )
    for copy in small[:3] + loads + small[3:]:
        copy.start()

    block_rows, block_cols = blk.shape
    small[0].wait()
    row = iota((EXT, block_rows), 0)
    row = gy * ROWS + jnp.where(row < ROWS + 4, row, row - EXT)
    edge = iota((EXT, block_rows), 1) * BLAT
    pick_rows = jnp.where((row >= edge) & (row < edge + BLAT), 1.0, 0.0)
    lane = iota((block_cols, WIDE), 1)
    total = block_cols * BLON
    col = gx * COLS + jnp.where(lane < COLS + 4, lane, lane - WIDE)
    col = jnp.where(col < 0, col + total, jnp.where(col >= total, col - total, col))
    edge = iota((block_cols, WIDE), 0) * BLON
    inside = (lane < COLS + 4) | (lane >= WIDE - 4)
    pick_cols = jnp.where(inside & (col >= edge) & (col < edge + BLON), 1.0, 0.0)
    coarse = jnp.dot(pick_rows, blk[...].astype(f32), preferred_element_type=f32)
    mask[...] = jnp.dot(coarse, pick_cols, preferred_element_type=f32)

    small[1].wait()
    level_inv[...] = jnp.zeros(level_inv.shape, f32)

    @pl.loop(1, LEV)
    def _(k):
        level_inv[pl.ds(k, 1), :] = 1.0 / jnp.full((1, WIDE), h[k - 1] + h[k], f32)


    small[2].wait()
    damp_low = padded(damp[0:8, :])
    damp_high = padded(damp[ROWS - 8 : ROWS, :])
    damp_rows = row_pack(damp_low, damp_high)
    for side in range(2):
        send_rows[side, 32:40, :] = damp_rows
    damp_all = padded(damp[...])
    send_cols[ROWS:, :] = column_pack(damp_all[:, 0:128], damp_all[:, 256:384])
    send_corner[...] = column_pack(damp_rows[:, 0:128], damp_rows[:, 256:384])

    def remote(source, target, index, step, sends=send_sem, recvs=recv_sem):
        return pltpu.make_async_remote_copy(
            src_ref=source,
            dst_ref=target,
            send_sem=sends.at[index],
            recv_sem=recvs.at[index],
            device_id=device(step),
            device_id_type=MESH,
        )

    loads[0].wait()
    loads[1].wait()
    pl.semaphore_wait(barrier, partners)
    first_round = []
    for side, (edge_row, step) in enumerate(((ROWS - 1, NORTH), (0, SOUTH))):
        edge_mask = mask[edge_row : edge_row + 1, :]
        heat = padded(state[0, :, edge_row, :]) * edge_mask
        salt = padded(state[1, :, edge_row, :]) * edge_mask
        send_heat[side] = heat
        send_rows[side, 0:16, :] = heat - 0.5 * salt
        send_rows[side, 16:32, :] = padded(state[3, :, edge_row, :]) * edge_mask
        copy = remote(send_rows.at[side], recv_rows.at[side], side, step)
        copy.start()
        first_round.append(copy)

    lane128 = iota((8, 128), 1)

    @pl.loop(0, TILES)
    def _(turn):
        @pl.when(turn == 2)
        def _():
            loads[2].wait()

        @pl.when(turn == 4)
        def _():
            loads[3].wait()

        i = jnp.where(turn == 0, 0, jnp.where(turn == 1, TILES - 1, turn - 1))
        rows = pl.ds(pl.multiple_of(8 * i, 8), 8)
        edge_mask = jnp.where(lane128 == 31, mask[rows, 256:384], mask[rows, 0:128])
        acc_west = jnp.zeros((8, 128), f32)
        acc_east = jnp.zeros((8, 128), f32)
        for field, base in ((0, 0), (1, 16), (2, 64)):
            for k in range(LEV):
                first = state[field, k, rows, 0:128]
                last = jnp.concatenate(
                    [state[field, k, rows, 256:COLS], jnp.zeros((8, WIDE - COLS), f32)], axis=1
                )
                merged = jnp.where(lane128 == 31, last, first)
                turned = pltpu.roll(merged, base + k, 1) if base + k else merged
                acc_west = jnp.where(lane128 == base + k, turned, acc_west)
                acc_east = jnp.where(lane128 == base + k + 31, turned, acc_east)
        west_mask = jnp.broadcast_to(edge_mask[:, 0:1], (8, 128))
        east_mask = jnp.broadcast_to(edge_mask[:, 31:32], (8, 128))
        send_cols[rows, :] = acc_west * west_mask + pltpu.roll(acc_east, 1, 1) * east_mask

    for side, step in enumerate((EAST, WEST)):
        copy = remote(send_cols, recv_cols.at[side], 2 + side, step)
        copy.start()
        first_round.append(copy)
    for place, step in enumerate(DIAGONAL):
        copy = remote(send_corner, recv_corner.at[place], 4 + place, step)
        copy.start()
        first_round.append(copy)
    heat_round = []
    for side, step in enumerate((NORTH, SOUTH)):
        copy = remote(send_heat.at[side], recv_heat.at[side], 8 + side, step)
        copy.start()
        heat_round.append(copy)

    sub = iota((8, WIDE), 0)

    def next_row(i):
        return jnp.minimum(8 * i + 8, ROWS - 1)

    def level_sums(i, _):
        rows = pl.ds(pl.multiple_of(8 * i, 8), 8)
        row = pl.ds(next_row(i), 1)
        here = mask[rows, :]
        beyond = mask[row, :]

        def level(k, carry):
            plain, lon, lat = carry
            s = padded(state[0, k, rows, :] - 0.5 * state[1, k, rows, :]) * here
            u = padded(state[2, k, rows, :]) * here
            v = padded(state[3, k, rows, :]) * here
            s_row = padded(state[0, k, row, :] - 0.5 * state[1, k, row, :]) * beyond
            v_row = padded(state[3, k, row, :]) * beyond
            s_north = jnp.where(sub == 7, s_row, pltpu.roll(s, 7, 0))
            v_north = jnp.where(sub == 7, v_row, pltpu.roll(v, 7, 0))
            weight = 0.05 * h[k]
            plain = plain + h[k] * s
            lon = lon + weight * (u + east_of(u)) * (s + east_of(s))
            lat = lat + weight * (v + v_north) * (s + s_north)
            return plain, lon, lat

        zero = jnp.zeros((8, WIDE), f32)
        plain, lon, lat = lax.fori_loop(0, LEV, level, (zero, zero, zero), unroll=4)
        flat[0, rows, :] = plain
        flat[1, rows, :] = lon
        flat[2, rows, :] = lat
        return 0

    lax.fori_loop(0, TILES, level_sums, 0)

    for copy in first_round:
        copy.wait()

    lane_c = iota((ROWS, 128), 1)
    own = send_cols[0:ROWS, :]
    is_east = (lane_c & 32) != 0
    other = jnp.where(
        is_east,
        pltpu.roll(recv_cols[1, 0:ROWS, :], 32, 1),
        pltpu.roll(recv_cols[0, 0:ROWS, :], 96, 1),
    )
    both = own + other
    speed = pltpu.roll(both, 64, 1)
    speed = jnp.where((lane_c & 16) != 0, pltpu.roll(speed, 16, 1), speed)
    slope = jnp.where(is_east, 0.1, -0.1) * (other - own)
    through = 0.05 * speed * both - slope
    flux_lon[...] = through
    weight = jnp.zeros((1, 128), f32)
    lane_w = iota((1, 128), 1)
    for k in range(LEV):
        weight = jnp.where((lane_w & 15) == k, h[k], weight)
    weight = weight * jnp.where((lane_w & 16) != 0, -0.5, 1.0)
    weighed = through * weight
    side_west = jnp.sum(jnp.where(lane_c < 32, weighed, 0.0), axis=1, keepdims=True)
    side_east = jnp.sum(
        jnp.where(is_east & (lane_c < 64), weighed, 0.0), axis=1, keepdims=True
    )

    level_weight = jnp.zeros((LEV, WIDE), f32)
    level_row = iota((LEV, WIDE), 0)
    for k in range(LEV):
        level_weight = jnp.where(level_row == k, h[k], level_weight)
    exists = (
        jnp.where(gy < ny - 1, 1.0, 0.0).astype(f32),
        jnp.where(gy > 0, 1.0, 0.0).astype(f32),
    )

    def side_flux(mine, theirs, speeds, sign):
        return speeds * (mine + theirs) - (0.1 * sign) * (theirs - mine)

    side_lat = []
    speed_lat = []
    for side, sign in ((0, 1.0), (1, -1.0)):
        slot = 1 - side
        s_mine = send_rows[side, 0:16, :]
        s_theirs = recv_rows[slot, 0:16, :] * exists[side]
        speeds = 0.05 * (send_rows[side, 16:32, :] + recv_rows[slot, 16:32, :] * exists[side])
        speed_lat.append(speeds)
        flux = side_flux(s_mine, s_theirs, speeds, sign)
        side_lat.append(jnp.sum(flux * level_weight, axis=0, keepdims=True))

    def assemble(center, rows_in, cols_in, corner_in):
        lane8 = iota((8, 128), 1)
        lane48 = iota((ROWS, 128), 1)
        third = jnp.where(
            lane48 < 32, center[:, 256:384], jnp.where(lane48 < 64, cols_in(1), cols_in(0))
        )
        upper = jnp.concatenate([center[:, 0:256], third], axis=1)
        north_south = jnp.where(sub < 4, rows_in(1), rows_in(0))
        north = jnp.where(lane8 < 64, corner_in(3), corner_in(2))
        south = jnp.where(lane8 < 64, corner_in(1), corner_in(0))
        corner = jnp.where(iota((8, 128), 0) < 4, north, south)
        third = jnp.where(lane8 < 32, north_south[:, 256:384], corner)
        lower = jnp.concatenate([north_south[:, 0:256], third], axis=1)
        return jnp.concatenate([upper, lower], axis=0)

    damp_ext = assemble(
        damp_all,
        lambda slot: recv_rows[slot, 32:40, :],
        lambda slot: recv_cols[slot, ROWS:, :],
        lambda place: recv_corner[place],
    )
    inv = mask[...] * inverse(6.0 + damp_ext)
    scale[...] = 1.5 * inv
    weigh[...] = jnp.where(iota((ROWS, WIDE), 1) < COLS, 6.0 + damp_all, 0.0)

    lane_f = iota((ROWS, WIDE), 1)
    row_f = iota((ROWS, WIDE), 0)
    plain = flat[0]
    lon = flat[1] - 0.1 * (east_of(plain) - plain)
    lon = jnp.where(lane_f == COLS - 1, side_east, jnp.where(lane_f == WIDE - 1, side_west, lon))
    lat = flat[2] - 0.1 * (pltpu.roll(plain, ROWS - 1, 0) - plain)
    lat = jnp.where(row_f == ROWS - 1, side_lat[0], lat)
    lat_south = jnp.where(row_f == 0, side_lat[1], pltpu.roll(lat, 1, 0))
    start = plain - (lon - west_of(lon)) - (lat - lat_south)
    start = jnp.where(lane_f < COLS, start, 0.0) * inv[0:ROWS, :]
    basis[0] = jnp.zeros((EXT, WIDE), f32)
    basis[1, 0:ROWS, :] = start

    packed_rows = row_pack(start[0:8, :], start[ROWS - 8 : ROWS, :])
    halo_rows[...] = packed_rows
    halo_cols[...] = column_pack(start[:, 0:128], start[:, 256:384])
    halo_corner[...] = column_pack(packed_rows[:, 0:128], packed_rows[:, 256:384])
    second_round = []
    for side, step in enumerate((NORTH, SOUTH)):
        second_round.append(
            remote(halo_rows, recv_halo_rows.at[side], side, step, halo_send_sem, halo_recv_sem)
        )
    for side, step in enumerate((EAST, WEST)):
        second_round.append(
            remote(halo_cols, recv_halo_cols.at[side], 2 + side, step, halo_send_sem, halo_recv_sem)
        )
    for place, step in enumerate(DIAGONAL):
        second_round.append(
            remote(
                halo_corner,
                recv_halo_corner.at[place],
                4 + place,
                step,
                halo_send_sem,
                halo_recv_sem,
            )
        )
    for copy in second_round:
        copy.start()

    for copy in heat_round:
        copy.wait()
    for side, sign in ((0, 1.0), (1, -1.0)):
        slot = 1 - side
        target = flux_north if side == 0 else flux_prev
        heat_mine = send_heat[side]
        heat_theirs = recv_heat[slot] * exists[side]
        salt_mine = 2.0 * (heat_mine - send_rows[side, 0:16, :])
        salt_theirs = 2.0 * (heat_theirs - recv_rows[slot, 0:16, :] * exists[side])
        target[0:16, :] = side_flux(heat_mine, heat_theirs, speed_lat[side], sign)
        target[16:32, :] = side_flux(salt_mine, salt_theirs, speed_lat[side], sign)
    small[3].wait()

    edge_lane = (lane128 == 31) | (lane128 == 127)

    def mix_tile(i, _):
        rows = pl.ds(pl.multiple_of(8 * i, 8), 8)
        row = pl.ds(next_row(i), 1)
        here = mask[rows, :]
        beyond = mask[row, :]
        coefficient = padded(mix[rows, :])
        through = flux_lon[rows, :]
        use_north = (sub == 7) & (i == TILES - 1)

        def level(k, carry):
            ratio_low, heat_low, salt_low = carry
            u = padded(state[2, k, rows, :]) * here
            v = padded(state[3, k, rows, :]) * here
            v_row = padded(state[3, k, row, :]) * beyond
            v_north = jnp.where(sub == 7, v_row, pltpu.roll(v, 7, 0))
            u_pair = 0.05 * (u + east_of(u))
            v_pair = 0.05 * (v + v_north)
            lon_far, lon_near = u_pair - 0.1, u_pair + 0.1
            lat_far, lat_near = v_pair - 0.1, v_pair + 0.1
            below = coefficient * level_inv[pl.ds(k, 1), :]
            above = coefficient * level_inv[pl.ds(k + 1, 1), :]
            pivot = inverse(h[k] + above + below * (1.0 - ratio_low))
            ratio_now = above * pivot
            ratio[k] = ratio_now
            found = []
            for tracer, low in ((0, heat_low), (1, salt_low)):
                plane = tracer * LEV + k
                c = padded(state[tracer, k, rows, :]) * here
                c_row = padded(state[tracer, k, row, :]) * beyond
                c_north = jnp.where(sub == 7, c_row, pltpu.roll(c, 7, 0))
                lon = lon_far * east_of(c) + lon_near * c
                turned = pltpu.roll(through, 127 - plane, 1)
                lon = jnp.concatenate(
                    [lon[:, 0:256], jnp.where(edge_lane, turned, lon[:, 256:384])], axis=1
                )
                lat = lat_far * c_north + lat_near * c
                lat = jnp.where(use_north, flux_north[pl.ds(plane, 1), :], lat)
                lat_south = jnp.where(
                    sub == 0, flux_prev[pl.ds(plane, 1), :], pltpu.roll(lat, 1, 0)
                )
                flux_prev[pl.ds(plane, 1), :] = lat[7:8, :]
                advected = here * (c - (lon - west_of(lon)) - (lat - lat_south))
                value = (h[k] * advected + below * low) * pivot
                tracer_out[tracer, k, rows, :] = value[:, 0:COLS]
                found.append(value)
            return ratio_now, found[0], found[1]

        zero = jnp.zeros((8, WIDE), f32)
        _, heat, salt = lax.fori_loop(0, LEV, level, (zero, zero, zero), unroll=4)

        def back(step, carry):
            k = LEV - 2 - step
            heat_up, salt_up = carry
            share = ratio[k][:, 0:COLS]
            heat_up = tracer_out[0, k, rows, :] + share * heat_up
            salt_up = tracer_out[1, k, rows, :] + share * salt_up
            tracer_out[0, k, rows, :] = heat_up
            tracer_out[1, k, rows, :] = salt_up
            return heat_up, salt_up

        lax.fori_loop(0, LEV - 1, back, (heat[:, 0:COLS], salt[:, 0:COLS]), unroll=5)
        return 0

    def moments():
        for copy in second_round:
            copy.wait()
        basis[1] = mask[...] * assemble(
            basis[1, 0:ROWS, :],
            lambda slot: recv_halo_rows[slot],
            lambda slot: recv_halo_cols[slot],
            lambda place: recv_halo_corner[place],
        )

        @pl.loop(0, 4)
        def _(index):
            q = basis[index + 1]
            pair = east_of(q) + west_of(q)
            column = q + 0.5 * pair
            around = pair + pltpu.roll(column, EXT - 1, 0) + pltpu.roll(column, 1, 0)
            image = scale[...] * around - 0.5 * q
            later = jnp.where(index == 0, 0.0, 1.0)
            after = image + later * (image - basis[index])
            basis[index + 2] = after
            weighed = weigh[...] * q[0:ROWS, :]
            message[pl.ds(2 * index, 1), :] = folded(weighed * q[0:ROWS, :])
            message[pl.ds(2 * index + 1, 1), :] = folded(weighed * after[0:ROWS, :])

    def folded(value):
        value = value[:, 0:128] + value[:, 128:256] + value[:, 256:384]
        return jnp.sum(value, axis=0, keepdims=True)

    def spread(source, target, count, along, mine, base):
        target[mine] = source[...]

        @pl.loop(1, count)
        def _(d):
            pltpu.make_async_remote_copy(
                src_ref=source,
                dst_ref=target.at[mine],
                send_sem=sum_send_sem.at[base],
                recv_sem=sum_recv_sem.at[base],
                device_id=device(along(d)),
                device_id_type=MESH,
            ).start()

    def gathered(target, count, base):
        part = target.at[pl.ds(0, count - 1)]
        done = pltpu.make_async_remote_copy(
            src_ref=part,
            dst_ref=part,
            send_sem=sum_send_sem.at[base],
            recv_sem=sum_recv_sem.at[base],
            device_id=device(EAST),
            device_id_type=MESH,
        )
        done.wait_recv()
        done.wait_send()
        return jnp.sum(target[...], axis=0)

    moments()
    spread(message, first_sum, nx, lambda d: (d, 0), gx, 0)
    second_message[...] = gathered(first_sum, nx, 0)
    spread(second_message, second_sum, ny, lambda d: (0, d), gy, 1)
    lax.fori_loop(0, TILES, mix_tile, 0)
    sums = gathered(second_sum, ny, 1)

    sums = jnp.broadcast_to(jnp.sum(sums, axis=1, keepdims=True), (8, 128))
    dots = [sums[i : i + 1, :] for i in range(8)]
    moment = dots[0:2] + [2.0 * dots[i] - dots[i % 2] for i in range(2, 8)]

    def gram(i, j):
        return 0.5 * (moment[i + j] + moment[abs(i - j)])

    lower = {}
    pivots = []
    right = []
    for i in range(4):
        value = moment[i]
        for j in range(i + 1):
            entry = gram(i, j) - 0.5 * (gram(j, i + 1) + gram(j, abs(i - 1)))
            for k in range(j):
                entry = entry - lower[i, k] * lower[j, k] * pivots[k]
            if j < i:
                lower[i, j] = entry / pivots[j]
                value = value - lower[i, j] * right[j]
            else:
                pivots.append(entry)
        right.append(value)
    solved = [None] * 4
    for i in range(3, -1, -1):
        value = right[i] / pivots[i]
        for j in range(i + 1, 4):
            value = value - lower[j, i] * solved[j]
        solved[i] = value
    surface = None
    for i in range(4):
        factor = 1.5 * solved[i]
        factor = jnp.concatenate([factor, factor, factor], axis=1)
        term = factor * basis[i + 1, 0:ROWS, :]
        surface = term if surface is None else surface + term
    surface_out[...] = surface[:, 0:COLS]


def scratch(nx, ny):
    vmem = lambda *shape: pltpu.VMEM(shape, f32)
    dma = pltpu.SemaphoreType.DMA
    return [
        vmem(4, LEV, ROWS, COLS),
        pltpu.SMEM((LEV,), f32),
        vmem(ROWS, COLS),
        vmem(ROWS, COLS),
        None,
        vmem(EXT, WIDE),
        vmem(24, WIDE),
        vmem(3, ROWS, WIDE),
        vmem(2, 40, WIDE),
        vmem(2, LEV, WIDE),
        vmem(2, 40, WIDE),
        vmem(2, LEV, WIDE),
        vmem(2 * ROWS, 128),
        vmem(2, 2 * ROWS, 128),
        vmem(8, 128),
        vmem(4, 8, 128),
        vmem(ROWS, 128),
        vmem(2 * LEV, WIDE),
        vmem(2 * LEV, WIDE),
        vmem(LEV, 8, WIDE),
        vmem(EXT, WIDE),
        vmem(ROWS, WIDE),
        vmem(6, EXT, WIDE),
        vmem(8, WIDE),
        vmem(ROWS, 128),
        vmem(8, 128),
        vmem(2, 8, WIDE),
        vmem(2, ROWS, 128),
        vmem(4, 8, 128),
        vmem(8, 128),
        vmem(nx, 8, 128),
        vmem(8, 128),
        vmem(ny, 8, 128),
        dma((4,)),
        dma((4,)),
        dma((10,)),
        dma((10,)),
        dma((8,)),
        dma((8,)),
        dma((2,)),
        dma((2,)),
    ]


def solution(mesh):
    nx, ny = mesh.shape["gx"], mesh.shape["gy"]

    def body(ocean_state, layer_thickness, vertical_mixing, damping, ocean_blocks):
        shapes = scratch(nx, ny)
        shapes[4] = pltpu.VMEM(ocean_blocks.shape, jnp.int32)
        call = pl.pallas_call(
            functools.partial(kernel, nx, ny),
            out_shape=[
                pltpu.VMEM((2, LEV, ROWS, COLS), f32),
                pltpu.VMEM((ROWS, COLS), f32),
            ],
            in_specs=[pl.BlockSpec(memory_space=pltpu.HBM)] * 5,
            out_specs=[pl.BlockSpec(memory_space=pltpu.VMEM)] * 2,
            scratch_shapes=shapes,
            compiler_params=pltpu.CompilerParams(
                collective_id=0, has_side_effects=True, vmem_limit_bytes=32 * 1024 * 1024
            ),
        )
        operands = [
            pltpu.with_memory_space_constraint(operand, pltpu.HBM)
            for operand in (ocean_state, layer_thickness, vertical_mixing, damping, ocean_blocks)
        ]
        return tuple(call(*operands))

    def wrapped(*args):
        with jax.sharding.use_abstract_mesh(mesh.abstract_mesh):
            return jax.shard_map(
                body,
                mesh=mesh,
                in_specs=(P(None, None, "gy", "gx"), P(), P("gy", "gx"), P("gy", "gx"), P()),
                out_specs=(P(None, None, "gy", "gx"), P("gy", "gx")),
                check_vma=False,
            )(*args)

    return wrapped
```

```python
import functools

import jax
import jax.numpy as jnp
from jax import lax
from jax.experimental import pallas as pl
from jax.experimental.pallas import tpu as pltpu
from jax.sharding import PartitionSpec as P

BLAT = 24
BLON = 36
LEV = 16
ROWS = 48
COLS = 288
WIDE = 384
EXT = 56
TILES = ROWS // 8

f32 = jnp.float32
MESH = pl.DeviceIdType.MESH

NORTH, SOUTH, EAST, WEST = (0, 1), (0, -1), (1, 0), (-1, 0)
DIAGONAL = ((1, 1), (-1, 1), (1, -1), (-1, -1))


def iota(shape, dim):
    return lax.broadcasted_iota(jnp.int32, shape, dim)


def padded(value):
    return jnp.concatenate([value, jnp.zeros((value.shape[0], WIDE - COLS), f32)], axis=1)


def east_of(value):
    return pltpu.roll(value, WIDE - 1, 1)


def west_of(value):
    return pltpu.roll(value, 1, 1)


def inverse(value):
    guess = pl.reciprocal(value, approx=True)
    return guess * (2.0 - value * guess)


def row_pack(low, high):
    return jnp.where(iota(low.shape, 0) < 4, low, high)


def column_pack(first, last):
    lane = iota(first.shape, 1)
    low = pltpu.roll(first, 32, 1)
    high = pltpu.roll(last, 96, 1)
    return jnp.where(
        (lane >= 32) & (lane < 36), low, jnp.where(lane >= 124, high, 0.0)
    )


def kernel(
    nx,
    ny,
    ocean,
    thick,
    mixing,
    damping,
    blocks,
    tracer_out,
    surface_out,
    state,
    h,
    mix,
    damp,
    blk,
    mask,
    level_inv,
    flat,
    send_rows,
    send_heat,
    recv_rows,
    recv_heat,
    send_cols,
    recv_cols,
    send_corner,
    recv_corner,
    flux_lon,
    flux_north,
    flux_prev,
    ratio,
    scale,
    weigh,
    basis,
    halo_rows,
    halo_cols,
    halo_corner,
    recv_halo_rows,
    recv_halo_cols,
    recv_halo_corner,
    message,
    first_sum,
    second_message,
    second_sum,
    third_message,
    third_sum,
    load_sem,
    small_sem,
    send_sem,
    recv_sem,
    halo_send_sem,
    halo_recv_sem,
    sum_send_sem,
    sum_recv_sem,
):
    gx = lax.axis_index("gx")
    gy = lax.axis_index("gy")

    def device(step):
        return {"gx": lax.rem(gx + step[0] + nx, nx), "gy": lax.rem(gy + step[1] + ny, ny)}

    def greet(step):
        pl.semaphore_signal(barrier, inc=1, device_id=device(step), device_id_type=MESH)

    barrier = pltpu.get_barrier_semaphore()
    for step in DIAGONAL:
        greet(step)
    pl.loop(1, nx)(lambda d: greet((d, 0)))
    inner = 4 if ny >= 16 else 2
    outer = ny // inner
    at_inner, at_outer = lax.rem(gy, inner), gy // inner

    def along_inner(d):
        return (0, lax.rem(at_inner + d, inner) - at_inner)

    def along_outer(d):
        return (0, (lax.rem(at_outer + d, outer) - at_outer) * inner)

    greet(NORTH)
    greet(SOUTH)
    pl.loop(1, inner)(lambda d: greet(along_inner(d)))
    pl.loop(1, outer)(lambda d: greet(along_outer(d)))
    partners = len(DIAGONAL) + nx - 1 + 2 + inner - 1 + outer - 1

    small = [
        pltpu.make_async_copy(blocks, blk, small_sem.at[0]),
        pltpu.make_async_copy(thick, h, small_sem.at[1]),
        pltpu.make_async_copy(damping, damp, small_sem.at[2]),
        pltpu.make_async_copy(mixing, mix, small_sem.at[3]),
    ]
    loads = []
    for index, (start, size) in enumerate(((0, 8), (40, 8), (8, 16), (24, 16))):
        rows = pl.ds(start, size)
        loads.append(
            pltpu.make_async_copy(
                ocean.at[:, :, rows, :], state.at[:, :, rows, :], load_sem.at[index]
            )
        )
    for copy in small[:3] + loads + small[3:]:
        copy.start()

    block_rows, block_cols = blk.shape
    small[0].wait()
    row = iota((EXT, block_rows), 0)
    row = gy * ROWS + jnp.where(row < ROWS + 4, row, row - EXT)
    edge = iota((EXT, block_rows), 1) * BLAT
    pick_rows = jnp.where((row >= edge) & (row < edge + BLAT), 1.0, 0.0)
    lane = iota((block_cols, WIDE), 1)
    total = block_cols * BLON
    col = gx * COLS + jnp.where(lane < COLS + 4, lane, lane - WIDE)
    col = jnp.where(col < 0, col + total, jnp.where(col >= total, col - total, col))
    edge = iota((block_cols, WIDE), 0) * BLON
    inside = (lane < COLS + 4) | (lane >= WIDE - 4)
    pick_cols = jnp.where(inside & (col >= edge) & (col < edge + BLON), 1.0, 0.0)
    coarse = jnp.dot(pick_rows, blk[...].astype(f32), preferred_element_type=f32)
    mask[...] = jnp.dot(coarse, pick_cols, preferred_element_type=f32)

    small[1].wait()
    level_inv[...] = jnp.zeros(level_inv.shape, f32)

    @pl.loop(1, LEV)
    def _(k):
        level_inv[pl.ds(k, 1), :] = 1.0 / jnp.full((1, WIDE), h[k - 1] + h[k], f32)


    small[2].wait()
    damp_low = padded(damp[0:8, :])
    damp_high = padded(damp[ROWS - 8 : ROWS, :])
    damp_rows = row_pack(damp_low, damp_high)
    for side in range(2):
        send_rows[side, 32:40, :] = damp_rows
    damp_all = padded(damp[...])
    send_cols[ROWS:, :] = column_pack(damp_all[:, 0:128], damp_all[:, 256:384])
    send_corner[...] = column_pack(damp_rows[:, 0:128], damp_rows[:, 256:384])

    def remote(source, target, index, step, sends=send_sem, recvs=recv_sem):
        return pltpu.make_async_remote_copy(
            src_ref=source,
            dst_ref=target,
            send_sem=sends.at[index],
            recv_sem=recvs.at[index],
            device_id=device(step),
            device_id_type=MESH,
        )

    loads[0].wait()
    loads[1].wait()
    pl.semaphore_wait(barrier, partners)
    first_round = []
    for side, (edge_row, step) in enumerate(((ROWS - 1, NORTH), (0, SOUTH))):
        edge_mask = mask[edge_row : edge_row + 1, :]
        heat = padded(state[0, :, edge_row, :]) * edge_mask
        salt = padded(state[1, :, edge_row, :]) * edge_mask
        send_heat[side] = heat
        send_rows[side, 0:16, :] = heat - 0.5 * salt
        send_rows[side, 16:32, :] = padded(state[3, :, edge_row, :]) * edge_mask
        copy = remote(send_rows.at[side], recv_rows.at[side], side, step)
        copy.start()
        first_round.append(copy)

    lane128 = iota((8, 128), 1)

    @pl.loop(0, TILES)
    def _(turn):
        @pl.when(turn == 2)
        def _():
            loads[2].wait()

        @pl.when(turn == 4)
        def _():
            loads[3].wait()

        i = jnp.where(turn == 0, 0, jnp.where(turn == 1, TILES - 1, turn - 1))
        rows = pl.ds(pl.multiple_of(8 * i, 8), 8)
        edge_mask = jnp.where(lane128 == 31, mask[rows, 256:384], mask[rows, 0:128])
        acc_west = jnp.zeros((8, 128), f32)
        acc_east = jnp.zeros((8, 128), f32)
        for field, base in ((0, 0), (1, 16), (2, 64)):
            for k in range(LEV):
                first = state[field, k, rows, 0:128]
                last = jnp.concatenate(
                    [state[field, k, rows, 256:COLS], jnp.zeros((8, WIDE - COLS), f32)], axis=1
                )
                merged = jnp.where(lane128 == 31, last, first)
                turned = pltpu.roll(merged, base + k, 1) if base + k else merged
                acc_west = jnp.where(lane128 == base + k, turned, acc_west)
                acc_east = jnp.where(lane128 == base + k + 31, turned, acc_east)
        west_mask = jnp.broadcast_to(edge_mask[:, 0:1], (8, 128))
        east_mask = jnp.broadcast_to(edge_mask[:, 31:32], (8, 128))
        send_cols[rows, :] = acc_west * west_mask + pltpu.roll(acc_east, 1, 1) * east_mask

    for side, step in enumerate((EAST, WEST)):
        copy = remote(send_cols, recv_cols.at[side], 2 + side, step)
        copy.start()
        first_round.append(copy)
    for place, step in enumerate(DIAGONAL):
        copy = remote(send_corner, recv_corner.at[place], 4 + place, step)
        copy.start()
        first_round.append(copy)
    heat_round = []
    for side, step in enumerate((NORTH, SOUTH)):
        copy = remote(send_heat.at[side], recv_heat.at[side], 8 + side, step)
        copy.start()
        heat_round.append(copy)

    sub = iota((8, WIDE), 0)

    def next_row(i):
        return jnp.minimum(8 * i + 8, ROWS - 1)

    def level_sums(i, _):
        rows = pl.ds(pl.multiple_of(8 * i, 8), 8)
        row = pl.ds(next_row(i), 1)
        here = mask[rows, :]
        beyond = mask[row, :]

        def level(k, carry):
            plain, lon, lat = carry
            s = padded(state[0, k, rows, :] - 0.5 * state[1, k, rows, :]) * here
            u = padded(state[2, k, rows, :]) * here
            v = padded(state[3, k, rows, :]) * here
            s_row = padded(state[0, k, row, :] - 0.5 * state[1, k, row, :]) * beyond
            v_row = padded(state[3, k, row, :]) * beyond
            s_north = jnp.where(sub == 7, s_row, pltpu.roll(s, 7, 0))
            v_north = jnp.where(sub == 7, v_row, pltpu.roll(v, 7, 0))
            weight = 0.05 * h[k]
            plain = plain + h[k] * s
            lon = lon + weight * (u + east_of(u)) * (s + east_of(s))
            lat = lat + weight * (v + v_north) * (s + s_north)
            return plain, lon, lat

        zero = jnp.zeros((8, WIDE), f32)
        plain, lon, lat = lax.fori_loop(0, LEV, level, (zero, zero, zero), unroll=4)
        flat[0, rows, :] = plain
        flat[1, rows, :] = lon
        flat[2, rows, :] = lat
        return 0

    lax.fori_loop(0, TILES, level_sums, 0)

    for copy in first_round:
        copy.wait()

    lane_c = iota((ROWS, 128), 1)
    own = send_cols[0:ROWS, :]
    is_east = (lane_c & 32) != 0
    other = jnp.where(
        is_east,
        pltpu.roll(recv_cols[1, 0:ROWS, :], 32, 1),
        pltpu.roll(recv_cols[0, 0:ROWS, :], 96, 1),
    )
    both = own + other
    speed = pltpu.roll(both, 64, 1)
    speed = jnp.where((lane_c & 16) != 0, pltpu.roll(speed, 16, 1), speed)
    slope = jnp.where(is_east, 0.1, -0.1) * (other - own)
    through = 0.05 * speed * both - slope
    flux_lon[...] = through
    weight = jnp.zeros((1, 128), f32)
    lane_w = iota((1, 128), 1)
    for k in range(LEV):
        weight = jnp.where((lane_w & 15) == k, h[k], weight)
    weight = weight * jnp.where((lane_w & 16) != 0, -0.5, 1.0)
    weighed = through * weight
    side_west = jnp.sum(jnp.where(lane_c < 32, weighed, 0.0), axis=1, keepdims=True)
    side_east = jnp.sum(
        jnp.where(is_east & (lane_c < 64), weighed, 0.0), axis=1, keepdims=True
    )

    level_weight = jnp.zeros((LEV, WIDE), f32)
    level_row = iota((LEV, WIDE), 0)
    for k in range(LEV):
        level_weight = jnp.where(level_row == k, h[k], level_weight)
    exists = (
        jnp.where(gy < ny - 1, 1.0, 0.0).astype(f32),
        jnp.where(gy > 0, 1.0, 0.0).astype(f32),
    )

    def side_flux(mine, theirs, speeds, sign):
        return speeds * (mine + theirs) - (0.1 * sign) * (theirs - mine)

    side_lat = []
    speed_lat = []
    for side, sign in ((0, 1.0), (1, -1.0)):
        slot = 1 - side
        s_mine = send_rows[side, 0:16, :]
        s_theirs = recv_rows[slot, 0:16, :] * exists[side]
        speeds = 0.05 * (send_rows[side, 16:32, :] + recv_rows[slot, 16:32, :] * exists[side])
        speed_lat.append(speeds)
        flux = side_flux(s_mine, s_theirs, speeds, sign)
        side_lat.append(jnp.sum(flux * level_weight, axis=0, keepdims=True))

    def assemble(center, rows_in, cols_in, corner_in):
        lane8 = iota((8, 128), 1)
        lane48 = iota((ROWS, 128), 1)
        third = jnp.where(
            lane48 < 32, center[:, 256:384], jnp.where(lane48 < 64, cols_in(1), cols_in(0))
        )
        upper = jnp.concatenate([center[:, 0:256], third], axis=1)
        north_south = jnp.where(sub < 4, rows_in(1), rows_in(0))
        north = jnp.where(lane8 < 64, corner_in(3), corner_in(2))
        south = jnp.where(lane8 < 64, corner_in(1), corner_in(0))
        corner = jnp.where(iota((8, 128), 0) < 4, north, south)
        third = jnp.where(lane8 < 32, north_south[:, 256:384], corner)
        lower = jnp.concatenate([north_south[:, 0:256], third], axis=1)
        return jnp.concatenate([upper, lower], axis=0)

    damp_ext = assemble(
        damp_all,
        lambda slot: recv_rows[slot, 32:40, :],
        lambda slot: recv_cols[slot, ROWS:, :],
        lambda place: recv_corner[place],
    )
    inv = mask[...] * inverse(6.0 + damp_ext)
    scale[...] = 1.5 * inv
    weigh[...] = jnp.where(iota((ROWS, WIDE), 1) < COLS, 6.0 + damp_all, 0.0)

    lane_f = iota((ROWS, WIDE), 1)
    row_f = iota((ROWS, WIDE), 0)
    plain = flat[0]
    lon = flat[1] - 0.1 * (east_of(plain) - plain)
    lon = jnp.where(lane_f == COLS - 1, side_east, jnp.where(lane_f == WIDE - 1, side_west, lon))
    lat = flat[2] - 0.1 * (pltpu.roll(plain, ROWS - 1, 0) - plain)
    lat = jnp.where(row_f == ROWS - 1, side_lat[0], lat)
    lat_south = jnp.where(row_f == 0, side_lat[1], pltpu.roll(lat, 1, 0))
    start = plain - (lon - west_of(lon)) - (lat - lat_south)
    start = jnp.where(lane_f < COLS, start, 0.0) * inv[0:ROWS, :]
    basis[0] = jnp.zeros((EXT, WIDE), f32)
    basis[1, 0:ROWS, :] = start

    packed_rows = row_pack(start[0:8, :], start[ROWS - 8 : ROWS, :])
    halo_rows[...] = packed_rows
    halo_cols[...] = column_pack(start[:, 0:128], start[:, 256:384])
    halo_corner[...] = column_pack(packed_rows[:, 0:128], packed_rows[:, 256:384])
    second_round = []
    for side, step in enumerate((NORTH, SOUTH)):
        second_round.append(
            remote(halo_rows, recv_halo_rows.at[side], side, step, halo_send_sem, halo_recv_sem)
        )
    for side, step in enumerate((EAST, WEST)):
        second_round.append(
            remote(halo_cols, recv_halo_cols.at[side], 2 + side, step, halo_send_sem, halo_recv_sem)
        )
    for place, step in enumerate(DIAGONAL):
        second_round.append(
            remote(
                halo_corner,
                recv_halo_corner.at[place],
                4 + place,
                step,
                halo_send_sem,
                halo_recv_sem,
            )
        )
    for copy in second_round:
        copy.start()

    for copy in heat_round:
        copy.wait()
    for side, sign in ((0, 1.0), (1, -1.0)):
        slot = 1 - side
        target = flux_north if side == 0 else flux_prev
        heat_mine = send_heat[side]
        heat_theirs = recv_heat[slot] * exists[side]
        salt_mine = 2.0 * (heat_mine - send_rows[side, 0:16, :])
        salt_theirs = 2.0 * (heat_theirs - recv_rows[slot, 0:16, :] * exists[side])
        target[0:16, :] = side_flux(heat_mine, heat_theirs, speed_lat[side], sign)
        target[16:32, :] = side_flux(salt_mine, salt_theirs, speed_lat[side], sign)
    small[3].wait()

    edge_lane = (lane128 == 31) | (lane128 == 127)

    def mix_tile(i, _):
        rows = pl.ds(pl.multiple_of(8 * i, 8), 8)
        row = pl.ds(next_row(i), 1)
        here = mask[rows, :]
        beyond = mask[row, :]
        coefficient = padded(mix[rows, :])
        through = flux_lon[rows, :]
        use_north = (sub == 7) & (i == TILES - 1)

        def level(k, carry):
            ratio_low, heat_low, salt_low = carry
            u = padded(state[2, k, rows, :]) * here
            v = padded(state[3, k, rows, :]) * here
            v_row = padded(state[3, k, row, :]) * beyond
            v_north = jnp.where(sub == 7, v_row, pltpu.roll(v, 7, 0))
            u_pair = 0.05 * (u + east_of(u))
            v_pair = 0.05 * (v + v_north)
            lon_far, lon_near = u_pair - 0.1, u_pair + 0.1
            lat_far, lat_near = v_pair - 0.1, v_pair + 0.1
            below = coefficient * level_inv[pl.ds(k, 1), :]
            above = coefficient * level_inv[pl.ds(k + 1, 1), :]
            pivot = inverse(h[k] + above + below * (1.0 - ratio_low))
            ratio_now = above * pivot
            ratio[k] = ratio_now
            found = []
            for tracer, low in ((0, heat_low), (1, salt_low)):
                plane = tracer * LEV + k
                c = padded(state[tracer, k, rows, :]) * here
                c_row = padded(state[tracer, k, row, :]) * beyond
                c_north = jnp.where(sub == 7, c_row, pltpu.roll(c, 7, 0))
                lon = lon_far * east_of(c) + lon_near * c
                turned = pltpu.roll(through, 127 - plane, 1)
                lon = jnp.concatenate(
                    [lon[:, 0:256], jnp.where(edge_lane, turned, lon[:, 256:384])], axis=1
                )
                lat = lat_far * c_north + lat_near * c
                lat = jnp.where(use_north, flux_north[pl.ds(plane, 1), :], lat)
                lat_south = jnp.where(
                    sub == 0, flux_prev[pl.ds(plane, 1), :], pltpu.roll(lat, 1, 0)
                )
                flux_prev[pl.ds(plane, 1), :] = lat[7:8, :]
                advected = here * (c - (lon - west_of(lon)) - (lat - lat_south))
                value = (h[k] * advected + below * low) * pivot
                tracer_out[tracer, k, rows, :] = value[:, 0:COLS]
                found.append(value)
            return ratio_now, found[0], found[1]

        zero = jnp.zeros((8, WIDE), f32)
        _, heat, salt = lax.fori_loop(0, LEV, level, (zero, zero, zero), unroll=4)

        def back(step, carry):
            k = LEV - 2 - step
            heat_up, salt_up = carry
            share = ratio[k][:, 0:COLS]
            heat_up = tracer_out[0, k, rows, :] + share * heat_up
            salt_up = tracer_out[1, k, rows, :] + share * salt_up
            tracer_out[0, k, rows, :] = heat_up
            tracer_out[1, k, rows, :] = salt_up
            return heat_up, salt_up

        lax.fori_loop(0, LEV - 1, back, (heat[:, 0:COLS], salt[:, 0:COLS]), unroll=5)
        return 0

    def moments():
        for copy in second_round:
            copy.wait()
        basis[1] = mask[...] * assemble(
            basis[1, 0:ROWS, :],
            lambda slot: recv_halo_rows[slot],
            lambda slot: recv_halo_cols[slot],
            lambda place: recv_halo_corner[place],
        )

        @pl.loop(0, 4)
        def _(index):
            q = basis[index + 1]
            pair = east_of(q) + west_of(q)
            column = q + 0.5 * pair
            around = pair + pltpu.roll(column, EXT - 1, 0) + pltpu.roll(column, 1, 0)
            image = scale[...] * around - 0.5 * q
            later = jnp.where(index == 0, 0.0, 1.0)
            after = image + later * (image - basis[index])
            basis[index + 2] = after
            weighed = weigh[...] * q[0:ROWS, :]
            message[pl.ds(2 * index, 1), :] = folded(weighed * q[0:ROWS, :])
            message[pl.ds(2 * index + 1, 1), :] = folded(weighed * after[0:ROWS, :])

    def folded(value):
        value = value[:, 0:128] + value[:, 128:256] + value[:, 256:384]
        return jnp.sum(value, axis=0, keepdims=True)

    def spread(source, target, count, along, mine, base):
        target[mine] = source[...]

        @pl.loop(1, count)
        def _(d):
            pltpu.make_async_remote_copy(
                src_ref=source,
                dst_ref=target.at[mine],
                send_sem=sum_send_sem.at[base],
                recv_sem=sum_recv_sem.at[base],
                device_id=device(along(d)),
                device_id_type=MESH,
            ).start()

    def gathered(target, count, base):
        part = target.at[pl.ds(0, count - 1)]
        done = pltpu.make_async_remote_copy(
            src_ref=part,
            dst_ref=part,
            send_sem=sum_send_sem.at[base],
            recv_sem=sum_recv_sem.at[base],
            device_id=device(EAST),
            device_id_type=MESH,
        )
        done.wait_recv()
        done.wait_send()
        return jnp.sum(target[...], axis=0)

    moments()
    spread(message, first_sum, nx, lambda d: (d, 0), gx, 0)
    second_message[...] = gathered(first_sum, nx, 0)
    spread(second_message, second_sum, inner, along_inner, at_inner, 1)
    lax.fori_loop(0, 3, mix_tile, 0)
    third_message[...] = gathered(second_sum, inner, 1)
    spread(third_message, third_sum, outer, along_outer, at_outer, 2)
    lax.fori_loop(3, TILES, mix_tile, 0)
    sums = gathered(third_sum, outer, 2)

    sums = jnp.broadcast_to(jnp.sum(sums, axis=1, keepdims=True), (8, 128))
    dots = [sums[i : i + 1, :] for i in range(8)]
    moment = dots[0:2] + [2.0 * dots[i] - dots[i % 2] for i in range(2, 8)]

    def gram(i, j):
        return 0.5 * (moment[i + j] + moment[abs(i - j)])

    lower = {}
    pivots = []
    right = []
    for i in range(4):
        value = moment[i]
        for j in range(i + 1):
            entry = gram(i, j) - 0.5 * (gram(j, i + 1) + gram(j, abs(i - 1)))
            for k in range(j):
                entry = entry - lower[i, k] * lower[j, k] * pivots[k]
            if j < i:
                lower[i, j] = entry / pivots[j]
                value = value - lower[i, j] * right[j]
            else:
                pivots.append(entry)
        right.append(value)
    solved = [None] * 4
    for i in range(3, -1, -1):
        value = right[i] / pivots[i]
        for j in range(i + 1, 4):
            value = value - lower[j, i] * solved[j]
        solved[i] = value
    surface = None
    for i in range(4):
        factor = 1.5 * solved[i]
        factor = jnp.concatenate([factor, factor, factor], axis=1)
        term = factor * basis[i + 1, 0:ROWS, :]
        surface = term if surface is None else surface + term
    surface_out[...] = surface[:, 0:COLS]


def scratch(nx, ny):
    vmem = lambda *shape: pltpu.VMEM(shape, f32)
    dma = pltpu.SemaphoreType.DMA
    return [
        vmem(4, LEV, ROWS, COLS),
        pltpu.SMEM((LEV,), f32),
        vmem(ROWS, COLS),
        vmem(ROWS, COLS),
        None,
        vmem(EXT, WIDE),
        vmem(24, WIDE),
        vmem(3, ROWS, WIDE),
        vmem(2, 40, WIDE),
        vmem(2, LEV, WIDE),
        vmem(2, 40, WIDE),
        vmem(2, LEV, WIDE),
        vmem(2 * ROWS, 128),
        vmem(2, 2 * ROWS, 128),
        vmem(8, 128),
        vmem(4, 8, 128),
        vmem(ROWS, 128),
        vmem(2 * LEV, WIDE),
        vmem(2 * LEV, WIDE),
        vmem(LEV, 8, WIDE),
        vmem(EXT, WIDE),
        vmem(ROWS, WIDE),
        vmem(6, EXT, WIDE),
        vmem(8, WIDE),
        vmem(ROWS, 128),
        vmem(8, 128),
        vmem(2, 8, WIDE),
        vmem(2, ROWS, 128),
        vmem(4, 8, 128),
        vmem(8, 128),
        vmem(nx, 8, 128),
        vmem(8, 128),
        vmem(4 if ny >= 16 else 2, 8, 128),
        vmem(8, 128),
        vmem(ny // (4 if ny >= 16 else 2), 8, 128),
        dma((4,)),
        dma((4,)),
        dma((10,)),
        dma((10,)),
        dma((8,)),
        dma((8,)),
        dma((3,)),
        dma((3,)),
    ]


def solution(mesh):
    nx, ny = mesh.shape["gx"], mesh.shape["gy"]

    def body(ocean_state, layer_thickness, vertical_mixing, damping, ocean_blocks):
        shapes = scratch(nx, ny)
        shapes[4] = pltpu.VMEM(ocean_blocks.shape, jnp.int32)
        call = pl.pallas_call(
            functools.partial(kernel, nx, ny),
            out_shape=[
                pltpu.VMEM((2, LEV, ROWS, COLS), f32),
                pltpu.VMEM((ROWS, COLS), f32),
            ],
            in_specs=[pl.BlockSpec(memory_space=pltpu.HBM)] * 5,
            out_specs=[pl.BlockSpec(memory_space=pltpu.VMEM)] * 2,
            scratch_shapes=shapes,
            compiler_params=pltpu.CompilerParams(
                collective_id=0, has_side_effects=True, vmem_limit_bytes=32 * 1024 * 1024
            ),
        )
        operands = [
            pltpu.with_memory_space_constraint(operand, pltpu.HBM)
            for operand in (ocean_state, layer_thickness, vertical_mixing, damping, ocean_blocks)
        ]
        return tuple(call(*operands))

    def wrapped(*args):
        with jax.sharding.use_abstract_mesh(mesh.abstract_mesh):
            return jax.shard_map(
                body,
                mesh=mesh,
                in_specs=(P(None, None, "gy", "gx"), P(), P("gy", "gx"), P("gy", "gx"), P()),
                out_specs=(P(None, None, "gy", "gx"), P("gy", "gx")),
                check_vma=False,
            )(*args)

    return wrapped
```

```python
import functools

import jax
import jax.numpy as jnp
from jax import lax
from jax.experimental import pallas as pl
from jax.experimental.pallas import tpu as pltpu
from jax.sharding import PartitionSpec as P

BLAT = 24
BLON = 36
LEV = 16
ROWS = 48
COLS = 288
WIDE = 384
EXT = 56
TILES = ROWS // 8

f32 = jnp.float32
MESH = pl.DeviceIdType.MESH

NORTH, SOUTH, EAST, WEST = (0, 1), (0, -1), (1, 0), (-1, 0)
DIAGONAL = ((1, 1), (-1, 1), (1, -1), (-1, -1))


def iota(shape, dim):
    return lax.broadcasted_iota(jnp.int32, shape, dim)


def padded(value):
    return jnp.concatenate([value, jnp.zeros((value.shape[0], WIDE - COLS), f32)], axis=1)


def east_of(value):
    return pltpu.roll(value, WIDE - 1, 1)


def west_of(value):
    return pltpu.roll(value, 1, 1)


def inverse(value):
    guess = pl.reciprocal(value, approx=True)
    return guess * (2.0 - value * guess)


def row_pack(low, high):
    return jnp.where(iota(low.shape, 0) < 4, low, high)


def column_pack(first, last):
    lane = iota(first.shape, 1)
    low = pltpu.roll(first, 32, 1)
    high = pltpu.roll(last, 96, 1)
    return jnp.where(
        (lane >= 32) & (lane < 36), low, jnp.where(lane >= 124, high, 0.0)
    )


def kernel(
    nx,
    ny,
    ocean,
    thick,
    mixing,
    damping,
    blocks,
    tracer_out,
    surface_out,
    state,
    h,
    mix,
    damp,
    blk,
    mask,
    level_inv,
    flat,
    send_rows,
    send_heat,
    recv_rows,
    recv_heat,
    send_cols,
    recv_cols,
    send_corner,
    recv_corner,
    recv_side,
    flux_lon,
    flux_north,
    flux_prev,
    ratio,
    scale,
    weigh,
    basis,
    halo_rows,
    halo_cols,
    halo_corner,
    recv_halo_rows,
    recv_halo_cols,
    recv_halo_corner,
    message,
    first_sum,
    second_message,
    second_sum,
    load_sem,
    small_sem,
    send_sem,
    recv_sem,
    halo_send_sem,
    halo_recv_sem,
    sum_send_sem,
    sum_recv_sem,
):
    gx = lax.axis_index("gx")
    gy = lax.axis_index("gy")

    def device(step):
        return {"gx": lax.rem(gx + step[0] + nx, nx), "gy": lax.rem(gy + step[1] + ny, ny)}

    def greet(step):
        pl.semaphore_signal(barrier, inc=1, device_id=device(step), device_id_type=MESH)

    barrier = pltpu.get_barrier_semaphore()
    for step in DIAGONAL:
        greet(step)
    pl.loop(1, nx)(lambda d: greet((d, 0)))
    pl.loop(1, ny)(lambda d: greet((0, d)))
    partners = len(DIAGONAL) + nx - 1 + ny - 1

    small = [
        pltpu.make_async_copy(blocks, blk, small_sem.at[0]),
        pltpu.make_async_copy(thick, h, small_sem.at[1]),
        pltpu.make_async_copy(damping, damp, small_sem.at[2]),
        pltpu.make_async_copy(mixing, mix, small_sem.at[3]),
    ]
    group = LEV // 4

    def load(index):
        levels = pl.ds(group * index, group)
        return pltpu.make_async_copy(
            ocean.at[:, levels, :, :], state.at[:, levels, :, :], load_sem.at[index]
        )

    for copy in small[:3] + [load(index) for index in range(4)] + small[3:]:
        copy.start()

    block_rows, block_cols = blk.shape
    small[0].wait()
    row = iota((EXT, block_rows), 0)
    row = gy * ROWS + jnp.where(row < ROWS + 4, row, row - EXT)
    edge = iota((EXT, block_rows), 1) * BLAT
    pick_rows = jnp.where((row >= edge) & (row < edge + BLAT), 1.0, 0.0)
    lane = iota((block_cols, WIDE), 1)
    total = block_cols * BLON
    col = gx * COLS + jnp.where(lane < COLS + 4, lane, lane - WIDE)
    col = jnp.where(col < 0, col + total, jnp.where(col >= total, col - total, col))
    edge = iota((block_cols, WIDE), 0) * BLON
    inside = (lane < COLS + 4) | (lane >= WIDE - 4)
    pick_cols = jnp.where(inside & (col >= edge) & (col < edge + BLON), 1.0, 0.0)
    coarse = jnp.dot(pick_rows, blk[...].astype(f32), preferred_element_type=f32)
    mask[...] = jnp.dot(coarse, pick_cols, preferred_element_type=f32)

    small[1].wait()
    level_inv[...] = jnp.zeros(level_inv.shape, f32)

    @pl.loop(1, LEV)
    def _(k):
        level_inv[pl.ds(k, 1), :] = 1.0 / jnp.full((1, WIDE), h[k - 1] + h[k], f32)


    small[2].wait()
    damp_low = padded(damp[0:8, :])
    damp_high = padded(damp[ROWS - 8 : ROWS, :])
    damp_rows = row_pack(damp_low, damp_high)
    for side in range(2):
        send_rows[side, 32:40, :] = damp_rows
    damp_all = padded(damp[...])
    send_cols[ROWS : 2 * ROWS, :] = column_pack(damp_all[:, 0:128], damp_all[:, 256:384])
    send_corner[16:24, :] = column_pack(damp_rows[:, 0:128], damp_rows[:, 256:384])

    def remote(source, target, index, step, sends=send_sem, recvs=recv_sem):
        return pltpu.make_async_remote_copy(
            src_ref=source,
            dst_ref=target,
            send_sem=sends.at[index],
            recv_sem=recvs.at[index],
            device_id=device(step),
            device_id_type=MESH,
        )

    sub = iota((8, WIDE), 0)

    def next_row(i):
        return jnp.minimum(8 * i + 8, ROWS - 1)

    tiles = [pl.ds(8 * i, 8) for i in range(TILES)]
    flat[...] = jnp.zeros(flat.shape, f32)

    def turned_up(values):
        turned = [pltpu.roll(value, 7, 0) for value in values]
        return [
            jnp.where(sub == 7, turned[(i + 1) % TILES], turned[i]) for i in range(TILES)
        ]

    @pl.loop(0, LEV // 2)
    def _(pair):
        @pl.when(lax.rem(pair, group // 2) == 0)
        def _():
            load(pair // (group // 2)).wait()

        sums = None
        for k in (2 * pair, 2 * pair + 1):
            s = [
                padded(state[0, k, rows, :] - 0.5 * state[1, k, rows, :]) * mask[rows, :] * h[k]
                for rows in tiles
            ]
            v = [padded(state[3, k, rows, :]) * mask[rows, :] for rows in tiles]
            s_north, v_north = turned_up(s), turned_up(v)
            found = []
            for i, rows in enumerate(tiles):
                u = padded(state[2, k, rows, :]) * mask[rows, :]
                found.append(
                    (
                        s[i],
                        (u + east_of(u)) * (s[i] + east_of(s[i])),
                        (v[i] + v_north[i]) * (s[i] + s_north[i]),
                    )
                )
            if sums is None:
                sums = found
            else:
                sums = [[a + b for a, b in zip(x, y)] for x, y in zip(sums, found)]
        for i, rows in enumerate(tiles):
            for part in range(3):
                flat[part, rows, :] += sums[i][part]

    first_round = []
    for side, (edge_row, step) in enumerate(((ROWS - 1, NORTH), (0, SOUTH))):
        edge_mask = mask[edge_row : edge_row + 1, :]
        heat = padded(state[0, :, edge_row, :]) * edge_mask
        salt = padded(state[1, :, edge_row, :]) * edge_mask
        send_heat[side] = heat
        send_rows[side, 0:16, :] = heat - 0.5 * salt
        send_rows[side, 16:32, :] = padded(state[3, :, edge_row, :]) * edge_mask
        first_round.append(remote(send_rows.at[side], recv_rows.at[side], side, step))

    pl.semaphore_wait(barrier, partners)
    for copy in first_round:
        copy.start()

    lane128 = iota((8, 128), 1)

    @pl.loop(0, TILES)
    def _(i):
        rows = pl.ds(pl.multiple_of(8 * i, 8), 8)
        edge_mask = jnp.where(lane128 == 31, mask[rows, 256:384], mask[rows, 0:128])
        acc_west = jnp.zeros((8, 128), f32)
        acc_east = jnp.zeros((8, 128), f32)
        for field, base in ((0, 0), (1, 16), (2, 64)):
            for k in range(LEV):
                first = state[field, k, rows, 0:128]
                last = jnp.concatenate(
                    [state[field, k, rows, 256:COLS], jnp.zeros((8, WIDE - COLS), f32)], axis=1
                )
                merged = jnp.where(lane128 == 31, last, first)
                turned = pltpu.roll(merged, base + k, 1) if base + k else merged
                acc_west = jnp.where(lane128 == base + k, turned, acc_west)
                acc_east = jnp.where(lane128 == base + k + 31, turned, acc_east)
        west_mask = jnp.broadcast_to(edge_mask[:, 0:1], (8, 128))
        east_mask = jnp.broadcast_to(edge_mask[:, 31:32], (8, 128))
        send_cols[rows, :] = acc_west * west_mask + pltpu.roll(acc_east, 1, 1) * east_mask


    compact = jnp.zeros((8, 128), f32)
    for side in range(2):
        for part in range(4):
            j = 4 * side + part
            rows = pl.ds(8 * part, 8)
            first = pltpu.roll(send_rows[side, rows, 0:128], 16 * j, 1)
            last = pltpu.roll(send_rows[side, rows, 256:384], (16 * j - 24) % 128, 1)
            inside = lane128 // 16 == j
            compact = jnp.where(inside & (lane128 % 16 < 4), first, compact)
            compact = jnp.where(
                inside & (lane128 % 16 >= 4) & (lane128 % 16 < 8), last, compact
            )
    send_corner[0:8, :] = compact
    send_cols[2 * ROWS :, :] = compact
    send_corner[8:16, :] = row_pack(send_cols[0:8, :], send_cols[ROWS - 8 : ROWS, :])

    second_round = []
    for side, step in enumerate((EAST, WEST)):
        second_round.append(remote(send_cols, recv_cols.at[side], 2 + side, step))
    for place, step in enumerate(DIAGONAL):
        second_round.append(remote(send_corner, recv_corner.at[place], 4 + place, step))
    for side, step in enumerate((NORTH, SOUTH)):
        second_round.append(
            remote(send_corner.at[pl.ds(8, 8)], recv_side.at[side], 10 + side, step)
        )
    for copy in second_round:
        copy.start()
    first_round = first_round + second_round

    lane_f = iota((ROWS, WIDE), 1)
    row_f = iota((ROWS, WIDE), 0)
    plain = flat[0]
    lon = 0.05 * flat[1] - 0.1 * (east_of(plain) - plain)
    lon = jnp.where(lane_f < COLS - 1, lon, 0.0)
    lat = 0.05 * flat[2] - 0.1 * (pltpu.roll(plain, ROWS - 1, 0) - plain)
    lat = jnp.where(row_f == ROWS - 1, 0.0, lat)
    start = plain - (lon - west_of(lon)) - (lat - pltpu.roll(lat, 1, 0))
    start = jnp.where(lane_f < COLS, start, 0.0)
    basis[1, 0:ROWS, :] = start
    packed_rows = row_pack(start[0:8, :], start[ROWS - 8 : ROWS, :])
    halo_rows[...] = packed_rows
    halo_cols[...] = column_pack(start[:, 0:128], start[:, 256:384])
    halo_corner[...] = column_pack(packed_rows[:, 0:128], packed_rows[:, 256:384])
    second_round = []
    for side, step in enumerate((NORTH, SOUTH)):
        second_round.append(
            remote(halo_rows, recv_halo_rows.at[side], side, step, halo_send_sem, halo_recv_sem)
        )
    for side, step in enumerate((EAST, WEST)):
        second_round.append(
            remote(halo_cols, recv_halo_cols.at[side], 2 + side, step, halo_send_sem, halo_recv_sem)
        )
    for place, step in enumerate(DIAGONAL):
        second_round.append(
            remote(
                halo_corner,
                recv_halo_corner.at[place],
                4 + place,
                step,
                halo_send_sem,
                halo_recv_sem,
            )
        )
    for copy in second_round:
        copy.start()
    heat_round = []
    for side, step in enumerate((NORTH, SOUTH)):
        copy = remote(send_heat.at[side], recv_heat.at[side], 8 + side, step)
        copy.start()
        heat_round.append(copy)

    for copy in first_round + second_round:
        copy.wait()

    def beside(north, south):
        return jnp.where(iota((8, 128), 0) < 4, north, south)

    own = jnp.concatenate([send_cols[0:ROWS, :], beside(recv_side[1], recv_side[0])], axis=0)
    from_east = jnp.concatenate(
        [recv_cols[1, 0:ROWS, :], beside(recv_corner[3, 8:16, :], recv_corner[1, 8:16, :])], axis=0
    )
    from_west = jnp.concatenate(
        [recv_cols[0, 0:ROWS, :], beside(recv_corner[2, 8:16, :], recv_corner[0, 8:16, :])], axis=0
    )
    lane_c = iota((EXT, 128), 1)
    is_east = (lane_c & 32) != 0
    other = jnp.where(is_east, pltpu.roll(from_east, 32, 1), pltpu.roll(from_west, 96, 1))
    both = own + other
    speed = pltpu.roll(both, 64, 1)
    speed = jnp.where((lane_c & 16) != 0, pltpu.roll(speed, 16, 1), speed)
    slope = jnp.where(is_east, 0.1, -0.1) * (other - own)
    through = 0.05 * speed * both - slope
    flux_lon[...] = through[0:ROWS, :]
    weight = jnp.zeros((1, 128), f32)
    lane_w = iota((1, 128), 1)
    for k in range(LEV):
        weight = jnp.where((lane_w & 15) == k, h[k], weight)
    weight = weight * jnp.where((lane_w & 16) != 0, -0.5, 1.0)
    weighed = through * weight
    side_west = jnp.sum(jnp.where(lane_c < 32, weighed, 0.0), axis=1, keepdims=True)
    side_east = jnp.sum(
        jnp.where(is_east & (lane_c < 64), weighed, 0.0), axis=1, keepdims=True
    )

    level_weight = jnp.zeros((LEV, WIDE), f32)
    level_row = iota((LEV, WIDE), 0)
    for k in range(LEV):
        level_weight = jnp.where(level_row == k, h[k], level_weight)
    exists = (
        jnp.where(gy < ny - 1, 1.0, 0.0).astype(f32),
        jnp.where(gy > 0, 1.0, 0.0).astype(f32),
    )

    def side_flux(mine, theirs, speeds, sign):
        return speeds * (mine + theirs) - (0.1 * sign) * (theirs - mine)

    side_lat = []
    speed_lat = []
    for side, sign in ((0, 1.0), (1, -1.0)):
        slot = 1 - side
        s_mine = send_rows[side, 0:16, :]
        s_theirs = recv_rows[slot, 0:16, :] * exists[side]
        speeds = 0.05 * (send_rows[side, 16:32, :] + recv_rows[slot, 16:32, :] * exists[side])
        speed_lat.append(speeds)
        flux = side_flux(s_mine, s_theirs, speeds, sign)
        side_lat.append(jnp.sum(flux * level_weight, axis=0, keepdims=True))

    is_first = (lane128 & 15) < 4
    is_north = lane128 < 64
    mine = jnp.where(is_first, recv_cols[1, 2 * ROWS :, :], recv_cols[0, 2 * ROWS :, :])
    theirs_north = jnp.where(is_first, recv_corner[3, 0:8, :], recv_corner[2, 0:8, :])
    theirs_south = jnp.where(is_first, recv_corner[1, 0:8, :], recv_corner[0, 0:8, :])
    theirs = pltpu.roll(
        jnp.where(is_north, theirs_south * exists[1], theirs_north * exists[0]), 64, 1
    )
    both = mine + theirs
    flux = 0.05 * pltpu.roll(both, 96, 1) * both - jnp.where(is_north, 0.1, -0.1) * (theirs - mine)
    flux = flux * jnp.where(
        (lane128 & 16) == 0, level_weight[0:8, 0:128], level_weight[8:16, 0:128]
    )
    flux = jnp.sum(flux, axis=0, keepdims=True)
    flux = flux + pltpu.roll(flux, 112, 1)
    for side in range(2):
        low = pltpu.roll(flux, 32 - 64 * side if side == 0 else 96, 1)
        high = pltpu.roll(flux, 120 if side == 0 else 56, 1)
        third = jnp.where(
            lane_w < 32, side_lat[side][:, 256:384], jnp.where(lane_w < 64, low, high)
        )
        side_lat[side] = jnp.concatenate([side_lat[side][:, 0:256], third], axis=1)

    def assemble(center, rows_in, cols_in, corner_in):
        lane8 = iota((8, 128), 1)
        lane48 = iota((ROWS, 128), 1)
        third = jnp.where(
            lane48 < 32, center[:, 256:384], jnp.where(lane48 < 64, cols_in(1), cols_in(0))
        )
        upper = jnp.concatenate([center[:, 0:256], third], axis=1)
        north_south = jnp.where(sub < 4, rows_in(1), rows_in(0))
        north = jnp.where(lane8 < 64, corner_in(3), corner_in(2))
        south = jnp.where(lane8 < 64, corner_in(1), corner_in(0))
        corner = jnp.where(iota((8, 128), 0) < 4, north, south)
        third = jnp.where(lane8 < 32, north_south[:, 256:384], corner)
        lower = jnp.concatenate([north_south[:, 0:256], third], axis=1)
        return jnp.concatenate([upper, lower], axis=0)

    damp_ext = assemble(
        damp_all,
        lambda slot: recv_rows[slot, 32:40, :],
        lambda slot: recv_cols[slot, ROWS : 2 * ROWS, :],
        lambda place: recv_corner[place, 16:24, :],
    )
    inv = mask[...] * inverse(6.0 + damp_ext)
    scale[...] = 1.5 * inv
    weigh[...] = jnp.where(iota((ROWS, WIDE), 1) < COLS, 6.0 + damp_all, 0.0)
    forcing = assemble(
        basis[1, 0:ROWS, :],
        lambda slot: recv_halo_rows[slot],
        lambda slot: recv_halo_cols[slot],
        lambda place: recv_halo_corner[place],
    )
    forcing = jnp.concatenate(
        [
            forcing[:, 0:128] + jnp.where(lane_c == 0, side_west, 0.0),
            forcing[:, 128:256],
            forcing[:, 256:384]
            + jnp.where(
                lane_c == 31,
                -side_east,
                jnp.where(lane_c == 32, side_east, jnp.where(lane_c == 127, -side_west, 0.0)),
            ),
        ],
        axis=1,
    )
    north, south = side_lat
    forcing = jnp.concatenate(
        [
            forcing[0:8, :] + jnp.where(sub == 0, south, 0.0),
            forcing[8:40, :],
            forcing[40:48, :] - jnp.where(sub == 7, north, 0.0),
            forcing[48:56, :]
            + jnp.where(sub == 0, north, jnp.where(sub == 7, -south, 0.0)),
        ],
        axis=0,
    )
    basis[0] = jnp.zeros((EXT, WIDE), f32)
    basis[1] = forcing * inv

    def folded(value):
        value = value[:, 0:128] + value[:, 128:256] + value[:, 256:384]
        return jnp.sum(value, axis=0, keepdims=True)

    @pl.loop(0, 4)
    def _(index):
        q = basis[index + 1]
        pair = east_of(q) + west_of(q)
        column = q + 0.5 * pair
        around = pair + pltpu.roll(column, EXT - 1, 0) + pltpu.roll(column, 1, 0)
        image = scale[...] * around - 0.5 * q
        later = jnp.where(index == 0, 0.0, 1.0)
        after = image + later * (image - basis[index])
        basis[index + 2] = after
        weighed = weigh[...] * q[0:ROWS, :]
        message[pl.ds(2 * index, 1), :] = folded(weighed * q[0:ROWS, :])
        message[pl.ds(2 * index + 1, 1), :] = folded(weighed * after[0:ROWS, :])

    def spread(source, target, count, along, mine, base):
        target[mine] = source[...]

        @pl.loop(1, count)
        def _(d):
            pltpu.make_async_remote_copy(
                src_ref=source,
                dst_ref=target.at[mine],
                send_sem=sum_send_sem.at[base],
                recv_sem=sum_recv_sem.at[base],
                device_id=device(along(d)),
                device_id_type=MESH,
            ).start()

    def gathered(target, count, base):
        part = target.at[pl.ds(0, count - 1)]
        done = pltpu.make_async_remote_copy(
            src_ref=part,
            dst_ref=part,
            send_sem=sum_send_sem.at[base],
            recv_sem=sum_recv_sem.at[base],
            device_id=device(EAST),
            device_id_type=MESH,
        )
        done.wait_recv()
        done.wait_send()
        return jnp.sum(target[...], axis=0)

    spread(message, first_sum, nx, lambda d: (d, 0), gx, 0)

    for copy in heat_round:
        copy.wait()
    for side, sign in ((0, 1.0), (1, -1.0)):
        slot = 1 - side
        target = flux_north if side == 0 else flux_prev
        heat_mine = send_heat[side]
        heat_theirs = recv_heat[slot] * exists[side]
        salt_mine = 2.0 * (heat_mine - send_rows[side, 0:16, :])
        salt_theirs = 2.0 * (heat_theirs - recv_rows[slot, 0:16, :] * exists[side])
        target[0:16, :] = side_flux(heat_mine, heat_theirs, speed_lat[side], sign)
        target[16:32, :] = side_flux(salt_mine, salt_theirs, speed_lat[side], sign)
    small[3].wait()

    edge_lane = (lane128 == 31) | (lane128 == 127)

    def mix_tile(i, _):
        rows = pl.ds(pl.multiple_of(8 * i, 8), 8)
        row = pl.ds(next_row(i), 1)
        here = mask[rows, :]
        beyond = mask[row, :]
        coefficient = padded(mix[rows, :])
        through = flux_lon[rows, :]
        use_north = (sub == 7) & (i == TILES - 1)

        def level(k, carry):
            ratio_low, heat_low, salt_low = carry
            u = padded(state[2, k, rows, :]) * here
            v = padded(state[3, k, rows, :]) * here
            v_row = padded(state[3, k, row, :]) * beyond
            v_north = jnp.where(sub == 7, v_row, pltpu.roll(v, 7, 0))
            u_pair = 0.05 * (u + east_of(u))
            v_pair = 0.05 * (v + v_north)
            lon_far, lon_near = u_pair - 0.1, u_pair + 0.1
            lat_far, lat_near = v_pair - 0.1, v_pair + 0.1
            below = coefficient * level_inv[pl.ds(k, 1), :]
            above = coefficient * level_inv[pl.ds(k + 1, 1), :]
            pivot = inverse(h[k] + above + below * (1.0 - ratio_low))
            ratio_now = above * pivot
            ratio[k] = ratio_now
            found = []
            for tracer, low in ((0, heat_low), (1, salt_low)):
                plane = tracer * LEV + k
                c = padded(state[tracer, k, rows, :]) * here
                c_row = padded(state[tracer, k, row, :]) * beyond
                c_north = jnp.where(sub == 7, c_row, pltpu.roll(c, 7, 0))
                lon = lon_far * east_of(c) + lon_near * c
                turned = pltpu.roll(through, 127 - plane, 1)
                lon = jnp.concatenate(
                    [lon[:, 0:256], jnp.where(edge_lane, turned, lon[:, 256:384])], axis=1
                )
                lat = lat_far * c_north + lat_near * c
                lat = jnp.where(use_north, flux_north[pl.ds(plane, 1), :], lat)
                lat_south = jnp.where(
                    sub == 0, flux_prev[pl.ds(plane, 1), :], pltpu.roll(lat, 1, 0)
                )
                flux_prev[pl.ds(plane, 1), :] = lat[7:8, :]
                advected = here * (c - (lon - west_of(lon)) - (lat - lat_south))
                value = (h[k] * advected + below * low) * pivot
                tracer_out[tracer, k, rows, :] = value[:, 0:COLS]
                found.append(value)
            return ratio_now, found[0], found[1]

        zero = jnp.zeros((8, WIDE), f32)
        _, heat, salt = lax.fori_loop(0, LEV, level, (zero, zero, zero), unroll=4)

        def back(step, carry):
            k = LEV - 2 - step
            heat_up, salt_up = carry
            share = ratio[k][:, 0:COLS]
            heat_up = tracer_out[0, k, rows, :] + share * heat_up
            salt_up = tracer_out[1, k, rows, :] + share * salt_up
            tracer_out[0, k, rows, :] = heat_up
            tracer_out[1, k, rows, :] = salt_up
            return heat_up, salt_up

        lax.fori_loop(0, LEV - 1, back, (heat[:, 0:COLS], salt[:, 0:COLS]), unroll=5)
        return 0

    lax.fori_loop(0, 2, mix_tile, 0)
    second_message[...] = gathered(first_sum, nx, 0)
    spread(second_message, second_sum, ny, lambda d: (0, d), gy, 1)
    lax.fori_loop(2, TILES, mix_tile, 0)
    sums = gathered(second_sum, ny, 1)

    sums = jnp.broadcast_to(jnp.sum(sums, axis=1, keepdims=True), (8, 128))
    dots = [sums[i : i + 1, :] for i in range(8)]
    moment = dots[0:2] + [2.0 * dots[i] - dots[i % 2] for i in range(2, 8)]

    def gram(i, j):
        return 0.5 * (moment[i + j] + moment[abs(i - j)])

    lower = {}
    pivots = []
    right = []
    for i in range(4):
        value = moment[i]
        for j in range(i + 1):
            entry = gram(i, j) - 0.5 * (gram(j, i + 1) + gram(j, abs(i - 1)))
            for k in range(j):
                entry = entry - lower[i, k] * lower[j, k] * pivots[k]
            if j < i:
                lower[i, j] = entry / pivots[j]
                value = value - lower[i, j] * right[j]
            else:
                pivots.append(entry)
        right.append(value)
    solved = [None] * 4
    for i in range(3, -1, -1):
        value = right[i] / pivots[i]
        for j in range(i + 1, 4):
            value = value - lower[j, i] * solved[j]
        solved[i] = value
    surface = None
    for i in range(4):
        factor = 1.5 * solved[i]
        factor = jnp.concatenate([factor, factor, factor], axis=1)
        term = factor * basis[i + 1, 0:ROWS, :]
        surface = term if surface is None else surface + term
    surface_out[...] = surface[:, 0:COLS]


def scratch(nx, ny):
    vmem = lambda *shape: pltpu.VMEM(shape, f32)
    dma = pltpu.SemaphoreType.DMA
    return [
        vmem(4, LEV, ROWS, COLS),
        pltpu.SMEM((LEV,), f32),
        vmem(ROWS, COLS),
        vmem(ROWS, COLS),
        None,
        vmem(EXT, WIDE),
        vmem(24, WIDE),
        vmem(3, ROWS, WIDE),
        vmem(2, 40, WIDE),
        vmem(2, LEV, WIDE),
        vmem(2, 40, WIDE),
        vmem(2, LEV, WIDE),
        vmem(2 * ROWS + 8, 128),
        vmem(2, 2 * ROWS + 8, 128),
        vmem(24, 128),
        vmem(4, 24, 128),
        vmem(2, 8, 128),
        vmem(ROWS, 128),
        vmem(2 * LEV, WIDE),
        vmem(2 * LEV, WIDE),
        vmem(LEV, 8, WIDE),
        vmem(EXT, WIDE),
        vmem(ROWS, WIDE),
        vmem(6, EXT, WIDE),
        vmem(8, WIDE),
        vmem(ROWS, 128),
        vmem(8, 128),
        vmem(2, 8, WIDE),
        vmem(2, ROWS, 128),
        vmem(4, 8, 128),
        vmem(8, 128),
        vmem(nx, 8, 128),
        vmem(8, 128),
        vmem(ny, 8, 128),
        dma((4,)),
        dma((4,)),
        dma((12,)),
        dma((12,)),
        dma((8,)),
        dma((8,)),
        dma((2,)),
        dma((2,)),
    ]


def solution(mesh):
    nx, ny = mesh.shape["gx"], mesh.shape["gy"]

    def body(ocean_state, layer_thickness, vertical_mixing, damping, ocean_blocks):
        shapes = scratch(nx, ny)
        shapes[4] = pltpu.VMEM(ocean_blocks.shape, jnp.int32)
        call = pl.pallas_call(
            functools.partial(kernel, nx, ny),
            out_shape=[
                pltpu.VMEM((2, LEV, ROWS, COLS), f32),
                pltpu.VMEM((ROWS, COLS), f32),
            ],
            in_specs=[pl.BlockSpec(memory_space=pltpu.HBM)] * 5,
            out_specs=[pl.BlockSpec(memory_space=pltpu.VMEM)] * 2,
            scratch_shapes=shapes,
            compiler_params=pltpu.CompilerParams(
                collective_id=0, has_side_effects=True, vmem_limit_bytes=32 * 1024 * 1024
            ),
        )
        operands = [
            pltpu.with_memory_space_constraint(operand, pltpu.HBM)
            for operand in (ocean_state, layer_thickness, vertical_mixing, damping, ocean_blocks)
        ]
        return tuple(call(*operands))

    def wrapped(*args):
        with jax.sharding.use_abstract_mesh(mesh.abstract_mesh):
            return jax.shard_map(
                body,
                mesh=mesh,
                in_specs=(P(None, None, "gy", "gx"), P(), P("gy", "gx"), P("gy", "gx"), P()),
                out_specs=(P(None, None, "gy", "gx"), P("gy", "gx")),
                check_vma=False,
            )(*args)

    return wrapped
```

```python
import functools

import jax
import jax.numpy as jnp
from jax import lax
from jax.experimental import pallas as pl
from jax.experimental.pallas import tpu as pltpu
from jax.sharding import PartitionSpec as P

BLAT = 24
BLON = 36
LEV = 16
ROWS = 48
COLS = 288
WIDE = 384
EXT = 56
TILES = ROWS // 8

f32 = jnp.float32
MESH = pl.DeviceIdType.MESH

NORTH, SOUTH, EAST, WEST = (0, 1), (0, -1), (1, 0), (-1, 0)
DIAGONAL = ((1, 1), (-1, 1), (1, -1), (-1, -1))


def iota(shape, dim):
    return lax.broadcasted_iota(jnp.int32, shape, dim)


def padded(value):
    return jnp.concatenate([value, jnp.zeros((value.shape[0], WIDE - COLS), f32)], axis=1)


def east_of(value):
    return pltpu.roll(value, WIDE - 1, 1)


def west_of(value):
    return pltpu.roll(value, 1, 1)


def inverse(value):
    guess = pl.reciprocal(value, approx=True)
    return guess * (2.0 - value * guess)


def row_pack(low, high):
    return jnp.where(iota(low.shape, 0) < 4, low, high)


def column_pack(first, last):
    lane = iota(first.shape, 1)
    low = pltpu.roll(first, 32, 1)
    high = pltpu.roll(last, 96, 1)
    return jnp.where(
        (lane >= 32) & (lane < 36), low, jnp.where(lane >= 124, high, 0.0)
    )


def kernel(
    nx,
    ny,
    ocean,
    thick,
    mixing,
    damping,
    blocks,
    tracer_out,
    surface_out,
    state,
    h,
    mix,
    damp,
    blk,
    mask,
    level_inv,
    flat,
    send_rows,
    send_heat,
    recv_rows,
    recv_heat,
    send_cols,
    recv_cols,
    send_corner,
    recv_corner,
    recv_side,
    flux_lon,
    flux_north,
    flux_prev,
    ratio,
    scale,
    weigh,
    basis,
    halo_rows,
    halo_cols,
    halo_corner,
    recv_halo_rows,
    recv_halo_cols,
    recv_halo_corner,
    message,
    first_sum,
    second_message,
    second_sum,
    load_sem,
    small_sem,
    send_sem,
    recv_sem,
    halo_send_sem,
    halo_recv_sem,
    sum_send_sem,
    sum_recv_sem,
):
    gx = lax.axis_index("gx")
    gy = lax.axis_index("gy")

    def device(step):
        return {"gx": lax.rem(gx + step[0] + nx, nx), "gy": lax.rem(gy + step[1] + ny, ny)}

    def greet(step):
        pl.semaphore_signal(barrier, inc=1, device_id=device(step), device_id_type=MESH)

    small = [
        pltpu.make_async_copy(blocks, blk, small_sem.at[0]),
        pltpu.make_async_copy(thick, h, small_sem.at[1]),
        pltpu.make_async_copy(damping, damp, small_sem.at[2]),
        pltpu.make_async_copy(mixing, mix, small_sem.at[3]),
    ]
    group = LEV // 4

    def load(index):
        levels = pl.ds(group * index, group)
        return pltpu.make_async_copy(
            ocean.at[:, levels, :, :], state.at[:, levels, :, :], load_sem.at[index]
        )

    for copy in small[:3] + [load(index) for index in range(4)] + small[3:]:
        copy.start()

    barrier = pltpu.get_barrier_semaphore()
    for step in DIAGONAL:
        greet(step)
    pl.loop(1, nx)(lambda d: greet((d, 0)))
    pl.loop(1, ny)(lambda d: greet((0, d)))
    partners = len(DIAGONAL) + nx - 1 + ny - 1

    block_rows, block_cols = blk.shape
    small[0].wait()
    row = iota((EXT, block_rows), 0)
    row = gy * ROWS + jnp.where(row < ROWS + 4, row, row - EXT)
    edge = iota((EXT, block_rows), 1) * BLAT
    pick_rows = jnp.where((row >= edge) & (row < edge + BLAT), 1.0, 0.0)
    lane = iota((block_cols, WIDE), 1)
    total = block_cols * BLON
    col = gx * COLS + jnp.where(lane < COLS + 4, lane, lane - WIDE)
    col = jnp.where(col < 0, col + total, jnp.where(col >= total, col - total, col))
    edge = iota((block_cols, WIDE), 0) * BLON
    inside = (lane < COLS + 4) | (lane >= WIDE - 4)
    pick_cols = jnp.where(inside & (col >= edge) & (col < edge + BLON), 1.0, 0.0)
    coarse = jnp.dot(pick_rows, blk[...].astype(f32), preferred_element_type=f32)
    mask[...] = jnp.dot(coarse, pick_cols, preferred_element_type=f32)

    small[1].wait()
    level_inv[...] = jnp.zeros(level_inv.shape, f32)

    @pl.loop(1, LEV)
    def _(k):
        level_inv[pl.ds(k, 1), :] = 1.0 / jnp.full((1, WIDE), h[k - 1] + h[k], f32)


    small[2].wait()
    damp_low = padded(damp[0:8, :])
    damp_high = padded(damp[ROWS - 8 : ROWS, :])
    damp_rows = row_pack(damp_low, damp_high)
    for side in range(2):
        send_rows[side, 32:40, :] = damp_rows
    damp_all = padded(damp[...])
    send_cols[ROWS : 2 * ROWS, :] = column_pack(damp_all[:, 0:128], damp_all[:, 256:384])
    send_corner[16:24, :] = column_pack(damp_rows[:, 0:128], damp_rows[:, 256:384])

    def remote(source, target, index, step, sends=send_sem, recvs=recv_sem):
        return pltpu.make_async_remote_copy(
            src_ref=source,
            dst_ref=target,
            send_sem=sends.at[index],
            recv_sem=recvs.at[index],
            device_id=device(step),
            device_id_type=MESH,
        )

    sub = iota((8, WIDE), 0)

    def next_row(i):
        return jnp.minimum(8 * i + 8, ROWS - 1)

    tiles = [pl.ds(8 * i, 8) for i in range(TILES)]
    flat[...] = jnp.zeros(flat.shape, f32)

    def turned_up(values):
        turned = [pltpu.roll(value, 7, 0) for value in values]
        return [
            jnp.where(sub == 7, turned[(i + 1) % TILES], turned[i]) for i in range(TILES)
        ]

    @pl.loop(0, LEV // 2)
    def _(pair):
        @pl.when(lax.rem(pair, group // 2) == 0)
        def _():
            load(pair // (group // 2)).wait()

        sums = None
        for k in (2 * pair, 2 * pair + 1):
            s = [
                padded(state[0, k, rows, :] - 0.5 * state[1, k, rows, :]) * mask[rows, :] * h[k]
                for rows in tiles
            ]
            v = [padded(state[3, k, rows, :]) * mask[rows, :] for rows in tiles]
            s_north, v_north = turned_up(s), turned_up(v)
            found = []
            for i, rows in enumerate(tiles):
                u = padded(state[2, k, rows, :]) * mask[rows, :]
                found.append(
                    (
                        s[i],
                        (u + east_of(u)) * (s[i] + east_of(s[i])),
                        (v[i] + v_north[i]) * (s[i] + s_north[i]),
                    )
                )
            if sums is None:
                sums = found
            else:
                sums = [[a + b for a, b in zip(x, y)] for x, y in zip(sums, found)]
        for i, rows in enumerate(tiles):
            for part in range(3):
                flat[part, rows, :] += sums[i][part]

    first_round = []
    for side, (edge_row, step) in enumerate(((ROWS - 1, NORTH), (0, SOUTH))):
        edge_mask = mask[edge_row : edge_row + 1, :]
        heat = padded(state[0, :, edge_row, :]) * edge_mask
        salt = padded(state[1, :, edge_row, :]) * edge_mask
        send_heat[side] = heat
        send_rows[side, 0:16, :] = heat - 0.5 * salt
        send_rows[side, 16:32, :] = padded(state[3, :, edge_row, :]) * edge_mask
        first_round.append(remote(send_rows.at[side], recv_rows.at[side], side, step))

    pl.semaphore_wait(barrier, partners)
    for copy in first_round:
        copy.start()

    lane128 = iota((8, 128), 1)

    @pl.loop(0, TILES)
    def _(i):
        rows = pl.ds(pl.multiple_of(8 * i, 8), 8)
        edge_mask = jnp.where(lane128 == 31, mask[rows, 256:384], mask[rows, 0:128])
        acc_west = jnp.zeros((8, 128), f32)
        acc_east = jnp.zeros((8, 128), f32)
        for field, base in ((0, 0), (1, 16), (2, 64)):
            for k in range(LEV):
                first = state[field, k, rows, 0:128]
                last = jnp.concatenate(
                    [state[field, k, rows, 256:COLS], jnp.zeros((8, WIDE - COLS), f32)], axis=1
                )
                merged = jnp.where(lane128 == 31, last, first)
                turned = pltpu.roll(merged, base + k, 1) if base + k else merged
                acc_west = jnp.where(lane128 == base + k, turned, acc_west)
                acc_east = jnp.where(lane128 == base + k + 31, turned, acc_east)
        west_mask = jnp.broadcast_to(edge_mask[:, 0:1], (8, 128))
        east_mask = jnp.broadcast_to(edge_mask[:, 31:32], (8, 128))
        send_cols[rows, :] = acc_west * west_mask + pltpu.roll(acc_east, 1, 1) * east_mask


    compact = jnp.zeros((8, 128), f32)
    for side in range(2):
        for part in range(4):
            j = 4 * side + part
            rows = pl.ds(8 * part, 8)
            first = pltpu.roll(send_rows[side, rows, 0:128], 16 * j, 1)
            last = pltpu.roll(send_rows[side, rows, 256:384], (16 * j - 24) % 128, 1)
            inside = lane128 // 16 == j
            compact = jnp.where(inside & (lane128 % 16 < 4), first, compact)
            compact = jnp.where(
                inside & (lane128 % 16 >= 4) & (lane128 % 16 < 8), last, compact
            )
    send_corner[0:8, :] = compact
    send_cols[2 * ROWS :, :] = compact
    send_corner[8:16, :] = row_pack(send_cols[0:8, :], send_cols[ROWS - 8 : ROWS, :])

    second_round = []
    for side, step in enumerate((EAST, WEST)):
        second_round.append(remote(send_cols, recv_cols.at[side], 2 + side, step))
    for place, step in enumerate(DIAGONAL):
        second_round.append(remote(send_corner, recv_corner.at[place], 4 + place, step))
    for side, step in enumerate((NORTH, SOUTH)):
        second_round.append(
            remote(send_corner.at[pl.ds(8, 8)], recv_side.at[side], 10 + side, step)
        )
    for copy in second_round:
        copy.start()
    first_round = first_round + second_round

    lane_f = iota((ROWS, WIDE), 1)
    row_f = iota((ROWS, WIDE), 0)
    plain = flat[0]
    lon = 0.05 * flat[1] - 0.1 * (east_of(plain) - plain)
    lon = jnp.where(lane_f < COLS - 1, lon, 0.0)
    lat = 0.05 * flat[2] - 0.1 * (pltpu.roll(plain, ROWS - 1, 0) - plain)
    lat = jnp.where(row_f == ROWS - 1, 0.0, lat)
    start = plain - (lon - west_of(lon)) - (lat - pltpu.roll(lat, 1, 0))
    start = jnp.where(lane_f < COLS, start, 0.0)
    basis[1, 0:ROWS, :] = start
    packed_rows = row_pack(start[0:8, :], start[ROWS - 8 : ROWS, :])
    halo_rows[...] = packed_rows
    halo_cols[...] = column_pack(start[:, 0:128], start[:, 256:384])
    halo_corner[...] = column_pack(packed_rows[:, 0:128], packed_rows[:, 256:384])
    second_round = []
    for side, step in enumerate((NORTH, SOUTH)):
        second_round.append(
            remote(halo_rows, recv_halo_rows.at[side], side, step, halo_send_sem, halo_recv_sem)
        )
    for side, step in enumerate((EAST, WEST)):
        second_round.append(
            remote(halo_cols, recv_halo_cols.at[side], 2 + side, step, halo_send_sem, halo_recv_sem)
        )
    for place, step in enumerate(DIAGONAL):
        second_round.append(
            remote(
                halo_corner,
                recv_halo_corner.at[place],
                4 + place,
                step,
                halo_send_sem,
                halo_recv_sem,
            )
        )
    for copy in second_round:
        copy.start()
    heat_round = []
    for side, step in enumerate((NORTH, SOUTH)):
        copy = remote(send_heat.at[side], recv_heat.at[side], 8 + side, step)
        copy.start()
        heat_round.append(copy)

    for copy in first_round + second_round:
        copy.wait()

    def beside(north, south):
        return jnp.where(iota((8, 128), 0) < 4, north, south)

    own = jnp.concatenate([send_cols[0:ROWS, :], beside(recv_side[1], recv_side[0])], axis=0)
    from_east = jnp.concatenate(
        [recv_cols[1, 0:ROWS, :], beside(recv_corner[3, 8:16, :], recv_corner[1, 8:16, :])], axis=0
    )
    from_west = jnp.concatenate(
        [recv_cols[0, 0:ROWS, :], beside(recv_corner[2, 8:16, :], recv_corner[0, 8:16, :])], axis=0
    )
    lane_c = iota((EXT, 128), 1)
    is_east = (lane_c & 32) != 0
    other = jnp.where(is_east, pltpu.roll(from_east, 32, 1), pltpu.roll(from_west, 96, 1))
    both = own + other
    speed = pltpu.roll(both, 64, 1)
    speed = jnp.where((lane_c & 16) != 0, pltpu.roll(speed, 16, 1), speed)
    slope = jnp.where(is_east, 0.1, -0.1) * (other - own)
    through = 0.05 * speed * both - slope
    flux_lon[...] = through[0:ROWS, :]
    weight = jnp.zeros((1, 128), f32)
    lane_w = iota((1, 128), 1)
    for k in range(LEV):
        weight = jnp.where((lane_w & 15) == k, h[k], weight)
    weight = weight * jnp.where((lane_w & 16) != 0, -0.5, 1.0)
    weighed = through * weight
    side_west = jnp.sum(jnp.where(lane_c < 32, weighed, 0.0), axis=1, keepdims=True)
    side_east = jnp.sum(
        jnp.where(is_east & (lane_c < 64), weighed, 0.0), axis=1, keepdims=True
    )

    level_weight = jnp.zeros((LEV, WIDE), f32)
    level_row = iota((LEV, WIDE), 0)
    for k in range(LEV):
        level_weight = jnp.where(level_row == k, h[k], level_weight)
    exists = (
        jnp.where(gy < ny - 1, 1.0, 0.0).astype(f32),
        jnp.where(gy > 0, 1.0, 0.0).astype(f32),
    )

    def side_flux(mine, theirs, speeds, sign):
        return speeds * (mine + theirs) - (0.1 * sign) * (theirs - mine)

    side_lat = []
    speed_lat = []
    for side, sign in ((0, 1.0), (1, -1.0)):
        slot = 1 - side
        s_mine = send_rows[side, 0:16, :]
        s_theirs = recv_rows[slot, 0:16, :] * exists[side]
        speeds = 0.05 * (send_rows[side, 16:32, :] + recv_rows[slot, 16:32, :] * exists[side])
        speed_lat.append(speeds)
        flux = side_flux(s_mine, s_theirs, speeds, sign)
        side_lat.append(jnp.sum(flux * level_weight, axis=0, keepdims=True))

    is_first = (lane128 & 15) < 4
    is_north = lane128 < 64
    mine = jnp.where(is_first, recv_cols[1, 2 * ROWS :, :], recv_cols[0, 2 * ROWS :, :])
    theirs_north = jnp.where(is_first, recv_corner[3, 0:8, :], recv_corner[2, 0:8, :])
    theirs_south = jnp.where(is_first, recv_corner[1, 0:8, :], recv_corner[0, 0:8, :])
    theirs = pltpu.roll(
        jnp.where(is_north, theirs_south * exists[1], theirs_north * exists[0]), 64, 1
    )
    both = mine + theirs
    flux = 0.05 * pltpu.roll(both, 96, 1) * both - jnp.where(is_north, 0.1, -0.1) * (theirs - mine)
    flux = flux * jnp.where(
        (lane128 & 16) == 0, level_weight[0:8, 0:128], level_weight[8:16, 0:128]
    )
    flux = jnp.sum(flux, axis=0, keepdims=True)
    flux = flux + pltpu.roll(flux, 112, 1)
    for side in range(2):
        low = pltpu.roll(flux, 32 - 64 * side if side == 0 else 96, 1)
        high = pltpu.roll(flux, 120 if side == 0 else 56, 1)
        third = jnp.where(
            lane_w < 32, side_lat[side][:, 256:384], jnp.where(lane_w < 64, low, high)
        )
        side_lat[side] = jnp.concatenate([side_lat[side][:, 0:256], third], axis=1)

    def assemble(center, rows_in, cols_in, corner_in):
        lane8 = iota((8, 128), 1)
        lane48 = iota((ROWS, 128), 1)
        third = jnp.where(
            lane48 < 32, center[:, 256:384], jnp.where(lane48 < 64, cols_in(1), cols_in(0))
        )
        upper = jnp.concatenate([center[:, 0:256], third], axis=1)
        north_south = jnp.where(sub < 4, rows_in(1), rows_in(0))
        north = jnp.where(lane8 < 64, corner_in(3), corner_in(2))
        south = jnp.where(lane8 < 64, corner_in(1), corner_in(0))
        corner = jnp.where(iota((8, 128), 0) < 4, north, south)
        third = jnp.where(lane8 < 32, north_south[:, 256:384], corner)
        lower = jnp.concatenate([north_south[:, 0:256], third], axis=1)
        return jnp.concatenate([upper, lower], axis=0)

    damp_ext = assemble(
        damp_all,
        lambda slot: recv_rows[slot, 32:40, :],
        lambda slot: recv_cols[slot, ROWS : 2 * ROWS, :],
        lambda place: recv_corner[place, 16:24, :],
    )
    inv = mask[...] * inverse(6.0 + damp_ext)
    scale[...] = 1.5 * inv
    weigh[...] = jnp.where(iota((ROWS, WIDE), 1) < COLS, 6.0 + damp_all, 0.0)
    forcing = assemble(
        basis[1, 0:ROWS, :],
        lambda slot: recv_halo_rows[slot],
        lambda slot: recv_halo_cols[slot],
        lambda place: recv_halo_corner[place],
    )
    forcing = jnp.concatenate(
        [
            forcing[:, 0:128] + jnp.where(lane_c == 0, side_west, 0.0),
            forcing[:, 128:256],
            forcing[:, 256:384]
            + jnp.where(
                lane_c == 31,
                -side_east,
                jnp.where(lane_c == 32, side_east, jnp.where(lane_c == 127, -side_west, 0.0)),
            ),
        ],
        axis=1,
    )
    north, south = side_lat
    forcing = jnp.concatenate(
        [
            forcing[0:8, :] + jnp.where(sub == 0, south, 0.0),
            forcing[8:40, :],
            forcing[40:48, :] - jnp.where(sub == 7, north, 0.0),
            forcing[48:56, :]
            + jnp.where(sub == 0, north, jnp.where(sub == 7, -south, 0.0)),
        ],
        axis=0,
    )
    basis[0] = jnp.zeros((EXT, WIDE), f32)
    basis[1] = forcing * inv

    def folded(value):
        value = value[:, 0:128] + value[:, 128:256] + value[:, 256:384]
        return jnp.sum(value, axis=0, keepdims=True)

    @pl.loop(0, 4)
    def _(index):
        q = basis[index + 1]
        pair = east_of(q) + west_of(q)
        column = q + 0.5 * pair
        around = pair + pltpu.roll(column, EXT - 1, 0) + pltpu.roll(column, 1, 0)
        image = scale[...] * around - 0.5 * q
        later = jnp.where(index == 0, 0.0, 1.0)
        after = image + later * (image - basis[index])
        basis[index + 2] = after
        weighed = weigh[...] * q[0:ROWS, :]
        message[pl.ds(2 * index, 1), :] = folded(weighed * q[0:ROWS, :])
        message[pl.ds(2 * index + 1, 1), :] = folded(weighed * after[0:ROWS, :])

    def spread(source, target, count, along, mine, base):
        target[mine] = source[...]

        @pl.loop(1, count)
        def _(d):
            pltpu.make_async_remote_copy(
                src_ref=source,
                dst_ref=target.at[mine],
                send_sem=sum_send_sem.at[base],
                recv_sem=sum_recv_sem.at[base],
                device_id=device(along(d)),
                device_id_type=MESH,
            ).start()

    def gathered(target, count, base):
        part = target.at[pl.ds(0, count - 1)]
        done = pltpu.make_async_remote_copy(
            src_ref=part,
            dst_ref=part,
            send_sem=sum_send_sem.at[base],
            recv_sem=sum_recv_sem.at[base],
            device_id=device(EAST),
            device_id_type=MESH,
        )
        done.wait_recv()
        done.wait_send()
        return jnp.sum(target[...], axis=0)

    spread(message, first_sum, nx, lambda d: (d, 0), gx, 0)

    for copy in heat_round:
        copy.wait()
    for side, sign in ((0, 1.0), (1, -1.0)):
        slot = 1 - side
        target = flux_north if side == 0 else flux_prev
        heat_mine = send_heat[side]
        heat_theirs = recv_heat[slot] * exists[side]
        salt_mine = 2.0 * (heat_mine - send_rows[side, 0:16, :])
        salt_theirs = 2.0 * (heat_theirs - recv_rows[slot, 0:16, :] * exists[side])
        target[0:16, :] = side_flux(heat_mine, heat_theirs, speed_lat[side], sign)
        target[16:32, :] = side_flux(salt_mine, salt_theirs, speed_lat[side], sign)
    small[3].wait()

    edge_lane = (lane128 == 31) | (lane128 == 127)

    def mix_tile(i, _):
        rows = pl.ds(pl.multiple_of(8 * i, 8), 8)
        row = pl.ds(next_row(i), 1)
        here = mask[rows, :]
        beyond = mask[row, :]
        coefficient = padded(mix[rows, :])
        through = flux_lon[rows, :]
        use_north = (sub == 7) & (i == TILES - 1)

        def level(k, carry):
            ratio_low, heat_low, salt_low = carry
            u = padded(state[2, k, rows, :]) * here
            v = padded(state[3, k, rows, :]) * here
            v_row = padded(state[3, k, row, :]) * beyond
            v_north = jnp.where(sub == 7, v_row, pltpu.roll(v, 7, 0))
            u_pair = 0.05 * (u + east_of(u))
            v_pair = 0.05 * (v + v_north)
            lon_far, lon_near = u_pair - 0.1, u_pair + 0.1
            lat_far, lat_near = v_pair - 0.1, v_pair + 0.1
            below = coefficient * level_inv[pl.ds(k, 1), :]
            above = coefficient * level_inv[pl.ds(k + 1, 1), :]
            pivot = inverse(h[k] + above + below * (1.0 - ratio_low))
            ratio_now = above * pivot
            ratio[k] = ratio_now
            found = []
            for tracer, low in ((0, heat_low), (1, salt_low)):
                plane = tracer * LEV + k
                c = padded(state[tracer, k, rows, :]) * here
                c_row = padded(state[tracer, k, row, :]) * beyond
                c_north = jnp.where(sub == 7, c_row, pltpu.roll(c, 7, 0))
                lon = lon_far * east_of(c) + lon_near * c
                turned = pltpu.roll(through, 127 - plane, 1)
                lon = jnp.concatenate(
                    [lon[:, 0:256], jnp.where(edge_lane, turned, lon[:, 256:384])], axis=1
                )
                lat = lat_far * c_north + lat_near * c
                lat = jnp.where(use_north, flux_north[pl.ds(plane, 1), :], lat)
                lat_south = jnp.where(
                    sub == 0, flux_prev[pl.ds(plane, 1), :], pltpu.roll(lat, 1, 0)
                )
                flux_prev[pl.ds(plane, 1), :] = lat[7:8, :]
                advected = here * (c - (lon - west_of(lon)) - (lat - lat_south))
                value = (h[k] * advected + below * low) * pivot
                tracer_out[tracer, k, rows, :] = value[:, 0:COLS]
                found.append(value)
            return ratio_now, found[0], found[1]

        zero = jnp.zeros((8, WIDE), f32)
        _, heat, salt = lax.fori_loop(0, LEV, level, (zero, zero, zero), unroll=4)

        def back(step, carry):
            k = LEV - 2 - step
            heat_up, salt_up = carry
            share = ratio[k][:, 0:COLS]
            heat_up = tracer_out[0, k, rows, :] + share * heat_up
            salt_up = tracer_out[1, k, rows, :] + share * salt_up
            tracer_out[0, k, rows, :] = heat_up
            tracer_out[1, k, rows, :] = salt_up
            return heat_up, salt_up

        lax.fori_loop(0, LEV - 1, back, (heat[:, 0:COLS], salt[:, 0:COLS]), unroll=5)
        return 0

    lax.fori_loop(0, 2, mix_tile, 0)
    second_message[...] = gathered(first_sum, nx, 0)
    spread(second_message, second_sum, ny, lambda d: (0, d), gy, 1)
    lax.fori_loop(2, TILES, mix_tile, 0)
    sums = gathered(second_sum, ny, 1)

    sums = jnp.broadcast_to(jnp.sum(sums, axis=1, keepdims=True), (8, 128))
    dots = [sums[i : i + 1, :] for i in range(8)]
    moment = dots[0:2] + [2.0 * dots[i] - dots[i % 2] for i in range(2, 8)]

    def gram(i, j):
        return 0.5 * (moment[i + j] + moment[abs(i - j)])

    lower = {}
    pivots = []
    right = []
    for i in range(4):
        value = moment[i]
        for j in range(i + 1):
            entry = gram(i, j) - 0.5 * (gram(j, i + 1) + gram(j, abs(i - 1)))
            for k in range(j):
                entry = entry - lower[i, k] * lower[j, k] * pivots[k]
            if j < i:
                lower[i, j] = entry / pivots[j]
                value = value - lower[i, j] * right[j]
            else:
                pivots.append(entry)
        right.append(value)
    solved = [None] * 4
    for i in range(3, -1, -1):
        value = right[i] / pivots[i]
        for j in range(i + 1, 4):
            value = value - lower[j, i] * solved[j]
        solved[i] = value
    surface = None
    for i in range(4):
        factor = 1.5 * solved[i]
        factor = jnp.concatenate([factor, factor, factor], axis=1)
        term = factor * basis[i + 1, 0:ROWS, :]
        surface = term if surface is None else surface + term
    surface_out[...] = surface[:, 0:COLS]


def store(tracer, surface, tracer_out, surface_out, sems):
    copies = [pltpu.make_async_copy(surface, surface_out, sems.at[8])]
    for index in range(8):
        levels = pl.ds(4 * (index % 4), 4)
        copies.append(
            pltpu.make_async_copy(
                tracer.at[index // 4, levels], tracer_out.at[index // 4, levels], sems.at[index]
            )
        )
    for copy in copies:
        copy.start()
    for copy in copies:
        copy.wait()


def scratch(nx, ny):
    vmem = lambda *shape: pltpu.VMEM(shape, f32)
    dma = pltpu.SemaphoreType.DMA
    return [
        vmem(4, LEV, ROWS, COLS),
        pltpu.SMEM((LEV,), f32),
        vmem(ROWS, COLS),
        vmem(ROWS, COLS),
        None,
        vmem(EXT, WIDE),
        vmem(24, WIDE),
        vmem(3, ROWS, WIDE),
        vmem(2, 40, WIDE),
        vmem(2, LEV, WIDE),
        vmem(2, 40, WIDE),
        vmem(2, LEV, WIDE),
        vmem(2 * ROWS + 8, 128),
        vmem(2, 2 * ROWS + 8, 128),
        vmem(24, 128),
        vmem(4, 24, 128),
        vmem(2, 8, 128),
        vmem(ROWS, 128),
        vmem(2 * LEV, WIDE),
        vmem(2 * LEV, WIDE),
        vmem(LEV, 8, WIDE),
        vmem(EXT, WIDE),
        vmem(ROWS, WIDE),
        vmem(6, EXT, WIDE),
        vmem(8, WIDE),
        vmem(ROWS, 128),
        vmem(8, 128),
        vmem(2, 8, WIDE),
        vmem(2, ROWS, 128),
        vmem(4, 8, 128),
        vmem(8, 128),
        vmem(nx, 8, 128),
        vmem(8, 128),
        vmem(ny, 8, 128),
        dma((4,)),
        dma((4,)),
        dma((12,)),
        dma((12,)),
        dma((8,)),
        dma((8,)),
        dma((2,)),
        dma((2,)),
    ]


def solution(mesh):
    nx, ny = mesh.shape["gx"], mesh.shape["gy"]

    def body(ocean_state, layer_thickness, vertical_mixing, damping, ocean_blocks):
        shapes = scratch(nx, ny)
        shapes[4] = pltpu.VMEM(ocean_blocks.shape, jnp.int32)
        call = pl.pallas_call(
            functools.partial(kernel, nx, ny),
            out_shape=[
                pltpu.VMEM((2, LEV, ROWS, COLS), f32),
                pltpu.VMEM((ROWS, COLS), f32),
            ],
            in_specs=[pl.BlockSpec(memory_space=pltpu.HBM)] * 5,
            out_specs=[pl.BlockSpec(memory_space=pltpu.VMEM)] * 2,
            scratch_shapes=shapes,
            compiler_params=pltpu.CompilerParams(
                collective_id=0, has_side_effects=True, vmem_limit_bytes=32 * 1024 * 1024
            ),
        )
        operands = [
            pltpu.with_memory_space_constraint(operand, pltpu.HBM)
            for operand in (ocean_state, layer_thickness, vertical_mixing, damping, ocean_blocks)
        ]
        tracer, surface = call(*operands)
        return tuple(
            pl.pallas_call(
                store,
                out_shape=[
                    jax.ShapeDtypeStruct((2, LEV, ROWS, COLS), f32),
                    jax.ShapeDtypeStruct((ROWS, COLS), f32),
                ],
                in_specs=[pl.BlockSpec(memory_space=pltpu.VMEM)] * 2,
                out_specs=[pl.BlockSpec(memory_space=pltpu.HBM)] * 2,
                scratch_shapes=[pltpu.SemaphoreType.DMA((9,))],
                compiler_params=pltpu.CompilerParams(vmem_limit_bytes=16 * 1024 * 1024),
            )(tracer, surface)
        )

    def wrapped(*args):
        with jax.sharding.use_abstract_mesh(mesh.abstract_mesh):
            return jax.shard_map(
                body,
                mesh=mesh,
                in_specs=(P(None, None, "gy", "gx"), P(), P("gy", "gx"), P("gy", "gx"), P()),
                out_specs=(P(None, None, "gy", "gx"), P("gy", "gx")),
                check_vma=False,
            )(*args)

    return wrapped
```

```python
import functools

import jax
import jax.numpy as jnp
from jax import lax
from jax.experimental import pallas as pl
from jax.experimental.pallas import tpu as pltpu
from jax.sharding import PartitionSpec as P

BLAT = 24
BLON = 36
LEV = 16
ROWS = 48
COLS = 288
WIDE = 384
EXT = 56
TILES = ROWS // 8

f32 = jnp.float32
MESH = pl.DeviceIdType.MESH

NORTH, SOUTH, EAST, WEST = (0, 1), (0, -1), (1, 0), (-1, 0)
DIAGONAL = ((1, 1), (-1, 1), (1, -1), (-1, -1))


def iota(shape, dim):
    return lax.broadcasted_iota(jnp.int32, shape, dim)


def padded(value):
    return jnp.concatenate([value, jnp.zeros((value.shape[0], WIDE - COLS), f32)], axis=1)


def east_of(value):
    return pltpu.roll(value, WIDE - 1, 1)


def west_of(value):
    return pltpu.roll(value, 1, 1)


def inverse(value):
    guess = pl.reciprocal(value, approx=True)
    return guess * (2.0 - value * guess)


def row_pack(low, high):
    return jnp.where(iota(low.shape, 0) < 4, low, high)


def column_pack(first, last):
    lane = iota(first.shape, 1)
    low = pltpu.roll(first, 32, 1)
    high = pltpu.roll(last, 96, 1)
    return jnp.where(
        (lane >= 32) & (lane < 36), low, jnp.where(lane >= 124, high, 0.0)
    )


def kernel(
    nx,
    ny,
    ocean,
    thick,
    mixing,
    damping,
    blocks,
    tracer_out,
    surface_out,
    state,
    h,
    mix,
    damp,
    blk,
    mask,
    level_inv,
    flat,
    ends,
    send_rows,
    send_heat,
    recv_rows,
    recv_heat,
    send_cols,
    recv_cols,
    send_corner,
    recv_corner,
    recv_side,
    flux_lon,
    flux_north,
    flux_prev,
    ratio,
    scale,
    weigh,
    basis,
    halo_rows,
    halo_cols,
    halo_corner,
    recv_halo_rows,
    recv_halo_cols,
    recv_halo_corner,
    message,
    first_sum,
    second_message,
    second_sum,
    load_sem,
    small_sem,
    send_sem,
    recv_sem,
    halo_send_sem,
    halo_recv_sem,
    sum_send_sem,
    sum_recv_sem,
):
    gx = lax.axis_index("gx")
    gy = lax.axis_index("gy")

    def device(step):
        return {"gx": lax.rem(gx + step[0] + nx, nx), "gy": lax.rem(gy + step[1] + ny, ny)}

    def greet(step):
        pl.semaphore_signal(barrier, inc=1, device_id=device(step), device_id_type=MESH)

    small = [
        pltpu.make_async_copy(blocks, blk, small_sem.at[0]),
        pltpu.make_async_copy(thick, h, small_sem.at[1]),
        pltpu.make_async_copy(damping, damp, small_sem.at[2]),
        pltpu.make_async_copy(mixing, mix, small_sem.at[3]),
    ]
    group = LEV // 4

    def load(index):
        levels = pl.ds(group * index, group)
        return pltpu.make_async_copy(
            ocean.at[:, levels, :, :], state.at[:, levels, :, :], load_sem.at[index]
        )

    for copy in small[:3] + [load(index) for index in range(4)] + small[3:]:
        copy.start()

    barrier = pltpu.get_barrier_semaphore()
    for step in DIAGONAL:
        greet(step)
    pl.loop(1, nx)(lambda d: greet((d, 0)))
    pl.loop(1, ny)(lambda d: greet((0, d)))
    partners = len(DIAGONAL) + nx - 1 + ny - 1

    block_rows, block_cols = blk.shape
    small[0].wait()
    row = iota((EXT, block_rows), 0)
    row = gy * ROWS + jnp.where(row < ROWS + 4, row, row - EXT)
    edge = iota((EXT, block_rows), 1) * BLAT
    pick_rows = jnp.where((row >= edge) & (row < edge + BLAT), 1.0, 0.0)
    lane = iota((block_cols, WIDE), 1)
    total = block_cols * BLON
    col = gx * COLS + jnp.where(lane < COLS + 4, lane, lane - WIDE)
    col = jnp.where(col < 0, col + total, jnp.where(col >= total, col - total, col))
    edge = iota((block_cols, WIDE), 0) * BLON
    inside = (lane < COLS + 4) | (lane >= WIDE - 4)
    pick_cols = jnp.where(inside & (col >= edge) & (col < edge + BLON), 1.0, 0.0)
    coarse = jnp.dot(pick_rows, blk[...].astype(f32), preferred_element_type=f32)
    mask[...] = jnp.dot(coarse, pick_cols, preferred_element_type=f32)

    small[1].wait()
    small[2].wait()
    damp_low = padded(damp[0:8, :])
    damp_high = padded(damp[ROWS - 8 : ROWS, :])
    damp_rows = row_pack(damp_low, damp_high)
    for side in range(2):
        send_rows[side, 32:40, :] = damp_rows
    damp_all = padded(damp[...])
    send_cols[ROWS : 2 * ROWS, :] = column_pack(damp_all[:, 0:128], damp_all[:, 256:384])
    send_corner[16:24, :] = column_pack(damp_rows[:, 0:128], damp_rows[:, 256:384])

    def remote(source, target, index, step, sends=send_sem, recvs=recv_sem):
        return pltpu.make_async_remote_copy(
            src_ref=source,
            dst_ref=target,
            send_sem=sends.at[index],
            recv_sem=recvs.at[index],
            device_id=device(step),
            device_id_type=MESH,
        )

    sub = iota((8, WIDE), 0)
    lane128 = iota((8, 128), 1)

    def next_row(i):
        return jnp.minimum(8 * i + 8, ROWS - 1)

    tiles = [pl.ds(8 * i, 8) for i in range(TILES)]
    flat[...] = jnp.zeros(flat.shape, f32)
    ends[...] = jnp.zeros(ends.shape, f32)
    end_mask = [
        jnp.where(lane128 == 31, mask[rows, 256:384], mask[rows, 0:128]) for rows in tiles
    ]

    def pack_ends(pair):
        for i, rows in enumerate(tiles):
            west, east = ends[0, rows, :], ends[1, rows, :]
            for k in (2 * pair, 2 * pair + 1):
                for field, base in ((0, 0), (1, 16), (2, 64)):
                    last = jnp.concatenate(
                        [state[field, k, rows, 256:COLS], jnp.zeros((8, WIDE - COLS), f32)], axis=1
                    )
                    both = jnp.where(lane128 == 31, last, state[field, k, rows, 0:128])
                    both = pltpu.roll(both * end_mask[i], base + k, 1)
                    west = jnp.where(lane128 == base + k, both, west)
                    east = jnp.where(lane128 == base + k + 31, both, east)
            ends[0, rows, :] = west
            ends[1, rows, :] = east


    def turned_up(values):
        turned = [pltpu.roll(value, 7, 0) for value in values]
        return [
            jnp.where(sub == 7, turned[(i + 1) % TILES], turned[i]) for i in range(TILES)
        ]

    @pl.loop(0, LEV // 2)
    def _(pair):
        @pl.when(lax.rem(pair, group // 2) == 0)
        def _():
            load(pair // (group // 2)).wait()

        sums = None
        for k in (2 * pair, 2 * pair + 1):
            s = [
                padded(state[0, k, rows, :] - 0.5 * state[1, k, rows, :]) * mask[rows, :] * h[k]
                for rows in tiles
            ]
            v = [padded(state[3, k, rows, :]) * mask[rows, :] for rows in tiles]
            s_north, v_north = turned_up(s), turned_up(v)
            found = []
            for i, rows in enumerate(tiles):
                u = padded(state[2, k, rows, :]) * mask[rows, :]
                found.append(
                    (
                        s[i],
                        (u + east_of(u)) * (s[i] + east_of(s[i])),
                        (v[i] + v_north[i]) * (s[i] + s_north[i]),
                    )
                )
            if sums is None:
                sums = found
            else:
                sums = [[a + b for a, b in zip(x, y)] for x, y in zip(sums, found)]
        for i, rows in enumerate(tiles):
            for part in range(3):
                flat[part, rows, :] += sums[i][part]
        pack_ends(pair)

    first_round = []
    for side, (edge_row, step) in enumerate(((ROWS - 1, NORTH), (0, SOUTH))):
        edge_mask = mask[edge_row : edge_row + 1, :]
        heat = padded(state[0, :, edge_row, :]) * edge_mask
        salt = padded(state[1, :, edge_row, :]) * edge_mask
        send_heat[side] = heat
        send_rows[side, 0:16, :] = heat - 0.5 * salt
        send_rows[side, 16:32, :] = padded(state[3, :, edge_row, :]) * edge_mask
        first_round.append(remote(send_rows.at[side], recv_rows.at[side], side, step))

    pl.semaphore_wait(barrier, partners)
    for copy in first_round:
        copy.start()

    send_cols[0:ROWS, :] = ends[0] + pltpu.roll(ends[1], 1, 1)

    compact = jnp.zeros((8, 128), f32)
    for side in range(2):
        for part in range(4):
            j = 4 * side + part
            rows = pl.ds(8 * part, 8)
            first = pltpu.roll(send_rows[side, rows, 0:128], 16 * j, 1)
            last = pltpu.roll(send_rows[side, rows, 256:384], (16 * j - 24) % 128, 1)
            inside = lane128 // 16 == j
            compact = jnp.where(inside & (lane128 % 16 < 4), first, compact)
            compact = jnp.where(
                inside & (lane128 % 16 >= 4) & (lane128 % 16 < 8), last, compact
            )
    send_corner[0:8, :] = compact
    send_cols[2 * ROWS :, :] = compact
    send_corner[8:16, :] = row_pack(send_cols[0:8, :], send_cols[ROWS - 8 : ROWS, :])

    second_round = []
    for side, step in enumerate((EAST, WEST)):
        second_round.append(remote(send_cols, recv_cols.at[side], 2 + side, step))
    for place, step in enumerate(DIAGONAL):
        second_round.append(remote(send_corner, recv_corner.at[place], 4 + place, step))
    for side, step in enumerate((NORTH, SOUTH)):
        second_round.append(
            remote(send_corner.at[pl.ds(8, 8)], recv_side.at[side], 10 + side, step)
        )
    for copy in second_round:
        copy.start()
    first_round = first_round + second_round

    lane_f = iota((ROWS, WIDE), 1)
    row_f = iota((ROWS, WIDE), 0)
    plain = flat[0]
    lon = 0.05 * flat[1] - 0.1 * (east_of(plain) - plain)
    lon = jnp.where(lane_f < COLS - 1, lon, 0.0)
    lat = 0.05 * flat[2] - 0.1 * (pltpu.roll(plain, ROWS - 1, 0) - plain)
    lat = jnp.where(row_f == ROWS - 1, 0.0, lat)
    start = plain - (lon - west_of(lon)) - (lat - pltpu.roll(lat, 1, 0))
    start = jnp.where(lane_f < COLS, start, 0.0)
    basis[1, 0:ROWS, :] = start
    packed_rows = row_pack(start[0:8, :], start[ROWS - 8 : ROWS, :])
    halo_rows[...] = packed_rows
    halo_cols[...] = column_pack(start[:, 0:128], start[:, 256:384])
    halo_corner[...] = column_pack(packed_rows[:, 0:128], packed_rows[:, 256:384])
    second_round = []
    for side, step in enumerate((NORTH, SOUTH)):
        second_round.append(
            remote(halo_rows, recv_halo_rows.at[side], side, step, halo_send_sem, halo_recv_sem)
        )
    for side, step in enumerate((EAST, WEST)):
        second_round.append(
            remote(halo_cols, recv_halo_cols.at[side], 2 + side, step, halo_send_sem, halo_recv_sem)
        )
    for place, step in enumerate(DIAGONAL):
        second_round.append(
            remote(
                halo_corner,
                recv_halo_corner.at[place],
                4 + place,
                step,
                halo_send_sem,
                halo_recv_sem,
            )
        )
    for copy in second_round:
        copy.start()
    heat_round = []
    for side, step in enumerate((NORTH, SOUTH)):
        copy = remote(send_heat.at[side], recv_heat.at[side], 8 + side, step)
        copy.start()
        heat_round.append(copy)

    level_inv[...] = jnp.zeros(level_inv.shape, f32)

    @pl.loop(1, LEV)
    def _(k):
        level_inv[pl.ds(k, 1), :] = 1.0 / jnp.full((1, WIDE), h[k - 1] + h[k], f32)


    weight = jnp.zeros((1, 128), f32)
    lane_w = iota((1, 128), 1)
    for k in range(LEV):
        weight = jnp.where((lane_w & 15) == k, h[k], weight)
    weight = weight * jnp.where((lane_w & 16) != 0, -0.5, 1.0)
    level_weight = jnp.zeros((LEV, WIDE), f32)
    level_row = iota((LEV, WIDE), 0)
    for k in range(LEV):
        level_weight = jnp.where(level_row == k, h[k], level_weight)
    exists = (
        jnp.where(gy < ny - 1, 1.0, 0.0).astype(f32),
        jnp.where(gy > 0, 1.0, 0.0).astype(f32),
    )

    basis[0] = jnp.zeros((EXT, WIDE), f32)
    weigh[...] = jnp.where(iota((ROWS, WIDE), 1) < COLS, 6.0 + damp_all, 0.0)

    for copy in first_round:
        copy.wait()

    def beside(north, south):
        return jnp.where(iota((8, 128), 0) < 4, north, south)

    own = jnp.concatenate([send_cols[0:ROWS, :], beside(recv_side[1], recv_side[0])], axis=0)
    from_east = jnp.concatenate(
        [recv_cols[1, 0:ROWS, :], beside(recv_corner[3, 8:16, :], recv_corner[1, 8:16, :])], axis=0
    )
    from_west = jnp.concatenate(
        [recv_cols[0, 0:ROWS, :], beside(recv_corner[2, 8:16, :], recv_corner[0, 8:16, :])], axis=0
    )
    lane_c = iota((EXT, 128), 1)
    is_east = (lane_c & 32) != 0
    other = jnp.where(is_east, pltpu.roll(from_east, 32, 1), pltpu.roll(from_west, 96, 1))
    both = own + other
    speed = pltpu.roll(both, 64, 1)
    speed = jnp.where((lane_c & 16) != 0, pltpu.roll(speed, 16, 1), speed)
    slope = jnp.where(is_east, 0.1, -0.1) * (other - own)
    through = 0.05 * speed * both - slope
    flux_lon[...] = through[0:ROWS, :]
    weighed = through * weight
    side_west = jnp.sum(jnp.where(lane_c < 32, weighed, 0.0), axis=1, keepdims=True)
    side_east = jnp.sum(
        jnp.where(is_east & (lane_c < 64), weighed, 0.0), axis=1, keepdims=True
    )

    def side_flux(mine, theirs, speeds, sign):
        return speeds * (mine + theirs) - (0.1 * sign) * (theirs - mine)

    side_lat = []
    speed_lat = []
    for side, sign in ((0, 1.0), (1, -1.0)):
        slot = 1 - side
        s_mine = send_rows[side, 0:16, :]
        s_theirs = recv_rows[slot, 0:16, :] * exists[side]
        speeds = 0.05 * (send_rows[side, 16:32, :] + recv_rows[slot, 16:32, :] * exists[side])
        speed_lat.append(speeds)
        flux = side_flux(s_mine, s_theirs, speeds, sign)
        side_lat.append(jnp.sum(flux * level_weight, axis=0, keepdims=True))

    is_first = (lane128 & 15) < 4
    is_north = lane128 < 64
    mine = jnp.where(is_first, recv_cols[1, 2 * ROWS :, :], recv_cols[0, 2 * ROWS :, :])
    theirs_north = jnp.where(is_first, recv_corner[3, 0:8, :], recv_corner[2, 0:8, :])
    theirs_south = jnp.where(is_first, recv_corner[1, 0:8, :], recv_corner[0, 0:8, :])
    theirs = pltpu.roll(
        jnp.where(is_north, theirs_south * exists[1], theirs_north * exists[0]), 64, 1
    )
    both = mine + theirs
    flux = 0.05 * pltpu.roll(both, 96, 1) * both - jnp.where(is_north, 0.1, -0.1) * (theirs - mine)
    flux = flux * jnp.where(
        (lane128 & 16) == 0, level_weight[0:8, 0:128], level_weight[8:16, 0:128]
    )
    flux = jnp.sum(flux, axis=0, keepdims=True)
    flux = flux + pltpu.roll(flux, 112, 1)
    for side in range(2):
        low = pltpu.roll(flux, 32 - 64 * side if side == 0 else 96, 1)
        high = pltpu.roll(flux, 120 if side == 0 else 56, 1)
        third = jnp.where(
            lane_w < 32, side_lat[side][:, 256:384], jnp.where(lane_w < 64, low, high)
        )
        side_lat[side] = jnp.concatenate([side_lat[side][:, 0:256], third], axis=1)

    def assemble(center, rows_in, cols_in, corner_in):
        lane8 = iota((8, 128), 1)
        lane48 = iota((ROWS, 128), 1)
        third = jnp.where(
            lane48 < 32, center[:, 256:384], jnp.where(lane48 < 64, cols_in(1), cols_in(0))
        )
        upper = jnp.concatenate([center[:, 0:256], third], axis=1)
        north_south = jnp.where(sub < 4, rows_in(1), rows_in(0))
        north = jnp.where(lane8 < 64, corner_in(3), corner_in(2))
        south = jnp.where(lane8 < 64, corner_in(1), corner_in(0))
        corner = jnp.where(iota((8, 128), 0) < 4, north, south)
        third = jnp.where(lane8 < 32, north_south[:, 256:384], corner)
        lower = jnp.concatenate([north_south[:, 0:256], third], axis=1)
        return jnp.concatenate([upper, lower], axis=0)

    damp_ext = assemble(
        damp_all,
        lambda slot: recv_rows[slot, 32:40, :],
        lambda slot: recv_cols[slot, ROWS : 2 * ROWS, :],
        lambda place: recv_corner[place, 16:24, :],
    )
    inv = mask[...] * inverse(6.0 + damp_ext)
    scale[...] = 1.5 * inv
    for copy in second_round:
        copy.wait()
    forcing = assemble(
        basis[1, 0:ROWS, :],
        lambda slot: recv_halo_rows[slot],
        lambda slot: recv_halo_cols[slot],
        lambda place: recv_halo_corner[place],
    )
    forcing = jnp.concatenate(
        [
            forcing[:, 0:128] + jnp.where(lane_c == 0, side_west, 0.0),
            forcing[:, 128:256],
            forcing[:, 256:384]
            + jnp.where(
                lane_c == 31,
                -side_east,
                jnp.where(lane_c == 32, side_east, jnp.where(lane_c == 127, -side_west, 0.0)),
            ),
        ],
        axis=1,
    )
    north, south = side_lat
    forcing = jnp.concatenate(
        [
            forcing[0:8, :] + jnp.where(sub == 0, south, 0.0),
            forcing[8:40, :],
            forcing[40:48, :] - jnp.where(sub == 7, north, 0.0),
            forcing[48:56, :]
            + jnp.where(sub == 0, north, jnp.where(sub == 7, -south, 0.0)),
        ],
        axis=0,
    )
    basis[1] = forcing * inv

    def folded(value):
        value = value[:, 0:128] + value[:, 128:256] + value[:, 256:384]
        return jnp.sum(value, axis=0, keepdims=True)

    @pl.loop(0, 4)
    def _(index):
        q = basis[index + 1]
        pair = east_of(q) + west_of(q)
        column = q + 0.5 * pair
        around = pair + pltpu.roll(column, EXT - 1, 0) + pltpu.roll(column, 1, 0)
        image = scale[...] * around - 0.5 * q
        later = jnp.where(index == 0, 0.0, 1.0)
        after = image + later * (image - basis[index])
        basis[index + 2] = after
        weighed = weigh[...] * q[0:ROWS, :]
        message[pl.ds(2 * index, 1), :] = folded(weighed * q[0:ROWS, :])
        message[pl.ds(2 * index + 1, 1), :] = folded(weighed * after[0:ROWS, :])

    def spread(source, target, count, along, mine, base):
        target[mine] = source[...]

        @pl.loop(1, count)
        def _(d):
            pltpu.make_async_remote_copy(
                src_ref=source,
                dst_ref=target.at[mine],
                send_sem=sum_send_sem.at[base],
                recv_sem=sum_recv_sem.at[base],
                device_id=device(along(d)),
                device_id_type=MESH,
            ).start()

    def gathered(target, count, base):
        part = target.at[pl.ds(0, count - 1)]
        done = pltpu.make_async_remote_copy(
            src_ref=part,
            dst_ref=part,
            send_sem=sum_send_sem.at[base],
            recv_sem=sum_recv_sem.at[base],
            device_id=device(EAST),
            device_id_type=MESH,
        )
        done.wait_recv()
        done.wait_send()
        return jnp.sum(target[...], axis=0)

    spread(message, first_sum, nx, lambda d: (d, 0), gx, 0)

    for copy in heat_round:
        copy.wait()
    for side, sign in ((0, 1.0), (1, -1.0)):
        slot = 1 - side
        target = flux_north if side == 0 else flux_prev
        heat_mine = send_heat[side]
        heat_theirs = recv_heat[slot] * exists[side]
        salt_mine = 2.0 * (heat_mine - send_rows[side, 0:16, :])
        salt_theirs = 2.0 * (heat_theirs - recv_rows[slot, 0:16, :] * exists[side])
        target[0:16, :] = side_flux(heat_mine, heat_theirs, speed_lat[side], sign)
        target[16:32, :] = side_flux(salt_mine, salt_theirs, speed_lat[side], sign)
    small[3].wait()

    edge_lane = (lane128 == 31) | (lane128 == 127)

    def mix_tile(i, _):
        rows = pl.ds(pl.multiple_of(8 * i, 8), 8)
        row = pl.ds(next_row(i), 1)
        here = mask[rows, :]
        beyond = mask[row, :]
        coefficient = padded(mix[rows, :])
        through = flux_lon[rows, :]
        use_north = (sub == 7) & (i == TILES - 1)

        def level(k, carry):
            ratio_low, heat_low, salt_low = carry
            u = padded(state[2, k, rows, :]) * here
            v = padded(state[3, k, rows, :]) * here
            v_row = padded(state[3, k, row, :]) * beyond
            v_north = jnp.where(sub == 7, v_row, pltpu.roll(v, 7, 0))
            u_pair = 0.05 * (u + east_of(u))
            v_pair = 0.05 * (v + v_north)
            lon_far, lon_near = u_pair - 0.1, u_pair + 0.1
            lat_far, lat_near = v_pair - 0.1, v_pair + 0.1
            below = coefficient * level_inv[pl.ds(k, 1), :]
            above = coefficient * level_inv[pl.ds(k + 1, 1), :]
            pivot = inverse(h[k] + above + below * (1.0 - ratio_low))
            ratio_now = above * pivot
            ratio[k] = ratio_now
            found = []
            for tracer, low in ((0, heat_low), (1, salt_low)):
                plane = tracer * LEV + k
                c = padded(state[tracer, k, rows, :]) * here
                c_row = padded(state[tracer, k, row, :]) * beyond
                c_north = jnp.where(sub == 7, c_row, pltpu.roll(c, 7, 0))
                lon = lon_far * east_of(c) + lon_near * c
                turned = pltpu.roll(through, 127 - plane, 1)
                lon = jnp.concatenate(
                    [lon[:, 0:256], jnp.where(edge_lane, turned, lon[:, 256:384])], axis=1
                )
                lat = lat_far * c_north + lat_near * c
                lat = jnp.where(use_north, flux_north[pl.ds(plane, 1), :], lat)
                lat_south = jnp.where(
                    sub == 0, flux_prev[pl.ds(plane, 1), :], pltpu.roll(lat, 1, 0)
                )
                flux_prev[pl.ds(plane, 1), :] = lat[7:8, :]
                advected = here * (c - (lon - west_of(lon)) - (lat - lat_south))
                value = (h[k] * advected + below * low) * pivot
                tracer_out[tracer, k, rows, :] = value[:, 0:COLS]
                found.append(value)
            return ratio_now, found[0], found[1]

        zero = jnp.zeros((8, WIDE), f32)
        _, heat, salt = lax.fori_loop(0, LEV, level, (zero, zero, zero), unroll=4)

        def back(step, carry):
            k = LEV - 2 - step
            heat_up, salt_up = carry
            share = ratio[k][:, 0:COLS]
            heat_up = tracer_out[0, k, rows, :] + share * heat_up
            salt_up = tracer_out[1, k, rows, :] + share * salt_up
            tracer_out[0, k, rows, :] = heat_up
            tracer_out[1, k, rows, :] = salt_up
            return heat_up, salt_up

        lax.fori_loop(0, LEV - 1, back, (heat[:, 0:COLS], salt[:, 0:COLS]), unroll=5)
        return 0

    lax.fori_loop(0, 2, mix_tile, 0)
    second_message[...] = gathered(first_sum, nx, 0)
    spread(second_message, second_sum, ny, lambda d: (0, d), gy, 1)
    lax.fori_loop(2, TILES, mix_tile, 0)
    sums = gathered(second_sum, ny, 1)

    sums = jnp.broadcast_to(jnp.sum(sums, axis=1, keepdims=True), (8, 128))
    dots = [sums[i : i + 1, :] for i in range(8)]
    moment = dots[0:2] + [2.0 * dots[i] - dots[i % 2] for i in range(2, 8)]

    def gram(i, j):
        return 0.5 * (moment[i + j] + moment[abs(i - j)])

    lower = {}
    pivots = []
    right = []
    for i in range(4):
        value = moment[i]
        for j in range(i + 1):
            entry = gram(i, j) - 0.5 * (gram(j, i + 1) + gram(j, abs(i - 1)))
            for k in range(j):
                entry = entry - lower[i, k] * lower[j, k] * pivots[k]
            if j < i:
                lower[i, j] = entry / pivots[j]
                value = value - lower[i, j] * right[j]
            else:
                pivots.append(entry)
        right.append(value)
    solved = [None] * 4
    for i in range(3, -1, -1):
        value = right[i] / pivots[i]
        for j in range(i + 1, 4):
            value = value - lower[j, i] * solved[j]
        solved[i] = value
    surface = None
    for i in range(4):
        factor = 1.5 * solved[i]
        factor = jnp.concatenate([factor, factor, factor], axis=1)
        term = factor * basis[i + 1, 0:ROWS, :]
        surface = term if surface is None else surface + term
    surface_out[...] = surface[:, 0:COLS]


def store(tracer, surface, tracer_out, surface_out, sems):
    copies = [pltpu.make_async_copy(surface, surface_out, sems.at[8])]
    for index in range(8):
        levels = pl.ds(4 * (index % 4), 4)
        copies.append(
            pltpu.make_async_copy(
                tracer.at[index // 4, levels], tracer_out.at[index // 4, levels], sems.at[index]
            )
        )
    for copy in copies:
        copy.start()
    for copy in copies:
        copy.wait()


def scratch(nx, ny):
    vmem = lambda *shape: pltpu.VMEM(shape, f32)
    dma = pltpu.SemaphoreType.DMA
    return [
        vmem(4, LEV, ROWS, COLS),
        pltpu.SMEM((LEV,), f32),
        vmem(ROWS, COLS),
        vmem(ROWS, COLS),
        None,
        vmem(EXT, WIDE),
        vmem(24, WIDE),
        vmem(3, ROWS, WIDE),
        vmem(2, ROWS, 128),
        vmem(2, 40, WIDE),
        vmem(2, LEV, WIDE),
        vmem(2, 40, WIDE),
        vmem(2, LEV, WIDE),
        vmem(2 * ROWS + 8, 128),
        vmem(2, 2 * ROWS + 8, 128),
        vmem(24, 128),
        vmem(4, 24, 128),
        vmem(2, 8, 128),
        vmem(ROWS, 128),
        vmem(2 * LEV, WIDE),
        vmem(2 * LEV, WIDE),
        vmem(LEV, 8, WIDE),
        vmem(EXT, WIDE),
        vmem(ROWS, WIDE),
        vmem(6, EXT, WIDE),
        vmem(8, WIDE),
        vmem(ROWS, 128),
        vmem(8, 128),
        vmem(2, 8, WIDE),
        vmem(2, ROWS, 128),
        vmem(4, 8, 128),
        vmem(8, 128),
        vmem(nx, 8, 128),
        vmem(8, 128),
        vmem(ny, 8, 128),
        dma((4,)),
        dma((4,)),
        dma((12,)),
        dma((12,)),
        dma((8,)),
        dma((8,)),
        dma((2,)),
        dma((2,)),
    ]


def solution(mesh):
    nx, ny = mesh.shape["gx"], mesh.shape["gy"]

    def body(ocean_state, layer_thickness, vertical_mixing, damping, ocean_blocks):
        shapes = scratch(nx, ny)
        shapes[4] = pltpu.VMEM(ocean_blocks.shape, jnp.int32)
        call = pl.pallas_call(
            functools.partial(kernel, nx, ny),
            out_shape=[
                pltpu.VMEM((2, LEV, ROWS, COLS), f32),
                pltpu.VMEM((ROWS, COLS), f32),
            ],
            in_specs=[pl.BlockSpec(memory_space=pltpu.HBM)] * 5,
            out_specs=[pl.BlockSpec(memory_space=pltpu.VMEM)] * 2,
            scratch_shapes=shapes,
            compiler_params=pltpu.CompilerParams(
                collective_id=0, has_side_effects=True, vmem_limit_bytes=32 * 1024 * 1024
            ),
        )
        operands = [
            pltpu.with_memory_space_constraint(operand, pltpu.HBM)
            for operand in (ocean_state, layer_thickness, vertical_mixing, damping, ocean_blocks)
        ]
        tracer, surface = call(*operands)
        return tuple(
            pl.pallas_call(
                store,
                out_shape=[
                    jax.ShapeDtypeStruct((2, LEV, ROWS, COLS), f32),
                    jax.ShapeDtypeStruct((ROWS, COLS), f32),
                ],
                in_specs=[pl.BlockSpec(memory_space=pltpu.VMEM)] * 2,
                out_specs=[pl.BlockSpec(memory_space=pltpu.HBM)] * 2,
                scratch_shapes=[pltpu.SemaphoreType.DMA((9,))],
                compiler_params=pltpu.CompilerParams(vmem_limit_bytes=16 * 1024 * 1024),
            )(tracer, surface)
        )

    def wrapped(*args):
        with jax.sharding.use_abstract_mesh(mesh.abstract_mesh):
            return jax.shard_map(
                body,
                mesh=mesh,
                in_specs=(P(None, None, "gy", "gx"), P(), P("gy", "gx"), P("gy", "gx"), P()),
                out_specs=(P(None, None, "gy", "gx"), P("gy", "gx")),
                check_vma=False,
            )(*args)

    return wrapped
```

```python
import functools

import jax
import jax.numpy as jnp
from jax import lax
from jax.experimental import pallas as pl
from jax.experimental.pallas import tpu as pltpu
from jax.sharding import PartitionSpec as P

BLAT = 24
BLON = 36
LEV = 16
ROWS = 48
COLS = 288
WIDE = 384
EXT = 56
TILES = ROWS // 8

f32 = jnp.float32
MESH = pl.DeviceIdType.MESH

NORTH, SOUTH, EAST, WEST = (0, 1), (0, -1), (1, 0), (-1, 0)
DIAGONAL = ((1, 1), (-1, 1), (1, -1), (-1, -1))


def iota(shape, dim):
    return lax.broadcasted_iota(jnp.int32, shape, dim)


def padded(value):
    return jnp.concatenate([value, jnp.zeros((value.shape[0], WIDE - COLS), f32)], axis=1)


def east_of(value):
    return pltpu.roll(value, WIDE - 1, 1)


def west_of(value):
    return pltpu.roll(value, 1, 1)


def inverse(value):
    guess = pl.reciprocal(value, approx=True)
    return guess * (2.0 - value * guess)


def row_pack(low, high):
    return jnp.where(iota(low.shape, 0) < 4, low, high)


def column_pack(first, last):
    lane = iota(first.shape, 1)
    low = pltpu.roll(first, 32, 1)
    high = pltpu.roll(last, 96, 1)
    return jnp.where(
        (lane >= 32) & (lane < 36), low, jnp.where(lane >= 124, high, 0.0)
    )


def kernel(
    nx,
    ny,
    ocean,
    thick,
    mixing,
    damping,
    blocks,
    tracer_out,
    surface_out,
    state,
    h,
    mix,
    damp,
    blk,
    mask,
    level_inv,
    flat,
    ends,
    send_rows,
    send_strip,
    send_heat,
    recv_strip,
    recv_rows,
    recv_heat,
    send_cols,
    recv_cols,
    send_corner,
    recv_corner,
    recv_side,
    flux_lon,
    flux_north,
    flux_prev,
    ratio,
    scale,
    weigh,
    basis,
    halo_rows,
    halo_cols,
    recv_halo_rows,
    recv_halo_cols,
    message,
    first_message,
    first_sum,
    second_message,
    second_sum,
    load_sem,
    small_sem,
    send_sem,
    recv_sem,
    halo_send_sem,
    halo_recv_sem,
    sum_send_sem,
    sum_recv_sem,
):
    gx = lax.axis_index("gx")
    gy = lax.axis_index("gy")

    def device(step):
        return {"gx": lax.rem(gx + step[0] + nx, nx), "gy": lax.rem(gy + step[1] + ny, ny)}

    def greet(step):
        pl.semaphore_signal(barrier, inc=1, device_id=device(step), device_id_type=MESH)

    small = [
        pltpu.make_async_copy(blocks, blk, small_sem.at[0]),
        pltpu.make_async_copy(thick, h, small_sem.at[1]),
        pltpu.make_async_copy(damping, damp, small_sem.at[2]),
        pltpu.make_async_copy(mixing, mix, small_sem.at[3]),
    ]
    group = LEV // 4

    def load(index):
        levels = pl.ds(group * index, group)
        return pltpu.make_async_copy(
            ocean.at[:, levels, :, :], state.at[:, levels, :, :], load_sem.at[index]
        )

    for copy in small[:3] + [load(index) for index in range(4)] + small[3:]:
        copy.start()

    barrier = pltpu.get_barrier_semaphore()
    for step in DIAGONAL:
        greet(step)
    pl.loop(1, nx)(lambda d: greet((d, 0)))
    pl.loop(1, ny)(lambda d: greet((0, d)))
    partners = len(DIAGONAL) + nx - 1 + ny - 1

    block_rows, block_cols = blk.shape
    small[0].wait()
    row = iota((EXT, block_rows), 0)
    row = gy * ROWS + jnp.where(row < ROWS + 4, row, row - EXT)
    edge = iota((EXT, block_rows), 1) * BLAT
    pick_rows = jnp.where((row >= edge) & (row < edge + BLAT), 1.0, 0.0)
    lane = iota((block_cols, WIDE), 1)
    total = block_cols * BLON
    col = gx * COLS + jnp.where(lane < COLS + 4, lane, lane - WIDE)
    col = jnp.where(col < 0, col + total, jnp.where(col >= total, col - total, col))
    edge = iota((block_cols, WIDE), 0) * BLON
    inside = (lane < COLS + 4) | (lane >= WIDE - 4)
    pick_cols = jnp.where(inside & (col >= edge) & (col < edge + BLON), 1.0, 0.0)
    coarse = jnp.dot(pick_rows, blk[...].astype(f32), preferred_element_type=f32)
    mask[...] = jnp.dot(coarse, pick_cols, preferred_element_type=f32)

    small[1].wait()
    small[2].wait()
    damp_low = padded(damp[0:8, :])
    damp_high = padded(damp[ROWS - 8 : ROWS, :])
    damp_rows = row_pack(damp_low, damp_high)
    damp_all = padded(damp[...])
    send_cols[ROWS : 2 * ROWS, :] = column_pack(damp_all[:, 0:128], damp_all[:, 256:384])

    def remote(source, target, index, step, sends=send_sem, recvs=recv_sem):
        return pltpu.make_async_remote_copy(
            src_ref=source,
            dst_ref=target,
            send_sem=sends.at[index],
            recv_sem=recvs.at[index],
            device_id=device(step),
            device_id_type=MESH,
        )

    sub = iota((8, WIDE), 0)
    lane128 = iota((8, 128), 1)

    def next_row(i):
        return jnp.minimum(8 * i + 8, ROWS - 1)

    tiles = [pl.ds(8 * i, 8) for i in range(TILES)]
    flat[...] = jnp.zeros(flat.shape, f32)
    ends[...] = jnp.zeros(ends.shape, f32)
    end_mask = [
        jnp.where(lane128 == 31, mask[rows, 256:384], mask[rows, 0:128]) for rows in tiles
    ]

    def pack_ends(pair):
        for i, rows in enumerate(tiles):
            west, east = ends[0, rows, :], ends[1, rows, :]
            for k in (2 * pair, 2 * pair + 1):
                for field, base in ((0, 0), (1, 16), (2, 64)):
                    last = jnp.concatenate(
                        [state[field, k, rows, 256:COLS], jnp.zeros((8, WIDE - COLS), f32)], axis=1
                    )
                    both = jnp.where(lane128 == 31, last, state[field, k, rows, 0:128])
                    both = pltpu.roll(both * end_mask[i], base + k, 1)
                    west = jnp.where(lane128 == base + k, both, west)
                    east = jnp.where(lane128 == base + k + 31, both, east)
            ends[0, rows, :] = west
            ends[1, rows, :] = east


    def turned_up(values):
        turned = [pltpu.roll(value, 7, 0) for value in values]
        return [
            jnp.where(sub == 7, turned[(i + 1) % TILES], turned[i]) for i in range(TILES)
        ]

    @pl.loop(0, LEV // 2)
    def _(pair):
        @pl.when(lax.rem(pair, group // 2) == 0)
        def _():
            load(pair // (group // 2)).wait()

        sums = None
        for k in (2 * pair, 2 * pair + 1):
            s = [
                padded(state[0, k, rows, :] - 0.5 * state[1, k, rows, :]) * mask[rows, :] * h[k]
                for rows in tiles
            ]
            v = [padded(state[3, k, rows, :]) * mask[rows, :] for rows in tiles]
            s_north, v_north = turned_up(s), turned_up(v)
            found = []
            for i, rows in enumerate(tiles):
                u = padded(state[2, k, rows, :]) * mask[rows, :]
                found.append(
                    (
                        s[i],
                        (u + east_of(u)) * (s[i] + east_of(s[i])),
                        (v[i] + v_north[i]) * (s[i] + s_north[i]),
                    )
                )
            if sums is None:
                sums = found
            else:
                sums = [[a + b for a, b in zip(x, y)] for x, y in zip(sums, found)]
        for i, rows in enumerate(tiles):
            for part in range(3):
                flat[part, rows, :] += sums[i][part]
        pack_ends(pair)

    first_round = []
    for side, (edge_row, step) in enumerate(((ROWS - 1, NORTH), (0, SOUTH))):
        edge_mask = mask[edge_row : edge_row + 1, :]
        heat = padded(state[0, :, edge_row, :]) * edge_mask
        salt = padded(state[1, :, edge_row, :]) * edge_mask
        send_heat[side] = heat
        send_rows[side, 0:16, :] = heat - 0.5 * salt
        send_rows[side, 16:32, :] = padded(state[3, :, edge_row, :]) * edge_mask
        send_strip[side, 0:32, :] = send_rows[side, :, 0:128]
        send_strip[side, 32:64, :] = send_rows[side, :, 128:256]
        tail = jnp.zeros((8, 128), f32)
        for part in range(4):
            third = send_rows[side, 8 * part : 8 * part + 8, 256:384]
            tail = jnp.where(lane128 // 32 == part, pltpu.roll(third, 32 * part, 1), tail)
        send_strip[side, 64:72, :] = tail
        first_round.append(remote(send_strip.at[side], recv_strip.at[side], side, step))

    pl.semaphore_wait(barrier, partners)
    for copy in first_round:
        copy.start()

    send_cols[0:ROWS, :] = ends[0] + pltpu.roll(ends[1], 1, 1)

    compact = jnp.zeros((8, 128), f32)
    for side in range(2):
        for part in range(4):
            j = 4 * side + part
            rows = pl.ds(8 * part, 8)
            first = pltpu.roll(send_rows[side, rows, 0:128], 16 * j, 1)
            last = pltpu.roll(send_rows[side, rows, 256:384], (16 * j - 24) % 128, 1)
            inside = lane128 // 16 == j
            compact = jnp.where(inside & (lane128 % 16 < 4), first, compact)
            compact = jnp.where(
                inside & (lane128 % 16 >= 4) & (lane128 % 16 < 8), last, compact
            )
    send_cols[2 * ROWS :, :] = compact
    send_corner[8:16, :] = row_pack(send_cols[0:8, :], send_cols[ROWS - 8 : ROWS, :])

    second_round = []
    for side, step in enumerate((EAST, WEST)):
        second_round.append(remote(send_cols, recv_cols.at[side], 2 + side, step))
    for side, step in enumerate((NORTH, SOUTH)):
        second_round.append(
            remote(send_corner.at[pl.ds(8, 8)], recv_side.at[side], 10 + side, step)
        )
    for copy in second_round:
        copy.start()
    first_round = first_round + second_round

    lane_f = iota((ROWS, WIDE), 1)
    row_f = iota((ROWS, WIDE), 0)
    plain = flat[0]
    lon = 0.05 * flat[1] - 0.1 * (east_of(plain) - plain)
    lon = jnp.where(lane_f < COLS - 1, lon, 0.0)
    lat = 0.05 * flat[2] - 0.1 * (pltpu.roll(plain, ROWS - 1, 0) - plain)
    lat = jnp.where(row_f == ROWS - 1, 0.0, lat)
    start = plain - (lon - west_of(lon)) - (lat - pltpu.roll(lat, 1, 0))
    start = jnp.where(lane_f < COLS, start, 0.0)
    basis[1, 0:ROWS, :] = start
    packed_rows = row_pack(start[0:8, :], start[ROWS - 8 : ROWS, :])
    halo_rows[0] = jnp.where(sub < 4, pltpu.roll(start[ROWS - 8 : ROWS, :], 4, 0), damp_high)
    halo_rows[1] = jnp.where(sub < 4, damp_low, pltpu.roll(start[0:8, :], 4, 0))
    halo_cols[...] = column_pack(start[:, 0:128], start[:, 256:384])
    for base, packed in ((8, damp_rows), (24, packed_rows)):
        first = pltpu.roll(packed[:, 0:128], base, 1)
        last = packed[:, 256:384]
        last = pltpu.roll(last, (base - 24) % 128, 1) if base != 24 else last
        compact = jnp.where((lane128 >= base) & (lane128 < base + 4), first, compact)
        compact = jnp.where((lane128 >= base + 4) & (lane128 < base + 8), last, compact)
    send_corner[0:8, :] = compact
    second_round = []
    for side, step in enumerate((NORTH, SOUTH)):
        second_round.append(
            remote(
                halo_rows.at[side], recv_halo_rows.at[side], side, step, halo_send_sem, halo_recv_sem
            )
        )
    for side, step in enumerate((EAST, WEST)):
        second_round.append(
            remote(halo_cols, recv_halo_cols.at[side], 2 + side, step, halo_send_sem, halo_recv_sem)
        )
    for place, step in enumerate(DIAGONAL):
        second_round.append(
            remote(
                send_corner,
                recv_corner.at[place],
                4 + place,
                step,
                halo_send_sem,
                halo_recv_sem,
            )
        )
    for copy in second_round:
        copy.start()
    heat_round = []
    for side, step in enumerate((NORTH, SOUTH)):
        copy = remote(send_heat.at[side], recv_heat.at[side], 8 + side, step)
        copy.start()
        heat_round.append(copy)

    level_inv[...] = jnp.zeros(level_inv.shape, f32)

    @pl.loop(1, LEV)
    def _(k):
        level_inv[pl.ds(k, 1), :] = 1.0 / jnp.full((1, WIDE), h[k - 1] + h[k], f32)


    weight = jnp.zeros((1, 128), f32)
    lane_w = iota((1, 128), 1)
    for k in range(LEV):
        weight = jnp.where((lane_w & 15) == k, h[k], weight)
    weight = weight * jnp.where((lane_w & 16) != 0, -0.5, 1.0)
    level_weight = jnp.zeros((LEV, WIDE), f32)
    level_row = iota((LEV, WIDE), 0)
    for k in range(LEV):
        level_weight = jnp.where(level_row == k, h[k], level_weight)
    exists = (
        jnp.where(gy < ny - 1, 1.0, 0.0).astype(f32),
        jnp.where(gy > 0, 1.0, 0.0).astype(f32),
    )

    basis[0] = jnp.zeros((EXT, WIDE), f32)
    weigh[...] = jnp.where(iota((ROWS, WIDE), 1) < COLS, 6.0 + damp_all, 0.0)

    for copy in first_round + second_round:
        copy.wait()
    for slot in range(2):
        recv_rows[slot, :, 0:128] = recv_strip[slot, 0:32, :]
        recv_rows[slot, :, 128:256] = recv_strip[slot, 32:64, :]
        for part in range(4):
            tail = recv_strip[slot, 64:72, :]
            tail = pltpu.roll(tail, 128 - 32 * part, 1) if part else tail
            recv_rows[slot, 8 * part : 8 * part + 8, 256:384] = jnp.where(lane128 < 32, tail, 0.0)

    def beside(north, south):
        return jnp.where(iota((8, 128), 0) < 4, north, south)

    own = jnp.concatenate([send_cols[0:ROWS, :], beside(recv_side[1], recv_side[0])], axis=0)
    from_east = jnp.concatenate(
        [recv_cols[1, 0:ROWS, :], beside(recv_corner[3, 8:16, :], recv_corner[1, 8:16, :])], axis=0
    )
    from_west = jnp.concatenate(
        [recv_cols[0, 0:ROWS, :], beside(recv_corner[2, 8:16, :], recv_corner[0, 8:16, :])], axis=0
    )
    lane_c = iota((EXT, 128), 1)
    is_east = (lane_c & 32) != 0
    other = jnp.where(is_east, pltpu.roll(from_east, 32, 1), pltpu.roll(from_west, 96, 1))
    both = own + other
    speed = pltpu.roll(both, 64, 1)
    speed = jnp.where((lane_c & 16) != 0, pltpu.roll(speed, 16, 1), speed)
    slope = jnp.where(is_east, 0.1, -0.1) * (other - own)
    through = 0.05 * speed * both - slope
    flux_lon[...] = through[0:ROWS, :]
    weighed = through * weight
    side_west = jnp.sum(jnp.where(lane_c < 32, weighed, 0.0), axis=1, keepdims=True)
    side_east = jnp.sum(
        jnp.where(is_east & (lane_c < 64), weighed, 0.0), axis=1, keepdims=True
    )

    def side_flux(mine, theirs, speeds, sign):
        return speeds * (mine + theirs) - (0.1 * sign) * (theirs - mine)

    side_lat = []
    speed_lat = []
    for side, sign in ((0, 1.0), (1, -1.0)):
        slot = 1 - side
        s_mine = send_rows[side, 0:16, :]
        s_theirs = recv_rows[slot, 0:16, :] * exists[side]
        speeds = 0.05 * (send_rows[side, 16:32, :] + recv_rows[slot, 16:32, :] * exists[side])
        speed_lat.append(speeds)
        flux = side_flux(s_mine, s_theirs, speeds, sign)
        side_lat.append(jnp.sum(flux * level_weight, axis=0, keepdims=True))

    is_first = (lane128 & 15) < 4
    is_north = lane128 < 64
    mine = jnp.where(is_first, recv_cols[1, 2 * ROWS :, :], recv_cols[0, 2 * ROWS :, :])
    theirs_north = jnp.where(is_first, recv_corner[3, 0:8, :], recv_corner[2, 0:8, :])
    theirs_south = jnp.where(is_first, recv_corner[1, 0:8, :], recv_corner[0, 0:8, :])
    theirs = pltpu.roll(
        jnp.where(is_north, theirs_south * exists[1], theirs_north * exists[0]), 64, 1
    )
    both = mine + theirs
    flux = 0.05 * pltpu.roll(both, 96, 1) * both - jnp.where(is_north, 0.1, -0.1) * (theirs - mine)
    flux = flux * jnp.where(
        (lane128 & 16) == 0, level_weight[0:8, 0:128], level_weight[8:16, 0:128]
    )
    flux = jnp.sum(flux, axis=0, keepdims=True)
    flux = flux + pltpu.roll(flux, 112, 1)
    for side in range(2):
        low = pltpu.roll(flux, 32 - 64 * side if side == 0 else 96, 1)
        high = pltpu.roll(flux, 120 if side == 0 else 56, 1)
        third = jnp.where(
            lane_w < 32, side_lat[side][:, 256:384], jnp.where(lane_w < 64, low, high)
        )
        side_lat[side] = jnp.concatenate([side_lat[side][:, 0:256], third], axis=1)

    def assemble(center, north_south, cols_in, base):
        lane48 = iota((ROWS, 128), 1)
        third = jnp.where(
            lane48 < 32, center[:, 256:384], jnp.where(lane48 < 64, cols_in(1), cols_in(0))
        )
        upper = jnp.concatenate([center[:, 0:256], third], axis=1)
        low = pltpu.roll(corners, 32 - base, 1)
        high = pltpu.roll(corners, 120 - base, 1)
        third = jnp.where(
            lane128 < 32, north_south[:, 256:384], jnp.where(lane128 < 64, low, high)
        )
        lower = jnp.concatenate([north_south[:, 0:256], third], axis=1)
        return jnp.concatenate([upper, lower], axis=0)

    is_low = (lane128 & 7) < 4
    corners = beside(
        jnp.where(is_low, recv_corner[3, 0:8, :], recv_corner[2, 0:8, :]),
        jnp.where(is_low, recv_corner[1, 0:8, :], recv_corner[0, 0:8, :]),
    )
    damp_ext = assemble(
        damp_all,
        jnp.where(sub < 4, recv_halo_rows[1], recv_halo_rows[0]),
        lambda slot: recv_cols[slot, ROWS : 2 * ROWS, :],
        8,
    )
    inv = mask[...] * inverse(6.0 + damp_ext)
    scale[...] = 1.5 * inv
    forcing = assemble(
        basis[1, 0:ROWS, :],
        pltpu.roll(jnp.where(sub < 4, recv_halo_rows[0], recv_halo_rows[1]), 4, 0),
        lambda slot: recv_halo_cols[slot],
        24,
    )
    forcing = jnp.concatenate(
        [
            forcing[:, 0:128] + jnp.where(lane_c == 0, side_west, 0.0),
            forcing[:, 128:256],
            forcing[:, 256:384]
            + jnp.where(
                lane_c == 31,
                -side_east,
                jnp.where(lane_c == 32, side_east, jnp.where(lane_c == 127, -side_west, 0.0)),
            ),
        ],
        axis=1,
    )
    north, south = side_lat
    forcing = jnp.concatenate(
        [
            forcing[0:8, :] + jnp.where(sub == 0, south, 0.0),
            forcing[8:40, :],
            forcing[40:48, :] - jnp.where(sub == 7, north, 0.0),
            forcing[48:56, :]
            + jnp.where(sub == 0, north, jnp.where(sub == 7, -south, 0.0)),
        ],
        axis=0,
    )
    basis[1] = forcing * inv

    def folded(value):
        value = value[:, 0:128] + value[:, 128:256] + value[:, 256:384]
        return jnp.sum(value, axis=0, keepdims=True)

    @pl.loop(0, 4)
    def _(index):
        q = basis[index + 1]
        pair = east_of(q) + west_of(q)
        column = q + 0.5 * pair
        around = pair + pltpu.roll(column, EXT - 1, 0) + pltpu.roll(column, 1, 0)
        image = scale[...] * around - 0.5 * q
        later = jnp.where(index == 0, 0.0, 1.0)
        after = image + later * (image - basis[index])
        basis[index + 2] = after
        weighed = weigh[...] * q[0:ROWS, :]
        message[pl.ds(2 * index, 1), :] = folded(weighed * q[0:ROWS, :])
        message[pl.ds(2 * index + 1, 1), :] = folded(weighed * after[0:ROWS, :])

    def spread(source, target, count, along, mine, base):
        target[mine] = source[...]

        @pl.loop(1, count)
        def _(d):
            pltpu.make_async_remote_copy(
                src_ref=source,
                dst_ref=target.at[mine],
                send_sem=sum_send_sem.at[base],
                recv_sem=sum_recv_sem.at[base],
                device_id=device(along(d)),
                device_id_type=MESH,
            ).start()

    def gathered(target, count, base):
        part = target.at[pl.ds(0, count - 1)]
        done = pltpu.make_async_remote_copy(
            src_ref=part,
            dst_ref=part,
            send_sem=sum_send_sem.at[base],
            recv_sem=sum_recv_sem.at[base],
            device_id=device(EAST),
            device_id_type=MESH,
        )
        done.wait_recv()
        done.wait_send()
        return jnp.sum(target[...], axis=0)

    parts = message[...]
    for shift in (64, 32, 16):
        parts = parts + pltpu.roll(parts, shift, 1)
    mine = lane128 // 16 == iota((8, 128), 0)
    first_message[...] = jnp.sum(jnp.where(mine, parts, 0.0), axis=0, keepdims=True)
    spread(first_message, first_sum, nx, lambda d: (d, 0), gx, 0)

    for copy in heat_round:
        copy.wait()
    for side, sign in ((0, 1.0), (1, -1.0)):
        slot = 1 - side
        target = flux_north if side == 0 else flux_prev
        heat_mine = send_heat[side]
        heat_theirs = recv_heat[slot] * exists[side]
        salt_mine = 2.0 * (heat_mine - send_rows[side, 0:16, :])
        salt_theirs = 2.0 * (heat_theirs - recv_rows[slot, 0:16, :] * exists[side])
        target[0:16, :] = side_flux(heat_mine, heat_theirs, speed_lat[side], sign)
        target[16:32, :] = side_flux(salt_mine, salt_theirs, speed_lat[side], sign)
    small[3].wait()

    edge_lane = (lane128 == 31) | (lane128 == 127)

    def mix_tile(i, _):
        rows = pl.ds(pl.multiple_of(8 * i, 8), 8)
        row = pl.ds(next_row(i), 1)
        here = mask[rows, :]
        beyond = mask[row, :]
        coefficient = padded(mix[rows, :])
        through = flux_lon[rows, :]
        use_north = (sub == 7) & (i == TILES - 1)

        def level(k, carry):
            ratio_low, heat_low, salt_low = carry
            u = padded(state[2, k, rows, :]) * here
            v = padded(state[3, k, rows, :]) * here
            v_row = padded(state[3, k, row, :]) * beyond
            v_north = jnp.where(sub == 7, v_row, pltpu.roll(v, 7, 0))
            u_pair = 0.05 * (u + east_of(u))
            v_pair = 0.05 * (v + v_north)
            lon_far, lon_near = u_pair - 0.1, u_pair + 0.1
            lat_far, lat_near = v_pair - 0.1, v_pair + 0.1
            below = coefficient * level_inv[pl.ds(k, 1), :]
            above = coefficient * level_inv[pl.ds(k + 1, 1), :]
            pivot = inverse(h[k] + above + below * (1.0 - ratio_low))
            ratio_now = above * pivot
            ratio[k] = ratio_now
            found = []
            for tracer, low in ((0, heat_low), (1, salt_low)):
                plane = tracer * LEV + k
                c = padded(state[tracer, k, rows, :]) * here
                c_row = padded(state[tracer, k, row, :]) * beyond
                c_north = jnp.where(sub == 7, c_row, pltpu.roll(c, 7, 0))
                lon = lon_far * east_of(c) + lon_near * c
                turned = pltpu.roll(through, 127 - plane, 1)
                lon = jnp.concatenate(
                    [lon[:, 0:256], jnp.where(edge_lane, turned, lon[:, 256:384])], axis=1
                )
                lat = lat_far * c_north + lat_near * c
                lat = jnp.where(use_north, flux_north[pl.ds(plane, 1), :], lat)
                lat_south = jnp.where(
                    sub == 0, flux_prev[pl.ds(plane, 1), :], pltpu.roll(lat, 1, 0)
                )
                flux_prev[pl.ds(plane, 1), :] = lat[7:8, :]
                advected = here * (c - (lon - west_of(lon)) - (lat - lat_south))
                value = (h[k] * advected + below * low) * pivot
                tracer_out[tracer, k, rows, :] = value[:, 0:COLS]
                found.append(value)
            return ratio_now, found[0], found[1]

        zero = jnp.zeros((8, WIDE), f32)
        _, heat, salt = lax.fori_loop(0, LEV, level, (zero, zero, zero), unroll=4)

        def back(step, carry):
            k = LEV - 2 - step
            heat_up, salt_up = carry
            share = ratio[k][:, 0:COLS]
            heat_up = tracer_out[0, k, rows, :] + share * heat_up
            salt_up = tracer_out[1, k, rows, :] + share * salt_up
            tracer_out[0, k, rows, :] = heat_up
            tracer_out[1, k, rows, :] = salt_up
            return heat_up, salt_up

        lax.fori_loop(0, LEV - 1, back, (heat[:, 0:COLS], salt[:, 0:COLS]), unroll=5)
        return 0

    lax.fori_loop(0, 2, mix_tile, 0)
    second_message[...] = gathered(first_sum, nx, 0)
    spread(second_message, second_sum, ny, lambda d: (0, d), gy, 1)
    lax.fori_loop(2, TILES, mix_tile, 0)
    sums = gathered(second_sum, ny, 1)

    sums = jnp.where(mine, jnp.broadcast_to(sums, (8, 128)), 0.0)
    sums = jnp.broadcast_to(jnp.sum(sums, axis=1, keepdims=True), (8, 128))
    dots = [sums[i : i + 1, :] for i in range(8)]
    moment = dots[0:2] + [2.0 * dots[i] - dots[i % 2] for i in range(2, 8)]

    def gram(i, j):
        return 0.5 * (moment[i + j] + moment[abs(i - j)])

    lower = {}
    pivots = []
    right = []
    for i in range(4):
        value = moment[i]
        for j in range(i + 1):
            entry = gram(i, j) - 0.5 * (gram(j, i + 1) + gram(j, abs(i - 1)))
            for k in range(j):
                entry = entry - lower[i, k] * lower[j, k] * pivots[k]
            if j < i:
                lower[i, j] = entry / pivots[j]
                value = value - lower[i, j] * right[j]
            else:
                pivots.append(entry)
        right.append(value)
    solved = [None] * 4
    for i in range(3, -1, -1):
        value = right[i] / pivots[i]
        for j in range(i + 1, 4):
            value = value - lower[j, i] * solved[j]
        solved[i] = value
    surface = None
    for i in range(4):
        factor = 1.5 * solved[i]
        factor = jnp.concatenate([factor, factor, factor], axis=1)
        term = factor * basis[i + 1, 0:ROWS, :]
        surface = term if surface is None else surface + term
    surface_out[...] = surface[:, 0:COLS]


def store(tracer, surface, tracer_out, surface_out, sems):
    copies = [pltpu.make_async_copy(surface, surface_out, sems.at[8])]
    for index in range(8):
        levels = pl.ds(4 * (index % 4), 4)
        copies.append(
            pltpu.make_async_copy(
                tracer.at[index // 4, levels], tracer_out.at[index // 4, levels], sems.at[index]
            )
        )
    for copy in copies:
        copy.start()
    for copy in copies:
        copy.wait()


def scratch(nx, ny):
    vmem = lambda *shape: pltpu.VMEM(shape, f32)
    dma = pltpu.SemaphoreType.DMA
    return [
        vmem(4, LEV, ROWS, COLS),
        pltpu.SMEM((LEV,), f32),
        vmem(ROWS, COLS),
        vmem(ROWS, COLS),
        None,
        vmem(EXT, WIDE),
        vmem(24, WIDE),
        vmem(3, ROWS, WIDE),
        vmem(2, ROWS, 128),
        vmem(2, 32, WIDE),
        vmem(2, 72, 128),
        vmem(2, LEV, WIDE),
        vmem(2, 72, 128),
        vmem(2, 32, WIDE),
        vmem(2, LEV, WIDE),
        vmem(2 * ROWS + 8, 128),
        vmem(2, 2 * ROWS + 8, 128),
        vmem(16, 128),
        vmem(4, 16, 128),
        vmem(2, 8, 128),
        vmem(ROWS, 128),
        vmem(2 * LEV, WIDE),
        vmem(2 * LEV, WIDE),
        vmem(LEV, 8, WIDE),
        vmem(EXT, WIDE),
        vmem(ROWS, WIDE),
        vmem(6, EXT, WIDE),
        vmem(2, 8, WIDE),
        vmem(ROWS, 128),
        vmem(2, 8, WIDE),
        vmem(2, ROWS, 128),
        vmem(8, 128),
        vmem(1, 128),
        vmem(nx, 1, 128),
        vmem(1, 128),
        vmem(ny, 1, 128),
        dma((4,)),
        dma((4,)),
        dma((12,)),
        dma((12,)),
        dma((8,)),
        dma((8,)),
        dma((2,)),
        dma((2,)),
    ]


def solution(mesh):
    nx, ny = mesh.shape["gx"], mesh.shape["gy"]

    def body(ocean_state, layer_thickness, vertical_mixing, damping, ocean_blocks):
        shapes = scratch(nx, ny)
        shapes[4] = pltpu.VMEM(ocean_blocks.shape, jnp.int32)
        call = pl.pallas_call(
            functools.partial(kernel, nx, ny),
            out_shape=[
                pltpu.VMEM((2, LEV, ROWS, COLS), f32),
                pltpu.VMEM((ROWS, COLS), f32),
            ],
            in_specs=[pl.BlockSpec(memory_space=pltpu.HBM)] * 5,
            out_specs=[pl.BlockSpec(memory_space=pltpu.VMEM)] * 2,
            scratch_shapes=shapes,
            compiler_params=pltpu.CompilerParams(
                collective_id=0, has_side_effects=True, vmem_limit_bytes=32 * 1024 * 1024
            ),
        )
        operands = [
            pltpu.with_memory_space_constraint(operand, pltpu.HBM)
            for operand in (ocean_state, layer_thickness, vertical_mixing, damping, ocean_blocks)
        ]
        tracer, surface = call(*operands)
        return tuple(
            pl.pallas_call(
                store,
                out_shape=[
                    jax.ShapeDtypeStruct((2, LEV, ROWS, COLS), f32),
                    jax.ShapeDtypeStruct((ROWS, COLS), f32),
                ],
                in_specs=[pl.BlockSpec(memory_space=pltpu.VMEM)] * 2,
                out_specs=[pl.BlockSpec(memory_space=pltpu.HBM)] * 2,
                scratch_shapes=[pltpu.SemaphoreType.DMA((9,))],
                compiler_params=pltpu.CompilerParams(vmem_limit_bytes=16 * 1024 * 1024),
            )(tracer, surface)
        )

    def wrapped(*args):
        with jax.sharding.use_abstract_mesh(mesh.abstract_mesh):
            return jax.shard_map(
                body,
                mesh=mesh,
                in_specs=(P(None, None, "gy", "gx"), P(), P("gy", "gx"), P("gy", "gx"), P()),
                out_specs=(P(None, None, "gy", "gx"), P("gy", "gx")),
                check_vma=False,
            )(*args)

    return wrapped
```

```python
import functools

import jax
import jax.numpy as jnp
from jax import lax
from jax.experimental import pallas as pl
from jax.experimental.pallas import tpu as pltpu
from jax.sharding import PartitionSpec as P

BLAT = 24
BLON = 36
LEV = 16
ROWS = 48
COLS = 288
WIDE = 384
EXT = 56
TILES = ROWS // 8

f32 = jnp.float32
MESH = pl.DeviceIdType.MESH

NORTH, SOUTH, EAST, WEST = (0, 1), (0, -1), (1, 0), (-1, 0)
DIAGONAL = ((1, 1), (-1, 1), (1, -1), (-1, -1))


def iota(shape, dim):
    return lax.broadcasted_iota(jnp.int32, shape, dim)


def padded(value):
    return jnp.concatenate([value, jnp.zeros((value.shape[0], WIDE - COLS), f32)], axis=1)


def east_of(value):
    return pltpu.roll(value, WIDE - 1, 1)


def west_of(value):
    return pltpu.roll(value, 1, 1)


def inverse(value):
    guess = pl.reciprocal(value, approx=True)
    return guess * (2.0 - value * guess)


def row_pack(low, high):
    return jnp.where(iota(low.shape, 0) < 4, low, high)


def column_pack(first, last):
    lane = iota(first.shape, 1)
    low = pltpu.roll(first, 32, 1)
    high = pltpu.roll(last, 96, 1)
    return jnp.where(
        (lane >= 32) & (lane < 36), low, jnp.where(lane >= 124, high, 0.0)
    )


def kernel(
    nx,
    ny,
    ocean,
    thick,
    mixing,
    damping,
    blocks,
    tracer_out,
    surface_out,
    state,
    h,
    mix,
    damp,
    blk,
    mask,
    level_inv,
    flat,
    ends,
    send_rows,
    send_strip,
    send_heat,
    recv_strip,
    recv_rows,
    recv_heat,
    send_cols,
    recv_cols,
    send_corner,
    recv_corner,
    recv_side,
    flux_lon,
    flux_north,
    flux_prev,
    ratio,
    scale,
    weigh,
    basis,
    halo_rows,
    halo_cols,
    recv_halo_rows,
    recv_halo_cols,
    first_message,
    first_sum,
    second_message,
    second_sum,
    load_sem,
    small_sem,
    send_sem,
    recv_sem,
    halo_send_sem,
    halo_recv_sem,
    sum_send_sem,
    sum_recv_sem,
):
    gx = lax.axis_index("gx")
    gy = lax.axis_index("gy")

    def device(step):
        return {"gx": lax.rem(gx + step[0] + nx, nx), "gy": lax.rem(gy + step[1] + ny, ny)}

    def greet(step):
        pl.semaphore_signal(barrier, inc=1, device_id=device(step), device_id_type=MESH)

    small = [
        pltpu.make_async_copy(blocks, blk, small_sem.at[0]),
        pltpu.make_async_copy(thick, h, small_sem.at[1]),
        pltpu.make_async_copy(damping, damp, small_sem.at[2]),
        pltpu.make_async_copy(mixing, mix, small_sem.at[3]),
    ]
    group = LEV // 4

    def load(index):
        levels = pl.ds(group * index, group)
        return pltpu.make_async_copy(
            ocean.at[:, levels, :, :], state.at[:, levels, :, :], load_sem.at[index]
        )

    for copy in small[:3] + [load(index) for index in range(4)] + small[3:]:
        copy.start()

    barrier = pltpu.get_barrier_semaphore()
    for step in DIAGONAL:
        greet(step)
    pl.loop(1, nx)(lambda d: greet((d, 0)))
    pl.loop(1, ny)(lambda d: greet((0, d)))
    partners = len(DIAGONAL) + nx - 1 + ny - 1

    block_rows, block_cols = blk.shape
    small[0].wait()
    row = iota((EXT, block_rows), 0)
    row = gy * ROWS + jnp.where(row < ROWS + 4, row, row - EXT)
    edge = iota((EXT, block_rows), 1) * BLAT
    pick_rows = jnp.where((row >= edge) & (row < edge + BLAT), 1.0, 0.0)
    lane = iota((block_cols, WIDE), 1)
    total = block_cols * BLON
    col = gx * COLS + jnp.where(lane < COLS + 4, lane, lane - WIDE)
    col = jnp.where(col < 0, col + total, jnp.where(col >= total, col - total, col))
    edge = iota((block_cols, WIDE), 0) * BLON
    inside = (lane < COLS + 4) | (lane >= WIDE - 4)
    pick_cols = jnp.where(inside & (col >= edge) & (col < edge + BLON), 1.0, 0.0)
    coarse = jnp.dot(pick_rows, blk[...].astype(f32), preferred_element_type=f32)
    mask[...] = jnp.dot(coarse, pick_cols, preferred_element_type=f32)

    small[1].wait()
    small[2].wait()
    damp_low = padded(damp[0:8, :])
    damp_high = padded(damp[ROWS - 8 : ROWS, :])
    damp_rows = row_pack(damp_low, damp_high)
    damp_all = padded(damp[...])
    send_cols[ROWS : 2 * ROWS, :] = column_pack(damp_all[:, 0:128], damp_all[:, 256:384])

    def remote(source, target, index, step, sends=send_sem, recvs=recv_sem):
        return pltpu.make_async_remote_copy(
            src_ref=source,
            dst_ref=target,
            send_sem=sends.at[index],
            recv_sem=recvs.at[index],
            device_id=device(step),
            device_id_type=MESH,
        )

    sub = iota((8, WIDE), 0)
    lane128 = iota((8, 128), 1)

    def next_row(i):
        return jnp.minimum(8 * i + 8, ROWS - 1)

    tiles = [pl.ds(8 * i, 8) for i in range(TILES)]
    flat[...] = jnp.zeros(flat.shape, f32)
    ends[...] = jnp.zeros(ends.shape, f32)
    end_mask = [
        jnp.where(lane128 == 31, mask[rows, 256:384], mask[rows, 0:128]) for rows in tiles
    ]

    def pack_ends(pair):
        for i, rows in enumerate(tiles):
            west, east = ends[0, rows, :], ends[1, rows, :]
            for k in (2 * pair, 2 * pair + 1):
                for field, base in ((0, 0), (1, 16), (2, 64)):
                    last = jnp.concatenate(
                        [state[field, k, rows, 256:COLS], jnp.zeros((8, WIDE - COLS), f32)], axis=1
                    )
                    both = jnp.where(lane128 == 31, last, state[field, k, rows, 0:128])
                    both = pltpu.roll(both * end_mask[i], base + k, 1)
                    west = jnp.where(lane128 == base + k, both, west)
                    east = jnp.where(lane128 == base + k + 31, both, east)
            ends[0, rows, :] = west
            ends[1, rows, :] = east


    def turned_up(values):
        turned = [pltpu.roll(value, 7, 0) for value in values]
        return [
            jnp.where(sub == 7, turned[(i + 1) % TILES], turned[i]) for i in range(TILES)
        ]

    @pl.loop(0, LEV // 2)
    def _(pair):
        @pl.when(lax.rem(pair, group // 2) == 0)
        def _():
            load(pair // (group // 2)).wait()

        sums = None
        for k in (2 * pair, 2 * pair + 1):
            s = [
                padded(state[0, k, rows, :] - 0.5 * state[1, k, rows, :]) * mask[rows, :] * h[k]
                for rows in tiles
            ]
            v = [padded(state[3, k, rows, :]) * mask[rows, :] for rows in tiles]
            s_north, v_north = turned_up(s), turned_up(v)
            found = []
            for i, rows in enumerate(tiles):
                u = padded(state[2, k, rows, :]) * mask[rows, :]
                found.append(
                    (
                        s[i],
                        (u + east_of(u)) * (s[i] + east_of(s[i])),
                        (v[i] + v_north[i]) * (s[i] + s_north[i]),
                    )
                )
            if sums is None:
                sums = found
            else:
                sums = [[a + b for a, b in zip(x, y)] for x, y in zip(sums, found)]
        for i, rows in enumerate(tiles):
            for part in range(3):
                flat[part, rows, :] += sums[i][part]
        pack_ends(pair)

    first_round = []
    for side, (edge_row, step) in enumerate(((ROWS - 1, NORTH), (0, SOUTH))):
        edge_mask = mask[edge_row : edge_row + 1, :]
        heat = padded(state[0, :, edge_row, :]) * edge_mask
        salt = padded(state[1, :, edge_row, :]) * edge_mask
        send_heat[side] = heat
        send_rows[side, 0:16, :] = heat - 0.5 * salt
        send_rows[side, 16:32, :] = padded(state[3, :, edge_row, :]) * edge_mask
        send_strip[side, 0:32, :] = send_rows[side, :, 0:128]
        send_strip[side, 32:64, :] = send_rows[side, :, 128:256]
        tail = jnp.zeros((8, 128), f32)
        for part in range(4):
            third = send_rows[side, 8 * part : 8 * part + 8, 256:384]
            tail = jnp.where(lane128 // 32 == part, pltpu.roll(third, 32 * part, 1), tail)
        send_strip[side, 64:72, :] = tail
        first_round.append(remote(send_strip.at[side], recv_strip.at[side], side, step))

    pl.semaphore_wait(barrier, partners)
    for copy in first_round:
        copy.start()

    send_cols[0:ROWS, :] = ends[0] + pltpu.roll(ends[1], 1, 1)

    compact = jnp.zeros((8, 128), f32)
    for side in range(2):
        for part in range(4):
            j = 4 * side + part
            rows = pl.ds(8 * part, 8)
            first = pltpu.roll(send_rows[side, rows, 0:128], 16 * j, 1)
            last = pltpu.roll(send_rows[side, rows, 256:384], (16 * j - 24) % 128, 1)
            inside = lane128 // 16 == j
            compact = jnp.where(inside & (lane128 % 16 < 4), first, compact)
            compact = jnp.where(
                inside & (lane128 % 16 >= 4) & (lane128 % 16 < 8), last, compact
            )
    send_cols[2 * ROWS :, :] = compact
    send_corner[8:16, :] = row_pack(send_cols[0:8, :], send_cols[ROWS - 8 : ROWS, :])

    second_round = []
    for side, step in enumerate((EAST, WEST)):
        second_round.append(remote(send_cols, recv_cols.at[side], 2 + side, step))
    for side, step in enumerate((NORTH, SOUTH)):
        second_round.append(
            remote(send_corner.at[pl.ds(8, 8)], recv_side.at[side], 10 + side, step)
        )
    for copy in second_round:
        copy.start()
    first_round = first_round + second_round

    lane_f = iota((ROWS, WIDE), 1)
    row_f = iota((ROWS, WIDE), 0)
    plain = flat[0]
    lon = 0.05 * flat[1] - 0.1 * (east_of(plain) - plain)
    lon = jnp.where(lane_f < COLS - 1, lon, 0.0)
    lat = 0.05 * flat[2] - 0.1 * (pltpu.roll(plain, ROWS - 1, 0) - plain)
    lat = jnp.where(row_f == ROWS - 1, 0.0, lat)
    start = plain - (lon - west_of(lon)) - (lat - pltpu.roll(lat, 1, 0))
    start = jnp.where(lane_f < COLS, start, 0.0)
    basis[1, 0:ROWS, :] = start
    packed_rows = row_pack(start[0:8, :], start[ROWS - 8 : ROWS, :])
    halo_rows[0] = jnp.where(sub < 4, pltpu.roll(start[ROWS - 8 : ROWS, :], 4, 0), damp_high)
    halo_rows[1] = jnp.where(sub < 4, damp_low, pltpu.roll(start[0:8, :], 4, 0))
    halo_cols[...] = column_pack(start[:, 0:128], start[:, 256:384])
    for base, packed in ((8, damp_rows), (24, packed_rows)):
        first = pltpu.roll(packed[:, 0:128], base, 1)
        last = packed[:, 256:384]
        last = pltpu.roll(last, (base - 24) % 128, 1) if base != 24 else last
        compact = jnp.where((lane128 >= base) & (lane128 < base + 4), first, compact)
        compact = jnp.where((lane128 >= base + 4) & (lane128 < base + 8), last, compact)
    send_corner[0:8, :] = compact
    second_round = []
    for place, step in enumerate(DIAGONAL):
        second_round.append(
            remote(
                send_corner,
                recv_corner.at[place],
                4 + place,
                step,
                halo_send_sem,
                halo_recv_sem,
            )
        )
    for side, step in enumerate((NORTH, SOUTH)):
        second_round.append(
            remote(
                halo_rows.at[side], recv_halo_rows.at[side], side, step, halo_send_sem, halo_recv_sem
            )
        )
    for side, step in enumerate((EAST, WEST)):
        second_round.append(
            remote(halo_cols, recv_halo_cols.at[side], 2 + side, step, halo_send_sem, halo_recv_sem)
        )
    for copy in second_round:
        copy.start()
    heat_round = []
    for side, step in enumerate((NORTH, SOUTH)):
        copy = remote(send_heat.at[side], recv_heat.at[side], 8 + side, step)
        copy.start()
        heat_round.append(copy)

    level_inv[...] = jnp.zeros(level_inv.shape, f32)

    @pl.loop(1, LEV)
    def _(k):
        level_inv[pl.ds(k, 1), :] = 1.0 / jnp.full((1, WIDE), h[k - 1] + h[k], f32)


    weight = jnp.zeros((1, 128), f32)
    lane_w = iota((1, 128), 1)
    for k in range(LEV):
        weight = jnp.where((lane_w & 15) == k, h[k], weight)
    weight = weight * jnp.where((lane_w & 16) != 0, -0.5, 1.0)
    level_weight = jnp.zeros((LEV, WIDE), f32)
    level_row = iota((LEV, WIDE), 0)
    for k in range(LEV):
        level_weight = jnp.where(level_row == k, h[k], level_weight)
    exists = (
        jnp.where(gy < ny - 1, 1.0, 0.0).astype(f32),
        jnp.where(gy > 0, 1.0, 0.0).astype(f32),
    )

    weigh[...] = jnp.where(iota((ROWS, WIDE), 1) < COLS, 6.0 + damp_all, 0.0)

    for copy in first_round:
        copy.wait()
    for slot in range(2):
        recv_rows[slot, :, 0:128] = recv_strip[slot, 0:32, :]
        recv_rows[slot, :, 128:256] = recv_strip[slot, 32:64, :]
        for part in range(4):
            tail = recv_strip[slot, 64:72, :]
            tail = pltpu.roll(tail, 128 - 32 * part, 1) if part else tail
            recv_rows[slot, 8 * part : 8 * part + 8, 256:384] = jnp.where(lane128 < 32, tail, 0.0)

    def side_flux(mine, theirs, speeds, sign):
        return speeds * (mine + theirs) - (0.1 * sign) * (theirs - mine)

    side_lat = []
    speed_lat = []
    for side, sign in ((0, 1.0), (1, -1.0)):
        slot = 1 - side
        s_mine = send_rows[side, 0:16, :]
        s_theirs = recv_rows[slot, 0:16, :] * exists[side]
        speeds = 0.05 * (send_rows[side, 16:32, :] + recv_rows[slot, 16:32, :] * exists[side])
        speed_lat.append(speeds)
        flux = side_flux(s_mine, s_theirs, speeds, sign)
        side_lat.append(jnp.sum(flux * level_weight, axis=0, keepdims=True))

    for copy in second_round:
        copy.wait()

    def beside(north, south):
        return jnp.where(iota((8, 128), 0) < 4, north, south)

    own = jnp.concatenate([send_cols[0:ROWS, :], beside(recv_side[1], recv_side[0])], axis=0)
    from_east = jnp.concatenate(
        [recv_cols[1, 0:ROWS, :], beside(recv_corner[3, 8:16, :], recv_corner[1, 8:16, :])], axis=0
    )
    from_west = jnp.concatenate(
        [recv_cols[0, 0:ROWS, :], beside(recv_corner[2, 8:16, :], recv_corner[0, 8:16, :])], axis=0
    )
    lane_c = iota((EXT, 128), 1)
    is_east = (lane_c & 32) != 0
    other = jnp.where(is_east, pltpu.roll(from_east, 32, 1), pltpu.roll(from_west, 96, 1))
    both = own + other
    speed = pltpu.roll(both, 64, 1)
    speed = jnp.where((lane_c & 16) != 0, pltpu.roll(speed, 16, 1), speed)
    slope = jnp.where(is_east, 0.1, -0.1) * (other - own)
    through = 0.05 * speed * both - slope
    flux_lon[...] = through[0:ROWS, :]
    weighed = through * weight
    side_west = jnp.sum(jnp.where(lane_c < 32, weighed, 0.0), axis=1, keepdims=True)
    side_east = jnp.sum(
        jnp.where(is_east & (lane_c < 64), weighed, 0.0), axis=1, keepdims=True
    )

    is_first = (lane128 & 15) < 4
    is_north = lane128 < 64
    mine = jnp.where(is_first, recv_cols[1, 2 * ROWS :, :], recv_cols[0, 2 * ROWS :, :])
    theirs_north = jnp.where(is_first, recv_corner[3, 0:8, :], recv_corner[2, 0:8, :])
    theirs_south = jnp.where(is_first, recv_corner[1, 0:8, :], recv_corner[0, 0:8, :])
    theirs = pltpu.roll(
        jnp.where(is_north, theirs_south * exists[1], theirs_north * exists[0]), 64, 1
    )
    both = mine + theirs
    flux = 0.05 * pltpu.roll(both, 96, 1) * both - jnp.where(is_north, 0.1, -0.1) * (theirs - mine)
    flux = flux * jnp.where(
        (lane128 & 16) == 0, level_weight[0:8, 0:128], level_weight[8:16, 0:128]
    )
    flux = jnp.sum(flux, axis=0, keepdims=True)
    flux = flux + pltpu.roll(flux, 112, 1)
    for side in range(2):
        low = pltpu.roll(flux, 32 - 64 * side if side == 0 else 96, 1)
        high = pltpu.roll(flux, 120 if side == 0 else 56, 1)
        third = jnp.where(
            lane_w < 32, side_lat[side][:, 256:384], jnp.where(lane_w < 64, low, high)
        )
        side_lat[side] = jnp.concatenate([side_lat[side][:, 0:256], third], axis=1)

    def assemble(center, north_south, cols_in, base):
        lane48 = iota((ROWS, 128), 1)
        third = jnp.where(
            lane48 < 32, center[:, 256:384], jnp.where(lane48 < 64, cols_in(1), cols_in(0))
        )
        upper = jnp.concatenate([center[:, 0:256], third], axis=1)
        low = pltpu.roll(corners, 32 - base, 1)
        high = pltpu.roll(corners, 120 - base, 1)
        third = jnp.where(
            lane128 < 32, north_south[:, 256:384], jnp.where(lane128 < 64, low, high)
        )
        lower = jnp.concatenate([north_south[:, 0:256], third], axis=1)
        return jnp.concatenate([upper, lower], axis=0)

    is_low = (lane128 & 7) < 4
    corners = beside(
        jnp.where(is_low, recv_corner[3, 0:8, :], recv_corner[2, 0:8, :]),
        jnp.where(is_low, recv_corner[1, 0:8, :], recv_corner[0, 0:8, :]),
    )
    damp_ext = assemble(
        damp_all,
        jnp.where(sub < 4, recv_halo_rows[1], recv_halo_rows[0]),
        lambda slot: recv_cols[slot, ROWS : 2 * ROWS, :],
        8,
    )
    inv = mask[...] * inverse(6.0 + damp_ext)
    scale[...] = 1.5 * inv
    forcing = assemble(
        basis[1, 0:ROWS, :],
        pltpu.roll(jnp.where(sub < 4, recv_halo_rows[0], recv_halo_rows[1]), 4, 0),
        lambda slot: recv_halo_cols[slot],
        24,
    )
    forcing = jnp.concatenate(
        [
            forcing[:, 0:128] + jnp.where(lane_c == 0, side_west, 0.0),
            forcing[:, 128:256],
            forcing[:, 256:384]
            + jnp.where(
                lane_c == 31,
                -side_east,
                jnp.where(lane_c == 32, side_east, jnp.where(lane_c == 127, -side_west, 0.0)),
            ),
        ],
        axis=1,
    )
    north, south = side_lat
    forcing = jnp.concatenate(
        [
            forcing[0:8, :] + jnp.where(sub == 0, south, 0.0),
            forcing[8:40, :],
            forcing[40:48, :] - jnp.where(sub == 7, north, 0.0),
            forcing[48:56, :]
            + jnp.where(sub == 0, north, jnp.where(sub == 7, -south, 0.0)),
        ],
        axis=0,
    )
    basis[1] = forcing * inv

    def folded(value):
        rows = [value[8 * i : 8 * i + 8, :] for i in range(TILES)]
        value = (rows[0] + rows[1]) + (rows[2] + rows[3]) + (rows[4] + rows[5])
        return value[:, 0:128] + value[:, 128:256] + value[:, 256:384]

    parts = []
    for index in range(4):
        q = basis[index + 1]
        pair = east_of(q) + west_of(q)
        column = q + 0.5 * pair
        around = pair + pltpu.roll(column, EXT - 1, 0) + pltpu.roll(column, 1, 0)
        image = scale[...] * around - 0.5 * q
        after = image if index == 0 else 2.0 * image - basis[index]
        if index < 3:
            basis[index + 2] = after
        weighed = weigh[...] * q[0:ROWS, :]
        parts.append(folded(weighed * q[0:ROWS, :]))
        parts.append(folded(weighed * after[0:ROWS, :]))

    for width in (64, 32, 16):
        half = len(parts) // 2
        parts = [
            jnp.where(
                (lane128 & width) == 0,
                low + pltpu.roll(low, 128 - width, 1),
                high + pltpu.roll(high, width, 1),
            )
            for low, high in zip(parts[:half], parts[half:])
        ]
    first_message[...] = jnp.sum(parts[0], axis=0, keepdims=True)

    def spread(source, target, count, along, mine, base):
        target[mine] = source[...]

        @pl.loop(1, count)
        def _(turn):
            d = count // 2 + jnp.where(turn % 2 == 0, -(turn // 2), turn // 2)
            pltpu.make_async_remote_copy(
                src_ref=source,
                dst_ref=target.at[mine],
                send_sem=sum_send_sem.at[base],
                recv_sem=sum_recv_sem.at[base],
                device_id=device(along(d)),
                device_id_type=MESH,
            ).start()

    def gathered(target, count, base):
        part = target.at[pl.ds(0, count - 1)]
        done = pltpu.make_async_remote_copy(
            src_ref=part,
            dst_ref=part,
            send_sem=sum_send_sem.at[base],
            recv_sem=sum_recv_sem.at[base],
            device_id=device(EAST),
            device_id_type=MESH,
        )
        done.wait_recv()
        done.wait_send()
        return jnp.sum(target[...], axis=0)

    spread(first_message, first_sum, nx, lambda d: (d, 0), gx, 0)

    for copy in heat_round:
        copy.wait()
    for side, sign in ((0, 1.0), (1, -1.0)):
        slot = 1 - side
        target = flux_north if side == 0 else flux_prev
        heat_mine = send_heat[side]
        heat_theirs = recv_heat[slot] * exists[side]
        salt_mine = 2.0 * (heat_mine - send_rows[side, 0:16, :])
        salt_theirs = 2.0 * (heat_theirs - recv_rows[slot, 0:16, :] * exists[side])
        target[0:16, :] = side_flux(heat_mine, heat_theirs, speed_lat[side], sign)
        target[16:32, :] = side_flux(salt_mine, salt_theirs, speed_lat[side], sign)
    small[3].wait()

    edge_lane = (lane128 == 31) | (lane128 == 127)

    def mix_tile(i, _):
        rows = pl.ds(pl.multiple_of(8 * i, 8), 8)
        row = pl.ds(next_row(i), 1)
        here = mask[rows, :]
        beyond = mask[row, :]
        coefficient = padded(mix[rows, :])
        through = flux_lon[rows, :]
        use_north = (sub == 7) & (i == TILES - 1)

        def level(k, carry):
            ratio_low, heat_low, salt_low = carry
            u = padded(state[2, k, rows, :]) * here
            v = padded(state[3, k, rows, :]) * here
            v_row = padded(state[3, k, row, :]) * beyond
            v_north = jnp.where(sub == 7, v_row, pltpu.roll(v, 7, 0))
            u_pair = 0.05 * (u + east_of(u))
            v_pair = 0.05 * (v + v_north)
            lon_far, lon_near = u_pair - 0.1, u_pair + 0.1
            lat_far, lat_near = v_pair - 0.1, v_pair + 0.1
            below = coefficient * level_inv[pl.ds(k, 1), :]
            above = coefficient * level_inv[pl.ds(k + 1, 1), :]
            pivot = inverse(h[k] + above + below * (1.0 - ratio_low))
            ratio_now = above * pivot
            ratio[k] = ratio_now
            found = []
            for tracer, low in ((0, heat_low), (1, salt_low)):
                plane = tracer * LEV + k
                c = padded(state[tracer, k, rows, :]) * here
                c_row = padded(state[tracer, k, row, :]) * beyond
                c_north = jnp.where(sub == 7, c_row, pltpu.roll(c, 7, 0))
                lon = lon_far * east_of(c) + lon_near * c
                turned = pltpu.roll(through, 127 - plane, 1)
                lon = jnp.concatenate(
                    [lon[:, 0:256], jnp.where(edge_lane, turned, lon[:, 256:384])], axis=1
                )
                lat = lat_far * c_north + lat_near * c
                lat = jnp.where(use_north, flux_north[pl.ds(plane, 1), :], lat)
                lat_south = jnp.where(
                    sub == 0, flux_prev[pl.ds(plane, 1), :], pltpu.roll(lat, 1, 0)
                )
                flux_prev[pl.ds(plane, 1), :] = lat[7:8, :]
                advected = here * (c - (lon - west_of(lon)) - (lat - lat_south))
                value = (h[k] * advected + below * low) * pivot
                tracer_out[tracer, k, rows, :] = value[:, 0:COLS]
                found.append(value)
            return ratio_now, found[0], found[1]

        zero = jnp.zeros((8, WIDE), f32)
        _, heat, salt = lax.fori_loop(0, LEV, level, (zero, zero, zero), unroll=4)

        def back(step, carry):
            k = LEV - 2 - step
            heat_up, salt_up = carry
            share = ratio[k][:, 0:COLS]
            heat_up = tracer_out[0, k, rows, :] + share * heat_up
            salt_up = tracer_out[1, k, rows, :] + share * salt_up
            tracer_out[0, k, rows, :] = heat_up
            tracer_out[1, k, rows, :] = salt_up
            return heat_up, salt_up

        lax.fori_loop(0, LEV - 1, back, (heat[:, 0:COLS], salt[:, 0:COLS]), unroll=5)
        return 0

    lax.fori_loop(0, 2, mix_tile, 0)
    second_message[...] = gathered(first_sum, nx, 0)
    spread(second_message, second_sum, ny, lambda d: (0, d), gy, 1)
    lax.fori_loop(2, TILES, mix_tile, 0)
    sums = gathered(second_sum, ny, 1)

    own_lanes = lane128 // 16 == iota((8, 128), 0)
    sums = jnp.where(own_lanes, jnp.broadcast_to(sums, (8, 128)), 0.0)
    sums = jnp.broadcast_to(jnp.sum(sums, axis=1, keepdims=True), (8, 128))
    dots = [sums[i : i + 1, :] for i in range(8)]
    moment = dots[0:2] + [2.0 * dots[i] - dots[i % 2] for i in range(2, 8)]

    def gram(i, j):
        return 0.5 * (moment[i + j] + moment[abs(i - j)])

    lower = {}
    pivots = []
    right = []
    for i in range(4):
        value = moment[i]
        for j in range(i + 1):
            entry = gram(i, j) - 0.5 * (gram(j, i + 1) + gram(j, abs(i - 1)))
            for k in range(j):
                entry = entry - lower[i, k] * lower[j, k] * pivots[k]
            if j < i:
                lower[i, j] = entry / pivots[j]
                value = value - lower[i, j] * right[j]
            else:
                pivots.append(entry)
        right.append(value)
    solved = [None] * 4
    for i in range(3, -1, -1):
        value = right[i] / pivots[i]
        for j in range(i + 1, 4):
            value = value - lower[j, i] * solved[j]
        solved[i] = value
    surface = None
    for i in range(4):
        factor = 1.5 * solved[i]
        factor = jnp.concatenate([factor, factor, factor], axis=1)
        term = factor * basis[i + 1, 0:ROWS, :]
        surface = term if surface is None else surface + term
    surface_out[...] = surface[:, 0:COLS]


def store(tracer, surface, tracer_out, surface_out, sems):
    copies = [pltpu.make_async_copy(surface, surface_out, sems.at[8])]
    for index in range(8):
        levels = pl.ds(4 * (index % 4), 4)
        copies.append(
            pltpu.make_async_copy(
                tracer.at[index // 4, levels], tracer_out.at[index // 4, levels], sems.at[index]
            )
        )
    for copy in copies:
        copy.start()
    for copy in copies:
        copy.wait()


def scratch(nx, ny):
    vmem = lambda *shape: pltpu.VMEM(shape, f32)
    dma = pltpu.SemaphoreType.DMA
    return [
        vmem(4, LEV, ROWS, COLS),
        pltpu.SMEM((LEV,), f32),
        vmem(ROWS, COLS),
        vmem(ROWS, COLS),
        None,
        vmem(EXT, WIDE),
        vmem(24, WIDE),
        vmem(3, ROWS, WIDE),
        vmem(2, ROWS, 128),
        vmem(2, 32, WIDE),
        vmem(2, 72, 128),
        vmem(2, LEV, WIDE),
        vmem(2, 72, 128),
        vmem(2, 32, WIDE),
        vmem(2, LEV, WIDE),
        vmem(2 * ROWS + 8, 128),
        vmem(2, 2 * ROWS + 8, 128),
        vmem(16, 128),
        vmem(4, 16, 128),
        vmem(2, 8, 128),
        vmem(ROWS, 128),
        vmem(2 * LEV, WIDE),
        vmem(2 * LEV, WIDE),
        vmem(LEV, 8, WIDE),
        vmem(EXT, WIDE),
        vmem(ROWS, WIDE),
        vmem(6, EXT, WIDE),
        vmem(2, 8, WIDE),
        vmem(ROWS, 128),
        vmem(2, 8, WIDE),
        vmem(2, ROWS, 128),
        vmem(1, 128),
        vmem(nx, 1, 128),
        vmem(1, 128),
        vmem(ny, 1, 128),
        dma((4,)),
        dma((4,)),
        dma((12,)),
        dma((12,)),
        dma((8,)),
        dma((8,)),
        dma((2,)),
        dma((2,)),
    ]


def solution(mesh):
    nx, ny = mesh.shape["gx"], mesh.shape["gy"]

    def body(ocean_state, layer_thickness, vertical_mixing, damping, ocean_blocks):
        shapes = scratch(nx, ny)
        shapes[4] = pltpu.VMEM(ocean_blocks.shape, jnp.int32)
        call = pl.pallas_call(
            functools.partial(kernel, nx, ny),
            out_shape=[
                pltpu.VMEM((2, LEV, ROWS, COLS), f32),
                pltpu.VMEM((ROWS, COLS), f32),
            ],
            in_specs=[pl.BlockSpec(memory_space=pltpu.HBM)] * 5,
            out_specs=[pl.BlockSpec(memory_space=pltpu.VMEM)] * 2,
            scratch_shapes=shapes,
            compiler_params=pltpu.CompilerParams(
                collective_id=0, has_side_effects=True, vmem_limit_bytes=32 * 1024 * 1024
            ),
        )
        operands = [
            pltpu.with_memory_space_constraint(operand, pltpu.HBM)
            for operand in (ocean_state, layer_thickness, vertical_mixing, damping, ocean_blocks)
        ]
        tracer, surface = call(*operands)
        return tuple(
            pl.pallas_call(
                store,
                out_shape=[
                    jax.ShapeDtypeStruct((2, LEV, ROWS, COLS), f32),
                    jax.ShapeDtypeStruct((ROWS, COLS), f32),
                ],
                in_specs=[pl.BlockSpec(memory_space=pltpu.VMEM)] * 2,
                out_specs=[pl.BlockSpec(memory_space=pltpu.HBM)] * 2,
                scratch_shapes=[pltpu.SemaphoreType.DMA((9,))],
                compiler_params=pltpu.CompilerParams(vmem_limit_bytes=16 * 1024 * 1024),
            )(tracer, surface)
        )

    def wrapped(*args):
        with jax.sharding.use_abstract_mesh(mesh.abstract_mesh):
            return jax.shard_map(
                body,
                mesh=mesh,
                in_specs=(P(None, None, "gy", "gx"), P(), P("gy", "gx"), P("gy", "gx"), P()),
                out_specs=(P(None, None, "gy", "gx"), P("gy", "gx")),
                check_vma=False,
            )(*args)

    return wrapped
```

```python
import functools

import jax
import jax.numpy as jnp
from jax import lax
from jax.experimental import pallas as pl
from jax.experimental.pallas import tpu as pltpu
from jax.sharding import PartitionSpec as P

BLAT = 24
BLON = 36
LEV = 16
ROWS = 48
COLS = 288
WIDE = 384
EXT = 56
TILES = ROWS // 8

f32 = jnp.float32
MESH = pl.DeviceIdType.MESH

NORTH, SOUTH, EAST, WEST = (0, 1), (0, -1), (1, 0), (-1, 0)
DIAGONAL = ((1, 1), (-1, 1), (1, -1), (-1, -1))


def iota(shape, dim):
    return lax.broadcasted_iota(jnp.int32, shape, dim)


def padded(value):
    return jnp.concatenate([value, jnp.zeros((value.shape[0], WIDE - COLS), f32)], axis=1)


def east_of(value):
    return pltpu.roll(value, WIDE - 1, 1)


def west_of(value):
    return pltpu.roll(value, 1, 1)


def inverse(value):
    guess = pl.reciprocal(value, approx=True)
    return guess * (2.0 - value * guess)


def row_pack(low, high):
    return jnp.where(iota(low.shape, 0) < 4, low, high)


def column_pack(first, last):
    lane = iota(first.shape, 1)
    low = pltpu.roll(first, 32, 1)
    high = pltpu.roll(last, 96, 1)
    return jnp.where(
        (lane >= 32) & (lane < 36), low, jnp.where(lane >= 124, high, 0.0)
    )


def kernel(
    nx,
    ny,
    ocean,
    thick,
    mixing,
    damping,
    blocks,
    tracer_out,
    surface_out,
    state,
    h,
    mix,
    damp,
    blk,
    mask,
    level_inv,
    flat,
    ends,
    send_rows,
    send_strip,
    send_heat,
    recv_strip,
    recv_rows,
    recv_heat,
    send_cols,
    recv_cols,
    send_corner,
    recv_corner,
    recv_side,
    flux_lon,
    flux_north,
    flux_prev,
    ratio,
    carried,
    taken,
    scale,
    weigh,
    basis,
    halo_rows,
    halo_cols,
    recv_halo_rows,
    recv_halo_cols,
    first_message,
    first_sum,
    second_message,
    second_sum,
    load_sem,
    small_sem,
    send_sem,
    recv_sem,
    halo_send_sem,
    halo_recv_sem,
    sum_send_sem,
    sum_recv_sem,
):
    gx = lax.axis_index("gx")
    gy = lax.axis_index("gy")

    def device(step):
        return {"gx": lax.rem(gx + step[0] + nx, nx), "gy": lax.rem(gy + step[1] + ny, ny)}

    def greet(step):
        pl.semaphore_signal(barrier, inc=1, device_id=device(step), device_id_type=MESH)

    small = [
        pltpu.make_async_copy(blocks, blk, small_sem.at[0]),
        pltpu.make_async_copy(thick, h, small_sem.at[1]),
        pltpu.make_async_copy(damping, damp, small_sem.at[2]),
        pltpu.make_async_copy(mixing, mix, small_sem.at[3]),
    ]
    group = LEV // 4

    def load(index):
        levels = pl.ds(group * index, group)
        return pltpu.make_async_copy(
            ocean.at[:, levels, :, :], state.at[:, levels, :, :], load_sem.at[index]
        )

    for copy in small[:3] + [load(index) for index in range(4)] + small[3:]:
        copy.start()

    barrier = pltpu.get_barrier_semaphore()
    for step in DIAGONAL:
        greet(step)
    pl.loop(1, nx)(lambda d: greet((d, 0)))
    pl.loop(1, ny)(lambda d: greet((0, d)))
    partners = len(DIAGONAL) + nx - 1 + ny - 1

    block_rows, block_cols = blk.shape
    small[0].wait()
    row = iota((EXT, block_rows), 0)
    row = gy * ROWS + jnp.where(row < ROWS + 4, row, row - EXT)
    edge = iota((EXT, block_rows), 1) * BLAT
    pick_rows = jnp.where((row >= edge) & (row < edge + BLAT), 1.0, 0.0)
    lane = iota((block_cols, WIDE), 1)
    total = block_cols * BLON
    col = gx * COLS + jnp.where(lane < COLS + 4, lane, lane - WIDE)
    col = jnp.where(col < 0, col + total, jnp.where(col >= total, col - total, col))
    edge = iota((block_cols, WIDE), 0) * BLON
    inside = (lane < COLS + 4) | (lane >= WIDE - 4)
    pick_cols = jnp.where(inside & (col >= edge) & (col < edge + BLON), 1.0, 0.0)
    coarse = jnp.dot(pick_rows, blk[...].astype(f32), preferred_element_type=f32)
    mask[...] = jnp.dot(coarse, pick_cols, preferred_element_type=f32)

    small[1].wait()
    small[2].wait()
    damp_low = padded(damp[0:8, :])
    damp_high = padded(damp[ROWS - 8 : ROWS, :])
    damp_rows = row_pack(damp_low, damp_high)
    damp_all = padded(damp[...])
    send_cols[ROWS : 2 * ROWS, :] = column_pack(damp_all[:, 0:128], damp_all[:, 256:384])

    def remote(source, target, index, step, sends=send_sem, recvs=recv_sem):
        return pltpu.make_async_remote_copy(
            src_ref=source,
            dst_ref=target,
            send_sem=sends.at[index],
            recv_sem=recvs.at[index],
            device_id=device(step),
            device_id_type=MESH,
        )

    sub = iota((8, WIDE), 0)
    lane128 = iota((8, 128), 1)

    def next_row(i):
        return jnp.minimum(8 * i + 8, ROWS - 1)

    tiles = [pl.ds(8 * i, 8) for i in range(TILES)]
    flat[...] = jnp.zeros(flat.shape, f32)
    ends[...] = jnp.zeros(ends.shape, f32)
    end_mask = [
        jnp.where(lane128 == 31, mask[rows, 256:384], mask[rows, 0:128]) for rows in tiles
    ]

    def pack_ends(pair):
        for i, rows in enumerate(tiles):
            west, east = ends[0, rows, :], ends[1, rows, :]
            for k in (2 * pair, 2 * pair + 1):
                for field, base in ((0, 0), (1, 16), (2, 64)):
                    last = jnp.concatenate(
                        [state[field, k, rows, 256:COLS], jnp.zeros((8, WIDE - COLS), f32)], axis=1
                    )
                    both = jnp.where(lane128 == 31, last, state[field, k, rows, 0:128])
                    both = pltpu.roll(both * end_mask[i], base + k, 1)
                    west = jnp.where(lane128 == base + k, both, west)
                    east = jnp.where(lane128 == base + k + 31, both, east)
            ends[0, rows, :] = west
            ends[1, rows, :] = east


    def turned_up(values):
        turned = [pltpu.roll(value, 7, 0) for value in values]
        return [
            jnp.where(sub == 7, turned[(i + 1) % TILES], turned[i]) for i in range(TILES)
        ]

    @pl.loop(0, LEV // 2)
    def _(pair):
        @pl.when(lax.rem(pair, group // 2) == 0)
        def _():
            load(pair // (group // 2)).wait()

        sums = None
        for k in (2 * pair, 2 * pair + 1):
            s = [
                padded(state[0, k, rows, :] - 0.5 * state[1, k, rows, :]) * mask[rows, :] * h[k]
                for rows in tiles
            ]
            v = [padded(state[3, k, rows, :]) * mask[rows, :] for rows in tiles]
            s_north, v_north = turned_up(s), turned_up(v)
            found = []
            for i, rows in enumerate(tiles):
                u = padded(state[2, k, rows, :]) * mask[rows, :]
                found.append(
                    (
                        s[i],
                        (u + east_of(u)) * (s[i] + east_of(s[i])),
                        (v[i] + v_north[i]) * (s[i] + s_north[i]),
                    )
                )
            if sums is None:
                sums = found
            else:
                sums = [[a + b for a, b in zip(x, y)] for x, y in zip(sums, found)]
        for i, rows in enumerate(tiles):
            for part in range(3):
                flat[part, rows, :] += sums[i][part]
        pack_ends(pair)

    first_round = []
    for side, (edge_row, step) in enumerate(((ROWS - 1, NORTH), (0, SOUTH))):
        edge_mask = mask[edge_row : edge_row + 1, :]
        heat = padded(state[0, :, edge_row, :]) * edge_mask
        salt = padded(state[1, :, edge_row, :]) * edge_mask
        send_heat[side] = heat
        send_rows[side, 0:16, :] = heat - 0.5 * salt
        send_rows[side, 16:32, :] = padded(state[3, :, edge_row, :]) * edge_mask
        send_strip[side, 0:32, :] = send_rows[side, :, 0:128]
        send_strip[side, 32:64, :] = send_rows[side, :, 128:256]
        tail = jnp.zeros((8, 128), f32)
        for part in range(4):
            third = send_rows[side, 8 * part : 8 * part + 8, 256:384]
            tail = jnp.where(lane128 // 32 == part, pltpu.roll(third, 32 * part, 1), tail)
        send_strip[side, 64:72, :] = tail
        first_round.append(remote(send_strip.at[side], recv_strip.at[side], side, step))

    pl.semaphore_wait(barrier, partners)
    for copy in first_round:
        copy.start()

    send_cols[0:ROWS, :] = ends[0] + pltpu.roll(ends[1], 1, 1)

    compact = jnp.zeros((8, 128), f32)
    for side in range(2):
        for part in range(4):
            j = 4 * side + part
            rows = pl.ds(8 * part, 8)
            first = pltpu.roll(send_rows[side, rows, 0:128], 16 * j, 1)
            last = pltpu.roll(send_rows[side, rows, 256:384], (16 * j - 24) % 128, 1)
            inside = lane128 // 16 == j
            compact = jnp.where(inside & (lane128 % 16 < 4), first, compact)
            compact = jnp.where(
                inside & (lane128 % 16 >= 4) & (lane128 % 16 < 8), last, compact
            )
    send_cols[2 * ROWS :, :] = compact
    send_corner[8:16, :] = row_pack(send_cols[0:8, :], send_cols[ROWS - 8 : ROWS, :])

    second_round = []
    for side, step in enumerate((EAST, WEST)):
        second_round.append(remote(send_cols, recv_cols.at[side], 2 + side, step))
    for side, step in enumerate((NORTH, SOUTH)):
        second_round.append(
            remote(send_corner.at[pl.ds(8, 8)], recv_side.at[side], 10 + side, step)
        )
    for copy in second_round:
        copy.start()
    first_round = first_round + second_round

    lane_f = iota((ROWS, WIDE), 1)
    row_f = iota((ROWS, WIDE), 0)
    plain = flat[0]
    lon = 0.05 * flat[1] - 0.1 * (east_of(plain) - plain)
    lon = jnp.where(lane_f < COLS - 1, lon, 0.0)
    lat = 0.05 * flat[2] - 0.1 * (pltpu.roll(plain, ROWS - 1, 0) - plain)
    lat = jnp.where(row_f == ROWS - 1, 0.0, lat)
    start = plain - (lon - west_of(lon)) - (lat - pltpu.roll(lat, 1, 0))
    start = jnp.where(lane_f < COLS, start, 0.0)
    basis[1, 0:ROWS, :] = start
    packed_rows = row_pack(start[0:8, :], start[ROWS - 8 : ROWS, :])
    halo_rows[0] = jnp.where(sub < 4, pltpu.roll(start[ROWS - 8 : ROWS, :], 4, 0), damp_high)
    halo_rows[1] = jnp.where(sub < 4, damp_low, pltpu.roll(start[0:8, :], 4, 0))
    halo_cols[...] = column_pack(start[:, 0:128], start[:, 256:384])
    for base, packed in ((8, damp_rows), (24, packed_rows)):
        first = pltpu.roll(packed[:, 0:128], base, 1)
        last = packed[:, 256:384]
        last = pltpu.roll(last, (base - 24) % 128, 1) if base != 24 else last
        compact = jnp.where((lane128 >= base) & (lane128 < base + 4), first, compact)
        compact = jnp.where((lane128 >= base + 4) & (lane128 < base + 8), last, compact)
    send_corner[0:8, :] = compact
    second_round = []
    for place, step in enumerate(DIAGONAL):
        second_round.append(
            remote(
                send_corner,
                recv_corner.at[place],
                4 + place,
                step,
                halo_send_sem,
                halo_recv_sem,
            )
        )
    for side, step in enumerate((NORTH, SOUTH)):
        second_round.append(
            remote(
                halo_rows.at[side], recv_halo_rows.at[side], side, step, halo_send_sem, halo_recv_sem
            )
        )
    for side, step in enumerate((EAST, WEST)):
        second_round.append(
            remote(halo_cols, recv_halo_cols.at[side], 2 + side, step, halo_send_sem, halo_recv_sem)
        )
    for copy in second_round:
        copy.start()
    heat_round = []
    for side, step in enumerate((NORTH, SOUTH)):
        copy = remote(send_heat.at[side], recv_heat.at[side], 8 + side, step)
        copy.start()
        heat_round.append(copy)

    level_inv[...] = jnp.zeros(level_inv.shape, f32)

    @pl.loop(1, LEV)
    def _(k):
        level_inv[pl.ds(k, 1), :] = 1.0 / jnp.full((1, WIDE), h[k - 1] + h[k], f32)


    weight = jnp.zeros((1, 128), f32)
    lane_w = iota((1, 128), 1)
    for k in range(LEV):
        weight = jnp.where((lane_w & 15) == k, h[k], weight)
    weight = weight * jnp.where((lane_w & 16) != 0, -0.5, 1.0)
    level_weight = jnp.zeros((LEV, WIDE), f32)
    level_row = iota((LEV, WIDE), 0)
    for k in range(LEV):
        level_weight = jnp.where(level_row == k, h[k], level_weight)
    exists = (
        jnp.where(gy < ny - 1, 1.0, 0.0).astype(f32),
        jnp.where(gy > 0, 1.0, 0.0).astype(f32),
    )

    weigh[...] = jnp.where(iota((ROWS, WIDE), 1) < COLS, 6.0 + damp_all, 0.0)

    small[3].wait()

    @pl.loop(0, 2)
    def _(part):
        rows = pl.ds(pl.multiple_of(ROWS // 2 * part, 8), ROWS // 2)
        coefficient = padded(mix[rows, :])
        here = mask[rows, :]

        def level(k, ratio_low):
            below = coefficient * level_inv[pl.ds(k, 1), :]
            above = coefficient * level_inv[pl.ds(k + 1, 1), :]
            pivot = inverse(h[k] + above + below * (1.0 - ratio_low))
            ratio_now = above * pivot
            ratio[k, rows, :] = ratio_now
            carried[k, rows, :] = below * pivot
            taken[k, rows, :] = h[k] * pivot * here
            return ratio_now

        lax.fori_loop(0, LEV, level, jnp.zeros((ROWS // 2, WIDE), f32), unroll=4)

    for copy in first_round:
        copy.wait()
    for slot in range(2):
        recv_rows[slot, :, 0:128] = recv_strip[slot, 0:32, :]
        recv_rows[slot, :, 128:256] = recv_strip[slot, 32:64, :]
        for part in range(4):
            tail = recv_strip[slot, 64:72, :]
            tail = pltpu.roll(tail, 128 - 32 * part, 1) if part else tail
            recv_rows[slot, 8 * part : 8 * part + 8, 256:384] = jnp.where(lane128 < 32, tail, 0.0)

    def side_flux(mine, theirs, speeds, sign):
        return speeds * (mine + theirs) - (0.1 * sign) * (theirs - mine)

    side_lat = []
    speed_lat = []
    for side, sign in ((0, 1.0), (1, -1.0)):
        slot = 1 - side
        s_mine = send_rows[side, 0:16, :]
        s_theirs = recv_rows[slot, 0:16, :] * exists[side]
        speeds = 0.05 * (send_rows[side, 16:32, :] + recv_rows[slot, 16:32, :] * exists[side])
        speed_lat.append(speeds)
        flux = side_flux(s_mine, s_theirs, speeds, sign)
        side_lat.append(jnp.sum(flux * level_weight, axis=0, keepdims=True))

    for copy in second_round:
        copy.wait()

    def beside(north, south):
        return jnp.where(iota((8, 128), 0) < 4, north, south)

    own = jnp.concatenate([send_cols[0:ROWS, :], beside(recv_side[1], recv_side[0])], axis=0)
    from_east = jnp.concatenate(
        [recv_cols[1, 0:ROWS, :], beside(recv_corner[3, 8:16, :], recv_corner[1, 8:16, :])], axis=0
    )
    from_west = jnp.concatenate(
        [recv_cols[0, 0:ROWS, :], beside(recv_corner[2, 8:16, :], recv_corner[0, 8:16, :])], axis=0
    )
    lane_c = iota((EXT, 128), 1)
    is_east = (lane_c & 32) != 0
    other = jnp.where(is_east, pltpu.roll(from_east, 32, 1), pltpu.roll(from_west, 96, 1))
    both = own + other
    speed = pltpu.roll(both, 64, 1)
    speed = jnp.where((lane_c & 16) != 0, pltpu.roll(speed, 16, 1), speed)
    slope = jnp.where(is_east, 0.1, -0.1) * (other - own)
    through = 0.05 * speed * both - slope
    flux_lon[...] = through[0:ROWS, :]
    weighed = through * weight
    side_west = jnp.sum(jnp.where(lane_c < 32, weighed, 0.0), axis=1, keepdims=True)
    side_east = jnp.sum(
        jnp.where(is_east & (lane_c < 64), weighed, 0.0), axis=1, keepdims=True
    )

    is_first = (lane128 & 15) < 4
    is_north = lane128 < 64
    mine = jnp.where(is_first, recv_cols[1, 2 * ROWS :, :], recv_cols[0, 2 * ROWS :, :])
    theirs_north = jnp.where(is_first, recv_corner[3, 0:8, :], recv_corner[2, 0:8, :])
    theirs_south = jnp.where(is_first, recv_corner[1, 0:8, :], recv_corner[0, 0:8, :])
    theirs = pltpu.roll(
        jnp.where(is_north, theirs_south * exists[1], theirs_north * exists[0]), 64, 1
    )
    both = mine + theirs
    flux = 0.05 * pltpu.roll(both, 96, 1) * both - jnp.where(is_north, 0.1, -0.1) * (theirs - mine)
    flux = flux * jnp.where(
        (lane128 & 16) == 0, level_weight[0:8, 0:128], level_weight[8:16, 0:128]
    )
    flux = jnp.sum(flux, axis=0, keepdims=True)
    flux = flux + pltpu.roll(flux, 112, 1)
    for side in range(2):
        low = pltpu.roll(flux, 32 - 64 * side if side == 0 else 96, 1)
        high = pltpu.roll(flux, 120 if side == 0 else 56, 1)
        third = jnp.where(
            lane_w < 32, side_lat[side][:, 256:384], jnp.where(lane_w < 64, low, high)
        )
        side_lat[side] = jnp.concatenate([side_lat[side][:, 0:256], third], axis=1)

    def assemble(center, north_south, cols_in, base):
        lane48 = iota((ROWS, 128), 1)
        third = jnp.where(
            lane48 < 32, center[:, 256:384], jnp.where(lane48 < 64, cols_in(1), cols_in(0))
        )
        upper = jnp.concatenate([center[:, 0:256], third], axis=1)
        low = pltpu.roll(corners, 32 - base, 1)
        high = pltpu.roll(corners, 120 - base, 1)
        third = jnp.where(
            lane128 < 32, north_south[:, 256:384], jnp.where(lane128 < 64, low, high)
        )
        lower = jnp.concatenate([north_south[:, 0:256], third], axis=1)
        return jnp.concatenate([upper, lower], axis=0)

    is_low = (lane128 & 7) < 4
    corners = beside(
        jnp.where(is_low, recv_corner[3, 0:8, :], recv_corner[2, 0:8, :]),
        jnp.where(is_low, recv_corner[1, 0:8, :], recv_corner[0, 0:8, :]),
    )
    damp_ext = assemble(
        damp_all,
        jnp.where(sub < 4, recv_halo_rows[1], recv_halo_rows[0]),
        lambda slot: recv_cols[slot, ROWS : 2 * ROWS, :],
        8,
    )
    inv = mask[...] * inverse(6.0 + damp_ext)
    scale[...] = 1.5 * inv
    forcing = assemble(
        basis[1, 0:ROWS, :],
        pltpu.roll(jnp.where(sub < 4, recv_halo_rows[0], recv_halo_rows[1]), 4, 0),
        lambda slot: recv_halo_cols[slot],
        24,
    )
    forcing = jnp.concatenate(
        [
            forcing[:, 0:128] + jnp.where(lane_c == 0, side_west, 0.0),
            forcing[:, 128:256],
            forcing[:, 256:384]
            + jnp.where(
                lane_c == 31,
                -side_east,
                jnp.where(lane_c == 32, side_east, jnp.where(lane_c == 127, -side_west, 0.0)),
            ),
        ],
        axis=1,
    )
    north, south = side_lat
    forcing = jnp.concatenate(
        [
            forcing[0:8, :] + jnp.where(sub == 0, south, 0.0),
            forcing[8:40, :],
            forcing[40:48, :] - jnp.where(sub == 7, north, 0.0),
            forcing[48:56, :]
            + jnp.where(sub == 0, north, jnp.where(sub == 7, -south, 0.0)),
        ],
        axis=0,
    )
    basis[1] = forcing * inv

    def folded(value):
        rows = [value[8 * i : 8 * i + 8, :] for i in range(TILES)]
        value = (rows[0] + rows[1]) + (rows[2] + rows[3]) + (rows[4] + rows[5])
        return value[:, 0:128] + value[:, 128:256] + value[:, 256:384]

    parts = []
    for index in range(4):
        q = basis[index + 1]
        pair = east_of(q) + west_of(q)
        column = q + 0.5 * pair
        around = pair + pltpu.roll(column, EXT - 1, 0) + pltpu.roll(column, 1, 0)
        image = scale[...] * around - 0.5 * q
        after = image if index == 0 else 2.0 * image - basis[index]
        if index < 3:
            basis[index + 2] = after
        weighed = weigh[...] * q[0:ROWS, :]
        parts.append(folded(weighed * q[0:ROWS, :]))
        parts.append(folded(weighed * after[0:ROWS, :]))

    for width in (64, 32, 16):
        half = len(parts) // 2
        parts = [
            jnp.where(
                (lane128 & width) == 0,
                low + pltpu.roll(low, 128 - width, 1),
                high + pltpu.roll(high, width, 1),
            )
            for low, high in zip(parts[:half], parts[half:])
        ]
    first_message[...] = jnp.sum(parts[0], axis=0, keepdims=True)

    def spread(source, target, count, along, mine, base):
        target[mine] = source[...]

        @pl.loop(1, count)
        def _(turn):
            d = count // 2 + jnp.where(turn % 2 == 0, -(turn // 2), turn // 2)
            pltpu.make_async_remote_copy(
                src_ref=source,
                dst_ref=target.at[mine],
                send_sem=sum_send_sem.at[base],
                recv_sem=sum_recv_sem.at[base],
                device_id=device(along(d)),
                device_id_type=MESH,
            ).start()

    def gathered(target, count, base):
        part = target.at[pl.ds(0, count - 1)]
        done = pltpu.make_async_remote_copy(
            src_ref=part,
            dst_ref=part,
            send_sem=sum_send_sem.at[base],
            recv_sem=sum_recv_sem.at[base],
            device_id=device(EAST),
            device_id_type=MESH,
        )
        done.wait_recv()
        done.wait_send()
        return jnp.sum(target[...], axis=0)

    spread(first_message, first_sum, nx, lambda d: (d, 0), gx, 0)

    for copy in heat_round:
        copy.wait()
    for side, sign in ((0, 1.0), (1, -1.0)):
        slot = 1 - side
        target = flux_north if side == 0 else flux_prev
        heat_mine = send_heat[side]
        heat_theirs = recv_heat[slot] * exists[side]
        salt_mine = 2.0 * (heat_mine - send_rows[side, 0:16, :])
        salt_theirs = 2.0 * (heat_theirs - recv_rows[slot, 0:16, :] * exists[side])
        target[0:16, :] = side_flux(heat_mine, heat_theirs, speed_lat[side], sign)
        target[16:32, :] = side_flux(salt_mine, salt_theirs, speed_lat[side], sign)
    edge_lane = (lane128 == 31) | (lane128 == 127)

    def mix_tile(i, _):
        rows = pl.ds(pl.multiple_of(8 * i, 8), 8)
        row = pl.ds(next_row(i), 1)
        here = mask[rows, :]
        beyond = mask[row, :]
        through = flux_lon[rows, :]
        use_north = (sub == 7) & (i == TILES - 1)

        def level(k, carry):
            heat_low, salt_low = carry
            u = padded(state[2, k, rows, :]) * here
            v = padded(state[3, k, rows, :]) * here
            v_row = padded(state[3, k, row, :]) * beyond
            v_north = jnp.where(sub == 7, v_row, pltpu.roll(v, 7, 0))
            u_pair = 0.05 * (u + east_of(u))
            v_pair = 0.05 * (v + v_north)
            lon_far, lon_near = u_pair - 0.1, u_pair + 0.1
            lat_far, lat_near = v_pair - 0.1, v_pair + 0.1
            found = []
            for tracer, low in ((0, heat_low), (1, salt_low)):
                plane = tracer * LEV + k
                c = padded(state[tracer, k, rows, :]) * here
                c_row = padded(state[tracer, k, row, :]) * beyond
                c_north = jnp.where(sub == 7, c_row, pltpu.roll(c, 7, 0))
                lon = lon_far * east_of(c) + lon_near * c
                turned = pltpu.roll(through, 127 - plane, 1)
                lon = jnp.concatenate(
                    [lon[:, 0:256], jnp.where(edge_lane, turned, lon[:, 256:384])], axis=1
                )
                lat = lat_far * c_north + lat_near * c
                lat = jnp.where(use_north, flux_north[pl.ds(plane, 1), :], lat)
                lat_south = jnp.where(
                    sub == 0, flux_prev[pl.ds(plane, 1), :], pltpu.roll(lat, 1, 0)
                )
                flux_prev[pl.ds(plane, 1), :] = lat[7:8, :]
                advected = c - (lon - west_of(lon)) - (lat - lat_south)
                value = taken[k, rows, :] * advected + carried[k, rows, :] * low
                tracer_out[tracer, k, rows, :] = value[:, 0:COLS]
                found.append(value)
            return found[0], found[1]

        zero = jnp.zeros((8, WIDE), f32)
        heat, salt = lax.fori_loop(0, LEV, level, (zero, zero), unroll=4)

        def back(step, carry):
            k = LEV - 2 - step
            heat_up, salt_up = carry
            share = ratio[k, rows, 0:COLS]
            heat_up = tracer_out[0, k, rows, :] + share * heat_up
            salt_up = tracer_out[1, k, rows, :] + share * salt_up
            tracer_out[0, k, rows, :] = heat_up
            tracer_out[1, k, rows, :] = salt_up
            return heat_up, salt_up

        lax.fori_loop(0, LEV - 1, back, (heat[:, 0:COLS], salt[:, 0:COLS]), unroll=5)
        return 0

    lax.fori_loop(0, 2, mix_tile, 0)
    second_message[...] = gathered(first_sum, nx, 0)
    spread(second_message, second_sum, ny, lambda d: (0, d), gy, 1)
    lax.fori_loop(2, TILES, mix_tile, 0)
    sums = gathered(second_sum, ny, 1)

    own_lanes = lane128 // 16 == iota((8, 128), 0)
    sums = jnp.where(own_lanes, jnp.broadcast_to(sums, (8, 128)), 0.0)
    sums = jnp.broadcast_to(jnp.sum(sums, axis=1, keepdims=True), (8, 128))
    dots = [sums[i : i + 1, :] for i in range(8)]
    moment = dots[0:2] + [2.0 * dots[i] - dots[i % 2] for i in range(2, 8)]

    def gram(i, j):
        return 0.5 * (moment[i + j] + moment[abs(i - j)])

    lower = {}
    pivots = []
    right = []
    for i in range(4):
        value = moment[i]
        for j in range(i + 1):
            entry = gram(i, j) - 0.5 * (gram(j, i + 1) + gram(j, abs(i - 1)))
            for k in range(j):
                entry = entry - lower[i, k] * lower[j, k] * pivots[k]
            if j < i:
                lower[i, j] = entry / pivots[j]
                value = value - lower[i, j] * right[j]
            else:
                pivots.append(entry)
        right.append(value)
    solved = [None] * 4
    for i in range(3, -1, -1):
        value = right[i] / pivots[i]
        for j in range(i + 1, 4):
            value = value - lower[j, i] * solved[j]
        solved[i] = value
    surface = None
    for i in range(4):
        factor = 1.5 * solved[i]
        factor = jnp.concatenate([factor, factor, factor], axis=1)
        term = factor * basis[i + 1, 0:ROWS, :]
        surface = term if surface is None else surface + term
    surface_out[...] = surface[:, 0:COLS]


def store(tracer, surface, tracer_out, surface_out, sems):
    copies = [pltpu.make_async_copy(surface, surface_out, sems.at[8])]
    for index in range(8):
        levels = pl.ds(4 * (index % 4), 4)
        copies.append(
            pltpu.make_async_copy(
                tracer.at[index // 4, levels], tracer_out.at[index // 4, levels], sems.at[index]
            )
        )
    for copy in copies:
        copy.start()
    for copy in copies:
        copy.wait()


def scratch(nx, ny):
    vmem = lambda *shape: pltpu.VMEM(shape, f32)
    dma = pltpu.SemaphoreType.DMA
    return [
        vmem(4, LEV, ROWS, COLS),
        pltpu.SMEM((LEV,), f32),
        vmem(ROWS, COLS),
        vmem(ROWS, COLS),
        None,
        vmem(EXT, WIDE),
        vmem(24, WIDE),
        vmem(3, ROWS, WIDE),
        vmem(2, ROWS, 128),
        vmem(2, 32, WIDE),
        vmem(2, 72, 128),
        vmem(2, LEV, WIDE),
        vmem(2, 72, 128),
        vmem(2, 32, WIDE),
        vmem(2, LEV, WIDE),
        vmem(2 * ROWS + 8, 128),
        vmem(2, 2 * ROWS + 8, 128),
        vmem(16, 128),
        vmem(4, 16, 128),
        vmem(2, 8, 128),
        vmem(ROWS, 128),
        vmem(2 * LEV, WIDE),
        vmem(2 * LEV, WIDE),
        vmem(LEV, ROWS, WIDE),
        vmem(LEV, ROWS, WIDE),
        vmem(LEV, ROWS, WIDE),
        vmem(EXT, WIDE),
        vmem(ROWS, WIDE),
        vmem(6, EXT, WIDE),
        vmem(2, 8, WIDE),
        vmem(ROWS, 128),
        vmem(2, 8, WIDE),
        vmem(2, ROWS, 128),
        vmem(1, 128),
        vmem(nx, 1, 128),
        vmem(1, 128),
        vmem(ny, 1, 128),
        dma((4,)),
        dma((4,)),
        dma((12,)),
        dma((12,)),
        dma((8,)),
        dma((8,)),
        dma((2,)),
        dma((2,)),
    ]


def solution(mesh):
    nx, ny = mesh.shape["gx"], mesh.shape["gy"]

    def body(ocean_state, layer_thickness, vertical_mixing, damping, ocean_blocks):
        shapes = scratch(nx, ny)
        shapes[4] = pltpu.VMEM(ocean_blocks.shape, jnp.int32)
        call = pl.pallas_call(
            functools.partial(kernel, nx, ny),
            out_shape=[
                pltpu.VMEM((2, LEV, ROWS, COLS), f32),
                pltpu.VMEM((ROWS, COLS), f32),
            ],
            in_specs=[pl.BlockSpec(memory_space=pltpu.HBM)] * 5,
            out_specs=[pl.BlockSpec(memory_space=pltpu.VMEM)] * 2,
            scratch_shapes=shapes,
            compiler_params=pltpu.CompilerParams(
                collective_id=0, has_side_effects=True, vmem_limit_bytes=32 * 1024 * 1024
            ),
        )
        operands = [
            pltpu.with_memory_space_constraint(operand, pltpu.HBM)
            for operand in (ocean_state, layer_thickness, vertical_mixing, damping, ocean_blocks)
        ]
        tracer, surface = call(*operands)
        return tuple(
            pl.pallas_call(
                store,
                out_shape=[
                    jax.ShapeDtypeStruct((2, LEV, ROWS, COLS), f32),
                    jax.ShapeDtypeStruct((ROWS, COLS), f32),
                ],
                in_specs=[pl.BlockSpec(memory_space=pltpu.VMEM)] * 2,
                out_specs=[pl.BlockSpec(memory_space=pltpu.HBM)] * 2,
                scratch_shapes=[pltpu.SemaphoreType.DMA((9,))],
                compiler_params=pltpu.CompilerParams(vmem_limit_bytes=16 * 1024 * 1024),
            )(tracer, surface)
        )

    def wrapped(*args):
        with jax.sharding.use_abstract_mesh(mesh.abstract_mesh):
            return jax.shard_map(
                body,
                mesh=mesh,
                in_specs=(P(None, None, "gy", "gx"), P(), P("gy", "gx"), P("gy", "gx"), P()),
                out_specs=(P(None, None, "gy", "gx"), P("gy", "gx")),
                check_vma=False,
            )(*args)

    return wrapped
```

```python
import functools

import jax
import jax.numpy as jnp
from jax import lax
from jax.experimental import pallas as pl
from jax.experimental.pallas import tpu as pltpu
from jax.sharding import PartitionSpec as P

BLAT = 24
BLON = 36
LEV = 16
ROWS = 48
COLS = 288
WIDE = 384
EXT = 56
TILES = ROWS // 8

f32 = jnp.float32
MESH = pl.DeviceIdType.MESH

NORTH, SOUTH, EAST, WEST = (0, 1), (0, -1), (1, 0), (-1, 0)
DIAGONAL = ((1, 1), (-1, 1), (1, -1), (-1, -1))


def iota(shape, dim):
    return lax.broadcasted_iota(jnp.int32, shape, dim)


def padded(value):
    return jnp.concatenate([value, jnp.zeros((value.shape[0], WIDE - COLS), f32)], axis=1)


def east_of(value):
    return pltpu.roll(value, WIDE - 1, 1)


def west_of(value):
    return pltpu.roll(value, 1, 1)


def inverse(value):
    guess = pl.reciprocal(value, approx=True)
    return guess * (2.0 - value * guess)


def row_pack(low, high):
    return jnp.where(iota(low.shape, 0) < 4, low, high)


def column_pack(first, last):
    lane = iota(first.shape, 1)
    low = pltpu.roll(first, 32, 1)
    high = pltpu.roll(last, 96, 1)
    return jnp.where(
        (lane >= 32) & (lane < 36), low, jnp.where(lane >= 124, high, 0.0)
    )


def kernel(
    nx,
    ny,
    ocean,
    thick,
    mixing,
    damping,
    blocks,
    tracer_out,
    surface_out,
    state,
    h,
    mix,
    damp,
    blk,
    mask,
    level_inv,
    flat,
    ends,
    send_rows,
    send_strip,
    send_heat,
    recv_strip,
    recv_rows,
    recv_heat,
    send_cols,
    recv_cols,
    send_corner,
    recv_corner,
    recv_side,
    flux_lon,
    flux_north,
    flux_prev,
    ratio,
    carried,
    taken,
    scale,
    weigh,
    basis,
    halo_rows,
    halo_cols,
    recv_halo_rows,
    recv_halo_cols,
    first_message,
    first_sum,
    second_message,
    second_sum,
    load_sem,
    small_sem,
    send_sem,
    recv_sem,
    halo_send_sem,
    halo_recv_sem,
    sum_send_sem,
    sum_recv_sem,
):
    gx = lax.axis_index("gx")
    gy = lax.axis_index("gy")

    def device(step):
        return {"gx": lax.rem(gx + step[0] + nx, nx), "gy": lax.rem(gy + step[1] + ny, ny)}

    def greet(step):
        pl.semaphore_signal(barrier, inc=1, device_id=device(step), device_id_type=MESH)

    small = [
        pltpu.make_async_copy(blocks, blk, small_sem.at[0]),
        pltpu.make_async_copy(thick, h, small_sem.at[1]),
        pltpu.make_async_copy(damping, damp, small_sem.at[2]),
        pltpu.make_async_copy(mixing, mix, small_sem.at[3]),
    ]
    group = LEV // 4

    def load(index):
        levels = pl.ds(group * index, group)
        rows = pl.ds(8, ROWS - 16)
        return pltpu.make_async_copy(
            ocean.at[:, levels, rows, :], state.at[:, levels, rows, :], load_sem.at[index]
        )

    edge_loads = [
        pltpu.make_async_copy(
            ocean.at[:, :, rows, :], state.at[:, :, rows, :], load_sem.at[4 + index]
        )
        for index, rows in enumerate((pl.ds(0, 8), pl.ds(ROWS - 8, 8)))
    ]
    for copy in small[:3] + edge_loads + [load(index) for index in range(4)] + small[3:]:
        copy.start()

    barrier = pltpu.get_barrier_semaphore()
    for step in DIAGONAL:
        greet(step)
    pl.loop(1, nx)(lambda d: greet((d, 0)))
    pl.loop(1, ny)(lambda d: greet((0, d)))
    partners = len(DIAGONAL) + nx - 1 + ny - 1

    block_rows, block_cols = blk.shape
    small[0].wait()
    row = iota((EXT, block_rows), 0)
    row = gy * ROWS + jnp.where(row < ROWS + 4, row, row - EXT)
    edge = iota((EXT, block_rows), 1) * BLAT
    pick_rows = jnp.where((row >= edge) & (row < edge + BLAT), 1.0, 0.0)
    lane = iota((block_cols, WIDE), 1)
    total = block_cols * BLON
    col = gx * COLS + jnp.where(lane < COLS + 4, lane, lane - WIDE)
    col = jnp.where(col < 0, col + total, jnp.where(col >= total, col - total, col))
    edge = iota((block_cols, WIDE), 0) * BLON
    inside = (lane < COLS + 4) | (lane >= WIDE - 4)
    pick_cols = jnp.where(inside & (col >= edge) & (col < edge + BLON), 1.0, 0.0)
    coarse = jnp.dot(pick_rows, blk[...].astype(f32), preferred_element_type=f32)
    mask[...] = jnp.dot(coarse, pick_cols, preferred_element_type=f32)

    small[1].wait()
    small[2].wait()
    damp_low = padded(damp[0:8, :])
    damp_high = padded(damp[ROWS - 8 : ROWS, :])
    damp_rows = row_pack(damp_low, damp_high)
    damp_all = padded(damp[...])
    send_cols[ROWS : 2 * ROWS, :] = column_pack(damp_all[:, 0:128], damp_all[:, 256:384])

    def remote(source, target, index, step, sends=send_sem, recvs=recv_sem):
        return pltpu.make_async_remote_copy(
            src_ref=source,
            dst_ref=target,
            send_sem=sends.at[index],
            recv_sem=recvs.at[index],
            device_id=device(step),
            device_id_type=MESH,
        )

    sub = iota((8, WIDE), 0)
    lane128 = iota((8, 128), 1)

    def next_row(i):
        return jnp.minimum(8 * i + 8, ROWS - 1)

    tiles = [pl.ds(8 * i, 8) for i in range(TILES)]
    flat[...] = jnp.zeros(flat.shape, f32)
    ends[...] = jnp.zeros(ends.shape, f32)
    end_mask = [
        jnp.where(lane128 == 31, mask[rows, 256:384], mask[rows, 0:128]) for rows in tiles
    ]

    def pack_ends(pair):
        for i, rows in enumerate(tiles):
            west, east = ends[0, rows, :], ends[1, rows, :]
            for k in (2 * pair, 2 * pair + 1):
                for field, base in ((0, 0), (1, 16), (2, 64)):
                    last = jnp.concatenate(
                        [state[field, k, rows, 256:COLS], jnp.zeros((8, WIDE - COLS), f32)], axis=1
                    )
                    both = jnp.where(lane128 == 31, last, state[field, k, rows, 0:128])
                    both = pltpu.roll(both * end_mask[i], base + k, 1)
                    west = jnp.where(lane128 == base + k, both, west)
                    east = jnp.where(lane128 == base + k + 31, both, east)
            ends[0, rows, :] = west
            ends[1, rows, :] = east


    def turned_up(values):
        turned = [pltpu.roll(value, 7, 0) for value in values]
        return [
            jnp.where(sub == 7, turned[(i + 1) % TILES], turned[i]) for i in range(TILES)
        ]

    def strips():
        return [
            remote(send_strip.at[side], recv_strip.at[side], side, step)
            for side, step in enumerate((NORTH, SOUTH))
        ]

    def send_edge_rows():
        for side, (edge_row, step) in enumerate(((ROWS - 1, NORTH), (0, SOUTH))):
            edge_mask = mask[edge_row : edge_row + 1, :]
            heat = padded(state[0, :, edge_row, :]) * edge_mask
            salt = padded(state[1, :, edge_row, :]) * edge_mask
            send_heat[side] = heat
            send_rows[side, 0:16, :] = heat - 0.5 * salt
            send_rows[side, 16:32, :] = padded(state[3, :, edge_row, :]) * edge_mask
            send_strip[side, 0:32, :] = send_rows[side, :, 0:128]
            send_strip[side, 32:64, :] = send_rows[side, :, 128:256]
            tail = jnp.zeros((8, 128), f32)
            for part in range(4):
                third = send_rows[side, 8 * part : 8 * part + 8, 256:384]
                tail = jnp.where(lane128 // 32 == part, pltpu.roll(third, 32 * part, 1), tail)
            send_strip[side, 64:72, :] = tail
        pl.semaphore_wait(barrier, partners)
        for copy in strips():
            copy.start()

    for copy in edge_loads:
        copy.wait()

    @pl.loop(0, LEV // 2)
    def _(pair):
        @pl.when(pair == LEV // 4)
        def _():
            send_edge_rows()

        @pl.when(lax.rem(pair, group // 2) == 0)
        def _():
            load(pair // (group // 2)).wait()

        sums = None
        for k in (2 * pair, 2 * pair + 1):
            s = [
                padded(state[0, k, rows, :] - 0.5 * state[1, k, rows, :]) * mask[rows, :] * h[k]
                for rows in tiles
            ]
            v = [padded(state[3, k, rows, :]) * mask[rows, :] for rows in tiles]
            s_north, v_north = turned_up(s), turned_up(v)
            found = []
            for i, rows in enumerate(tiles):
                u = padded(state[2, k, rows, :]) * mask[rows, :]
                found.append(
                    (
                        s[i],
                        (u + east_of(u)) * (s[i] + east_of(s[i])),
                        (v[i] + v_north[i]) * (s[i] + s_north[i]),
                    )
                )
            if sums is None:
                sums = found
            else:
                sums = [[a + b for a, b in zip(x, y)] for x, y in zip(sums, found)]
        for i, rows in enumerate(tiles):
            for part in range(3):
                flat[part, rows, :] += sums[i][part]
        pack_ends(pair)

    send_cols[0:ROWS, :] = ends[0] + pltpu.roll(ends[1], 1, 1)

    compact = jnp.zeros((8, 128), f32)
    for side in range(2):
        for part in range(4):
            j = 4 * side + part
            rows = pl.ds(8 * part, 8)
            first = pltpu.roll(send_rows[side, rows, 0:128], 16 * j, 1)
            last = pltpu.roll(send_rows[side, rows, 256:384], (16 * j - 24) % 128, 1)
            inside = lane128 // 16 == j
            compact = jnp.where(inside & (lane128 % 16 < 4), first, compact)
            compact = jnp.where(
                inside & (lane128 % 16 >= 4) & (lane128 % 16 < 8), last, compact
            )
    send_cols[2 * ROWS :, :] = compact
    send_corner[8:16, :] = row_pack(send_cols[0:8, :], send_cols[ROWS - 8 : ROWS, :])

    second_round = []
    for side, step in enumerate((EAST, WEST)):
        second_round.append(remote(send_cols, recv_cols.at[side], 2 + side, step))
    for side, step in enumerate((NORTH, SOUTH)):
        second_round.append(
            remote(send_corner.at[pl.ds(8, 8)], recv_side.at[side], 10 + side, step)
        )
    for copy in second_round:
        copy.start()
    first_round = strips() + second_round

    lane_f = iota((ROWS, WIDE), 1)
    row_f = iota((ROWS, WIDE), 0)
    plain = flat[0]
    lon = 0.05 * flat[1] - 0.1 * (east_of(plain) - plain)
    lon = jnp.where(lane_f < COLS - 1, lon, 0.0)
    lat = 0.05 * flat[2] - 0.1 * (pltpu.roll(plain, ROWS - 1, 0) - plain)
    lat = jnp.where(row_f == ROWS - 1, 0.0, lat)
    start = plain - (lon - west_of(lon)) - (lat - pltpu.roll(lat, 1, 0))
    start = jnp.where(lane_f < COLS, start, 0.0)
    basis[1, 0:ROWS, :] = start
    packed_rows = row_pack(start[0:8, :], start[ROWS - 8 : ROWS, :])
    halo_rows[0] = jnp.where(sub < 4, pltpu.roll(start[ROWS - 8 : ROWS, :], 4, 0), damp_high)
    halo_rows[1] = jnp.where(sub < 4, damp_low, pltpu.roll(start[0:8, :], 4, 0))
    halo_cols[...] = column_pack(start[:, 0:128], start[:, 256:384])
    for base, packed in ((8, damp_rows), (24, packed_rows)):
        first = pltpu.roll(packed[:, 0:128], base, 1)
        last = packed[:, 256:384]
        last = pltpu.roll(last, (base - 24) % 128, 1) if base != 24 else last
        compact = jnp.where((lane128 >= base) & (lane128 < base + 4), first, compact)
        compact = jnp.where((lane128 >= base + 4) & (lane128 < base + 8), last, compact)
    send_corner[0:8, :] = compact
    second_round = []
    for place, step in enumerate(DIAGONAL):
        second_round.append(
            remote(
                send_corner,
                recv_corner.at[place],
                4 + place,
                step,
                halo_send_sem,
                halo_recv_sem,
            )
        )
    for side, step in enumerate((NORTH, SOUTH)):
        second_round.append(
            remote(
                halo_rows.at[side], recv_halo_rows.at[side], side, step, halo_send_sem, halo_recv_sem
            )
        )
    for side, step in enumerate((EAST, WEST)):
        second_round.append(
            remote(halo_cols, recv_halo_cols.at[side], 2 + side, step, halo_send_sem, halo_recv_sem)
        )
    for copy in second_round:
        copy.start()
    heat_round = []
    for side, step in enumerate((NORTH, SOUTH)):
        copy = remote(send_heat.at[side], recv_heat.at[side], 8 + side, step)
        copy.start()
        heat_round.append(copy)

    level_inv[...] = jnp.zeros(level_inv.shape, f32)

    @pl.loop(1, LEV)
    def _(k):
        level_inv[pl.ds(k, 1), :] = 1.0 / jnp.full((1, WIDE), h[k - 1] + h[k], f32)


    weight = jnp.zeros((1, 128), f32)
    lane_w = iota((1, 128), 1)
    for k in range(LEV):
        weight = jnp.where((lane_w & 15) == k, h[k], weight)
    weight = weight * jnp.where((lane_w & 16) != 0, -0.5, 1.0)
    level_weight = jnp.zeros((LEV, WIDE), f32)
    level_row = iota((LEV, WIDE), 0)
    for k in range(LEV):
        level_weight = jnp.where(level_row == k, h[k], level_weight)
    exists = (
        jnp.where(gy < ny - 1, 1.0, 0.0).astype(f32),
        jnp.where(gy > 0, 1.0, 0.0).astype(f32),
    )

    weigh[...] = jnp.where(iota((ROWS, WIDE), 1) < COLS, 6.0 + damp_all, 0.0)

    small[3].wait()

    @pl.loop(0, 2)
    def _(part):
        rows = pl.ds(pl.multiple_of(ROWS // 2 * part, 8), ROWS // 2)
        coefficient = padded(mix[rows, :])
        here = mask[rows, :]

        def level(k, ratio_low):
            below = coefficient * level_inv[pl.ds(k, 1), :]
            above = coefficient * level_inv[pl.ds(k + 1, 1), :]
            pivot = inverse(h[k] + above + below * (1.0 - ratio_low))
            ratio_now = above * pivot
            ratio[k, rows, :] = ratio_now
            carried[k, rows, :] = below * pivot
            taken[k, rows, :] = h[k] * pivot * here
            return ratio_now

        lax.fori_loop(0, LEV, level, jnp.zeros((ROWS // 2, WIDE), f32), unroll=4)

    for copy in first_round:
        copy.wait()
    for slot in range(2):
        recv_rows[slot, :, 0:128] = recv_strip[slot, 0:32, :]
        recv_rows[slot, :, 128:256] = recv_strip[slot, 32:64, :]
        for part in range(4):
            tail = recv_strip[slot, 64:72, :]
            tail = pltpu.roll(tail, 128 - 32 * part, 1) if part else tail
            recv_rows[slot, 8 * part : 8 * part + 8, 256:384] = jnp.where(lane128 < 32, tail, 0.0)

    def side_flux(mine, theirs, speeds, sign):
        return speeds * (mine + theirs) - (0.1 * sign) * (theirs - mine)

    side_lat = []
    speed_lat = []
    for side, sign in ((0, 1.0), (1, -1.0)):
        slot = 1 - side
        s_mine = send_rows[side, 0:16, :]
        s_theirs = recv_rows[slot, 0:16, :] * exists[side]
        speeds = 0.05 * (send_rows[side, 16:32, :] + recv_rows[slot, 16:32, :] * exists[side])
        speed_lat.append(speeds)
        flux = side_flux(s_mine, s_theirs, speeds, sign)
        side_lat.append(jnp.sum(flux * level_weight, axis=0, keepdims=True))

    for copy in second_round:
        copy.wait()

    def beside(north, south):
        return jnp.where(iota((8, 128), 0) < 4, north, south)

    own = jnp.concatenate([send_cols[0:ROWS, :], beside(recv_side[1], recv_side[0])], axis=0)
    from_east = jnp.concatenate(
        [recv_cols[1, 0:ROWS, :], beside(recv_corner[3, 8:16, :], recv_corner[1, 8:16, :])], axis=0
    )
    from_west = jnp.concatenate(
        [recv_cols[0, 0:ROWS, :], beside(recv_corner[2, 8:16, :], recv_corner[0, 8:16, :])], axis=0
    )
    lane_c = iota((EXT, 128), 1)
    is_east = (lane_c & 32) != 0
    other = jnp.where(is_east, pltpu.roll(from_east, 32, 1), pltpu.roll(from_west, 96, 1))
    both = own + other
    speed = pltpu.roll(both, 64, 1)
    speed = jnp.where((lane_c & 16) != 0, pltpu.roll(speed, 16, 1), speed)
    slope = jnp.where(is_east, 0.1, -0.1) * (other - own)
    through = 0.05 * speed * both - slope
    flux_lon[...] = through[0:ROWS, :]
    weighed = through * weight
    side_west = jnp.sum(jnp.where(lane_c < 32, weighed, 0.0), axis=1, keepdims=True)
    side_east = jnp.sum(
        jnp.where(is_east & (lane_c < 64), weighed, 0.0), axis=1, keepdims=True
    )

    is_first = (lane128 & 15) < 4
    is_north = lane128 < 64
    mine = jnp.where(is_first, recv_cols[1, 2 * ROWS :, :], recv_cols[0, 2 * ROWS :, :])
    theirs_north = jnp.where(is_first, recv_corner[3, 0:8, :], recv_corner[2, 0:8, :])
    theirs_south = jnp.where(is_first, recv_corner[1, 0:8, :], recv_corner[0, 0:8, :])
    theirs = pltpu.roll(
        jnp.where(is_north, theirs_south * exists[1], theirs_north * exists[0]), 64, 1
    )
    both = mine + theirs
    flux = 0.05 * pltpu.roll(both, 96, 1) * both - jnp.where(is_north, 0.1, -0.1) * (theirs - mine)
    flux = flux * jnp.where(
        (lane128 & 16) == 0, level_weight[0:8, 0:128], level_weight[8:16, 0:128]
    )
    flux = jnp.sum(flux, axis=0, keepdims=True)
    flux = flux + pltpu.roll(flux, 112, 1)
    for side in range(2):
        low = pltpu.roll(flux, 32 - 64 * side if side == 0 else 96, 1)
        high = pltpu.roll(flux, 120 if side == 0 else 56, 1)
        third = jnp.where(
            lane_w < 32, side_lat[side][:, 256:384], jnp.where(lane_w < 64, low, high)
        )
        side_lat[side] = jnp.concatenate([side_lat[side][:, 0:256], third], axis=1)

    def assemble(center, north_south, cols_in, base):
        lane48 = iota((ROWS, 128), 1)
        third = jnp.where(
            lane48 < 32, center[:, 256:384], jnp.where(lane48 < 64, cols_in(1), cols_in(0))
        )
        upper = jnp.concatenate([center[:, 0:256], third], axis=1)
        low = pltpu.roll(corners, 32 - base, 1)
        high = pltpu.roll(corners, 120 - base, 1)
        third = jnp.where(
            lane128 < 32, north_south[:, 256:384], jnp.where(lane128 < 64, low, high)
        )
        lower = jnp.concatenate([north_south[:, 0:256], third], axis=1)
        return jnp.concatenate([upper, lower], axis=0)

    is_low = (lane128 & 7) < 4
    corners = beside(
        jnp.where(is_low, recv_corner[3, 0:8, :], recv_corner[2, 0:8, :]),
        jnp.where(is_low, recv_corner[1, 0:8, :], recv_corner[0, 0:8, :]),
    )
    damp_ext = assemble(
        damp_all,
        jnp.where(sub < 4, recv_halo_rows[1], recv_halo_rows[0]),
        lambda slot: recv_cols[slot, ROWS : 2 * ROWS, :],
        8,
    )
    inv = mask[...] * inverse(6.0 + damp_ext)
    scale[...] = 1.5 * inv
    forcing = assemble(
        basis[1, 0:ROWS, :],
        pltpu.roll(jnp.where(sub < 4, recv_halo_rows[0], recv_halo_rows[1]), 4, 0),
        lambda slot: recv_halo_cols[slot],
        24,
    )
    forcing = jnp.concatenate(
        [
            forcing[:, 0:128] + jnp.where(lane_c == 0, side_west, 0.0),
            forcing[:, 128:256],
            forcing[:, 256:384]
            + jnp.where(
                lane_c == 31,
                -side_east,
                jnp.where(lane_c == 32, side_east, jnp.where(lane_c == 127, -side_west, 0.0)),
            ),
        ],
        axis=1,
    )
    north, south = side_lat
    forcing = jnp.concatenate(
        [
            forcing[0:8, :] + jnp.where(sub == 0, south, 0.0),
            forcing[8:40, :],
            forcing[40:48, :] - jnp.where(sub == 7, north, 0.0),
            forcing[48:56, :]
            + jnp.where(sub == 0, north, jnp.where(sub == 7, -south, 0.0)),
        ],
        axis=0,
    )
    basis[1] = forcing * inv

    def folded(value):
        rows = [value[8 * i : 8 * i + 8, :] for i in range(TILES)]
        value = (rows[0] + rows[1]) + (rows[2] + rows[3]) + (rows[4] + rows[5])
        return value[:, 0:128] + value[:, 128:256] + value[:, 256:384]

    parts = []
    for index in range(4):
        q = basis[index + 1]
        pair = east_of(q) + west_of(q)
        column = q + 0.5 * pair
        around = pair + pltpu.roll(column, EXT - 1, 0) + pltpu.roll(column, 1, 0)
        image = scale[...] * around - 0.5 * q
        after = image if index == 0 else 2.0 * image - basis[index]
        if index < 3:
            basis[index + 2] = after
        weighed = weigh[...] * q[0:ROWS, :]
        parts.append(folded(weighed * q[0:ROWS, :]))
        parts.append(folded(weighed * after[0:ROWS, :]))

    for width in (64, 32, 16):
        half = len(parts) // 2
        parts = [
            jnp.where(
                (lane128 & width) == 0,
                low + pltpu.roll(low, 128 - width, 1),
                high + pltpu.roll(high, width, 1),
            )
            for low, high in zip(parts[:half], parts[half:])
        ]
    first_message[...] = jnp.sum(parts[0], axis=0, keepdims=True)

    def spread(source, target, count, along, mine, base):
        target[mine] = source[...]

        @pl.loop(1, count)
        def _(turn):
            d = count // 2 + jnp.where(turn % 2 == 0, -(turn // 2), turn // 2)
            pltpu.make_async_remote_copy(
                src_ref=source,
                dst_ref=target.at[mine],
                send_sem=sum_send_sem.at[base],
                recv_sem=sum_recv_sem.at[base],
                device_id=device(along(d)),
                device_id_type=MESH,
            ).start()

    def gathered(target, count, base):
        part = target.at[pl.ds(0, count - 1)]
        done = pltpu.make_async_remote_copy(
            src_ref=part,
            dst_ref=part,
            send_sem=sum_send_sem.at[base],
            recv_sem=sum_recv_sem.at[base],
            device_id=device(EAST),
            device_id_type=MESH,
        )
        done.wait_recv()
        done.wait_send()
        return jnp.sum(target[...], axis=0)

    spread(first_message, first_sum, nx, lambda d: (d, 0), gx, 0)

    for copy in heat_round:
        copy.wait()
    for side, sign in ((0, 1.0), (1, -1.0)):
        slot = 1 - side
        target = flux_north if side == 0 else flux_prev
        heat_mine = send_heat[side]
        heat_theirs = recv_heat[slot] * exists[side]
        salt_mine = 2.0 * (heat_mine - send_rows[side, 0:16, :])
        salt_theirs = 2.0 * (heat_theirs - recv_rows[slot, 0:16, :] * exists[side])
        target[0:16, :] = side_flux(heat_mine, heat_theirs, speed_lat[side], sign)
        target[16:32, :] = side_flux(salt_mine, salt_theirs, speed_lat[side], sign)
    edge_lane = (lane128 == 31) | (lane128 == 127)

    def mix_tile(i, _):
        rows = pl.ds(pl.multiple_of(8 * i, 8), 8)
        row = pl.ds(next_row(i), 1)
        here = mask[rows, :]
        beyond = mask[row, :]
        through = flux_lon[rows, :]
        use_north = (sub == 7) & (i == TILES - 1)

        def level(k, carry):
            heat_low, salt_low = carry
            u = padded(state[2, k, rows, :]) * here
            v = padded(state[3, k, rows, :]) * here
            v_row = padded(state[3, k, row, :]) * beyond
            v_north = jnp.where(sub == 7, v_row, pltpu.roll(v, 7, 0))
            u_pair = 0.05 * (u + east_of(u))
            v_pair = 0.05 * (v + v_north)
            lon_far, lon_near = u_pair - 0.1, u_pair + 0.1
            lat_far, lat_near = v_pair - 0.1, v_pair + 0.1
            found = []
            for tracer, low in ((0, heat_low), (1, salt_low)):
                plane = tracer * LEV + k
                c = padded(state[tracer, k, rows, :]) * here
                c_row = padded(state[tracer, k, row, :]) * beyond
                c_north = jnp.where(sub == 7, c_row, pltpu.roll(c, 7, 0))
                lon = lon_far * east_of(c) + lon_near * c
                turned = pltpu.roll(through, 127 - plane, 1)
                lon = jnp.concatenate(
                    [lon[:, 0:256], jnp.where(edge_lane, turned, lon[:, 256:384])], axis=1
                )
                lat = lat_far * c_north + lat_near * c
                lat = jnp.where(use_north, flux_north[pl.ds(plane, 1), :], lat)
                lat_south = jnp.where(
                    sub == 0, flux_prev[pl.ds(plane, 1), :], pltpu.roll(lat, 1, 0)
                )
                flux_prev[pl.ds(plane, 1), :] = lat[7:8, :]
                advected = c - (lon - west_of(lon)) - (lat - lat_south)
                value = taken[k, rows, :] * advected + carried[k, rows, :] * low
                tracer_out[tracer, k, rows, :] = value[:, 0:COLS]
                found.append(value)
            return found[0], found[1]

        zero = jnp.zeros((8, WIDE), f32)
        heat, salt = lax.fori_loop(0, LEV, level, (zero, zero), unroll=4)

        def back(step, carry):
            k = LEV - 2 - step
            heat_up, salt_up = carry
            share = ratio[k, rows, 0:COLS]
            heat_up = tracer_out[0, k, rows, :] + share * heat_up
            salt_up = tracer_out[1, k, rows, :] + share * salt_up
            tracer_out[0, k, rows, :] = heat_up
            tracer_out[1, k, rows, :] = salt_up
            return heat_up, salt_up

        lax.fori_loop(0, LEV - 1, back, (heat[:, 0:COLS], salt[:, 0:COLS]), unroll=5)
        return 0

    lax.fori_loop(0, 2, mix_tile, 0)
    second_message[...] = gathered(first_sum, nx, 0)
    spread(second_message, second_sum, ny, lambda d: (0, d), gy, 1)
    lax.fori_loop(2, TILES, mix_tile, 0)
    sums = gathered(second_sum, ny, 1)

    own_lanes = lane128 // 16 == iota((8, 128), 0)
    sums = jnp.where(own_lanes, jnp.broadcast_to(sums, (8, 128)), 0.0)
    sums = jnp.broadcast_to(jnp.sum(sums, axis=1, keepdims=True), (8, 128))
    dots = [sums[i : i + 1, :] for i in range(8)]
    moment = dots[0:2] + [2.0 * dots[i] - dots[i % 2] for i in range(2, 8)]

    def gram(i, j):
        return 0.5 * (moment[i + j] + moment[abs(i - j)])

    lower = {}
    pivots = []
    right = []
    for i in range(4):
        value = moment[i]
        for j in range(i + 1):
            entry = gram(i, j) - 0.5 * (gram(j, i + 1) + gram(j, abs(i - 1)))
            for k in range(j):
                entry = entry - lower[i, k] * lower[j, k] * pivots[k]
            if j < i:
                lower[i, j] = entry / pivots[j]
                value = value - lower[i, j] * right[j]
            else:
                pivots.append(entry)
        right.append(value)
    solved = [None] * 4
    for i in range(3, -1, -1):
        value = right[i] / pivots[i]
        for j in range(i + 1, 4):
            value = value - lower[j, i] * solved[j]
        solved[i] = value
    surface = None
    for i in range(4):
        factor = 1.5 * solved[i]
        factor = jnp.concatenate([factor, factor, factor], axis=1)
        term = factor * basis[i + 1, 0:ROWS, :]
        surface = term if surface is None else surface + term
    surface_out[...] = surface[:, 0:COLS]


def store(tracer, surface, tracer_out, surface_out, sems):
    copies = [pltpu.make_async_copy(surface, surface_out, sems.at[8])]
    for index in range(8):
        levels = pl.ds(4 * (index % 4), 4)
        copies.append(
            pltpu.make_async_copy(
                tracer.at[index // 4, levels], tracer_out.at[index // 4, levels], sems.at[index]
            )
        )
    for copy in copies:
        copy.start()
    for copy in copies:
        copy.wait()


def scratch(nx, ny):
    vmem = lambda *shape: pltpu.VMEM(shape, f32)
    dma = pltpu.SemaphoreType.DMA
    return [
        vmem(4, LEV, ROWS, COLS),
        pltpu.SMEM((LEV,), f32),
        vmem(ROWS, COLS),
        vmem(ROWS, COLS),
        None,
        vmem(EXT, WIDE),
        vmem(24, WIDE),
        vmem(3, ROWS, WIDE),
        vmem(2, ROWS, 128),
        vmem(2, 32, WIDE),
        vmem(2, 72, 128),
        vmem(2, LEV, WIDE),
        vmem(2, 72, 128),
        vmem(2, 32, WIDE),
        vmem(2, LEV, WIDE),
        vmem(2 * ROWS + 8, 128),
        vmem(2, 2 * ROWS + 8, 128),
        vmem(16, 128),
        vmem(4, 16, 128),
        vmem(2, 8, 128),
        vmem(ROWS, 128),
        vmem(2 * LEV, WIDE),
        vmem(2 * LEV, WIDE),
        vmem(LEV, ROWS, WIDE),
        vmem(LEV, ROWS, WIDE),
        vmem(LEV, ROWS, WIDE),
        vmem(EXT, WIDE),
        vmem(ROWS, WIDE),
        vmem(6, EXT, WIDE),
        vmem(2, 8, WIDE),
        vmem(ROWS, 128),
        vmem(2, 8, WIDE),
        vmem(2, ROWS, 128),
        vmem(1, 128),
        vmem(nx, 1, 128),
        vmem(1, 128),
        vmem(ny, 1, 128),
        dma((6,)),
        dma((4,)),
        dma((12,)),
        dma((12,)),
        dma((8,)),
        dma((8,)),
        dma((2,)),
        dma((2,)),
    ]


def solution(mesh):
    nx, ny = mesh.shape["gx"], mesh.shape["gy"]

    def body(ocean_state, layer_thickness, vertical_mixing, damping, ocean_blocks):
        shapes = scratch(nx, ny)
        shapes[4] = pltpu.VMEM(ocean_blocks.shape, jnp.int32)
        call = pl.pallas_call(
            functools.partial(kernel, nx, ny),
            out_shape=[
                pltpu.VMEM((2, LEV, ROWS, COLS), f32),
                pltpu.VMEM((ROWS, COLS), f32),
            ],
            in_specs=[pl.BlockSpec(memory_space=pltpu.HBM)] * 5,
            out_specs=[pl.BlockSpec(memory_space=pltpu.VMEM)] * 2,
            scratch_shapes=shapes,
            compiler_params=pltpu.CompilerParams(
                collective_id=0, has_side_effects=True, vmem_limit_bytes=32 * 1024 * 1024
            ),
        )
        operands = [
            pltpu.with_memory_space_constraint(operand, pltpu.HBM)
            for operand in (ocean_state, layer_thickness, vertical_mixing, damping, ocean_blocks)
        ]
        tracer, surface = call(*operands)
        return tuple(
            pl.pallas_call(
                store,
                out_shape=[
                    jax.ShapeDtypeStruct((2, LEV, ROWS, COLS), f32),
                    jax.ShapeDtypeStruct((ROWS, COLS), f32),
                ],
                in_specs=[pl.BlockSpec(memory_space=pltpu.VMEM)] * 2,
                out_specs=[pl.BlockSpec(memory_space=pltpu.HBM)] * 2,
                scratch_shapes=[pltpu.SemaphoreType.DMA((9,))],
                compiler_params=pltpu.CompilerParams(vmem_limit_bytes=16 * 1024 * 1024),
            )(tracer, surface)
        )

    def wrapped(*args):
        with jax.sharding.use_abstract_mesh(mesh.abstract_mesh):
            return jax.shard_map(
                body,
                mesh=mesh,
                in_specs=(P(None, None, "gy", "gx"), P(), P("gy", "gx"), P("gy", "gx"), P()),
                out_specs=(P(None, None, "gy", "gx"), P("gy", "gx")),
                check_vma=False,
            )(*args)

    return wrapped
```

```python
import functools

import jax
import jax.numpy as jnp
from jax import lax
from jax.experimental import pallas as pl
from jax.experimental.pallas import tpu as pltpu
from jax.sharding import PartitionSpec as P

BLAT = 24
BLON = 36
LEV = 16
ROWS = 48
COLS = 288
WIDE = 384
EXT = 56
TILES = ROWS // 8

f32 = jnp.float32
MESH = pl.DeviceIdType.MESH

NORTH, SOUTH, EAST, WEST = (0, 1), (0, -1), (1, 0), (-1, 0)
DIAGONAL = ((1, 1), (-1, 1), (1, -1), (-1, -1))


def iota(shape, dim):
    return lax.broadcasted_iota(jnp.int32, shape, dim)


def padded(value):
    return jnp.concatenate([value, jnp.zeros((value.shape[0], WIDE - COLS), f32)], axis=1)


def east_of(value):
    return pltpu.roll(value, WIDE - 1, 1)


def west_of(value):
    return pltpu.roll(value, 1, 1)


def inverse(value):
    guess = pl.reciprocal(value, approx=True)
    return guess * (2.0 - value * guess)


def row_pack(low, high):
    return jnp.where(iota(low.shape, 0) < 4, low, high)


def column_pack(first, last):
    lane = iota(first.shape, 1)
    low = pltpu.roll(first, 32, 1)
    high = pltpu.roll(last, 96, 1)
    return jnp.where(
        (lane >= 32) & (lane < 36), low, jnp.where(lane >= 124, high, 0.0)
    )


def kernel(
    nx,
    ny,
    ocean,
    thick,
    mixing,
    damping,
    blocks,
    tracer_out,
    surface_out,
    state,
    h,
    mix,
    damp,
    blk,
    mask,
    level_inv,
    flat,
    ends,
    send_rows,
    send_strip,
    send_heat,
    recv_strip,
    recv_rows,
    recv_heat,
    send_cols,
    recv_cols,
    send_corner,
    recv_corner,
    recv_side,
    flux_lon,
    flux_north,
    flux_prev,
    ratio,
    carried,
    taken,
    scale,
    weigh,
    basis,
    halo_rows,
    halo_cols,
    recv_halo_rows,
    recv_halo_cols,
    first_message,
    first_sum,
    second_message,
    second_sum,
    load_sem,
    small_sem,
    send_sem,
    recv_sem,
    halo_send_sem,
    halo_recv_sem,
    sum_send_sem,
    sum_recv_sem,
):
    gx = lax.axis_index("gx")
    gy = lax.axis_index("gy")

    def device(step):
        return {"gx": lax.rem(gx + step[0] + nx, nx), "gy": lax.rem(gy + step[1] + ny, ny)}

    def greet(step):
        pl.semaphore_signal(barrier, inc=1, device_id=device(step), device_id_type=MESH)

    small = [
        pltpu.make_async_copy(blocks, blk, small_sem.at[0]),
        pltpu.make_async_copy(thick, h, small_sem.at[1]),
        pltpu.make_async_copy(damping, damp, small_sem.at[2]),
        pltpu.make_async_copy(mixing, mix, small_sem.at[3]),
    ]
    group = LEV // 8

    def load(index):
        levels = pl.ds(group * index, group)
        return pltpu.make_async_copy(
            ocean.at[:, levels, :, :], state.at[:, levels, :, :], load_sem.at[index]
        )

    for copy in small[:3] + [load(index) for index in range(8)] + small[3:]:
        copy.start()

    barrier = pltpu.get_barrier_semaphore()
    for step in DIAGONAL:
        greet(step)
    pl.loop(1, nx)(lambda d: greet((d, 0)))
    pl.loop(1, ny)(lambda d: greet((0, d)))
    partners = len(DIAGONAL) + nx - 1 + ny - 1

    block_rows, block_cols = blk.shape
    small[0].wait()
    row = iota((EXT, block_rows), 0)
    row = gy * ROWS + jnp.where(row < ROWS + 4, row, row - EXT)
    edge = iota((EXT, block_rows), 1) * BLAT
    pick_rows = jnp.where((row >= edge) & (row < edge + BLAT), 1.0, 0.0)
    lane = iota((block_cols, WIDE), 1)
    total = block_cols * BLON
    col = gx * COLS + jnp.where(lane < COLS + 4, lane, lane - WIDE)
    col = jnp.where(col < 0, col + total, jnp.where(col >= total, col - total, col))
    edge = iota((block_cols, WIDE), 0) * BLON
    inside = (lane < COLS + 4) | (lane >= WIDE - 4)
    pick_cols = jnp.where(inside & (col >= edge) & (col < edge + BLON), 1.0, 0.0)
    coarse = jnp.dot(pick_rows, blk[...].astype(f32), preferred_element_type=f32)
    mask[...] = jnp.dot(coarse, pick_cols, preferred_element_type=f32)

    small[1].wait()
    small[2].wait()
    damp_low = padded(damp[0:8, :])
    damp_high = padded(damp[ROWS - 8 : ROWS, :])
    damp_rows = row_pack(damp_low, damp_high)
    damp_all = padded(damp[...])
    send_cols[ROWS : 2 * ROWS, :] = column_pack(damp_all[:, 0:128], damp_all[:, 256:384])

    def remote(source, target, index, step, sends=send_sem, recvs=recv_sem):
        return pltpu.make_async_remote_copy(
            src_ref=source,
            dst_ref=target,
            send_sem=sends.at[index],
            recv_sem=recvs.at[index],
            device_id=device(step),
            device_id_type=MESH,
        )

    sub = iota((8, WIDE), 0)
    lane128 = iota((8, 128), 1)

    def next_row(i):
        return jnp.minimum(8 * i + 8, ROWS - 1)

    tiles = [pl.ds(8 * i, 8) for i in range(TILES)]
    flat[...] = jnp.zeros(flat.shape, f32)
    ends[...] = jnp.zeros(ends.shape, f32)
    end_mask = [
        jnp.where(lane128 == 31, mask[rows, 256:384], mask[rows, 0:128]) for rows in tiles
    ]

    def pack_ends(pair):
        for i, rows in enumerate(tiles):
            west, east = ends[0, rows, :], ends[1, rows, :]
            for k in (2 * pair, 2 * pair + 1):
                for field, base in ((0, 0), (1, 16), (2, 64)):
                    last = jnp.concatenate(
                        [state[field, k, rows, 256:COLS], jnp.zeros((8, WIDE - COLS), f32)], axis=1
                    )
                    both = jnp.where(lane128 == 31, last, state[field, k, rows, 0:128])
                    both = pltpu.roll(both * end_mask[i], base + k, 1)
                    west = jnp.where(lane128 == base + k, both, west)
                    east = jnp.where(lane128 == base + k + 31, both, east)
            ends[0, rows, :] = west
            ends[1, rows, :] = east


    def turned_up(values):
        turned = [pltpu.roll(value, 7, 0) for value in values]
        return [
            jnp.where(sub == 7, turned[(i + 1) % TILES], turned[i]) for i in range(TILES)
        ]

    @pl.loop(0, LEV // 2)
    def _(pair):
        @pl.when(lax.rem(pair, group // 2) == 0)
        def _():
            load(pair // (group // 2)).wait()

        sums = None
        for k in (2 * pair, 2 * pair + 1):
            s = [
                padded(state[0, k, rows, :] - 0.5 * state[1, k, rows, :]) * mask[rows, :] * h[k]
                for rows in tiles
            ]
            v = [padded(state[3, k, rows, :]) * mask[rows, :] for rows in tiles]
            s_north, v_north = turned_up(s), turned_up(v)
            found = []
            for i, rows in enumerate(tiles):
                u = padded(state[2, k, rows, :]) * mask[rows, :]
                found.append(
                    (
                        s[i],
                        (u + east_of(u)) * (s[i] + east_of(s[i])),
                        (v[i] + v_north[i]) * (s[i] + s_north[i]),
                    )
                )
            if sums is None:
                sums = found
            else:
                sums = [[a + b for a, b in zip(x, y)] for x, y in zip(sums, found)]
        for i, rows in enumerate(tiles):
            for part in range(3):
                flat[part, rows, :] += sums[i][part]
        pack_ends(pair)

    first_round = []
    for side, (edge_row, step) in enumerate(((ROWS - 1, NORTH), (0, SOUTH))):
        edge_mask = mask[edge_row : edge_row + 1, :]
        heat = padded(state[0, :, edge_row, :]) * edge_mask
        salt = padded(state[1, :, edge_row, :]) * edge_mask
        send_heat[side] = heat
        send_rows[side, 0:16, :] = heat - 0.5 * salt
        send_rows[side, 16:32, :] = padded(state[3, :, edge_row, :]) * edge_mask
        send_strip[side, 0:32, :] = send_rows[side, :, 0:128]
        send_strip[side, 32:64, :] = send_rows[side, :, 128:256]
        tail = jnp.zeros((8, 128), f32)
        for part in range(4):
            third = send_rows[side, 8 * part : 8 * part + 8, 256:384]
            tail = jnp.where(lane128 // 32 == part, pltpu.roll(third, 32 * part, 1), tail)
        send_strip[side, 64:72, :] = tail
        first_round.append(remote(send_strip.at[side], recv_strip.at[side], side, step))

    pl.semaphore_wait(barrier, partners)
    for copy in first_round:
        copy.start()

    send_cols[0:ROWS, :] = ends[0] + pltpu.roll(ends[1], 1, 1)

    compact = jnp.zeros((8, 128), f32)
    for side in range(2):
        for part in range(4):
            j = 4 * side + part
            rows = pl.ds(8 * part, 8)
            first = pltpu.roll(send_rows[side, rows, 0:128], 16 * j, 1)
            last = pltpu.roll(send_rows[side, rows, 256:384], (16 * j - 24) % 128, 1)
            inside = lane128 // 16 == j
            compact = jnp.where(inside & (lane128 % 16 < 4), first, compact)
            compact = jnp.where(
                inside & (lane128 % 16 >= 4) & (lane128 % 16 < 8), last, compact
            )
    send_cols[2 * ROWS :, :] = compact
    send_corner[8:16, :] = row_pack(send_cols[0:8, :], send_cols[ROWS - 8 : ROWS, :])

    second_round = []
    for side, step in enumerate((EAST, WEST)):
        second_round.append(remote(send_cols, recv_cols.at[side], 2 + side, step))
    for side, step in enumerate((NORTH, SOUTH)):
        second_round.append(
            remote(send_corner.at[pl.ds(8, 8)], recv_side.at[side], 10 + side, step)
        )
    for copy in second_round:
        copy.start()
    first_round = first_round + second_round

    lane_f = iota((ROWS, WIDE), 1)
    row_f = iota((ROWS, WIDE), 0)
    plain = flat[0]
    lon = 0.05 * flat[1] - 0.1 * (east_of(plain) - plain)
    lon = jnp.where(lane_f < COLS - 1, lon, 0.0)
    lat = 0.05 * flat[2] - 0.1 * (pltpu.roll(plain, ROWS - 1, 0) - plain)
    lat = jnp.where(row_f == ROWS - 1, 0.0, lat)
    start = plain - (lon - west_of(lon)) - (lat - pltpu.roll(lat, 1, 0))
    start = jnp.where(lane_f < COLS, start, 0.0)
    basis[1, 0:ROWS, :] = start
    packed_rows = row_pack(start[0:8, :], start[ROWS - 8 : ROWS, :])
    halo_rows[0] = jnp.where(sub < 4, pltpu.roll(start[ROWS - 8 : ROWS, :], 4, 0), damp_high)
    halo_rows[1] = jnp.where(sub < 4, damp_low, pltpu.roll(start[0:8, :], 4, 0))
    halo_cols[...] = column_pack(start[:, 0:128], start[:, 256:384])
    for base, packed in ((8, damp_rows), (24, packed_rows)):
        first = pltpu.roll(packed[:, 0:128], base, 1)
        last = packed[:, 256:384]
        last = pltpu.roll(last, (base - 24) % 128, 1) if base != 24 else last
        compact = jnp.where((lane128 >= base) & (lane128 < base + 4), first, compact)
        compact = jnp.where((lane128 >= base + 4) & (lane128 < base + 8), last, compact)
    send_corner[0:8, :] = compact
    second_round = []
    for place, step in enumerate(DIAGONAL):
        second_round.append(
            remote(
                send_corner,
                recv_corner.at[place],
                4 + place,
                step,
                halo_send_sem,
                halo_recv_sem,
            )
        )
    for side, step in enumerate((NORTH, SOUTH)):
        second_round.append(
            remote(
                halo_rows.at[side], recv_halo_rows.at[side], side, step, halo_send_sem, halo_recv_sem
            )
        )
    for side, step in enumerate((EAST, WEST)):
        second_round.append(
            remote(halo_cols, recv_halo_cols.at[side], 2 + side, step, halo_send_sem, halo_recv_sem)
        )
    for copy in second_round:
        copy.start()
    heat_round = []
    for side, step in enumerate((NORTH, SOUTH)):
        copy = remote(send_heat.at[side], recv_heat.at[side], 8 + side, step)
        copy.start()
        heat_round.append(copy)

    level_inv[...] = jnp.zeros(level_inv.shape, f32)

    @pl.loop(1, LEV)
    def _(k):
        level_inv[pl.ds(k, 1), :] = 1.0 / jnp.full((1, WIDE), h[k - 1] + h[k], f32)


    weight = jnp.zeros((1, 128), f32)
    lane_w = iota((1, 128), 1)
    for k in range(LEV):
        weight = jnp.where((lane_w & 15) == k, h[k], weight)
    weight = weight * jnp.where((lane_w & 16) != 0, -0.5, 1.0)
    level_weight = jnp.zeros((LEV, WIDE), f32)
    level_row = iota((LEV, WIDE), 0)
    for k in range(LEV):
        level_weight = jnp.where(level_row == k, h[k], level_weight)
    exists = (
        jnp.where(gy < ny - 1, 1.0, 0.0).astype(f32),
        jnp.where(gy > 0, 1.0, 0.0).astype(f32),
    )

    weigh[...] = jnp.where(iota((ROWS, WIDE), 1) < COLS, 6.0 + damp_all, 0.0)

    small[3].wait()

    @pl.loop(0, 2)
    def _(part):
        rows = pl.ds(pl.multiple_of(ROWS // 2 * part, 8), ROWS // 2)
        coefficient = padded(mix[rows, :])
        here = mask[rows, :]

        def level(k, ratio_low):
            below = coefficient * level_inv[pl.ds(k, 1), :]
            above = coefficient * level_inv[pl.ds(k + 1, 1), :]
            pivot = inverse(h[k] + above + below * (1.0 - ratio_low))
            ratio_now = above * pivot
            ratio[k, rows, :] = ratio_now
            carried[k, rows, :] = below * pivot
            taken[k, rows, :] = h[k] * pivot * here
            return ratio_now

        lax.fori_loop(0, LEV, level, jnp.zeros((ROWS // 2, WIDE), f32), unroll=4)

    for copy in first_round:
        copy.wait()
    for slot in range(2):
        recv_rows[slot, :, 0:128] = recv_strip[slot, 0:32, :]
        recv_rows[slot, :, 128:256] = recv_strip[slot, 32:64, :]
        for part in range(4):
            tail = recv_strip[slot, 64:72, :]
            tail = pltpu.roll(tail, 128 - 32 * part, 1) if part else tail
            recv_rows[slot, 8 * part : 8 * part + 8, 256:384] = jnp.where(lane128 < 32, tail, 0.0)

    def side_flux(mine, theirs, speeds, sign):
        return speeds * (mine + theirs) - (0.1 * sign) * (theirs - mine)

    side_lat = []
    speed_lat = []
    for side, sign in ((0, 1.0), (1, -1.0)):
        slot = 1 - side
        s_mine = send_rows[side, 0:16, :]
        s_theirs = recv_rows[slot, 0:16, :] * exists[side]
        speeds = 0.05 * (send_rows[side, 16:32, :] + recv_rows[slot, 16:32, :] * exists[side])
        speed_lat.append(speeds)
        flux = side_flux(s_mine, s_theirs, speeds, sign)
        side_lat.append(jnp.sum(flux * level_weight, axis=0, keepdims=True))

    for copy in second_round:
        copy.wait()

    def beside(north, south):
        return jnp.where(iota((8, 128), 0) < 4, north, south)

    own = jnp.concatenate([send_cols[0:ROWS, :], beside(recv_side[1], recv_side[0])], axis=0)
    from_east = jnp.concatenate(
        [recv_cols[1, 0:ROWS, :], beside(recv_corner[3, 8:16, :], recv_corner[1, 8:16, :])], axis=0
    )
    from_west = jnp.concatenate(
        [recv_cols[0, 0:ROWS, :], beside(recv_corner[2, 8:16, :], recv_corner[0, 8:16, :])], axis=0
    )
    lane_c = iota((EXT, 128), 1)
    is_east = (lane_c & 32) != 0
    other = jnp.where(is_east, pltpu.roll(from_east, 32, 1), pltpu.roll(from_west, 96, 1))
    both = own + other
    speed = pltpu.roll(both, 64, 1)
    speed = jnp.where((lane_c & 16) != 0, pltpu.roll(speed, 16, 1), speed)
    slope = jnp.where(is_east, 0.1, -0.1) * (other - own)
    through = 0.05 * speed * both - slope
    flux_lon[...] = through[0:ROWS, :]
    weighed = through * weight
    side_west = jnp.sum(jnp.where(lane_c < 32, weighed, 0.0), axis=1, keepdims=True)
    side_east = jnp.sum(
        jnp.where(is_east & (lane_c < 64), weighed, 0.0), axis=1, keepdims=True
    )

    is_first = (lane128 & 15) < 4
    is_north = lane128 < 64
    mine = jnp.where(is_first, recv_cols[1, 2 * ROWS :, :], recv_cols[0, 2 * ROWS :, :])
    theirs_north = jnp.where(is_first, recv_corner[3, 0:8, :], recv_corner[2, 0:8, :])
    theirs_south = jnp.where(is_first, recv_corner[1, 0:8, :], recv_corner[0, 0:8, :])
    theirs = pltpu.roll(
        jnp.where(is_north, theirs_south * exists[1], theirs_north * exists[0]), 64, 1
    )
    both = mine + theirs
    flux = 0.05 * pltpu.roll(both, 96, 1) * both - jnp.where(is_north, 0.1, -0.1) * (theirs - mine)
    flux = flux * jnp.where(
        (lane128 & 16) == 0, level_weight[0:8, 0:128], level_weight[8:16, 0:128]
    )
    flux = jnp.sum(flux, axis=0, keepdims=True)
    flux = flux + pltpu.roll(flux, 112, 1)
    for side in range(2):
        low = pltpu.roll(flux, 32 - 64 * side if side == 0 else 96, 1)
        high = pltpu.roll(flux, 120 if side == 0 else 56, 1)
        third = jnp.where(
            lane_w < 32, side_lat[side][:, 256:384], jnp.where(lane_w < 64, low, high)
        )
        side_lat[side] = jnp.concatenate([side_lat[side][:, 0:256], third], axis=1)

    def assemble(center, north_south, cols_in, base):
        lane48 = iota((ROWS, 128), 1)
        third = jnp.where(
            lane48 < 32, center[:, 256:384], jnp.where(lane48 < 64, cols_in(1), cols_in(0))
        )
        upper = jnp.concatenate([center[:, 0:256], third], axis=1)
        low = pltpu.roll(corners, 32 - base, 1)
        high = pltpu.roll(corners, 120 - base, 1)
        third = jnp.where(
            lane128 < 32, north_south[:, 256:384], jnp.where(lane128 < 64, low, high)
        )
        lower = jnp.concatenate([north_south[:, 0:256], third], axis=1)
        return jnp.concatenate([upper, lower], axis=0)

    is_low = (lane128 & 7) < 4
    corners = beside(
        jnp.where(is_low, recv_corner[3, 0:8, :], recv_corner[2, 0:8, :]),
        jnp.where(is_low, recv_corner[1, 0:8, :], recv_corner[0, 0:8, :]),
    )
    damp_ext = assemble(
        damp_all,
        jnp.where(sub < 4, recv_halo_rows[1], recv_halo_rows[0]),
        lambda slot: recv_cols[slot, ROWS : 2 * ROWS, :],
        8,
    )
    inv = mask[...] * inverse(6.0 + damp_ext)
    scale[...] = 1.5 * inv
    forcing = assemble(
        basis[1, 0:ROWS, :],
        pltpu.roll(jnp.where(sub < 4, recv_halo_rows[0], recv_halo_rows[1]), 4, 0),
        lambda slot: recv_halo_cols[slot],
        24,
    )
    forcing = jnp.concatenate(
        [
            forcing[:, 0:128] + jnp.where(lane_c == 0, side_west, 0.0),
            forcing[:, 128:256],
            forcing[:, 256:384]
            + jnp.where(
                lane_c == 31,
                -side_east,
                jnp.where(lane_c == 32, side_east, jnp.where(lane_c == 127, -side_west, 0.0)),
            ),
        ],
        axis=1,
    )
    north, south = side_lat
    forcing = jnp.concatenate(
        [
            forcing[0:8, :] + jnp.where(sub == 0, south, 0.0),
            forcing[8:40, :],
            forcing[40:48, :] - jnp.where(sub == 7, north, 0.0),
            forcing[48:56, :]
            + jnp.where(sub == 0, north, jnp.where(sub == 7, -south, 0.0)),
        ],
        axis=0,
    )
    basis[1] = forcing * inv

    def folded(value):
        rows = [value[8 * i : 8 * i + 8, :] for i in range(TILES)]
        value = (rows[0] + rows[1]) + (rows[2] + rows[3]) + (rows[4] + rows[5])
        return value[:, 0:128] + value[:, 128:256] + value[:, 256:384]

    parts = []
    for index in range(4):
        q = basis[index + 1]
        pair = east_of(q) + west_of(q)
        column = q + 0.5 * pair
        around = pair + pltpu.roll(column, EXT - 1, 0) + pltpu.roll(column, 1, 0)
        image = scale[...] * around - 0.5 * q
        after = image if index == 0 else 2.0 * image - basis[index]
        if index < 3:
            basis[index + 2] = after
        weighed = weigh[...] * q[0:ROWS, :]
        parts.append(folded(weighed * q[0:ROWS, :]))
        parts.append(folded(weighed * after[0:ROWS, :]))

    for width in (64, 32, 16):
        half = len(parts) // 2
        parts = [
            jnp.where(
                (lane128 & width) == 0,
                low + pltpu.roll(low, 128 - width, 1),
                high + pltpu.roll(high, width, 1),
            )
            for low, high in zip(parts[:half], parts[half:])
        ]
    first_message[...] = jnp.sum(parts[0], axis=0, keepdims=True)

    def spread(source, target, count, along, mine, base):
        target[mine] = source[...]

        @pl.loop(1, count)
        def _(turn):
            d = count // 2 + jnp.where(turn % 2 == 0, -(turn // 2), turn // 2)
            pltpu.make_async_remote_copy(
                src_ref=source,
                dst_ref=target.at[mine],
                send_sem=sum_send_sem.at[base],
                recv_sem=sum_recv_sem.at[base],
                device_id=device(along(d)),
                device_id_type=MESH,
            ).start()

    def gathered(target, count, base):
        part = target.at[pl.ds(0, count - 1)]
        done = pltpu.make_async_remote_copy(
            src_ref=part,
            dst_ref=part,
            send_sem=sum_send_sem.at[base],
            recv_sem=sum_recv_sem.at[base],
            device_id=device(EAST),
            device_id_type=MESH,
        )
        done.wait_recv()
        done.wait_send()
        return jnp.sum(target[...], axis=0)

    spread(first_message, first_sum, nx, lambda d: (d, 0), gx, 0)

    for copy in heat_round:
        copy.wait()
    for side, sign in ((0, 1.0), (1, -1.0)):
        slot = 1 - side
        target = flux_north if side == 0 else flux_prev
        heat_mine = send_heat[side]
        heat_theirs = recv_heat[slot] * exists[side]
        salt_mine = 2.0 * (heat_mine - send_rows[side, 0:16, :])
        salt_theirs = 2.0 * (heat_theirs - recv_rows[slot, 0:16, :] * exists[side])
        target[0:16, :] = side_flux(heat_mine, heat_theirs, speed_lat[side], sign)
        target[16:32, :] = side_flux(salt_mine, salt_theirs, speed_lat[side], sign)
    edge_lane = (lane128 == 31) | (lane128 == 127)

    def mix_tile(i, _):
        rows = pl.ds(pl.multiple_of(8 * i, 8), 8)
        row = pl.ds(next_row(i), 1)
        here = mask[rows, :]
        beyond = mask[row, :]
        through = flux_lon[rows, :]
        use_north = (sub == 7) & (i == TILES - 1)

        def level(k, carry):
            heat_low, salt_low = carry
            u = padded(state[2, k, rows, :]) * here
            v = padded(state[3, k, rows, :]) * here
            v_row = padded(state[3, k, row, :]) * beyond
            v_north = jnp.where(sub == 7, v_row, pltpu.roll(v, 7, 0))
            u_pair = 0.05 * (u + east_of(u))
            v_pair = 0.05 * (v + v_north)
            lon_far, lon_near = u_pair - 0.1, u_pair + 0.1
            lat_far, lat_near = v_pair - 0.1, v_pair + 0.1
            found = []
            for tracer, low in ((0, heat_low), (1, salt_low)):
                plane = tracer * LEV + k
                c = padded(state[tracer, k, rows, :]) * here
                c_row = padded(state[tracer, k, row, :]) * beyond
                c_north = jnp.where(sub == 7, c_row, pltpu.roll(c, 7, 0))
                lon = lon_far * east_of(c) + lon_near * c
                turned = pltpu.roll(through, 127 - plane, 1)
                lon = jnp.concatenate(
                    [lon[:, 0:256], jnp.where(edge_lane, turned, lon[:, 256:384])], axis=1
                )
                lat = lat_far * c_north + lat_near * c
                lat = jnp.where(use_north, flux_north[pl.ds(plane, 1), :], lat)
                lat_south = jnp.where(
                    sub == 0, flux_prev[pl.ds(plane, 1), :], pltpu.roll(lat, 1, 0)
                )
                flux_prev[pl.ds(plane, 1), :] = lat[7:8, :]
                advected = c - (lon - west_of(lon)) - (lat - lat_south)
                value = taken[k, rows, :] * advected + carried[k, rows, :] * low
                tracer_out[tracer, k, rows, :] = value[:, 0:COLS]
                found.append(value)
            return found[0], found[1]

        zero = jnp.zeros((8, WIDE), f32)
        heat, salt = lax.fori_loop(0, LEV, level, (zero, zero), unroll=4)

        def back(step, carry):
            k = LEV - 2 - step
            heat_up, salt_up = carry
            share = ratio[k, rows, 0:COLS]
            heat_up = tracer_out[0, k, rows, :] + share * heat_up
            salt_up = tracer_out[1, k, rows, :] + share * salt_up
            tracer_out[0, k, rows, :] = heat_up
            tracer_out[1, k, rows, :] = salt_up
            return heat_up, salt_up

        lax.fori_loop(0, LEV - 1, back, (heat[:, 0:COLS], salt[:, 0:COLS]), unroll=5)
        return 0

    lax.fori_loop(0, 2, mix_tile, 0)
    second_message[...] = gathered(first_sum, nx, 0)
    spread(second_message, second_sum, ny, lambda d: (0, d), gy, 1)
    lax.fori_loop(2, TILES, mix_tile, 0)
    sums = gathered(second_sum, ny, 1)

    own_lanes = lane128 // 16 == iota((8, 128), 0)
    sums = jnp.where(own_lanes, jnp.broadcast_to(sums, (8, 128)), 0.0)
    sums = jnp.broadcast_to(jnp.sum(sums, axis=1, keepdims=True), (8, 128))
    dots = [sums[i : i + 1, :] for i in range(8)]
    moment = dots[0:2] + [2.0 * dots[i] - dots[i % 2] for i in range(2, 8)]

    def gram(i, j):
        return 0.5 * (moment[i + j] + moment[abs(i - j)])

    lower = {}
    pivots = []
    right = []
    for i in range(4):
        value = moment[i]
        for j in range(i + 1):
            entry = gram(i, j) - 0.5 * (gram(j, i + 1) + gram(j, abs(i - 1)))
            for k in range(j):
                entry = entry - lower[i, k] * lower[j, k] * pivots[k]
            if j < i:
                lower[i, j] = entry / pivots[j]
                value = value - lower[i, j] * right[j]
            else:
                pivots.append(entry)
        right.append(value)
    solved = [None] * 4
    for i in range(3, -1, -1):
        value = right[i] / pivots[i]
        for j in range(i + 1, 4):
            value = value - lower[j, i] * solved[j]
        solved[i] = value
    surface = None
    for i in range(4):
        factor = 1.5 * solved[i]
        factor = jnp.concatenate([factor, factor, factor], axis=1)
        term = factor * basis[i + 1, 0:ROWS, :]
        surface = term if surface is None else surface + term
    surface_out[...] = surface[:, 0:COLS]


def store(tracer, surface, tracer_out, surface_out, sems):
    copies = [pltpu.make_async_copy(surface, surface_out, sems.at[8])]
    for index in range(8):
        levels = pl.ds(4 * (index % 4), 4)
        copies.append(
            pltpu.make_async_copy(
                tracer.at[index // 4, levels], tracer_out.at[index // 4, levels], sems.at[index]
            )
        )
    for copy in copies:
        copy.start()
    for copy in copies:
        copy.wait()


def scratch(nx, ny):
    vmem = lambda *shape: pltpu.VMEM(shape, f32)
    dma = pltpu.SemaphoreType.DMA
    return [
        vmem(4, LEV, ROWS, COLS),
        pltpu.SMEM((LEV,), f32),
        vmem(ROWS, COLS),
        vmem(ROWS, COLS),
        None,
        vmem(EXT, WIDE),
        vmem(24, WIDE),
        vmem(3, ROWS, WIDE),
        vmem(2, ROWS, 128),
        vmem(2, 32, WIDE),
        vmem(2, 72, 128),
        vmem(2, LEV, WIDE),
        vmem(2, 72, 128),
        vmem(2, 32, WIDE),
        vmem(2, LEV, WIDE),
        vmem(2 * ROWS + 8, 128),
        vmem(2, 2 * ROWS + 8, 128),
        vmem(16, 128),
        vmem(4, 16, 128),
        vmem(2, 8, 128),
        vmem(ROWS, 128),
        vmem(2 * LEV, WIDE),
        vmem(2 * LEV, WIDE),
        vmem(LEV, ROWS, WIDE),
        vmem(LEV, ROWS, WIDE),
        vmem(LEV, ROWS, WIDE),
        vmem(EXT, WIDE),
        vmem(ROWS, WIDE),
        vmem(6, EXT, WIDE),
        vmem(2, 8, WIDE),
        vmem(ROWS, 128),
        vmem(2, 8, WIDE),
        vmem(2, ROWS, 128),
        vmem(1, 128),
        vmem(nx, 1, 128),
        vmem(1, 128),
        vmem(ny, 1, 128),
        dma((8,)),
        dma((4,)),
        dma((12,)),
        dma((12,)),
        dma((8,)),
        dma((8,)),
        dma((2,)),
        dma((2,)),
    ]


def solution(mesh):
    nx, ny = mesh.shape["gx"], mesh.shape["gy"]

    def body(ocean_state, layer_thickness, vertical_mixing, damping, ocean_blocks):
        shapes = scratch(nx, ny)
        shapes[4] = pltpu.VMEM(ocean_blocks.shape, jnp.int32)
        call = pl.pallas_call(
            functools.partial(kernel, nx, ny),
            out_shape=[
                pltpu.VMEM((2, LEV, ROWS, COLS), f32),
                pltpu.VMEM((ROWS, COLS), f32),
            ],
            in_specs=[pl.BlockSpec(memory_space=pltpu.HBM)] * 5,
            out_specs=[pl.BlockSpec(memory_space=pltpu.VMEM)] * 2,
            scratch_shapes=shapes,
            compiler_params=pltpu.CompilerParams(
                collective_id=0, has_side_effects=True, vmem_limit_bytes=32 * 1024 * 1024
            ),
        )
        operands = [
            pltpu.with_memory_space_constraint(operand, pltpu.HBM)
            for operand in (ocean_state, layer_thickness, vertical_mixing, damping, ocean_blocks)
        ]
        tracer, surface = call(*operands)
        return tuple(
            pl.pallas_call(
                store,
                out_shape=[
                    jax.ShapeDtypeStruct((2, LEV, ROWS, COLS), f32),
                    jax.ShapeDtypeStruct((ROWS, COLS), f32),
                ],
                in_specs=[pl.BlockSpec(memory_space=pltpu.VMEM)] * 2,
                out_specs=[pl.BlockSpec(memory_space=pltpu.HBM)] * 2,
                scratch_shapes=[pltpu.SemaphoreType.DMA((9,))],
                compiler_params=pltpu.CompilerParams(vmem_limit_bytes=16 * 1024 * 1024),
            )(tracer, surface)
        )

    def wrapped(*args):
        with jax.sharding.use_abstract_mesh(mesh.abstract_mesh):
            return jax.shard_map(
                body,
                mesh=mesh,
                in_specs=(P(None, None, "gy", "gx"), P(), P("gy", "gx"), P("gy", "gx"), P()),
                out_specs=(P(None, None, "gy", "gx"), P("gy", "gx")),
                check_vma=False,
            )(*args)

    return wrapped
```

```python
import functools

import jax
import jax.numpy as jnp
from jax import lax
from jax.experimental import pallas as pl
from jax.experimental.pallas import tpu as pltpu
from jax.sharding import PartitionSpec as P

BLAT = 24
BLON = 36
LEV = 16
ROWS = 48
COLS = 288
WIDE = 384
EXT = 56
TILES = ROWS // 8

f32 = jnp.float32
MESH = pl.DeviceIdType.MESH

NORTH, SOUTH, EAST, WEST = (0, 1), (0, -1), (1, 0), (-1, 0)
DIAGONAL = ((1, 1), (-1, 1), (1, -1), (-1, -1))


def iota(shape, dim):
    return lax.broadcasted_iota(jnp.int32, shape, dim)


def padded(value):
    return jnp.concatenate([value, jnp.zeros((value.shape[0], WIDE - COLS), f32)], axis=1)


def east_of(value):
    return pltpu.roll(value, WIDE - 1, 1)


def west_of(value):
    return pltpu.roll(value, 1, 1)


def inverse(value):
    guess = pl.reciprocal(value, approx=True)
    return guess * (2.0 - value * guess)


def row_pack(low, high):
    return jnp.where(iota(low.shape, 0) < 4, low, high)


def column_pack(first, last):
    lane = iota(first.shape, 1)
    low = pltpu.roll(first, 32, 1)
    high = pltpu.roll(last, 96, 1)
    return jnp.where(
        (lane >= 32) & (lane < 36), low, jnp.where(lane >= 124, high, 0.0)
    )


def kernel(
    nx,
    ny,
    ocean,
    thick,
    mixing,
    damping,
    blocks,
    tracer_out,
    surface_out,
    state,
    h,
    mix,
    damp,
    blk,
    mask,
    level_inv,
    flat,
    ends,
    send_rows,
    send_strip,
    send_heat,
    recv_strip,
    recv_rows,
    recv_heat,
    send_cols,
    recv_cols,
    send_corner,
    recv_corner,
    recv_side,
    flux_lon,
    flux_north,
    flux_prev,
    ratio,
    carried,
    taken,
    scale,
    weigh,
    basis,
    halo_rows,
    halo_cols,
    recv_halo_rows,
    recv_halo_cols,
    first_message,
    first_sum,
    second_message,
    second_sum,
    load_sem,
    small_sem,
    send_sem,
    recv_sem,
    halo_send_sem,
    halo_recv_sem,
    sum_send_sem,
    sum_recv_sem,
):
    gx = lax.axis_index("gx")
    gy = lax.axis_index("gy")

    def device(step):
        return {"gx": lax.rem(gx + step[0] + nx, nx), "gy": lax.rem(gy + step[1] + ny, ny)}

    def greet(step):
        pl.semaphore_signal(barrier, inc=1, device_id=device(step), device_id_type=MESH)

    small = [
        pltpu.make_async_copy(blocks, blk, small_sem.at[0]),
        pltpu.make_async_copy(thick, h, small_sem.at[1]),
        pltpu.make_async_copy(damping, damp, small_sem.at[2]),
        pltpu.make_async_copy(mixing, mix, small_sem.at[3]),
    ]
    group = LEV // 4

    def load(index):
        levels = pl.ds(group * index, group)
        return pltpu.make_async_copy(
            ocean.at[:, levels, :, :], state.at[:, levels, :, :], load_sem.at[index]
        )

    for copy in small[:3] + [load(index) for index in range(4)] + small[3:]:
        copy.start()

    barrier = pltpu.get_barrier_semaphore()
    for step in DIAGONAL:
        greet(step)
    pl.loop(1, nx)(lambda d: greet((d, 0)))
    pl.loop(1, ny)(lambda d: greet((0, d)))
    partners = len(DIAGONAL) + nx - 1 + ny - 1

    block_rows, block_cols = blk.shape
    small[0].wait()
    row = iota((EXT, block_rows), 0)
    row = gy * ROWS + jnp.where(row < ROWS + 4, row, row - EXT)
    edge = iota((EXT, block_rows), 1) * BLAT
    pick_rows = jnp.where((row >= edge) & (row < edge + BLAT), 1.0, 0.0)
    lane = iota((block_cols, WIDE), 1)
    total = block_cols * BLON
    col = gx * COLS + jnp.where(lane < COLS + 4, lane, lane - WIDE)
    col = jnp.where(col < 0, col + total, jnp.where(col >= total, col - total, col))
    edge = iota((block_cols, WIDE), 0) * BLON
    inside = (lane < COLS + 4) | (lane >= WIDE - 4)
    pick_cols = jnp.where(inside & (col >= edge) & (col < edge + BLON), 1.0, 0.0)
    coarse = jnp.dot(pick_rows, blk[...].astype(f32), preferred_element_type=f32)
    mask[...] = jnp.dot(coarse, pick_cols, preferred_element_type=f32)

    small[1].wait()
    small[2].wait()
    damp_low = padded(damp[0:8, :])
    damp_high = padded(damp[ROWS - 8 : ROWS, :])
    damp_rows = row_pack(damp_low, damp_high)
    damp_all = padded(damp[...])
    send_cols[ROWS : 2 * ROWS, :] = column_pack(damp_all[:, 0:128], damp_all[:, 256:384])

    def remote(source, target, index, step, sends=send_sem, recvs=recv_sem):
        return pltpu.make_async_remote_copy(
            src_ref=source,
            dst_ref=target,
            send_sem=sends.at[index],
            recv_sem=recvs.at[index],
            device_id=device(step),
            device_id_type=MESH,
        )

    sub = iota((8, WIDE), 0)
    lane128 = iota((8, 128), 1)

    def next_row(i):
        return jnp.minimum(8 * i + 8, ROWS - 1)

    tiles = [pl.ds(8 * i, 8) for i in range(TILES)]
    flat[...] = jnp.zeros(flat.shape, f32)
    ends[...] = jnp.zeros(ends.shape, f32)
    end_mask = [
        jnp.where(lane128 == 31, mask[rows, 256:384], mask[rows, 0:128]) for rows in tiles
    ]

    def pack_ends(pair):
        for i, rows in enumerate(tiles):
            west, east = ends[0, rows, :], ends[1, rows, :]
            for k in (2 * pair, 2 * pair + 1):
                for field, base in ((0, 0), (1, 16), (2, 64)):
                    last = jnp.concatenate(
                        [state[field, k, rows, 256:COLS], jnp.zeros((8, WIDE - COLS), f32)], axis=1
                    )
                    both = jnp.where(lane128 == 31, last, state[field, k, rows, 0:128])
                    both = pltpu.roll(both * end_mask[i], base + k, 1)
                    west = jnp.where(lane128 == base + k, both, west)
                    east = jnp.where(lane128 == base + k + 31, both, east)
            ends[0, rows, :] = west
            ends[1, rows, :] = east


    def turned_up(values):
        turned = [pltpu.roll(value, 7, 0) for value in values]
        return [
            jnp.where(sub == 7, turned[(i + 1) % TILES], turned[i]) for i in range(TILES)
        ]

    @pl.loop(0, LEV // 2)
    def _(pair):
        @pl.when(lax.rem(pair, group // 2) == 0)
        def _():
            load(pair // (group // 2)).wait()

        sums = None
        for k in (2 * pair, 2 * pair + 1):
            s = [
                padded(state[0, k, rows, :] - 0.5 * state[1, k, rows, :]) * mask[rows, :] * h[k]
                for rows in tiles
            ]
            v = [padded(state[3, k, rows, :]) * mask[rows, :] for rows in tiles]
            s_north, v_north = turned_up(s), turned_up(v)
            found = []
            for i, rows in enumerate(tiles):
                u = padded(state[2, k, rows, :]) * mask[rows, :]
                found.append(
                    (
                        s[i],
                        (u + east_of(u)) * (s[i] + east_of(s[i])),
                        (v[i] + v_north[i]) * (s[i] + s_north[i]),
                    )
                )
            if sums is None:
                sums = found
            else:
                sums = [[a + b for a, b in zip(x, y)] for x, y in zip(sums, found)]
        for i, rows in enumerate(tiles):
            for part in range(3):
                flat[part, rows, :] += sums[i][part]
        pack_ends(pair)

    first_round = []
    for side, (edge_row, step) in enumerate(((ROWS - 1, NORTH), (0, SOUTH))):
        edge_mask = mask[edge_row : edge_row + 1, :]
        heat = padded(state[0, :, edge_row, :]) * edge_mask
        salt = padded(state[1, :, edge_row, :]) * edge_mask
        send_heat[side] = heat
        send_rows[side, 0:16, :] = heat - 0.5 * salt
        send_rows[side, 16:32, :] = padded(state[3, :, edge_row, :]) * edge_mask
        send_strip[side, 0:32, :] = send_rows[side, :, 0:128]
        send_strip[side, 32:64, :] = send_rows[side, :, 128:256]
        tail = jnp.zeros((8, 128), f32)
        for part in range(4):
            third = send_rows[side, 8 * part : 8 * part + 8, 256:384]
            tail = jnp.where(lane128 // 32 == part, pltpu.roll(third, 32 * part, 1), tail)
        send_strip[side, 64:72, :] = tail
        first_round.append(remote(send_strip.at[side], recv_strip.at[side], side, step))

    pl.semaphore_wait(barrier, partners)
    for copy in first_round:
        copy.start()

    send_cols[0:ROWS, :] = ends[0] + pltpu.roll(ends[1], 1, 1)

    compact = jnp.zeros((8, 128), f32)
    for side in range(2):
        for part in range(4):
            j = 4 * side + part
            rows = pl.ds(8 * part, 8)
            first = pltpu.roll(send_rows[side, rows, 0:128], 16 * j, 1)
            last = pltpu.roll(send_rows[side, rows, 256:384], (16 * j - 24) % 128, 1)
            inside = lane128 // 16 == j
            compact = jnp.where(inside & (lane128 % 16 < 4), first, compact)
            compact = jnp.where(
                inside & (lane128 % 16 >= 4) & (lane128 % 16 < 8), last, compact
            )
    send_cols[2 * ROWS :, :] = compact
    send_corner[8:16, :] = row_pack(send_cols[0:8, :], send_cols[ROWS - 8 : ROWS, :])

    second_round = []
    for side, step in enumerate((EAST, WEST)):
        second_round.append(remote(send_cols, recv_cols.at[side], 2 + side, step))
    for side, step in enumerate((NORTH, SOUTH)):
        second_round.append(
            remote(send_corner.at[pl.ds(8, 8)], recv_side.at[side], 10 + side, step)
        )
    for copy in second_round:
        copy.start()
    first_round = first_round + second_round

    lane_f = iota((ROWS, WIDE), 1)
    row_f = iota((ROWS, WIDE), 0)
    plain = flat[0]
    lon = 0.05 * flat[1] - 0.1 * (east_of(plain) - plain)
    lon = jnp.where(lane_f < COLS - 1, lon, 0.0)
    lat = 0.05 * flat[2] - 0.1 * (pltpu.roll(plain, ROWS - 1, 0) - plain)
    lat = jnp.where(row_f == ROWS - 1, 0.0, lat)
    start = plain - (lon - west_of(lon)) - (lat - pltpu.roll(lat, 1, 0))
    start = jnp.where(lane_f < COLS, start, 0.0)
    basis[1, 0:ROWS, :] = start
    packed_rows = row_pack(start[0:8, :], start[ROWS - 8 : ROWS, :])
    halo_rows[0] = jnp.where(sub < 4, pltpu.roll(start[ROWS - 8 : ROWS, :], 4, 0), damp_high)
    halo_rows[1] = jnp.where(sub < 4, damp_low, pltpu.roll(start[0:8, :], 4, 0))
    halo_cols[...] = column_pack(start[:, 0:128], start[:, 256:384])
    for base, packed in ((8, damp_rows), (24, packed_rows)):
        first = pltpu.roll(packed[:, 0:128], base, 1)
        last = packed[:, 256:384]
        last = pltpu.roll(last, (base - 24) % 128, 1) if base != 24 else last
        compact = jnp.where((lane128 >= base) & (lane128 < base + 4), first, compact)
        compact = jnp.where((lane128 >= base + 4) & (lane128 < base + 8), last, compact)
    send_corner[0:8, :] = compact
    second_round = []
    for place, step in enumerate(DIAGONAL):
        second_round.append(
            remote(
                send_corner,
                recv_corner.at[place],
                4 + place,
                step,
                halo_send_sem,
                halo_recv_sem,
            )
        )
    for side, step in enumerate((NORTH, SOUTH)):
        second_round.append(
            remote(
                halo_rows.at[side], recv_halo_rows.at[side], side, step, halo_send_sem, halo_recv_sem
            )
        )
    for side, step in enumerate((EAST, WEST)):
        second_round.append(
            remote(halo_cols, recv_halo_cols.at[side], 2 + side, step, halo_send_sem, halo_recv_sem)
        )
    for copy in second_round:
        copy.start()
    heat_round = []
    for side, step in enumerate((NORTH, SOUTH)):
        copy = remote(send_heat.at[side], recv_heat.at[side], 8 + side, step)
        copy.start()
        heat_round.append(copy)

    level_inv[...] = jnp.zeros(level_inv.shape, f32)

    @pl.loop(1, LEV)
    def _(k):
        level_inv[pl.ds(k, 1), :] = 1.0 / jnp.full((1, WIDE), h[k - 1] + h[k], f32)


    weight = jnp.zeros((1, 128), f32)
    lane_w = iota((1, 128), 1)
    for k in range(LEV):
        weight = jnp.where((lane_w & 15) == k, h[k], weight)
    weight = weight * jnp.where((lane_w & 16) != 0, -0.5, 1.0)
    level_weight = jnp.zeros((LEV, WIDE), f32)
    level_row = iota((LEV, WIDE), 0)
    for k in range(LEV):
        level_weight = jnp.where(level_row == k, h[k], level_weight)
    exists = (
        jnp.where(gy < ny - 1, 1.0, 0.0).astype(f32),
        jnp.where(gy > 0, 1.0, 0.0).astype(f32),
    )

    weigh[...] = jnp.where(iota((ROWS, WIDE), 1) < COLS, 6.0 + damp_all, 0.0)

    small[3].wait()

    @pl.loop(0, 2)
    def _(part):
        rows = pl.ds(pl.multiple_of(ROWS // 2 * part, 8), ROWS // 2)
        coefficient = padded(mix[rows, :])
        here = mask[rows, :]

        def level(k, ratio_low):
            below = coefficient * level_inv[pl.ds(k, 1), :]
            above = coefficient * level_inv[pl.ds(k + 1, 1), :]
            pivot = inverse(h[k] + above + below * (1.0 - ratio_low))
            ratio_now = above * pivot
            ratio[k, rows, :] = ratio_now
            carried[k, rows, :] = below * pivot
            taken[k, rows, :] = h[k] * pivot * here
            return ratio_now

        lax.fori_loop(0, LEV, level, jnp.zeros((ROWS // 2, WIDE), f32), unroll=4)

    for copy in first_round:
        copy.wait()
    for slot in range(2):
        recv_rows[slot, :, 0:128] = recv_strip[slot, 0:32, :]
        recv_rows[slot, :, 128:256] = recv_strip[slot, 32:64, :]
        for part in range(4):
            tail = recv_strip[slot, 64:72, :]
            tail = pltpu.roll(tail, 128 - 32 * part, 1) if part else tail
            recv_rows[slot, 8 * part : 8 * part + 8, 256:384] = jnp.where(lane128 < 32, tail, 0.0)

    def side_flux(mine, theirs, speeds, sign):
        return speeds * (mine + theirs) - (0.1 * sign) * (theirs - mine)

    side_lat = []
    speed_lat = []
    for side, sign in ((0, 1.0), (1, -1.0)):
        slot = 1 - side
        s_mine = send_rows[side, 0:16, :]
        s_theirs = recv_rows[slot, 0:16, :] * exists[side]
        speeds = 0.05 * (send_rows[side, 16:32, :] + recv_rows[slot, 16:32, :] * exists[side])
        speed_lat.append(speeds)
        flux = side_flux(s_mine, s_theirs, speeds, sign)
        side_lat.append(jnp.sum(flux * level_weight, axis=0, keepdims=True))

    for copy in second_round:
        copy.wait()

    def beside(north, south):
        return jnp.where(iota((8, 128), 0) < 4, north, south)

    own = jnp.concatenate([send_cols[0:ROWS, :], beside(recv_side[1], recv_side[0])], axis=0)
    from_east = jnp.concatenate(
        [recv_cols[1, 0:ROWS, :], beside(recv_corner[3, 8:16, :], recv_corner[1, 8:16, :])], axis=0
    )
    from_west = jnp.concatenate(
        [recv_cols[0, 0:ROWS, :], beside(recv_corner[2, 8:16, :], recv_corner[0, 8:16, :])], axis=0
    )
    lane_c = iota((EXT, 128), 1)
    is_east = (lane_c & 32) != 0
    other = jnp.where(is_east, pltpu.roll(from_east, 32, 1), pltpu.roll(from_west, 96, 1))
    both = own + other
    speed = pltpu.roll(both, 64, 1)
    speed = jnp.where((lane_c & 16) != 0, pltpu.roll(speed, 16, 1), speed)
    slope = jnp.where(is_east, 0.1, -0.1) * (other - own)
    through = 0.05 * speed * both - slope
    flux_lon[...] = through[0:ROWS, :]
    weighed = through * weight
    side_west = jnp.sum(jnp.where(lane_c < 32, weighed, 0.0), axis=1, keepdims=True)
    side_east = jnp.sum(
        jnp.where(is_east & (lane_c < 64), weighed, 0.0), axis=1, keepdims=True
    )

    is_first = (lane128 & 15) < 4
    is_north = lane128 < 64
    mine = jnp.where(is_first, recv_cols[1, 2 * ROWS :, :], recv_cols[0, 2 * ROWS :, :])
    theirs_north = jnp.where(is_first, recv_corner[3, 0:8, :], recv_corner[2, 0:8, :])
    theirs_south = jnp.where(is_first, recv_corner[1, 0:8, :], recv_corner[0, 0:8, :])
    theirs = pltpu.roll(
        jnp.where(is_north, theirs_south * exists[1], theirs_north * exists[0]), 64, 1
    )
    both = mine + theirs
    flux = 0.05 * pltpu.roll(both, 96, 1) * both - jnp.where(is_north, 0.1, -0.1) * (theirs - mine)
    flux = flux * jnp.where(
        (lane128 & 16) == 0, level_weight[0:8, 0:128], level_weight[8:16, 0:128]
    )
    flux = jnp.sum(flux, axis=0, keepdims=True)
    flux = flux + pltpu.roll(flux, 112, 1)
    for side in range(2):
        low = pltpu.roll(flux, 32 - 64 * side if side == 0 else 96, 1)
        high = pltpu.roll(flux, 120 if side == 0 else 56, 1)
        third = jnp.where(
            lane_w < 32, side_lat[side][:, 256:384], jnp.where(lane_w < 64, low, high)
        )
        side_lat[side] = jnp.concatenate([side_lat[side][:, 0:256], third], axis=1)

    def assemble(center, north_south, cols_in, base):
        lane48 = iota((ROWS, 128), 1)
        third = jnp.where(
            lane48 < 32, center[:, 256:384], jnp.where(lane48 < 64, cols_in(1), cols_in(0))
        )
        upper = jnp.concatenate([center[:, 0:256], third], axis=1)
        low = pltpu.roll(corners, 32 - base, 1)
        high = pltpu.roll(corners, 120 - base, 1)
        third = jnp.where(
            lane128 < 32, north_south[:, 256:384], jnp.where(lane128 < 64, low, high)
        )
        lower = jnp.concatenate([north_south[:, 0:256], third], axis=1)
        return jnp.concatenate([upper, lower], axis=0)

    is_low = (lane128 & 7) < 4
    corners = beside(
        jnp.where(is_low, recv_corner[3, 0:8, :], recv_corner[2, 0:8, :]),
        jnp.where(is_low, recv_corner[1, 0:8, :], recv_corner[0, 0:8, :]),
    )
    damp_ext = assemble(
        damp_all,
        jnp.where(sub < 4, recv_halo_rows[1], recv_halo_rows[0]),
        lambda slot: recv_cols[slot, ROWS : 2 * ROWS, :],
        8,
    )
    inv = mask[...] * inverse(6.0 + damp_ext)
    scale[...] = 1.5 * inv
    forcing = assemble(
        basis[1, 0:ROWS, :],
        pltpu.roll(jnp.where(sub < 4, recv_halo_rows[0], recv_halo_rows[1]), 4, 0),
        lambda slot: recv_halo_cols[slot],
        24,
    )
    forcing = jnp.concatenate(
        [
            forcing[:, 0:128] + jnp.where(lane_c == 0, side_west, 0.0),
            forcing[:, 128:256],
            forcing[:, 256:384]
            + jnp.where(
                lane_c == 31,
                -side_east,
                jnp.where(lane_c == 32, side_east, jnp.where(lane_c == 127, -side_west, 0.0)),
            ),
        ],
        axis=1,
    )
    north, south = side_lat
    forcing = jnp.concatenate(
        [
            forcing[0:8, :] + jnp.where(sub == 0, south, 0.0),
            forcing[8:40, :],
            forcing[40:48, :] - jnp.where(sub == 7, north, 0.0),
            forcing[48:56, :]
            + jnp.where(sub == 0, north, jnp.where(sub == 7, -south, 0.0)),
        ],
        axis=0,
    )
    basis[1] = forcing * inv

    def folded(value):
        rows = [value[8 * i : 8 * i + 8, :] for i in range(TILES)]
        value = (rows[0] + rows[1]) + (rows[2] + rows[3]) + (rows[4] + rows[5])
        return value[:, 0:128] + value[:, 128:256] + value[:, 256:384]

    parts = []
    for index in range(4):
        q = basis[index + 1]
        pair = east_of(q) + west_of(q)
        column = q + 0.5 * pair
        around = pair + pltpu.roll(column, EXT - 1, 0) + pltpu.roll(column, 1, 0)
        image = scale[...] * around - 0.5 * q
        after = image if index == 0 else 2.0 * image - basis[index]
        if index < 3:
            basis[index + 2] = after
        weighed = weigh[...] * q[0:ROWS, :]
        parts.append(folded(weighed * q[0:ROWS, :]))
        parts.append(folded(weighed * after[0:ROWS, :]))

    for width in (64, 32, 16):
        half = len(parts) // 2
        parts = [
            jnp.where(
                (lane128 & width) == 0,
                low + pltpu.roll(low, 128 - width, 1),
                high + pltpu.roll(high, width, 1),
            )
            for low, high in zip(parts[:half], parts[half:])
        ]
    first_message[...] = jnp.sum(parts[0], axis=0, keepdims=True)

    def spread(source, target, count, along, mine, base):
        target[mine] = source[...]

        @pl.loop(1, count)
        def _(turn):
            d = count // 2 + jnp.where(turn % 2 == 0, -(turn // 2), turn // 2)
            pltpu.make_async_remote_copy(
                src_ref=source,
                dst_ref=target.at[mine],
                send_sem=sum_send_sem.at[base],
                recv_sem=sum_recv_sem.at[base],
                device_id=device(along(d)),
                device_id_type=MESH,
            ).start()

    def gathered(target, count, base):
        part = target.at[pl.ds(0, count - 1)]
        done = pltpu.make_async_remote_copy(
            src_ref=part,
            dst_ref=part,
            send_sem=sum_send_sem.at[base],
            recv_sem=sum_recv_sem.at[base],
            device_id=device(EAST),
            device_id_type=MESH,
        )
        done.wait_recv()
        done.wait_send()
        return jnp.sum(target[...], axis=0)

    spread(first_message, first_sum, nx, lambda d: (d, 0), gx, 0)

    for copy in heat_round:
        copy.wait()
    for side, sign in ((0, 1.0), (1, -1.0)):
        slot = 1 - side
        target = flux_north if side == 0 else flux_prev
        heat_mine = send_heat[side]
        heat_theirs = recv_heat[slot] * exists[side]
        salt_mine = 2.0 * (heat_mine - send_rows[side, 0:16, :])
        salt_theirs = 2.0 * (heat_theirs - recv_rows[slot, 0:16, :] * exists[side])
        target[0:16, :] = side_flux(heat_mine, heat_theirs, speed_lat[side], sign)
        target[16:32, :] = side_flux(salt_mine, salt_theirs, speed_lat[side], sign)
    edge_lane = (lane128 == 31) | (lane128 == 127)

    def mix_tile(i, _):
        rows = pl.ds(pl.multiple_of(8 * i, 8), 8)
        row = pl.ds(next_row(i), 1)
        here = mask[rows, :]
        beyond = mask[row, :]
        through = flux_lon[rows, :]
        use_north = (sub == 7) & (i == TILES - 1)

        def level(k, carry):
            heat_low, salt_low = carry
            u = padded(state[2, k, rows, :]) * here
            v = padded(state[3, k, rows, :]) * here
            v_row = padded(state[3, k, row, :]) * beyond
            v_north = jnp.where(sub == 7, v_row, pltpu.roll(v, 7, 0))
            u_pair = 0.05 * (u + east_of(u))
            v_pair = 0.05 * (v + v_north)
            lon_far, lon_near = u_pair - 0.1, u_pair + 0.1
            lat_far, lat_near = v_pair - 0.1, v_pair + 0.1
            found = []
            for tracer, low in ((0, heat_low), (1, salt_low)):
                plane = tracer * LEV + k
                c = padded(state[tracer, k, rows, :]) * here
                c_row = padded(state[tracer, k, row, :]) * beyond
                c_north = jnp.where(sub == 7, c_row, pltpu.roll(c, 7, 0))
                lon = lon_far * east_of(c) + lon_near * c
                turned = pltpu.roll(through, 127 - plane, 1)
                lon = jnp.concatenate(
                    [lon[:, 0:256], jnp.where(edge_lane, turned, lon[:, 256:384])], axis=1
                )
                lat = lat_far * c_north + lat_near * c
                lat = jnp.where(use_north, flux_north[pl.ds(plane, 1), :], lat)
                lat_south = jnp.where(
                    sub == 0, flux_prev[pl.ds(plane, 1), :], pltpu.roll(lat, 1, 0)
                )
                flux_prev[pl.ds(plane, 1), :] = lat[7:8, :]
                advected = c - (lon - west_of(lon)) - (lat - lat_south)
                value = taken[k, rows, :] * advected + carried[k, rows, :] * low
                tracer_out[tracer, k, rows, :] = value[:, 0:COLS]
                found.append(value)
            return found[0], found[1]

        zero = jnp.zeros((8, WIDE), f32)
        heat, salt = lax.fori_loop(0, LEV, level, (zero, zero), unroll=4)

        def back(step, carry):
            k = LEV - 2 - step
            heat_up, salt_up = carry
            share = ratio[k, rows, 0:COLS]
            heat_up = tracer_out[0, k, rows, :] + share * heat_up
            salt_up = tracer_out[1, k, rows, :] + share * salt_up
            tracer_out[0, k, rows, :] = heat_up
            tracer_out[1, k, rows, :] = salt_up
            return heat_up, salt_up

        lax.fori_loop(0, LEV - 1, back, (heat[:, 0:COLS], salt[:, 0:COLS]), unroll=5)
        return 0

    lax.fori_loop(0, 1, mix_tile, 0)
    second_message[...] = gathered(first_sum, nx, 0)
    spread(second_message, second_sum, ny, lambda d: (0, d), gy, 1)
    lax.fori_loop(1, TILES, mix_tile, 0)
    sums = gathered(second_sum, ny, 1)

    own_lanes = lane128 // 16 == iota((8, 128), 0)
    sums = jnp.where(own_lanes, jnp.broadcast_to(sums, (8, 128)), 0.0)
    sums = jnp.broadcast_to(jnp.sum(sums, axis=1, keepdims=True), (8, 128))
    dots = [sums[i : i + 1, :] for i in range(8)]
    moment = dots[0:2] + [2.0 * dots[i] - dots[i % 2] for i in range(2, 8)]

    def gram(i, j):
        return 0.5 * (moment[i + j] + moment[abs(i - j)])

    lower = {}
    pivots = []
    right = []
    for i in range(4):
        value = moment[i]
        for j in range(i + 1):
            entry = gram(i, j) - 0.5 * (gram(j, i + 1) + gram(j, abs(i - 1)))
            for k in range(j):
                entry = entry - lower[i, k] * lower[j, k] * pivots[k]
            if j < i:
                lower[i, j] = entry / pivots[j]
                value = value - lower[i, j] * right[j]
            else:
                pivots.append(entry)
        right.append(value)
    solved = [None] * 4
    for i in range(3, -1, -1):
        value = right[i] / pivots[i]
        for j in range(i + 1, 4):
            value = value - lower[j, i] * solved[j]
        solved[i] = value
    surface = None
    for i in range(4):
        factor = 1.5 * solved[i]
        factor = jnp.concatenate([factor, factor, factor], axis=1)
        term = factor * basis[i + 1, 0:ROWS, :]
        surface = term if surface is None else surface + term
    surface_out[...] = surface[:, 0:COLS]


def store(tracer, surface, tracer_out, surface_out, sems):
    copies = [pltpu.make_async_copy(surface, surface_out, sems.at[8])]
    for index in range(8):
        levels = pl.ds(4 * (index % 4), 4)
        copies.append(
            pltpu.make_async_copy(
                tracer.at[index // 4, levels], tracer_out.at[index // 4, levels], sems.at[index]
            )
        )
    for copy in copies:
        copy.start()
    for copy in copies:
        copy.wait()


def scratch(nx, ny):
    vmem = lambda *shape: pltpu.VMEM(shape, f32)
    dma = pltpu.SemaphoreType.DMA
    return [
        vmem(4, LEV, ROWS, COLS),
        pltpu.SMEM((LEV,), f32),
        vmem(ROWS, COLS),
        vmem(ROWS, COLS),
        None,
        vmem(EXT, WIDE),
        vmem(24, WIDE),
        vmem(3, ROWS, WIDE),
        vmem(2, ROWS, 128),
        vmem(2, 32, WIDE),
        vmem(2, 72, 128),
        vmem(2, LEV, WIDE),
        vmem(2, 72, 128),
        vmem(2, 32, WIDE),
        vmem(2, LEV, WIDE),
        vmem(2 * ROWS + 8, 128),
        vmem(2, 2 * ROWS + 8, 128),
        vmem(16, 128),
        vmem(4, 16, 128),
        vmem(2, 8, 128),
        vmem(ROWS, 128),
        vmem(2 * LEV, WIDE),
        vmem(2 * LEV, WIDE),
        vmem(LEV, ROWS, WIDE),
        vmem(LEV, ROWS, WIDE),
        vmem(LEV, ROWS, WIDE),
        vmem(EXT, WIDE),
        vmem(ROWS, WIDE),
        vmem(6, EXT, WIDE),
        vmem(2, 8, WIDE),
        vmem(ROWS, 128),
        vmem(2, 8, WIDE),
        vmem(2, ROWS, 128),
        vmem(1, 128),
        vmem(nx, 1, 128),
        vmem(1, 128),
        vmem(ny, 1, 128),
        dma((4,)),
        dma((4,)),
        dma((12,)),
        dma((12,)),
        dma((8,)),
        dma((8,)),
        dma((2,)),
        dma((2,)),
    ]


def solution(mesh):
    nx, ny = mesh.shape["gx"], mesh.shape["gy"]

    def body(ocean_state, layer_thickness, vertical_mixing, damping, ocean_blocks):
        shapes = scratch(nx, ny)
        shapes[4] = pltpu.VMEM(ocean_blocks.shape, jnp.int32)
        call = pl.pallas_call(
            functools.partial(kernel, nx, ny),
            out_shape=[
                pltpu.VMEM((2, LEV, ROWS, COLS), f32),
                pltpu.VMEM((ROWS, COLS), f32),
            ],
            in_specs=[pl.BlockSpec(memory_space=pltpu.HBM)] * 5,
            out_specs=[pl.BlockSpec(memory_space=pltpu.VMEM)] * 2,
            scratch_shapes=shapes,
            compiler_params=pltpu.CompilerParams(
                collective_id=0, has_side_effects=True, vmem_limit_bytes=32 * 1024 * 1024
            ),
        )
        operands = [
            pltpu.with_memory_space_constraint(operand, pltpu.HBM)
            for operand in (ocean_state, layer_thickness, vertical_mixing, damping, ocean_blocks)
        ]
        tracer, surface = call(*operands)
        return tuple(
            pl.pallas_call(
                store,
                out_shape=[
                    jax.ShapeDtypeStruct((2, LEV, ROWS, COLS), f32),
                    jax.ShapeDtypeStruct((ROWS, COLS), f32),
                ],
                in_specs=[pl.BlockSpec(memory_space=pltpu.VMEM)] * 2,
                out_specs=[pl.BlockSpec(memory_space=pltpu.HBM)] * 2,
                scratch_shapes=[pltpu.SemaphoreType.DMA((9,))],
                compiler_params=pltpu.CompilerParams(vmem_limit_bytes=16 * 1024 * 1024),
            )(tracer, surface)
        )

    def wrapped(*args):
        with jax.sharding.use_abstract_mesh(mesh.abstract_mesh):
            return jax.shard_map(
                body,
                mesh=mesh,
                in_specs=(P(None, None, "gy", "gx"), P(), P("gy", "gx"), P("gy", "gx"), P()),
                out_specs=(P(None, None, "gy", "gx"), P("gy", "gx")),
                check_vma=False,
            )(*args)

    return wrapped
```

```python
import functools

import jax
import jax.numpy as jnp
from jax import lax
from jax.experimental import pallas as pl
from jax.experimental.pallas import tpu as pltpu
from jax.sharding import PartitionSpec as P

BLAT = 24
BLON = 36
LEV = 16
ROWS = 48
COLS = 288
WIDE = 384
EXT = 56
TILES = ROWS // 8

f32 = jnp.float32
MESH = pl.DeviceIdType.MESH

NORTH, SOUTH, EAST, WEST = (0, 1), (0, -1), (1, 0), (-1, 0)
DIAGONAL = ((1, 1), (-1, 1), (1, -1), (-1, -1))


def iota(shape, dim):
    return lax.broadcasted_iota(jnp.int32, shape, dim)


def padded(value):
    return jnp.concatenate([value, jnp.zeros((value.shape[0], WIDE - COLS), f32)], axis=1)


def east_of(value):
    return pltpu.roll(value, WIDE - 1, 1)


def west_of(value):
    return pltpu.roll(value, 1, 1)


def inverse(value):
    guess = pl.reciprocal(value, approx=True)
    return guess * (2.0 - value * guess)


def row_pack(low, high):
    return jnp.where(iota(low.shape, 0) < 4, low, high)


def column_pack(first, last):
    lane = iota(first.shape, 1)
    low = pltpu.roll(first, 32, 1)
    high = pltpu.roll(last, 96, 1)
    return jnp.where(
        (lane >= 32) & (lane < 36), low, jnp.where(lane >= 124, high, 0.0)
    )


def kernel(
    nx,
    ny,
    ocean,
    thick,
    mixing,
    damping,
    blocks,
    tracer_out,
    surface_out,
    state,
    h,
    mix,
    damp,
    blk,
    mask,
    level_inv,
    flat,
    ends,
    send_rows,
    send_strip,
    send_heat,
    recv_strip,
    recv_rows,
    recv_heat,
    send_cols,
    recv_cols,
    send_corner,
    recv_corner,
    recv_side,
    flux_lon,
    flux_north,
    flux_prev,
    ratio,
    carried,
    taken,
    scale,
    weigh,
    basis,
    halo_rows,
    halo_cols,
    recv_halo_rows,
    recv_halo_cols,
    first_message,
    first_sum,
    second_message,
    second_sum,
    load_sem,
    small_sem,
    send_sem,
    recv_sem,
    halo_send_sem,
    halo_recv_sem,
    sum_send_sem,
    sum_recv_sem,
):
    gx = lax.axis_index("gx")
    gy = lax.axis_index("gy")

    def device(step):
        return {"gx": lax.rem(gx + step[0] + nx, nx), "gy": lax.rem(gy + step[1] + ny, ny)}

    def greet(step):
        pl.semaphore_signal(barrier, inc=1, device_id=device(step), device_id_type=MESH)

    small = [
        pltpu.make_async_copy(blocks, blk, small_sem.at[0]),
        pltpu.make_async_copy(thick, h, small_sem.at[1]),
        pltpu.make_async_copy(damping, damp, small_sem.at[2]),
        pltpu.make_async_copy(mixing, mix, small_sem.at[3]),
    ]
    group = LEV // 4

    def load(index):
        levels = pl.ds(group * index, group)
        return pltpu.make_async_copy(
            ocean.at[:, levels, :, :], state.at[:, levels, :, :], load_sem.at[index]
        )

    for copy in small[:3] + [load(index) for index in range(4)] + small[3:]:
        copy.start()

    barrier = pltpu.get_barrier_semaphore()
    for step in DIAGONAL:
        greet(step)
    def nearest(turn, count):
        return jnp.where(turn % 2 == 1, (turn + 1) // 2, count - turn // 2)

    pl.loop(1, ny)(lambda turn: greet((0, nearest(turn, ny))))
    pl.loop(1, nx)(lambda turn: greet((nearest(turn, nx), 0)))
    partners = len(DIAGONAL) + nx - 1 + ny - 1

    block_rows, block_cols = blk.shape
    small[0].wait()
    row = iota((EXT, block_rows), 0)
    row = gy * ROWS + jnp.where(row < ROWS + 4, row, row - EXT)
    edge = iota((EXT, block_rows), 1) * BLAT
    pick_rows = jnp.where((row >= edge) & (row < edge + BLAT), 1.0, 0.0)
    lane = iota((block_cols, WIDE), 1)
    total = block_cols * BLON
    col = gx * COLS + jnp.where(lane < COLS + 4, lane, lane - WIDE)
    col = jnp.where(col < 0, col + total, jnp.where(col >= total, col - total, col))
    edge = iota((block_cols, WIDE), 0) * BLON
    inside = (lane < COLS + 4) | (lane >= WIDE - 4)
    pick_cols = jnp.where(inside & (col >= edge) & (col < edge + BLON), 1.0, 0.0)
    coarse = jnp.dot(pick_rows, blk[...].astype(f32), preferred_element_type=f32)
    mask[...] = jnp.dot(coarse, pick_cols, preferred_element_type=f32)

    small[1].wait()
    small[2].wait()
    damp_low = padded(damp[0:8, :])
    damp_high = padded(damp[ROWS - 8 : ROWS, :])
    damp_rows = row_pack(damp_low, damp_high)
    damp_all = padded(damp[...])
    send_cols[ROWS : 2 * ROWS, :] = column_pack(damp_all[:, 0:128], damp_all[:, 256:384])

    def remote(source, target, index, step, sends=send_sem, recvs=recv_sem):
        return pltpu.make_async_remote_copy(
            src_ref=source,
            dst_ref=target,
            send_sem=sends.at[index],
            recv_sem=recvs.at[index],
            device_id=device(step),
            device_id_type=MESH,
        )

    sub = iota((8, WIDE), 0)
    lane128 = iota((8, 128), 1)

    def next_row(i):
        return jnp.minimum(8 * i + 8, ROWS - 1)

    tiles = [pl.ds(8 * i, 8) for i in range(TILES)]
    flat[...] = jnp.zeros(flat.shape, f32)
    ends[...] = jnp.zeros(ends.shape, f32)
    end_mask = [
        jnp.where(lane128 == 31, mask[rows, 256:384], mask[rows, 0:128]) for rows in tiles
    ]

    def pack_ends(pair):
        for i, rows in enumerate(tiles):
            west, east = ends[0, rows, :], ends[1, rows, :]
            for k in (2 * pair, 2 * pair + 1):
                for field, base in ((0, 0), (1, 16), (2, 64)):
                    last = jnp.concatenate(
                        [state[field, k, rows, 256:COLS], jnp.zeros((8, WIDE - COLS), f32)], axis=1
                    )
                    both = jnp.where(lane128 == 31, last, state[field, k, rows, 0:128])
                    both = pltpu.roll(both * end_mask[i], base + k, 1)
                    west = jnp.where(lane128 == base + k, both, west)
                    east = jnp.where(lane128 == base + k + 31, both, east)
            ends[0, rows, :] = west
            ends[1, rows, :] = east


    def turned_up(values):
        turned = [pltpu.roll(value, 7, 0) for value in values]
        return [
            jnp.where(sub == 7, turned[(i + 1) % TILES], turned[i]) for i in range(TILES)
        ]

    @pl.loop(0, LEV // 2)
    def _(pair):
        @pl.when(lax.rem(pair, group // 2) == 0)
        def _():
            load(pair // (group // 2)).wait()

        sums = None
        for k in (2 * pair, 2 * pair + 1):
            s = [
                padded(state[0, k, rows, :] - 0.5 * state[1, k, rows, :]) * mask[rows, :] * h[k]
                for rows in tiles
            ]
            v = [padded(state[3, k, rows, :]) * mask[rows, :] for rows in tiles]
            s_north, v_north = turned_up(s), turned_up(v)
            found = []
            for i, rows in enumerate(tiles):
                u = padded(state[2, k, rows, :]) * mask[rows, :]
                found.append(
                    (
                        s[i],
                        (u + east_of(u)) * (s[i] + east_of(s[i])),
                        (v[i] + v_north[i]) * (s[i] + s_north[i]),
                    )
                )
            if sums is None:
                sums = found
            else:
                sums = [[a + b for a, b in zip(x, y)] for x, y in zip(sums, found)]
        for i, rows in enumerate(tiles):
            for part in range(3):
                flat[part, rows, :] += sums[i][part]
        pack_ends(pair)

    first_round = []
    for side, (edge_row, step) in enumerate(((ROWS - 1, NORTH), (0, SOUTH))):
        edge_mask = mask[edge_row : edge_row + 1, :]
        heat = padded(state[0, :, edge_row, :]) * edge_mask
        salt = padded(state[1, :, edge_row, :]) * edge_mask
        send_heat[side] = heat
        send_rows[side, 0:16, :] = heat - 0.5 * salt
        send_rows[side, 16:32, :] = padded(state[3, :, edge_row, :]) * edge_mask
        send_strip[side, 0:32, :] = send_rows[side, :, 0:128]
        send_strip[side, 32:64, :] = send_rows[side, :, 128:256]
        tail = jnp.zeros((8, 128), f32)
        for part in range(4):
            third = send_rows[side, 8 * part : 8 * part + 8, 256:384]
            tail = jnp.where(lane128 // 32 == part, pltpu.roll(third, 32 * part, 1), tail)
        send_strip[side, 64:72, :] = tail
        first_round.append(remote(send_strip.at[side], recv_strip.at[side], side, step))

    pl.semaphore_wait(barrier, partners)
    for copy in first_round:
        copy.start()

    send_cols[0:ROWS, :] = ends[0] + pltpu.roll(ends[1], 1, 1)

    compact = jnp.zeros((8, 128), f32)
    for side in range(2):
        for part in range(4):
            j = 4 * side + part
            rows = pl.ds(8 * part, 8)
            first = pltpu.roll(send_rows[side, rows, 0:128], 16 * j, 1)
            last = pltpu.roll(send_rows[side, rows, 256:384], (16 * j - 24) % 128, 1)
            inside = lane128 // 16 == j
            compact = jnp.where(inside & (lane128 % 16 < 4), first, compact)
            compact = jnp.where(
                inside & (lane128 % 16 >= 4) & (lane128 % 16 < 8), last, compact
            )
    send_cols[2 * ROWS :, :] = compact
    send_corner[8:16, :] = row_pack(send_cols[0:8, :], send_cols[ROWS - 8 : ROWS, :])

    second_round = []
    for side, step in enumerate((EAST, WEST)):
        second_round.append(remote(send_cols, recv_cols.at[side], 2 + side, step))
    for side, step in enumerate((NORTH, SOUTH)):
        second_round.append(
            remote(send_corner.at[pl.ds(8, 8)], recv_side.at[side], 10 + side, step)
        )
    for copy in second_round:
        copy.start()
    first_round = first_round + second_round

    lane_f = iota((ROWS, WIDE), 1)
    row_f = iota((ROWS, WIDE), 0)
    plain = flat[0]
    lon = 0.05 * flat[1] - 0.1 * (east_of(plain) - plain)
    lon = jnp.where(lane_f < COLS - 1, lon, 0.0)
    lat = 0.05 * flat[2] - 0.1 * (pltpu.roll(plain, ROWS - 1, 0) - plain)
    lat = jnp.where(row_f == ROWS - 1, 0.0, lat)
    start = plain - (lon - west_of(lon)) - (lat - pltpu.roll(lat, 1, 0))
    start = jnp.where(lane_f < COLS, start, 0.0)
    basis[1, 0:ROWS, :] = start
    packed_rows = row_pack(start[0:8, :], start[ROWS - 8 : ROWS, :])
    halo_rows[0] = jnp.where(sub < 4, pltpu.roll(start[ROWS - 8 : ROWS, :], 4, 0), damp_high)
    halo_rows[1] = jnp.where(sub < 4, damp_low, pltpu.roll(start[0:8, :], 4, 0))
    halo_cols[...] = column_pack(start[:, 0:128], start[:, 256:384])
    for base, packed in ((8, damp_rows), (24, packed_rows)):
        first = pltpu.roll(packed[:, 0:128], base, 1)
        last = packed[:, 256:384]
        last = pltpu.roll(last, (base - 24) % 128, 1) if base != 24 else last
        compact = jnp.where((lane128 >= base) & (lane128 < base + 4), first, compact)
        compact = jnp.where((lane128 >= base + 4) & (lane128 < base + 8), last, compact)
    send_corner[0:8, :] = compact
    second_round = []
    for place, step in enumerate(DIAGONAL):
        second_round.append(
            remote(
                send_corner,
                recv_corner.at[place],
                4 + place,
                step,
                halo_send_sem,
                halo_recv_sem,
            )
        )
    for side, step in enumerate((NORTH, SOUTH)):
        second_round.append(
            remote(
                halo_rows.at[side], recv_halo_rows.at[side], side, step, halo_send_sem, halo_recv_sem
            )
        )
    for side, step in enumerate((EAST, WEST)):
        second_round.append(
            remote(halo_cols, recv_halo_cols.at[side], 2 + side, step, halo_send_sem, halo_recv_sem)
        )
    for copy in second_round:
        copy.start()
    heat_round = []
    for side, step in enumerate((NORTH, SOUTH)):
        copy = remote(send_heat.at[side], recv_heat.at[side], 8 + side, step)
        copy.start()
        heat_round.append(copy)

    level_inv[...] = jnp.zeros(level_inv.shape, f32)

    @pl.loop(1, LEV)
    def _(k):
        level_inv[pl.ds(k, 1), :] = 1.0 / jnp.full((1, WIDE), h[k - 1] + h[k], f32)


    weight = jnp.zeros((1, 128), f32)
    lane_w = iota((1, 128), 1)
    for k in range(LEV):
        weight = jnp.where((lane_w & 15) == k, h[k], weight)
    weight = weight * jnp.where((lane_w & 16) != 0, -0.5, 1.0)
    level_weight = jnp.zeros((LEV, WIDE), f32)
    level_row = iota((LEV, WIDE), 0)
    for k in range(LEV):
        level_weight = jnp.where(level_row == k, h[k], level_weight)
    exists = (
        jnp.where(gy < ny - 1, 1.0, 0.0).astype(f32),
        jnp.where(gy > 0, 1.0, 0.0).astype(f32),
    )

    weigh[...] = jnp.where(iota((ROWS, WIDE), 1) < COLS, 6.0 + damp_all, 0.0)

    small[3].wait()

    @pl.loop(0, 2)
    def _(part):
        rows = pl.ds(pl.multiple_of(ROWS // 2 * part, 8), ROWS // 2)
        coefficient = padded(mix[rows, :])
        here = mask[rows, :]

        def level(k, ratio_low):
            below = coefficient * level_inv[pl.ds(k, 1), :]
            above = coefficient * level_inv[pl.ds(k + 1, 1), :]
            pivot = inverse(h[k] + above + below * (1.0 - ratio_low))
            ratio_now = above * pivot
            ratio[k, rows, :] = ratio_now
            carried[k, rows, :] = below * pivot
            taken[k, rows, :] = h[k] * pivot * here
            return ratio_now

        lax.fori_loop(0, LEV, level, jnp.zeros((ROWS // 2, WIDE), f32), unroll=4)

    for copy in first_round:
        copy.wait()
    for slot in range(2):
        recv_rows[slot, :, 0:128] = recv_strip[slot, 0:32, :]
        recv_rows[slot, :, 128:256] = recv_strip[slot, 32:64, :]
        for part in range(4):
            tail = recv_strip[slot, 64:72, :]
            tail = pltpu.roll(tail, 128 - 32 * part, 1) if part else tail
            recv_rows[slot, 8 * part : 8 * part + 8, 256:384] = jnp.where(lane128 < 32, tail, 0.0)

    def side_flux(mine, theirs, speeds, sign):
        return speeds * (mine + theirs) - (0.1 * sign) * (theirs - mine)

    side_lat = []
    speed_lat = []
    for side, sign in ((0, 1.0), (1, -1.0)):
        slot = 1 - side
        s_mine = send_rows[side, 0:16, :]
        s_theirs = recv_rows[slot, 0:16, :] * exists[side]
        speeds = 0.05 * (send_rows[side, 16:32, :] + recv_rows[slot, 16:32, :] * exists[side])
        speed_lat.append(speeds)
        flux = side_flux(s_mine, s_theirs, speeds, sign)
        side_lat.append(jnp.sum(flux * level_weight, axis=0, keepdims=True))

    for copy in second_round:
        copy.wait()

    def beside(north, south):
        return jnp.where(iota((8, 128), 0) < 4, north, south)

    own = jnp.concatenate([send_cols[0:ROWS, :], beside(recv_side[1], recv_side[0])], axis=0)
    from_east = jnp.concatenate(
        [recv_cols[1, 0:ROWS, :], beside(recv_corner[3, 8:16, :], recv_corner[1, 8:16, :])], axis=0
    )
    from_west = jnp.concatenate(
        [recv_cols[0, 0:ROWS, :], beside(recv_corner[2, 8:16, :], recv_corner[0, 8:16, :])], axis=0
    )
    lane_c = iota((EXT, 128), 1)
    is_east = (lane_c & 32) != 0
    other = jnp.where(is_east, pltpu.roll(from_east, 32, 1), pltpu.roll(from_west, 96, 1))
    both = own + other
    speed = pltpu.roll(both, 64, 1)
    speed = jnp.where((lane_c & 16) != 0, pltpu.roll(speed, 16, 1), speed)
    slope = jnp.where(is_east, 0.1, -0.1) * (other - own)
    through = 0.05 * speed * both - slope
    flux_lon[...] = through[0:ROWS, :]
    weighed = through * weight
    side_west = jnp.sum(jnp.where(lane_c < 32, weighed, 0.0), axis=1, keepdims=True)
    side_east = jnp.sum(
        jnp.where(is_east & (lane_c < 64), weighed, 0.0), axis=1, keepdims=True
    )

    is_first = (lane128 & 15) < 4
    is_north = lane128 < 64
    mine = jnp.where(is_first, recv_cols[1, 2 * ROWS :, :], recv_cols[0, 2 * ROWS :, :])
    theirs_north = jnp.where(is_first, recv_corner[3, 0:8, :], recv_corner[2, 0:8, :])
    theirs_south = jnp.where(is_first, recv_corner[1, 0:8, :], recv_corner[0, 0:8, :])
    theirs = pltpu.roll(
        jnp.where(is_north, theirs_south * exists[1], theirs_north * exists[0]), 64, 1
    )
    both = mine + theirs
    flux = 0.05 * pltpu.roll(both, 96, 1) * both - jnp.where(is_north, 0.1, -0.1) * (theirs - mine)
    flux = flux * jnp.where(
        (lane128 & 16) == 0, level_weight[0:8, 0:128], level_weight[8:16, 0:128]
    )
    flux = jnp.sum(flux, axis=0, keepdims=True)
    flux = flux + pltpu.roll(flux, 112, 1)
    for side in range(2):
        low = pltpu.roll(flux, 32 - 64 * side if side == 0 else 96, 1)
        high = pltpu.roll(flux, 120 if side == 0 else 56, 1)
        third = jnp.where(
            lane_w < 32, side_lat[side][:, 256:384], jnp.where(lane_w < 64, low, high)
        )
        side_lat[side] = jnp.concatenate([side_lat[side][:, 0:256], third], axis=1)

    def assemble(center, north_south, cols_in, base):
        lane48 = iota((ROWS, 128), 1)
        third = jnp.where(
            lane48 < 32, center[:, 256:384], jnp.where(lane48 < 64, cols_in(1), cols_in(0))
        )
        upper = jnp.concatenate([center[:, 0:256], third], axis=1)
        low = pltpu.roll(corners, 32 - base, 1)
        high = pltpu.roll(corners, 120 - base, 1)
        third = jnp.where(
            lane128 < 32, north_south[:, 256:384], jnp.where(lane128 < 64, low, high)
        )
        lower = jnp.concatenate([north_south[:, 0:256], third], axis=1)
        return jnp.concatenate([upper, lower], axis=0)

    is_low = (lane128 & 7) < 4
    corners = beside(
        jnp.where(is_low, recv_corner[3, 0:8, :], recv_corner[2, 0:8, :]),
        jnp.where(is_low, recv_corner[1, 0:8, :], recv_corner[0, 0:8, :]),
    )
    damp_ext = assemble(
        damp_all,
        jnp.where(sub < 4, recv_halo_rows[1], recv_halo_rows[0]),
        lambda slot: recv_cols[slot, ROWS : 2 * ROWS, :],
        8,
    )
    inv = mask[...] * inverse(6.0 + damp_ext)
    scale[...] = 1.5 * inv
    forcing = assemble(
        basis[1, 0:ROWS, :],
        pltpu.roll(jnp.where(sub < 4, recv_halo_rows[0], recv_halo_rows[1]), 4, 0),
        lambda slot: recv_halo_cols[slot],
        24,
    )
    forcing = jnp.concatenate(
        [
            forcing[:, 0:128] + jnp.where(lane_c == 0, side_west, 0.0),
            forcing[:, 128:256],
            forcing[:, 256:384]
            + jnp.where(
                lane_c == 31,
                -side_east,
                jnp.where(lane_c == 32, side_east, jnp.where(lane_c == 127, -side_west, 0.0)),
            ),
        ],
        axis=1,
    )
    north, south = side_lat
    forcing = jnp.concatenate(
        [
            forcing[0:8, :] + jnp.where(sub == 0, south, 0.0),
            forcing[8:40, :],
            forcing[40:48, :] - jnp.where(sub == 7, north, 0.0),
            forcing[48:56, :]
            + jnp.where(sub == 0, north, jnp.where(sub == 7, -south, 0.0)),
        ],
        axis=0,
    )
    basis[1] = forcing * inv

    def folded(value):
        rows = [value[8 * i : 8 * i + 8, :] for i in range(TILES)]
        value = (rows[0] + rows[1]) + (rows[2] + rows[3]) + (rows[4] + rows[5])
        return value[:, 0:128] + value[:, 128:256] + value[:, 256:384]

    parts = []
    for index in range(4):
        q = basis[index + 1]
        pair = east_of(q) + west_of(q)
        column = q + 0.5 * pair
        around = pair + pltpu.roll(column, EXT - 1, 0) + pltpu.roll(column, 1, 0)
        image = scale[...] * around - 0.5 * q
        after = image if index == 0 else 2.0 * image - basis[index]
        if index < 3:
            basis[index + 2] = after
        weighed = weigh[...] * q[0:ROWS, :]
        parts.append(folded(weighed * q[0:ROWS, :]))
        parts.append(folded(weighed * after[0:ROWS, :]))

    for width in (64, 32, 16):
        half = len(parts) // 2
        parts = [
            jnp.where(
                (lane128 & width) == 0,
                low + pltpu.roll(low, 128 - width, 1),
                high + pltpu.roll(high, width, 1),
            )
            for low, high in zip(parts[:half], parts[half:])
        ]
    first_message[...] = jnp.sum(parts[0], axis=0, keepdims=True)

    def spread(source, target, count, along, mine, base):
        target[mine] = source[...]

        @pl.loop(1, count)
        def _(turn):
            d = count // 2 + jnp.where(turn % 2 == 0, -(turn // 2), turn // 2)
            pltpu.make_async_remote_copy(
                src_ref=source,
                dst_ref=target.at[mine],
                send_sem=sum_send_sem.at[base],
                recv_sem=sum_recv_sem.at[base],
                device_id=device(along(d)),
                device_id_type=MESH,
            ).start()

    def gathered(target, count, base):
        part = target.at[pl.ds(0, count - 1)]
        done = pltpu.make_async_remote_copy(
            src_ref=part,
            dst_ref=part,
            send_sem=sum_send_sem.at[base],
            recv_sem=sum_recv_sem.at[base],
            device_id=device(EAST),
            device_id_type=MESH,
        )
        done.wait_recv()
        done.wait_send()
        return jnp.sum(target[...], axis=0)

    spread(first_message, first_sum, nx, lambda d: (d, 0), gx, 0)

    for copy in heat_round:
        copy.wait()
    for side, sign in ((0, 1.0), (1, -1.0)):
        slot = 1 - side
        target = flux_north if side == 0 else flux_prev
        heat_mine = send_heat[side]
        heat_theirs = recv_heat[slot] * exists[side]
        salt_mine = 2.0 * (heat_mine - send_rows[side, 0:16, :])
        salt_theirs = 2.0 * (heat_theirs - recv_rows[slot, 0:16, :] * exists[side])
        target[0:16, :] = side_flux(heat_mine, heat_theirs, speed_lat[side], sign)
        target[16:32, :] = side_flux(salt_mine, salt_theirs, speed_lat[side], sign)
    edge_lane = (lane128 == 31) | (lane128 == 127)

    def mix_tile(i, _):
        rows = pl.ds(pl.multiple_of(8 * i, 8), 8)
        row = pl.ds(next_row(i), 1)
        here = mask[rows, :]
        beyond = mask[row, :]
        through = flux_lon[rows, :]
        use_north = (sub == 7) & (i == TILES - 1)

        def level(k, carry):
            heat_low, salt_low = carry
            u = padded(state[2, k, rows, :]) * here
            v = padded(state[3, k, rows, :]) * here
            v_row = padded(state[3, k, row, :]) * beyond
            v_north = jnp.where(sub == 7, v_row, pltpu.roll(v, 7, 0))
            u_pair = 0.05 * (u + east_of(u))
            v_pair = 0.05 * (v + v_north)
            lon_far, lon_near = u_pair - 0.1, u_pair + 0.1
            lat_far, lat_near = v_pair - 0.1, v_pair + 0.1
            found = []
            for tracer, low in ((0, heat_low), (1, salt_low)):
                plane = tracer * LEV + k
                c = padded(state[tracer, k, rows, :]) * here
                c_row = padded(state[tracer, k, row, :]) * beyond
                c_north = jnp.where(sub == 7, c_row, pltpu.roll(c, 7, 0))
                lon = lon_far * east_of(c) + lon_near * c
                turned = pltpu.roll(through, 127 - plane, 1)
                lon = jnp.concatenate(
                    [lon[:, 0:256], jnp.where(edge_lane, turned, lon[:, 256:384])], axis=1
                )
                lat = lat_far * c_north + lat_near * c
                lat = jnp.where(use_north, flux_north[pl.ds(plane, 1), :], lat)
                lat_south = jnp.where(
                    sub == 0, flux_prev[pl.ds(plane, 1), :], pltpu.roll(lat, 1, 0)
                )
                flux_prev[pl.ds(plane, 1), :] = lat[7:8, :]
                advected = c - (lon - west_of(lon)) - (lat - lat_south)
                value = taken[k, rows, :] * advected + carried[k, rows, :] * low
                tracer_out[tracer, k, rows, :] = value[:, 0:COLS]
                found.append(value)
            return found[0], found[1]

        zero = jnp.zeros((8, WIDE), f32)
        heat, salt = lax.fori_loop(0, LEV, level, (zero, zero), unroll=4)

        def back(step, carry):
            k = LEV - 2 - step
            heat_up, salt_up = carry
            share = ratio[k, rows, 0:COLS]
            heat_up = tracer_out[0, k, rows, :] + share * heat_up
            salt_up = tracer_out[1, k, rows, :] + share * salt_up
            tracer_out[0, k, rows, :] = heat_up
            tracer_out[1, k, rows, :] = salt_up
            return heat_up, salt_up

        lax.fori_loop(0, LEV - 1, back, (heat[:, 0:COLS], salt[:, 0:COLS]), unroll=5)
        return 0

    lax.fori_loop(0, 2, mix_tile, 0)
    second_message[...] = gathered(first_sum, nx, 0)
    spread(second_message, second_sum, ny, lambda d: (0, d), gy, 1)
    lax.fori_loop(2, TILES, mix_tile, 0)
    sums = gathered(second_sum, ny, 1)

    own_lanes = lane128 // 16 == iota((8, 128), 0)
    sums = jnp.where(own_lanes, jnp.broadcast_to(sums, (8, 128)), 0.0)
    sums = jnp.broadcast_to(jnp.sum(sums, axis=1, keepdims=True), (8, 128))
    dots = [sums[i : i + 1, :] for i in range(8)]
    moment = dots[0:2] + [2.0 * dots[i] - dots[i % 2] for i in range(2, 8)]

    def gram(i, j):
        return 0.5 * (moment[i + j] + moment[abs(i - j)])

    lower = {}
    pivots = []
    right = []
    for i in range(4):
        value = moment[i]
        for j in range(i + 1):
            entry = gram(i, j) - 0.5 * (gram(j, i + 1) + gram(j, abs(i - 1)))
            for k in range(j):
                entry = entry - lower[i, k] * lower[j, k] * pivots[k]
            if j < i:
                lower[i, j] = entry / pivots[j]
                value = value - lower[i, j] * right[j]
            else:
                pivots.append(entry)
        right.append(value)
    solved = [None] * 4
    for i in range(3, -1, -1):
        value = right[i] / pivots[i]
        for j in range(i + 1, 4):
            value = value - lower[j, i] * solved[j]
        solved[i] = value
    surface = None
    for i in range(4):
        factor = 1.5 * solved[i]
        factor = jnp.concatenate([factor, factor, factor], axis=1)
        term = factor * basis[i + 1, 0:ROWS, :]
        surface = term if surface is None else surface + term
    surface_out[...] = surface[:, 0:COLS]


def store(tracer, surface, tracer_out, surface_out, sems):
    copies = [pltpu.make_async_copy(surface, surface_out, sems.at[8])]
    for index in range(8):
        levels = pl.ds(4 * (index % 4), 4)
        copies.append(
            pltpu.make_async_copy(
                tracer.at[index // 4, levels], tracer_out.at[index // 4, levels], sems.at[index]
            )
        )
    for copy in copies:
        copy.start()
    for copy in copies:
        copy.wait()


def scratch(nx, ny):
    vmem = lambda *shape: pltpu.VMEM(shape, f32)
    dma = pltpu.SemaphoreType.DMA
    return [
        vmem(4, LEV, ROWS, COLS),
        pltpu.SMEM((LEV,), f32),
        vmem(ROWS, COLS),
        vmem(ROWS, COLS),
        None,
        vmem(EXT, WIDE),
        vmem(24, WIDE),
        vmem(3, ROWS, WIDE),
        vmem(2, ROWS, 128),
        vmem(2, 32, WIDE),
        vmem(2, 72, 128),
        vmem(2, LEV, WIDE),
        vmem(2, 72, 128),
        vmem(2, 32, WIDE),
        vmem(2, LEV, WIDE),
        vmem(2 * ROWS + 8, 128),
        vmem(2, 2 * ROWS + 8, 128),
        vmem(16, 128),
        vmem(4, 16, 128),
        vmem(2, 8, 128),
        vmem(ROWS, 128),
        vmem(2 * LEV, WIDE),
        vmem(2 * LEV, WIDE),
        vmem(LEV, ROWS, WIDE),
        vmem(LEV, ROWS, WIDE),
        vmem(LEV, ROWS, WIDE),
        vmem(EXT, WIDE),
        vmem(ROWS, WIDE),
        vmem(6, EXT, WIDE),
        vmem(2, 8, WIDE),
        vmem(ROWS, 128),
        vmem(2, 8, WIDE),
        vmem(2, ROWS, 128),
        vmem(1, 128),
        vmem(nx, 1, 128),
        vmem(1, 128),
        vmem(ny, 1, 128),
        dma((4,)),
        dma((4,)),
        dma((12,)),
        dma((12,)),
        dma((8,)),
        dma((8,)),
        dma((2,)),
        dma((2,)),
    ]


def solution(mesh):
    nx, ny = mesh.shape["gx"], mesh.shape["gy"]

    def body(ocean_state, layer_thickness, vertical_mixing, damping, ocean_blocks):
        shapes = scratch(nx, ny)
        shapes[4] = pltpu.VMEM(ocean_blocks.shape, jnp.int32)
        call = pl.pallas_call(
            functools.partial(kernel, nx, ny),
            out_shape=[
                pltpu.VMEM((2, LEV, ROWS, COLS), f32),
                pltpu.VMEM((ROWS, COLS), f32),
            ],
            in_specs=[pl.BlockSpec(memory_space=pltpu.HBM)] * 5,
            out_specs=[pl.BlockSpec(memory_space=pltpu.VMEM)] * 2,
            scratch_shapes=shapes,
            compiler_params=pltpu.CompilerParams(
                collective_id=0, has_side_effects=True, vmem_limit_bytes=32 * 1024 * 1024
            ),
        )
        operands = [
            pltpu.with_memory_space_constraint(operand, pltpu.HBM)
            for operand in (ocean_state, layer_thickness, vertical_mixing, damping, ocean_blocks)
        ]
        tracer, surface = call(*operands)
        return tuple(
            pl.pallas_call(
                store,
                out_shape=[
                    jax.ShapeDtypeStruct((2, LEV, ROWS, COLS), f32),
                    jax.ShapeDtypeStruct((ROWS, COLS), f32),
                ],
                in_specs=[pl.BlockSpec(memory_space=pltpu.VMEM)] * 2,
                out_specs=[pl.BlockSpec(memory_space=pltpu.HBM)] * 2,
                scratch_shapes=[pltpu.SemaphoreType.DMA((9,))],
                compiler_params=pltpu.CompilerParams(vmem_limit_bytes=16 * 1024 * 1024),
            )(tracer, surface)
        )

    def wrapped(*args):
        with jax.sharding.use_abstract_mesh(mesh.abstract_mesh):
            return jax.shard_map(
                body,
                mesh=mesh,
                in_specs=(P(None, None, "gy", "gx"), P(), P("gy", "gx"), P("gy", "gx"), P()),
                out_specs=(P(None, None, "gy", "gx"), P("gy", "gx")),
                check_vma=False,
            )(*args)

    return wrapped
```
